32 devices in a mesh: dp: 8 (over z, x), expert: 4 (over y, core).
Axes of the slice: x: 2, y: 2, z: 4, core: 2. Of those that a mesh axis runs over, the one named last changes fastest.
Arguments:
- hidden_in: float32 [12288, 1024], P(('dp', 'expert')), may hold values from -6 to 6
- out_grad: float32 [12288, 1024], P(('dp', 'expert')), may hold values from -6 to 6
- segment_ids: int32 [12288], P(('dp', 'expert')), may hold values from 0 to 415, as said below
- parent_ids: int32 [12288], P(('dp', 'expert')), may hold values from 0 to 413, as said below
- positions: int32 [12288], P(('dp', 'expert')), may hold values from 0 to 190, as said below
- expert_ids: int32 [12288, 8], P(('dp', 'expert')), may hold values from 0 to 31, all different within a row; in each aligned block of 384 rows (0 to 383, 384 to 767, ...) at most 144 rows name the same one
- gate_weights: float32 [12288, 8], P(('dp', 'expert')), may hold values from 0.05 to 0.25
- norm_gains: bfloat16 [2, 1024], replicated, may hold values from 0.5 to 1.5
- qkv_weight: bfloat16 [1024, 2048], replicated, may hold values from -0.1875 to 0.1875
- out_weight: bfloat16 [1024, 1024], replicated, may hold values from -1.5 to 1.5
- gate_up_weight: bfloat16 [32, 1024, 1024], P('expert'), may hold values from -0.1875 to 0.1875
- down_weight: bfloat16 [32, 512, 1024], P('expert'), may hold values from -1 to 1
- gain_moment: float32 [2, 1024], replicated, may hold values from 6144 to 737280
- qkv_rows: float32 [1024], replicated, may hold values from 24576 to 2949120
- qkv_cols: float32 [2048], replicated, may hold values from 3072 to 393216
- out_rows: float32 [1024], replicated, may hold values from 1 to 1000
- out_cols: float32 [1024], replicated, may hold values from 1 to 1000
- gateup_rows: float32 [32, 1024], P('expert'), may hold values from 307 to 36864
- gateup_cols: float32 [32, 1024], P('expert'), may hold values from 1 to 1000
- down_rows: float32 [32, 512], P('expert'), may hold values from 1 to 1000
- down_cols: float32 [32, 1024], P('expert'), may hold values from 1 to 1000
Outputs:
- block_out: float32 [12288, 1024], P(('dp', 'expert'))
- input_grad: float32 [12288, 1024], P(('dp', 'expert'))
- update_rms: float32 [5], replicated
- gains_update: float32 [2, 1024], P(None, 'dp')
- gain_moment_new: float32 [2, 1024], P(None, 'dp')
- qkv_new: float32 [1024, 2048], P('dp')
- qkv_rows_new: float32 [1024], P('dp')
- qkv_cols_new: float32 [2048], replicated
- out_new: float32 [1024, 1024], P('dp')
- out_rows_new: float32 [1024], P('dp')
- out_cols_new: float32 [1024], replicated
- gate_up_new: float32 [32, 1024, 1024], P('expert', 'dp')
- gateup_rows_new: float32 [32, 1024], P('expert', 'dp')
- gateup_cols_new: float32 [32, 1024], P('expert')
- down_new: float32 [32, 512, 1024], P('expert', 'dp')
- down_rows_new: float32 [32, 512], P('expert', 'dp')
- down_cols_new: float32 [32, 1024], P('expert')
The draws below stay inside these ranges and needn't reach their ends.
Inputs may be any that keep to these rules, and one draw needn't show every extreme that they name: `segment_ids`: each 384 consecutive tokens form one tree: a trunk of 128 tokens, then four regions of 64 tokens, each a branch followed by two leaves, every segment nonempty. Tree t's trunk is segment 13 t, its branch b (0 to 3) is 13 t + 1 + 3 b, that branch's leaves 13 t + 2 + 3 b and 13 t + 3 + 3 b. `parent_ids`: A leaf token's entry is its branch's segment, a branch token's is its trunk's segment, a trunk token's is its own segment. `positions`: A token's distance from its tree's root along its path: trunk tokens 0 to 127 in order, a branch continues from 128, each of its leaves from the end of the branch. `expert_ids`: each row names 8 different experts. In the rows of one device no expert is named by more than 144 rows, a bound that some block reaches in some devices' rows.
All inputs are finite; a program needn't handle non-finite values.
Results may differ from the reference program's by a relative error of at most 0.019.
Values may be sent and summed in bfloat16 or wider, within the bound.
A program may use at most 256 MiB of HBM per device.

```python
import math
import jax
import jax.numpy as jnp
import numpy as np
from jax import lax

D = 1024
HEADS = 16
KV_HEADS = 8
HEAD_DIM = 64
FF = 512
TOP = 8
TRUNK = 128
REGION = 64
EXPERTS = 32
TREE = 384
TOK_DEV = 384
TOKENS = 12288
CAP = 144
ATT = 1024
QKV = 2048


def tree_layout(key):
    tree_count = TOKENS // TREE
    branch_key, leaf_key = jax.random.split(jax.random.fold_in(key, 11))
    branch_len = jax.random.randint(branch_key, (tree_count, 4), REGION // 4, REGION // 2 + 1)
    leaf_len = jax.random.randint(leaf_key, (tree_count, 4), 1, REGION - branch_len)
    leaf_len = leaf_len.at[:, 0].set(REGION - branch_len[:, 0] - 1)
    offset = jnp.arange(TREE, dtype=jnp.int32)
    region = jnp.clip((offset - TRUNK) // REGION, 0, 3)
    within = (offset - TRUNK - region * REGION)[None, :]
    in_trunk = (offset < TRUNK)[None, :]
    branch_here = jnp.take(branch_len, region, axis=1)
    leaf_here = jnp.take(leaf_len, region, axis=1)
    root_seg = 13 * jnp.arange(tree_count, dtype=jnp.int32)[:, None]
    branch_seg = root_seg + 1 + 3 * region[None, :]
    on_branch = within < branch_here
    on_first = within < branch_here + leaf_here
    segment = jnp.where(in_trunk, root_seg, jnp.where(on_branch, branch_seg, jnp.where(on_first, branch_seg + 1, branch_seg + 2)))
    parent = jnp.where(in_trunk, root_seg, jnp.where(on_branch, root_seg, branch_seg))
    position = jnp.where(in_trunk, offset[None, :], jnp.where(on_first, TRUNK + within, TRUNK + within - leaf_here))
    return (segment.reshape(-1), parent.reshape(-1), position.reshape(-1))


def draw_segment_ids(key, part):
    return tree_layout(key)[0].astype(jnp.int32)


def draw_parent_ids(key, part):
    return tree_layout(key)[1].astype(jnp.int32)


def draw_positions(key, part):
    return tree_layout(key)[2].astype(jnp.int32)


def rising_stat(key, shape, base):
    length = shape[-1]
    span = 10.0
    ramp = jnp.exp(jnp.log(span) * jnp.arange(length, dtype=jnp.float32) / max(length - 1, 1))
    noise = jnp.exp(jax.random.uniform(jax.random.fold_in(key, 23), shape, jnp.float32, jnp.log(0.5), jnp.log(2.0)))
    return (base * ramp * noise).astype(jnp.float32)


def draw_gain_moment(key, part):
    return rising_stat(key, (2, D), 1.0 * TOKENS)


def draw_qkv_rows(key, part):
    return rising_stat(key, (D,), 4.0 * TOKENS)


def draw_gateup_rows(key, part):
    return rising_stat(key, (EXPERTS, D), 0.05 * TOKENS)


def levels(own_key, extent, shards, least, top_value):
    factor_of, own = 1.0, jax.random.fold_in(own_key, 6)
    for axis_at, shards_of in shards:
        steps = jnp.exp(jax.random.uniform(jax.random.fold_in(own, axis_at), (shards_of,), jnp.float32, least / len(shards), top_value / len(shards)))
        factor_of = factor_of * jnp.repeat(steps, extent[axis_at] // shards_of).reshape([-1 if axis == axis_at else 1 for axis in range(len(extent))])
    return factor_of


def deal_out(stream_key, own, number, rows, amount, top, bound, slope):
    sequence = jax.random.permutation(stream_key, amount)
    crowded, ordinary = portions_of(amount, rows * top, bound, slope, True), portions_of(amount, rows * top, bound, slope, False)
    places = jnp.arange(amount)

    def named(tallies, rotation):
        used = int((tallies > 0).sum())
        fixed = max(1, used // 4)
        passed = fixed + (places - fixed + rotation * (used - fixed)) % max(1, amount - fixed)
        return jnp.zeros((amount,), jnp.int32).at[sequence[jnp.where(places < fixed, places, passed)]].set(jnp.asarray(tallies, jnp.int32))

    tallies = jnp.where(number % 4 == 0, named(crowded, number // 4), named(ordinary, number - number // 4 - 1))
    mixed = jax.random.permutation(jax.random.fold_in(own, 3), amount)
    source_of, taker = mixed[0:amount // 2 * 2:2], mixed[1:amount // 2 * 2:2]
    slack = jnp.minimum(tallies[source_of] - 1, bound - tallies[taker]) // 2
    slack = jnp.where((source_of == sequence[0]) | (taker == sequence[0]) | (tallies[taker] == 0), 0, jnp.maximum(slack, 0))
    passed = jax.random.randint(jax.random.fold_in(own, 4), (amount // 2,), 0, 1 << 20) % (slack + 1)
    tallies = tallies.at[source_of].add(-passed).at[taker].add(passed)
    members = jnp.searchsorted(jnp.cumsum(tallies), jnp.arange(rows * top), side="right").astype(jnp.int32)
    listing = members.reshape(top, rows).T
    listing = listing[jax.random.permutation(jax.random.fold_in(own, 1), rows)]
    rotation = jax.random.randint(jax.random.fold_in(own, 2), (rows, 1), 0, top)
    return jnp.take_along_axis(listing, (jnp.arange(top)[None, :] + rotation) % top, axis=1)


def portions_of(count, total, most, lean, full):
    weights = [(1 << 20) // math.isqrt(standing ** lean) + 1 for standing in range(1, count + 1)]
    largest = most if full else min(most, max(-(-total // count), total * weights[0] // sum(weights)))
    least = 1 if total - largest >= count - 1 else 0
    given, rest = [largest] + [least] * (count - 1), total - largest - least * (count - 1)
    while rest > 0:
        candidates = [i for i in range(1, count) if given[i] < largest] or [i for i in range(1, count) if given[i] < most]
        mass, budget = sum([weights[i] for i in candidates]), rest
        for i in candidates:
            more = min(most - given[i], max(1, budget * weights[i] // mass), rest)
            given[i] = given[i] + more
            rest = rest - more
    return np.array(given)


def normal_values(stream_key, extent, deviation, limit, cuts=(), held_as=jnp.bfloat16):
    level = levels(stream_key, extent, cuts, -0.22, 0.18) if cuts else 1.0
    result = jax.random.normal(stream_key, extent, jnp.float32) * deviation * level
    return jnp.minimum(jnp.maximum(result, -limit), limit).astype(held_as)


def setup_inputs(seed: int = 0) -> dict:
    key_of = jax.random.split(jax.random.key(seed), 22)
    hidden_in = normal_values(key_of[0], (TOKENS, D), 1.0, 6.0, ((0, 32),), jnp.float32)
    out_grad = normal_values(key_of[1], (TOKENS, D), 1.0, 6.0, ((0, 32),), jnp.float32)
    segment_ids = draw_segment_ids(jax.random.fold_in(key_of[21], 71), 0)
    parent_ids = draw_parent_ids(jax.random.fold_in(key_of[21], 71), 0)
    positions = draw_positions(jax.random.fold_in(key_of[21], 71), 0)
    expert_ids_keys = jax.random.split(jax.random.fold_in(key_of[5], 1), TOKENS // TOK_DEV)
    expert_ids_turns = jax.random.permutation(jax.random.fold_in(key_of[5], 3), TOKENS // TOK_DEV)
    expert_ids = jax.vmap(lambda own, number: deal_out(jax.random.fold_in(key_of[5], 2), own, number, TOK_DEV, EXPERTS, TOP, CAP, 2))(expert_ids_keys, expert_ids_turns).reshape((TOKENS, TOP))
    gate_weights = jnp.clip(0.05 + 0.2 * jax.random.uniform(key_of[6], (TOKENS, TOP), jnp.float32) ** levels(key_of[6], (TOKENS, TOP), ((0, 32),), -0.2, 0.2), 0.05, 0.25)
    norm_gains = jnp.clip(1.0 + 0.1 * jax.random.normal(key_of[7], (2, D), jnp.float32), 0.5, 1.5).astype(jnp.bfloat16)
    qkv_weight = normal_values(key_of[8], (D, QKV), D ** -0.5, 0.1875)
    out_weight = normal_values(key_of[9], (ATT, D), (max(1, ATT // 64)) ** -0.5, 1.5)
    gate_up_weight = normal_values(key_of[10], (EXPERTS, D, 2 * FF), D ** -0.5, 0.1875, ((0, 4),))
    down_weight = normal_values(key_of[11], (EXPERTS, FF, D), (FF // 16) ** -0.5, 1.0, ((0, 4),))
    gain_moment = draw_gain_moment(jax.random.fold_in(key_of[21], 71), 0)
    qkv_rows = draw_qkv_rows(jax.random.fold_in(key_of[21], 71), 0)
    qkv_cols = jnp.clip(jnp.exp(jax.random.uniform(key_of[14], (QKV,), jnp.float32, math.log(3072.0), math.log(393216.0))), 3072.0, 393216.0)
    out_rows = jnp.clip(jnp.exp(jax.random.uniform(key_of[15], (ATT,), jnp.float32, math.log(1.0), math.log(1000.0))), 1.0, 1000.0)
    out_cols = jnp.clip(jnp.exp(jax.random.uniform(key_of[16], (D,), jnp.float32, math.log(1.0), math.log(1000.0))), 1.0, 1000.0)
    gateup_rows = draw_gateup_rows(jax.random.fold_in(key_of[21], 71), 0)
    gateup_cols = jnp.clip(jnp.exp(math.log(1000.0) - 6.9077553 * jax.random.uniform(key_of[18], (EXPERTS, 2 * FF), jnp.float32) ** levels(key_of[18], (EXPERTS, 2 * FF), ((0, 4),), -0.2, 0.2)), 1.0, 1000.0)
    down_rows = jnp.clip(jnp.exp(math.log(1000.0) - 6.9077553 * jax.random.uniform(key_of[19], (EXPERTS, FF), jnp.float32) ** levels(key_of[19], (EXPERTS, FF), ((0, 4),), -0.2, 0.2)), 1.0, 1000.0)
    down_cols = jnp.clip(jnp.exp(math.log(1000.0) - 6.9077553 * jax.random.uniform(key_of[20], (EXPERTS, D), jnp.float32) ** levels(key_of[20], (EXPERTS, D), ((0, 4),), -0.2, 0.2)), 1.0, 1000.0)
    return dict(hidden_in=hidden_in, out_grad=out_grad, segment_ids=segment_ids, parent_ids=parent_ids, positions=positions, expert_ids=expert_ids, gate_weights=gate_weights, norm_gains=norm_gains, qkv_weight=qkv_weight, out_weight=out_weight, gate_up_weight=gate_up_weight, down_weight=down_weight, gain_moment=gain_moment, qkv_rows=qkv_rows, qkv_cols=qkv_cols, out_rows=out_rows, out_cols=out_cols, gateup_rows=gateup_rows, gateup_cols=gateup_cols, down_rows=down_rows, down_cols=down_cols)


PRECISE = lax.Precision.HIGHEST
EPS_NORM = 1e-06
EPS_STAT = 1e-30
STAT_DECAY = 0.5
LEARN_RATE = 0.5
CLIP_LEVEL = 0.05
ROPE_BASE = 10000.0
MASKED = -1e+30

@jax.custom_vjp
def low(v):
    return lax.optimization_barrier(v.astype(jnp.bfloat16)).astype(jnp.float32)

@jax.custom_vjp
def low_back(v):
    return v

def low_keep(v):
    return (low(v), None)

def low_pass(kept, grad):
    return (grad,)

def back_keep(v):
    return (v, None)

def back_low(kept, grad):
    return (low(grad),)
low.defvjp(low_keep, low_pass)
low_back.defvjp(back_keep, back_low)

def rms_norm(values, gain_vec):
    inverse = lax.rsqrt(lax.optimization_barrier(jnp.mean(values * values, axis=-1, keepdims=True)) + EPS_NORM)
    return values * inverse * gain_vec

def rotary(vectors, places):
    half_dim = HEAD_DIM // 2
    frequency = jnp.exp(jnp.arange(half_dim, dtype=jnp.float32) * (-2.0 * math.log(ROPE_BASE) / HEAD_DIM))
    angles = places.astype(jnp.float32)[:, None] * frequency[None, :]
    cos_table = jnp.cos(angles)[:, None, :]
    sine_table = jnp.sin(angles)[:, None, :]
    front_half = vectors[..., :half_dim]
    back_half = vectors[..., half_dim:]
    return jnp.concatenate([front_half * cos_table - back_half * sine_table, back_half * cos_table + front_half * sine_table], axis=-1)

def tree_attention(queries, key_rows, value_rows, segments, parents, places):
    raw_scores = jnp.einsum('qhgd,khd->hgqk', queries, key_rows, precision=PRECISE) * HEAD_DIM ** (-0.5)
    scores = low_back(raw_scores)
    allowed = (segments[None, :] == segments[:, None]) | (segments[None, :] == parents[:, None]) | (segments == parents)[None, :]
    allowed = allowed & (places[None, :] <= places[:, None])
    weights = low(jax.nn.softmax(jnp.where(allowed, scores, MASKED), axis=-1))
    return jnp.einsum('hgqk,khd->qhgd', weights, value_rows, precision=PRECISE)

def factored_step(gradient, rows_old, cols_old):
    squares = gradient * gradient + EPS_STAT
    rows_new = STAT_DECAY * rows_old + (1.0 - STAT_DECAY) * lax.optimization_barrier(jnp.mean(squares, axis=-1))
    cols_new = STAT_DECAY * cols_old + (1.0 - STAT_DECAY) * lax.optimization_barrier(jnp.mean(squares, axis=-2))
    row_mean = lax.optimization_barrier(jnp.mean(rows_new, axis=-1, keepdims=True))
    direction = gradient * lax.rsqrt(rows_new / row_mean)[..., :, None] * lax.rsqrt(cols_new)[..., None, :]
    return (direction, rows_new, cols_new)

def clipped_change(direction):
    root = jnp.sqrt(jnp.mean(direction * direction))
    return (-LEARN_RATE * direction / jnp.maximum(1.0, root / CLIP_LEVEL), root)

def reference(hidden_in, out_grad, segment_ids, parent_ids, positions, expert_ids, gate_weights, norm_gains, qkv_weight, out_weight, gate_up_weight, down_weight, gain_moment, qkv_rows, qkv_cols, out_rows, out_cols, gateup_rows, gateup_cols, down_rows, down_cols):
    tree_count = TOKENS // TREE
    block_count = TOKENS // TOK_DEV
    group_size = HEADS // KV_HEADS
    kv_width = KV_HEADS * HEAD_DIM
    flat_ids = expert_ids.reshape(block_count, TOK_DEV * TOP)
    onehot = (flat_ids[:, :, None] == jnp.arange(EXPERTS, dtype=jnp.int32)[None, None, :]).astype(jnp.int32)
    slot_index = lax.optimization_barrier(jnp.sum((jnp.cumsum(onehot, axis=1) - onehot) * onehot, axis=2))
    column = jnp.arange(block_count, dtype=jnp.int32)[:, None] * CAP + slot_index
    slot_table = jnp.full((EXPERTS, block_count * CAP), TOKENS * TOP, dtype=jnp.int32)
    slot_table = slot_table.at[flat_ids.reshape(-1), column.reshape(-1)].set(jnp.arange(TOKENS * TOP, dtype=jnp.int32))
    gate_ext = jnp.concatenate([gate_weights.reshape(-1), jnp.zeros((1,), jnp.float32)])
    attend_tree = jax.checkpoint(tree_attention)
    tree_segments = segment_ids.reshape(tree_count, TREE)
    tree_parents = parent_ids.reshape(tree_count, TREE)
    tree_places = positions.reshape(tree_count, TREE)

    def forward(hidden, gains, qkv_w, out_w, gate_up_w, down_w):
        normed = low(rms_norm(hidden, gains[0]))
        projected = low_back(jnp.dot(normed, qkv_w, precision=PRECISE))
        queries = projected[:, :ATT].reshape(TOKENS, HEADS, HEAD_DIM)
        key_rows = projected[:, ATT:ATT + kv_width].reshape(TOKENS, KV_HEADS, HEAD_DIM)
        value_rows = low(projected[:, ATT + kv_width:]).reshape(tree_count, TREE, KV_HEADS, HEAD_DIM)
        queries = low(rotary(queries, positions)).reshape(tree_count, TREE, KV_HEADS, group_size, HEAD_DIM)
        key_rows = low(rotary(key_rows, positions)).reshape(tree_count, TREE, KV_HEADS, HEAD_DIM)
        attended = lax.map(lambda pieces: attend_tree(*pieces), (queries, key_rows, value_rows, tree_segments, tree_parents, tree_places))
        attended = low(low_back(attended.reshape(TOKENS, ATT)))
        middle = hidden + low_back(jnp.dot(attended, out_w, precision=PRECISE))
        normed_ffn = low(rms_norm(middle, gains[1]))
        padded = jnp.concatenate([normed_ffn, jnp.zeros((1, D), jnp.float32)], axis=0)

        def one_expert(inputs):
            expert_slots, weight_gu, weight_down = inputs
            token_index = expert_slots // TOP
            rows_in = low_back(padded[token_index])
            gate_up = low_back(jnp.dot(rows_in, weight_gu, precision=PRECISE))
            activated = low(jax.nn.silu(gate_up[:, :FF]) * gate_up[:, FF:])
            produced = low(low_back(jnp.dot(activated, weight_down, precision=PRECISE)))
            return produced * gate_ext[expert_slots][:, None]
        weighted = lax.map(jax.checkpoint(one_expert), (slot_table, gate_up_w, down_w))
        mix_total = jnp.zeros((TOKENS + 1, D), jnp.float32).at[(slot_table // TOP).reshape(-1)].add(weighted.reshape(-1, D))
        return middle + mix_total[:TOKENS]
    block_out, pullback = jax.vjp(forward, hidden_in, norm_gains.astype(jnp.float32), qkv_weight.astype(jnp.float32), out_weight.astype(jnp.float32), gate_up_weight.astype(jnp.float32), down_weight.astype(jnp.float32))
    input_grad, gains_grad, qkv_wgrad, out_wgrad, gate_up_wgrad, down_wgrad = pullback(out_grad)
    gain_moment_new = STAT_DECAY * gain_moment + (1.0 - STAT_DECAY) * (gains_grad * gains_grad + EPS_STAT)
    gains_update, gains_root = clipped_change(gains_grad * lax.rsqrt(gain_moment_new))
    qkv_dir, qkv_rows_new, qkv_cols_new = factored_step(qkv_wgrad, qkv_rows, qkv_cols)
    qkv_change, qkv_root = clipped_change(qkv_dir)
    qkv_new = qkv_weight.astype(jnp.float32) + qkv_change
    out_dir, out_rows_new, out_cols_new = factored_step(out_wgrad, out_rows, out_cols)
    out_change, out_root = clipped_change(out_dir)
    out_new = out_weight.astype(jnp.float32) + out_change
    gateup_dir, gateup_rows_new, gateup_cols_new = factored_step(gate_up_wgrad, gateup_rows, gateup_cols)
    gateup_change, gateup_root = clipped_change(gateup_dir)
    gate_up_new = gate_up_weight.astype(jnp.float32) + gateup_change
    down_dir, down_rows_new, down_cols_new = factored_step(down_wgrad, down_rows, down_cols)
    down_change, down_root = clipped_change(down_dir)
    down_new = down_weight.astype(jnp.float32) + down_change
    update_rms = jnp.stack([gains_root, qkv_root, out_root, gateup_root, down_root])
    return (block_out, input_grad, update_rms, gains_update, gain_moment_new, qkv_new, qkv_rows_new, qkv_cols_new, out_new, out_rows_new, out_cols_new, gate_up_new, gateup_rows_new, gateup_cols_new, down_new, down_rows_new, down_cols_new)
```

```python
import math

import jax
import jax.numpy as jnp
from jax import lax
from jax.sharding import PartitionSpec as P

D = 1024
HEADS = 16
KV_HEADS = 8
HEAD_DIM = 64
FF = 512
TOP = 8


EPS_NORM = 1e-06
EPS_STAT = 1e-30
STAT_DECAY = 0.5
LEARN_RATE = 0.5
CLIP_LEVEL = 0.05
ROPE_BASE = 10000.0
MASKED = -1e30


def rotation_tables(places):
    half_dim = HEAD_DIM // 2
    frequency = jnp.exp(
        jnp.arange(half_dim, dtype=jnp.float32) * (-2.0 * math.log(ROPE_BASE) / HEAD_DIM)
    )
    angles = places.astype(jnp.float32)[:, None] * frequency[None, :]
    return (jnp.cos(angles)[:, None, :], jnp.sin(angles)[:, None, :])


def rotate(vectors, cos_table, sine_table):
    half_dim = vectors.shape[-1] // 2
    front_half = vectors[..., :half_dim]
    back_half = vectors[..., half_dim:]
    return jnp.concatenate(
        [
            front_half * cos_table - back_half * sine_table,
            back_half * cos_table + front_half * sine_table,
        ],
        axis=-1,
    )


def rotate_back(gradients, cos_table, sine_table):
    half_dim = gradients.shape[-1] // 2
    front_half = gradients[..., :half_dim]
    back_half = gradients[..., half_dim:]
    return jnp.concatenate(
        [
            front_half * cos_table + back_half * sine_table,
            back_half * cos_table - front_half * sine_table,
        ],
        axis=-1,
    )


def path_mask(segments, parents, places):
    allowed = (
        (segments[None, :] == segments[:, None])
        | (segments[None, :] == parents[:, None])
        | (segments == parents)[None, :]
    )
    return allowed & (places[None, :] <= places[:, None])


def masked_scores(queries, key_rows, allowed, score_scale):
    raw_scores = (
        jnp.einsum("qhgd,khd->hgqk", queries, key_rows, preferred_element_type=jnp.float32)
        * score_scale
    )
    return jnp.where(allowed, raw_scores, MASKED)


def norm_back(values, inverse, gain_vec, gradient):
    weighted = gradient * gain_vec
    gain_grad = jnp.sum(gradient * values * inverse, axis=0)
    value_grad = inverse * weighted - values * inverse * inverse * inverse * jnp.mean(
        weighted * values, axis=-1, keepdims=True
    )
    return (value_grad, gain_grad)


def up_project(received, weights):
    return jnp.einsum("secd,edf->secf", received, weights, preferred_element_type=jnp.float32)


def activate(gate_up):
    return (jax.nn.silu(gate_up[..., :FF]) * gate_up[..., FF:]).astype(jnp.bfloat16)


def own_share(matrix, share_count, share_index, along):
    width = matrix.shape[along] // share_count
    return lax.dynamic_slice_in_dim(matrix, share_index * width, width, along)


def swap(values, axis, mask):
    count = lax.axis_size(axis)
    return lax.ppermute(values, axis, [(i, i ^ mask) for i in range(count)])


def swap_pair(values):
    return swap(values, "dp", 1)


def swap_chip(values):
    return swap(values, "expert", 2)


def swap_core(values):
    return swap(values, "expert", 1)


def gather_group(shard):
    from_pair = swap_pair(shard)
    from_chip = swap_chip(shard)
    half = shard.shape[0] // 2
    from_both = jnp.concatenate([swap_chip(from_pair[:half]), swap_pair(from_chip[half:])], axis=0)
    here = [shard, from_chip, from_pair, from_both]
    out = []
    for piece in here:
        out += [piece, swap_core(piece)]
    return out


def plus(a, b):
    return (a.astype(jnp.float32) + b.astype(jnp.float32)).astype(jnp.bfloat16)


def scatter_group(partial):
    partial = partial.reshape((4, 2) + partial.shape[1:])
    summed = [plus(partial[i, 0], swap_core(partial[i, 1])) for i in range(4)]
    half = partial.shape[2] // 2
    for_chip = jnp.concatenate(
        [plus(summed[1][:half], swap_pair(summed[3][:half])), summed[1][half:]], axis=0
    )
    for_pair = jnp.concatenate(
        [summed[2][:half], plus(summed[2][half:], swap_chip(summed[3][half:]))], axis=0
    )
    return (
        summed[0].astype(jnp.float32)
        + swap_chip(for_chip).astype(jnp.float32)
        + swap_pair(for_pair).astype(jnp.float32)
    )


def by_owner(matrix):
    count = lax.axis_size("dp")
    return matrix.reshape(count, matrix.shape[0] // count, matrix.shape[1])


def halve(blocks, axis, mask):
    bit = lax.rem(lax.axis_index(axis) // mask, 2)
    keep = lax.dynamic_index_in_dim(blocks, bit, 1, keepdims=False)
    give = lax.dynamic_index_in_dim(blocks, 1 - bit, 1, keepdims=False)
    return keep, swap(give, axis, mask)


def reduce_expert(blocks):
    count = blocks.shape[0]
    rest = blocks.shape[1:]
    low = 2
    while low < count:
        keep, got = halve(blocks.reshape((-1, 2, 2) + rest), "dp", low)
        blocks = plus(keep, got)
        low *= 2
    return halve(blocks.reshape((1, 2) + rest), "dp", 1)[0][0], halve(blocks.reshape((1, 2) + rest), "dp", 1)[1][0]


def reduce_dense(blocks):
    count, rows, columns = blocks.shape
    blocks = blocks.reshape(count, 2, 2, rows // 4, columns)
    keep, got = halve(jnp.moveaxis(blocks, 2, 1), "expert", 1)
    keep, got = halve(plus(keep, got), "expert", 2)
    blocks = plus(keep, got)
    low = 1
    while low < count:
        keep, got = halve(blocks.reshape((-1, 2, 1) + blocks.shape[1:]), "dp", low)
        blocks = plus(keep, got).reshape((-1,) + blocks.shape[1:])
        low *= 2
    mine = blocks[0]
    chip = lax.axis_index("expert") // 2
    core = lax.rem(lax.axis_index("expert"), 2)
    other = swap_chip(mine)
    both = jnp.where(chip == 0, jnp.stack([mine, other]), jnp.stack([other, mine]))
    across = swap_core(both)
    all_four = jnp.where(core == 0, jnp.stack([both, across], 1), jnp.stack([across, both], 1))
    return all_four.reshape(rows, columns)


def per_device(
    hidden_in,
    out_grad,
    segment_ids,
    parent_ids,
    positions,
    expert_ids,
    gate_weights,
    norm_gains,
    qkv_weight,
    out_weight,
    gate_up_weight,
    down_weight,
    gain_moment,
    qkv_rows,
    qkv_cols,
    out_rows,
    out_cols,
    gateup_rows,
    gateup_cols,
    down_rows,
    down_cols,
):
    rows_here = hidden_in.shape[0]
    att_width = HEADS * HEAD_DIM
    kv_width = KV_HEADS * HEAD_DIM
    group_size = HEADS // KV_HEADS
    score_scale = HEAD_DIM ** (-0.5)
    cos_table, sine_table = rotation_tables(positions)
    gain_attn = norm_gains[0].astype(jnp.float32)
    gain_ffn = norm_gains[1].astype(jnp.float32)
    inverse_attn = lax.rsqrt(jnp.mean(hidden_in * hidden_in, axis=-1, keepdims=True) + EPS_NORM)
    normed = (hidden_in * inverse_attn * gain_attn).astype(jnp.bfloat16)
    projected = jnp.dot(normed, qkv_weight, preferred_element_type=jnp.float32)
    queries = rotate(
        projected[:, :att_width].reshape(rows_here, HEADS, HEAD_DIM), cos_table, sine_table
    )
    queries = queries.astype(jnp.bfloat16).reshape(rows_here, KV_HEADS, group_size, HEAD_DIM)
    key_rows = rotate(
        projected[:, att_width : att_width + kv_width].reshape(rows_here, KV_HEADS, HEAD_DIM),
        cos_table,
        sine_table,
    ).astype(jnp.bfloat16)
    value_rows = (
        projected[:, att_width + kv_width :]
        .reshape(rows_here, KV_HEADS, HEAD_DIM)
        .astype(jnp.bfloat16)
    )
    allowed = path_mask(segment_ids, parent_ids, positions)
    scores = masked_scores(queries, key_rows, allowed, score_scale)
    row_max = jnp.max(scores, axis=-1, keepdims=True)
    exponent = jnp.exp(scores - row_max)
    row_total = jnp.sum(exponent, axis=-1, keepdims=True)
    log_total = row_max + jnp.log(row_total)
    probs_low = (exponent / row_total).astype(jnp.bfloat16)
    attended = jnp.einsum(
        "hgqk,khd->qhgd", probs_low, value_rows, preferred_element_type=jnp.float32
    )
    attended = attended.reshape(rows_here, att_width).astype(jnp.bfloat16)
    middle = hidden_in + jnp.dot(attended, out_weight, preferred_element_type=jnp.float32)
    inverse_ffn = lax.rsqrt(jnp.mean(middle * middle, axis=-1, keepdims=True) + EPS_NORM)
    normed_ffn = (middle * inverse_ffn * gain_ffn).astype(jnp.bfloat16)
    experts_here = gate_up_weight.shape[0]
    groups = lax.axis_size("expert")
    total_experts = experts_here * groups
    capacity = 3 * rows_here * TOP // (2 * total_experts)
    half_experts = experts_here // 2
    pair_bit = lax.rem(lax.axis_index("dp"), 2)
    first_local = pair_bit * half_experts
    first_expert = lax.axis_index("expert") * experts_here + first_local
    routing = jnp.concatenate([expert_ids.T.astype(jnp.float32), gate_weights.T], axis=0)
    routes = jnp.stack(gather_group(routing))
    named_ids = routes[:, :TOP]
    my_experts = (first_expert + jnp.arange(half_experts, dtype=jnp.int32)).astype(jnp.float32)
    hits = named_ids[:, None, :, :] == my_experts[None, :, None, None]
    named = jnp.any(hits, axis=2)
    weight_of = jnp.sum(jnp.where(hits, routes[:, None, TOP:], 0.0), axis=2)
    before = (
        jnp.arange(rows_here, dtype=jnp.int32)[:, None]
        < jnp.arange(rows_here, dtype=jnp.int32)[None, :]
    ).astype(jnp.bfloat16)
    rank = jnp.einsum(
        "sjt,tu->sju", named.astype(jnp.bfloat16), before, preferred_element_type=jnp.float32
    )
    code = jnp.where(named, rank, -1.0)
    places = jnp.arange(capacity, dtype=jnp.int32).astype(jnp.float32)
    chosen = code[:, :, None, :] == places[None, None, :, None]
    slot_weight = jnp.sum(jnp.where(chosen, weight_of[:, :, None, :], 0.0), axis=-1)
    pick = chosen.astype(jnp.bfloat16)
    grads_all = jnp.stack(gather_group(out_grad.astype(jnp.bfloat16)))
    tokens_all = jnp.stack(gather_group(normed_ffn))
    mixed = None
    back = None
    own_parts = []
    other_parts = []
    for j in range(half_experts):
        up_w = lax.dynamic_index_in_dim(gate_up_weight, first_local + j, 0, keepdims=False)
        down_w = lax.dynamic_index_in_dim(down_weight, first_local + j, 0, keepdims=False)
        pick_j = pick[:, j]
        weight_j = slot_weight[:, j][..., None]
        received = jnp.einsum(
            "sct,std->scd", pick_j, tokens_all, preferred_element_type=jnp.float32
        ).astype(jnp.bfloat16)
        arrived = (
            jnp.einsum("sct,std->scd", pick_j, grads_all, preferred_element_type=jnp.float32)
            * weight_j
        ).astype(jnp.bfloat16)
        gate_up = jnp.einsum("scd,df->scf", received, up_w, preferred_element_type=jnp.float32)
        act_grad = jnp.einsum("scd,fd->scf", arrived, down_w, preferred_element_type=jnp.float32)
        gate_part = gate_up[..., :FF]
        up_part = gate_up[..., FF:]
        sigmoid_gate = jax.nn.sigmoid(gate_part)
        silu_gate = gate_part * sigmoid_gate
        activated = (silu_gate * up_part).astype(jnp.bfloat16)
        gate_grad = act_grad * up_part * sigmoid_gate * (1.0 + gate_part * (1.0 - sigmoid_gate))
        gate_up_grad = jnp.concatenate([gate_grad, act_grad * silu_gate], axis=-1).astype(
            jnp.bfloat16
        )
        down_wgrad = jnp.einsum(
            "scf,scd->fd", activated, arrived, preferred_element_type=jnp.float32
        ).astype(jnp.bfloat16)
        gate_up_wgrad = jnp.einsum(
            "scd,scf->df", received, gate_up_grad, preferred_element_type=jnp.float32
        ).astype(jnp.bfloat16)
        own, other = reduce_expert(
            jnp.concatenate([by_owner(gate_up_wgrad), by_owner(down_wgrad)], axis=1)
        )
        own_parts.append(own)
        other_parts.append(other)
        input_slots = jnp.einsum(
            "scf,df->scd", gate_up_grad, up_w, preferred_element_type=jnp.float32
        ).astype(jnp.bfloat16)
        back_j = jnp.einsum("sct,scd->std", pick_j, input_slots, preferred_element_type=jnp.float32)
        produced = (
            jnp.einsum("scf,fd->scd", activated, down_w, preferred_element_type=jnp.float32)
            * weight_j
        ).astype(jnp.bfloat16)
        mixed_j = jnp.einsum("sct,scd->std", pick_j, produced, preferred_element_type=jnp.float32)
        mixed = mixed_j if mixed is None else mixed + mixed_j
        back = back_j if back is None else back + back_j
    normed_ffn_grad = scatter_group(back.astype(jnp.bfloat16))
    block_out = middle + scatter_group(mixed.astype(jnp.bfloat16))
    middle_norm_grad, gain_ffn_grad = norm_back(middle, inverse_ffn, gain_ffn, normed_ffn_grad)
    middle_grad = out_grad + middle_norm_grad
    branch_grad = middle_grad.astype(jnp.bfloat16)
    out_wgrad = jnp.einsum("ta,tc->ac", attended, branch_grad, preferred_element_type=jnp.float32)
    attended_grad = jnp.einsum(
        "tc,ac->ta", branch_grad, out_weight, preferred_element_type=jnp.float32
    )
    attended_grad = attended_grad.astype(jnp.bfloat16).reshape(
        rows_here, KV_HEADS, group_size, HEAD_DIM
    )
    scores = masked_scores(queries, key_rows, allowed, score_scale)
    probs = jnp.exp(scores - log_total)
    probs_low = probs.astype(jnp.bfloat16)
    prob_grad = jnp.einsum(
        "qhgd,khd->hgqk", attended_grad, value_rows, preferred_element_type=jnp.float32
    )
    row_dot = jnp.sum(probs * prob_grad, axis=-1, keepdims=True)
    score_grad = (probs * (prob_grad - row_dot)).astype(jnp.bfloat16)
    query_grad = (
        jnp.einsum("hgqk,khd->qhgd", score_grad, key_rows, preferred_element_type=jnp.float32)
        * score_scale
    )
    key_grad = (
        jnp.einsum("hgqk,qhgd->khd", score_grad, queries, preferred_element_type=jnp.float32)
        * score_scale
    )
    value_grad = jnp.einsum(
        "hgqk,qhgd->khd", probs_low, attended_grad, preferred_element_type=jnp.float32
    )
    projected_grad = jnp.concatenate(
        [
            rotate_back(
                query_grad.reshape(rows_here, HEADS, HEAD_DIM), cos_table, sine_table
            ).reshape(rows_here, att_width),
            rotate_back(key_grad, cos_table, sine_table).reshape(rows_here, kv_width),
            value_grad.reshape(rows_here, kv_width),
        ],
        axis=1,
    ).astype(jnp.bfloat16)
    qkv_wgrad = jnp.einsum("tc,tq->cq", normed, projected_grad, preferred_element_type=jnp.float32)
    normed_grad = jnp.einsum(
        "tq,cq->tc", projected_grad, qkv_weight, preferred_element_type=jnp.float32
    )
    hidden_norm_grad, gain_attn_grad = norm_back(hidden_in, inverse_attn, gain_attn, normed_grad)
    input_grad = middle_grad + hidden_norm_grad
    gains_grad = jnp.stack([gain_attn_grad, gain_ffn_grad])
    dp_count = lax.axis_size("dp")
    dp_index = lax.axis_index("dp")
    own = jnp.stack(own_parts).astype(jnp.float32)
    other = jnp.stack(other_parts).astype(jnp.float32)
    parts = jnp.where(
        pair_bit == 0, jnp.concatenate([own, other]), jnp.concatenate([other, own])
    )
    gateup_part = parts[:, : D // dp_count]
    down_part = parts[:, D // dp_count :]
    gateup_square = gateup_part * gateup_part + EPS_STAT
    gateup_rows_new = STAT_DECAY * own_share(gateup_rows, dp_count, dp_index, 1) + (
        1.0 - STAT_DECAY
    ) * jnp.mean(gateup_square, axis=-1)
    down_square = down_part * down_part + EPS_STAT
    down_rows_new = STAT_DECAY * own_share(down_rows, dp_count, dp_index, 1) + (
        1.0 - STAT_DECAY
    ) * jnp.mean(down_square, axis=-1)
    dense_own = jnp.concatenate(
        [reduce_dense(by_owner(qkv_wgrad.astype(jnp.bfloat16))), reduce_dense(by_owner(out_wgrad.astype(jnp.bfloat16)))], axis=1
    ).astype(jnp.float32)
    qkv_own = dense_own[:, : qkv_wgrad.shape[1]]
    out_own = dense_own[:, qkv_wgrad.shape[1] :]
    qkv_square = qkv_own * qkv_own + EPS_STAT
    out_square = out_own * out_own + EPS_STAT
    qkv_rows_new = STAT_DECAY * own_share(qkv_rows, dp_count, dp_index, 0) + (
        1.0 - STAT_DECAY
    ) * jnp.mean(qkv_square, axis=1)
    out_rows_new = STAT_DECAY * own_share(out_rows, dp_count, dp_index, 0) + (
        1.0 - STAT_DECAY
    ) * jnp.mean(out_square, axis=1)
    gains_full = lax.psum(gains_grad, ("dp", "expert"))
    gains_own = own_share(gains_full, dp_count, dp_index, 1)
    qkv_col_sum, out_col_sum, qkv_row_sum, out_row_sum = lax.psum(
        (
            jnp.sum(qkv_square, axis=0),
            jnp.sum(out_square, axis=0),
            jnp.sum(qkv_rows_new),
            jnp.sum(out_rows_new),
        ),
        "dp",
    )
    qkv_cols_new = STAT_DECAY * qkv_cols + (1.0 - STAT_DECAY) * (qkv_col_sum / D)
    qkv_row_mean = qkv_row_sum / D
    out_cols_new = STAT_DECAY * out_cols + (1.0 - STAT_DECAY) * (out_col_sum / att_width)
    out_row_mean = out_row_sum / att_width
    gateup_col_sum, gateup_row_sum, down_col_sum, down_row_sum = lax.psum(
        (
            jnp.sum(gateup_square, axis=1),
            jnp.sum(gateup_rows_new, axis=1),
            jnp.sum(down_square, axis=1),
            jnp.sum(down_rows_new, axis=1),
        ),
        "dp",
    )
    gateup_cols_new = STAT_DECAY * gateup_cols + (1.0 - STAT_DECAY) * (gateup_col_sum / D)
    gateup_row_mean = gateup_row_sum / D
    gateup_step = (
        gateup_part
        * lax.rsqrt(gateup_rows_new / gateup_row_mean[:, None])[:, :, None]
        * lax.rsqrt(gateup_cols_new)[:, None, :]
    )
    down_cols_new = STAT_DECAY * down_cols + (1.0 - STAT_DECAY) * (down_col_sum / FF)
    down_row_mean = down_row_sum / FF
    down_step = (
        down_part
        * lax.rsqrt(down_rows_new / down_row_mean[:, None])[:, :, None]
        * lax.rsqrt(down_cols_new)[:, None, :]
    )
    qkv_step = (
        qkv_own * lax.rsqrt(qkv_rows_new / qkv_row_mean)[:, None] * lax.rsqrt(qkv_cols_new)[None, :]
    )
    out_step = (
        out_own * lax.rsqrt(out_rows_new / out_row_mean)[:, None] * lax.rsqrt(out_cols_new)[None, :]
    )
    gain_moment_new = STAT_DECAY * own_share(gain_moment, dp_count, dp_index, 1) + (
        1.0 - STAT_DECAY
    ) * (gains_own * gains_own + EPS_STAT)
    gains_step = gains_own * lax.rsqrt(gain_moment_new)
    dense_flag = (lax.axis_index("expert") == 0).astype(jnp.float32)
    dense_squares, expert_squares = lax.psum(
        (
            jnp.stack(
                [
                    jnp.sum(gains_step * gains_step),
                    jnp.sum(qkv_step * qkv_step),
                    jnp.sum(out_step * out_step),
                ]
            )
            * dense_flag,
            jnp.stack([jnp.sum(gateup_step * gateup_step), jnp.sum(down_step * down_step)]),
        ),
        ("dp", "expert"),
    )
    element_counts = jnp.array(
        [
            2 * D,
            D * qkv_weight.shape[1],
            att_width * D,
            total_experts * D * 2 * FF,
            total_experts * FF * D,
        ],
        jnp.float32,
    )
    update_rms = jnp.sqrt(jnp.concatenate([dense_squares, expert_squares]) / element_counts)
    factors = LEARN_RATE / jnp.maximum(1.0, update_rms / CLIP_LEVEL)
    gains_update = -factors[0] * gains_step
    qkv_new = (
        own_share(qkv_weight, dp_count, dp_index, 0).astype(jnp.float32) - factors[1] * qkv_step
    )
    out_new = (
        own_share(out_weight, dp_count, dp_index, 0).astype(jnp.float32) - factors[2] * out_step
    )
    gate_up_new = (
        own_share(gate_up_weight, dp_count, dp_index, 1).astype(jnp.float32)
        - factors[3] * gateup_step
    )
    down_new = (
        own_share(down_weight, dp_count, dp_index, 1).astype(jnp.float32) - factors[4] * down_step
    )
    return (
        block_out,
        input_grad,
        update_rms,
        gains_update,
        gain_moment_new,
        qkv_new,
        qkv_rows_new,
        qkv_cols_new,
        out_new,
        out_rows_new,
        out_cols_new,
        gate_up_new,
        gateup_rows_new,
        gateup_cols_new,
        down_new,
        down_rows_new,
        down_cols_new,
    )


def solution(mesh):
    placed = (
        P(("dp", "expert"), None),
        P(("dp", "expert"), None),
        P(("dp", "expert")),
        P(("dp", "expert")),
        P(("dp", "expert")),
        P(("dp", "expert"), None),
        P(("dp", "expert"), None),
        P(),
        P(),
        P(),
        P("expert", None, None),
        P("expert", None, None),
        P(),
        P(),
        P(),
        P(),
        P(),
        P("expert", None),
        P("expert", None),
        P("expert", None),
        P("expert", None),
    )
    return jax.shard_map(
        per_device,
        mesh=mesh,
        in_specs=placed,
        out_specs=(
            P(("dp", "expert"), None),
            P(("dp", "expert"), None),
            P(),
            P(None, "dp"),
            P(None, "dp"),
            P("dp", None),
            P("dp"),
            P(),
            P("dp", None),
            P("dp"),
            P(),
            P("expert", "dp", None),
            P("expert", "dp"),
            P("expert", None),
            P("expert", "dp", None),
            P("expert", "dp"),
            P("expert", None),
        ),
        check_vma=False,
    )
```

```python
import functools
import math

import jax
import jax.numpy as jnp
from jax import lax
from jax.experimental import pallas as pl
from jax.experimental.pallas import tpu as pltpu
from jax.sharding import PartitionSpec as P

VM = 60 * 1024 * 1024


def dot(a, b, ca=1, cb=0):
    return lax.dot_general(a, b, (((ca,), (cb,)), ((), ())), preferred_element_type=jnp.float32)


def route_kernel(first_ref, *refs):
    routes, (code_ref, weight_ref, named_ref) = refs[:-3], refs[-3:]
    count = weight_ref.shape[0] // len(routes)
    first = first_ref[0]
    top = routes[0].shape[0] // 2
    rows = routes[0].shape[1]
    for r, route in enumerate(routes):
        ids = route[:top, :]
        gates = route[top:, :]
        for j in range(count):
            hit = ids == (first + j).astype(jnp.float32)
            at = r * count + j
            named_ref[at : at + 1, :] = jnp.max(jnp.where(hit, 1.0, 0.0), axis=0, keepdims=True)
            weight_ref[at : at + 1, :] = jnp.sum(jnp.where(hit, gates, 0.0), axis=0, keepdims=True)
    earlier = lax.broadcasted_iota(jnp.int32, (rows, rows), 0)
    later = lax.broadcasted_iota(jnp.int32, (rows, rows), 1)
    before = jnp.where(earlier < later, 1.0, 0.0).astype(jnp.bfloat16)
    rank = dot(named_ref[...].astype(jnp.bfloat16), before)
    code_ref[...] = jnp.where(named_ref[...] > 0.0, rank, -1.0)


def route_slots(first_expert, routes, count):
    rows = routes[0].shape[1]
    out = jax.ShapeDtypeStruct((len(routes) * count, rows), jnp.float32)
    code, weight = pl.pallas_call(
        route_kernel,
        out_shape=(out, out),
        in_specs=[pl.BlockSpec(memory_space=pltpu.SMEM)]
        + [pl.BlockSpec(memory_space=pltpu.VMEM)] * len(routes),
        out_specs=[pl.BlockSpec(memory_space=pltpu.VMEM)] * 2,
        scratch_shapes=[pltpu.VMEM(out.shape, jnp.float32)],
        compiler_params=pltpu.CompilerParams(vmem_limit_bytes=VM),
        name="route_slots",
    )(first_expert.reshape(1), *routes)
    shape = (len(routes), count, rows)
    return code.reshape(shape), weight.reshape(shape)


def one_hot(code, capacity):
    count, rows = code.shape
    place = lax.broadcasted_iota(jnp.int32, (capacity, rows), 0).astype(jnp.float32)
    return [place == code[j : j + 1, :] for j in range(count)]


def dispatch_kernel(weighted, capacity, *refs):
    code_ref, weight_ref, a_ref, b_ref = refs[:4]
    outs = refs[-2:] if weighted else refs[-1:]
    out_ref = outs[0]
    count = code_ref.shape[1]
    for s, source in enumerate((a_ref, b_ref)):
        chosen = one_hot(code_ref[s], capacity)
        pick = jnp.concatenate([c.astype(jnp.float32) for c in chosen], axis=0).astype(jnp.bfloat16)
        rows = dot(pick, source[...])
        for j in range(count):
            part = rows[j * capacity : (j + 1) * capacity]
            if weighted:
                scale = jnp.sum(
                    jnp.where(chosen[j], weight_ref[s, j : j + 1, :], 0.0), axis=1, keepdims=True
                )
                outs[1][j, s] = scale
                part = part * scale
            out_ref[j, s] = part.astype(jnp.bfloat16)


def dispatch(code, weight, pairs, capacity, weighted):
    sources, count, rows = code.shape
    width = pairs[0][0].shape[1]
    shapes = [jax.ShapeDtypeStruct((count, sources, capacity, width), jnp.bfloat16)]
    if weighted:
        shapes.append(jax.ShapeDtypeStruct((count, sources, capacity, 1), jnp.float32))
    made = []
    for i, (a, b) in enumerate(pairs):
        blocks = [pl.BlockSpec((count, 2, capacity, width), lambda g, i=i: (0, i, 0, 0))]
        if weighted:
            blocks.append(pl.BlockSpec((count, 2, capacity, 1), lambda g, i=i: (0, i, 0, 0)))
        small = pl.BlockSpec((2, count, rows), lambda g, i=i: (i, 0, 0))
        whole = pl.BlockSpec((rows, width), lambda g: (0, 0))
        made = pl.pallas_call(
            functools.partial(dispatch_kernel, weighted, capacity),
            grid=(1,),
            out_shape=shapes,
            in_specs=[small, small, whole, whole] + [pl.BlockSpec(memory_space=pl.ANY)] * len(made),
            out_specs=blocks,
            input_output_aliases={4 + k: k for k in range(len(made))},
            compiler_params=pltpu.CompilerParams(vmem_limit_bytes=VM),
            cost_estimate=pl.CostEstimate(
                flops=4 * count * capacity * rows * width,
                bytes_accessed=4 * rows * width + 4 * count * capacity * width,
                transcendentals=0,
            ),
            name="dispatch_%d%s" % (i, "_w" if weighted else ""),
        )(code, weight, a, b, *made)
    return made


def expert_kernel(owners, s_ref, rec_ref, arr_ref, scale_ref, up_ref, down_ref,
                  keep_ref, give_ref, back_ref, mix_ref, act_s, gug_s, wg_s, wd_s):
    ff = down_ref.shape[1]
    rows, width = act_s.shape[0], up_ref.shape[1]
    tile = rows // 3
    up_w = up_ref[0]
    down_w = down_ref[0]
    received = rec_ref[0].reshape(rows, width)
    arrived = arr_ref[0].reshape(rows, width)
    scale = scale_ref[0].reshape(rows, 1)
    for t in range(3):
        at = slice(t * tile, (t + 1) * tile)
        gate_up = dot(received[at], up_w)
        act_grad = dot(arrived[at], down_w, 1, 1)
        gate = gate_up[:, :ff]
        up = gate_up[:, ff:]
        sig = 1.0 / (1.0 + jnp.exp(-gate))
        silu = gate * sig
        act_s[at, :] = (silu * up).astype(jnp.bfloat16)
        gug_s[at, :ff] = (act_grad * up * sig * (1.0 + gate * (1.0 - sig))).astype(jnp.bfloat16)
        gug_s[at, ff:] = (act_grad * silu).astype(jnp.bfloat16)
    wg_s[...] = dot(received, gug_s[...], 0, 0)
    wd_s[...] = dot(act_s[...], arrived, 0, 0)
    bit = s_ref[1]
    up_rows = width // owners
    down_rows = ff // owners
    for slot in range(owners // 2):
        high, low = slot // 2, slot % 2
        for ref, side in ((keep_ref, bit), (give_ref, 1 - bit)):
            owner = high * 4 + side * 2 + low
            ref[slot, :up_rows, :] = wg_s[
                pl.ds(pl.multiple_of(owner * up_rows, up_rows), up_rows), :
            ].astype(jnp.bfloat16)
            ref[slot, up_rows:, :] = wd_s[
                pl.ds(pl.multiple_of(owner * down_rows, down_rows), down_rows), :
            ].astype(jnp.bfloat16)
    per = rows // rec_ref.shape[1]
    for t in range(3):
        at = slice(t * tile, (t + 1) * tile)
        back = dot(gug_s[at, :], up_w, 1, 1).astype(jnp.bfloat16)
        mix = (dot(act_s[at, :], down_w) * scale[at]).astype(jnp.bfloat16)
        back_ref[at, :] = back
        mix_ref[at, :] = mix


def run_expert(scalars, j, received, arrived, scale, up_w, down_w, owners):
    count, sources, capacity, width = received.shape
    ff = down_w.shape[1]
    rows = sources * capacity
    share = (owners // 2, (width + ff) // owners, width)
    rows_spec = pl.BlockSpec((1, sources, capacity, width), lambda g, s: (j, 0, 0, 0))
    whole2 = lambda *shape: pl.BlockSpec(shape, lambda g, s: (0,) * len(shape))
    slots = jax.ShapeDtypeStruct((rows, width), jnp.bfloat16)
    parts = jax.ShapeDtypeStruct(share, jnp.bfloat16)
    return pl.pallas_call(
        functools.partial(expert_kernel, owners),
        out_shape=(parts, parts, slots, slots),
        grid_spec=pltpu.PrefetchScalarGridSpec(
            num_scalar_prefetch=1,
            grid=(1,),
            in_specs=[
                rows_spec,
                rows_spec,
                pl.BlockSpec((1, sources, capacity, 1), lambda g, s: (j, 0, 0, 0)),
                pl.BlockSpec((1, width, 2 * ff), lambda g, s: (s[0] + j, 0, 0)),
                pl.BlockSpec((1, ff, width), lambda g, s: (s[0] + j, 0, 0)),
            ],
            out_specs=[whole2(*share), whole2(*share), whole2(rows, width), whole2(rows, width)],
            scratch_shapes=[
                pltpu.VMEM((rows, ff), jnp.bfloat16),
                pltpu.VMEM((rows, 2 * ff), jnp.bfloat16),
                pltpu.VMEM((width, 2 * ff), jnp.float32),
                pltpu.VMEM((ff, width), jnp.float32),
            ],
        ),
        compiler_params=pltpu.CompilerParams(vmem_limit_bytes=VM),
        cost_estimate=pl.CostEstimate(
            flops=18 * rows * width * ff, bytes_accessed=16 * width * width, transcendentals=rows * ff
        ),
        name="expert_%d" % j,
    )(scalars, received, arrived, scale, up_w, down_w)


def combine_kernel(capacity, code_ref, *refs):
    slots, (a_ref, b_ref) = refs[:-2], refs[-2:]
    for s, out_ref in enumerate((a_ref, b_ref)):
        chosen = one_hot(code_ref[s], capacity)
        pick = jnp.concatenate([c.astype(jnp.float32) for c in chosen], axis=0).astype(jnp.bfloat16)
        rows = jnp.concatenate([ref[s * capacity : (s + 1) * capacity, :] for ref in slots], axis=0)
        out_ref[...] = dot(pick, rows, 0, 0).astype(jnp.bfloat16)


def combine(code, slots, i, capacity, label):
    sources, count, rows = code.shape
    width = slots[0].shape[1]
    out = jax.ShapeDtypeStruct((rows, width), jnp.bfloat16)
    whole = pl.BlockSpec((rows, width), lambda g: (0, 0))
    return pl.pallas_call(
        functools.partial(combine_kernel, capacity),
        grid=(1,),
        out_shape=(out, out),
        in_specs=[pl.BlockSpec((2, count, rows), lambda g: (i, 0, 0))]
        + [pl.BlockSpec((2 * capacity, width), lambda g: (i, 0))] * count,
        out_specs=[whole, whole],
        compiler_params=pltpu.CompilerParams(vmem_limit_bytes=VM),
        cost_estimate=pl.CostEstimate(
            flops=4 * count * capacity * rows * width,
            bytes_accessed=4 * rows * width + 4 * count * capacity * width,
            transcendentals=0,
        ),
        name="combine_%s_%d" % (label, i),
    )(code, *slots)


HEADS = 16
KV_HEADS = 8
HEAD_DIM = 64
EPS_NORM = 1e-06
ROPE_BASE = 10000.0
MASKED = -1e30
LANES = 128


def spread(row):
    rows = row.shape[1]
    by_column = jnp.broadcast_to(row.astype(jnp.float32), (rows, rows))
    return by_column, by_column.T


def mask_and_angles(ids_ref):
    seg_k, seg_q = spread(ids_ref[0:1, :])
    par_k, par_q = spread(ids_ref[1:2, :])
    pos_k, pos_q = spread(ids_ref[2:3, :])
    seen = ((seg_k == seg_q) | (seg_k == par_q) | (seg_k == par_k)) & (pos_k <= pos_q)
    bias = jnp.where(seen, 0.0, MASKED)
    lane = lax.broadcasted_iota(jnp.int32, (seg_k.shape[0], LANES), 1)
    half = HEAD_DIM // 2
    place = lax.rem(lane, half).astype(jnp.float32)
    frequency = jnp.exp(place * (-2.0 * math.log(ROPE_BASE) / HEAD_DIM))
    angles = pos_q[:, :LANES] * frequency
    front = lax.rem(lane, HEAD_DIM) < half
    sine = jnp.sin(angles)
    return bias, jnp.cos(angles), jnp.where(front, -sine, sine), front, lane


def turned(block, cosine, sine, front):
    other = jnp.where(
        front,
        pltpu.roll(block, LANES - HEAD_DIM // 2, 1),
        pltpu.roll(block, HEAD_DIM // 2, 1),
    )
    return block * cosine + other * sine


def two_diagonal(pair, which, lane):
    rolled = pltpu.roll(pair, HEAD_DIM, 1)
    first, last = (pair, rolled) if which == 0 else (rolled, pair)
    low = lane < HEAD_DIM
    return jnp.concatenate(
        [jnp.where(low, first, 0.0), jnp.where(low, 0.0, last)], axis=0
    ).astype(jnp.bfloat16)


def column_block(index):
    return pl.ds(pl.multiple_of(index * LANES, LANES), LANES)


def attend_kernel(hidden_ref, ids_ref, gains_ref, qkv_w_ref, out_w_ref,
                  normed_ref, qkv_ref, attended_ref, lse_ref, middle_ref, normed_f_ref, proj_s, bias_s):
    rows = hidden_ref.shape[0]
    att = HEADS * HEAD_DIM
    kv = KV_HEADS * HEAD_DIM
    hidden = hidden_ref[...]
    gains = gains_ref[...].astype(jnp.float32)
    inverse = lax.rsqrt(jnp.mean(hidden * hidden, axis=-1, keepdims=True) + EPS_NORM)
    normed_ref[...] = (hidden * inverse * gains[0:1, :]).astype(jnp.bfloat16)
    proj_s[...] = dot(normed_ref[...], qkv_w_ref[...])
    bias, cosine, sine, front, lane = mask_and_angles(ids_ref)
    bias_s[...] = bias
    lse_ref[...] = jnp.zeros_like(lse_ref)

    def pair_step(p, carry):
        key_at = column_block(att // LANES + p)
        value_at = column_block((att + kv) // LANES + p)
        keys = turned(proj_s[:, key_at], cosine, sine, front).astype(jnp.bfloat16)
        values = proj_s[:, value_at].astype(jnp.bfloat16)
        qkv_ref[:, key_at] = keys
        qkv_ref[:, value_at] = values
        keys = keys.astype(jnp.float32)
        values = values.astype(jnp.float32)
        for which in range(2):
            query_at = column_block(2 * p + which)
            queries = turned(proj_s[:, query_at], cosine, sine, front).astype(jnp.bfloat16)
            queries = (queries.astype(jnp.float32) * HEAD_DIM**-0.5).astype(jnp.bfloat16)
            qkv_ref[:, query_at] = queries
            scores = dot(queries, two_diagonal(keys, which, lane), 1, 1)
            probs = []
            for head in range(2):
                part = scores[:, head * rows : (head + 1) * rows] + bias_s[...]
                top = jnp.max(part, axis=-1, keepdims=True)
                part = jnp.exp(part - top)
                total = jnp.sum(part, axis=-1, keepdims=True)
                probs.append((part * (1.0 / total)).astype(jnp.bfloat16))
                at = 4 * p + 2 * which + head
                lse_ref[...] = jnp.where(lane == at, top + jnp.log(total), lse_ref[...])
            attended_ref[:, query_at] = dot(
                jnp.concatenate(probs, axis=1), two_diagonal(values, which, lane)
            ).astype(jnp.bfloat16)
        return carry

    lax.fori_loop(0, KV_HEADS // 2, pair_step, 0)
    middle = hidden + dot(attended_ref[...], out_w_ref[...])
    middle_ref[...] = middle
    inverse_f = lax.rsqrt(jnp.mean(middle * middle, axis=-1, keepdims=True) + EPS_NORM)
    normed_f_ref[...] = (middle * inverse_f * gains[1:2, :]).astype(jnp.bfloat16)


def attend(hidden, ids, gains, qkv_w, out_w):
    rows, width = hidden.shape
    shape = jax.ShapeDtypeStruct
    return pl.pallas_call(
        attend_kernel,
        out_shape=(
            shape((rows, width), jnp.bfloat16),
            shape((rows, qkv_w.shape[1]), jnp.bfloat16),
            shape((rows, out_w.shape[0]), jnp.bfloat16),
            shape((rows, LANES), jnp.float32),
            shape((rows, width), jnp.float32),
            shape((rows, width), jnp.bfloat16),
        ),
        in_specs=[pl.BlockSpec(memory_space=pltpu.VMEM)] * 5,
        out_specs=[pl.BlockSpec(memory_space=pltpu.VMEM)] * 6,
        scratch_shapes=[
            pltpu.VMEM((rows, qkv_w.shape[1]), jnp.float32),
            pltpu.VMEM((rows, rows), jnp.float32),
        ],
        compiler_params=pltpu.CompilerParams(vmem_limit_bytes=VM),
        cost_estimate=pl.CostEstimate(
            flops=10 * rows * width * width, bytes_accessed=12 * width * width, transcendentals=HEADS * rows * rows
        ),
        name="attend",
    )(hidden, ids, gains, qkv_w, out_w)


def attend_back_kernel(hidden_ref, grad_ref, middle_ref, a_ref, b_ref, c_ref, normed_ref, qkv_ref, attended_ref, lse_ref,
                       ids_ref, gains_ref, qkv_w_ref, out_w_ref, input_grad_ref, dense_ref, proj_s, bias_s, back_s):
    rows, width = hidden_ref.shape
    att = HEADS * HEAD_DIM
    kv = KV_HEADS * HEAD_DIM
    gains = gains_ref[...].astype(jnp.float32)
    normed_grad = (
        a_ref[...].astype(jnp.float32) + b_ref[...].astype(jnp.float32) + c_ref[...].astype(jnp.float32)
    )
    middle = middle_ref[...]
    inverse_f = lax.rsqrt(jnp.mean(middle * middle, axis=-1, keepdims=True) + EPS_NORM)
    gain_f = jnp.sum(normed_grad * middle * inverse_f, axis=0, keepdims=True)
    weighted = normed_grad * gains[1:2, :]
    middle_grad = grad_ref[...] + (
        inverse_f * weighted
        - middle * (inverse_f * inverse_f * inverse_f)
        * jnp.mean(weighted * middle, axis=-1, keepdims=True)
    )
    input_grad_ref[...] = middle_grad
    branch = middle_grad.astype(jnp.bfloat16)
    columns = att + 2 * kv
    dense_ref[:, columns : columns + width] = dot(attended_ref[...], branch, 0, 0).astype(jnp.bfloat16)
    back_s[...] = dot(branch, out_w_ref[...], 1, 1).astype(jnp.bfloat16)
    bias, cosine, sine, front, lane = mask_and_angles(ids_ref)
    bias_s[...] = bias
    low = lane < HEAD_DIM

    def pair_step(p, carry):
        key_at = column_block(att // LANES + p)
        value_at = column_block((att + kv) // LANES + p)
        keys = qkv_ref[:, key_at].astype(jnp.float32)
        values = qkv_ref[:, value_at].astype(jnp.float32)
        key_grads = []
        value_grads = []
        for which in range(2):
            query_at = column_block(2 * p + which)
            queries = qkv_ref[:, query_at]
            back = back_s[:, query_at]
            key_two = two_diagonal(keys, which, lane)
            scores = dot(queries, key_two, 1, 1)
            prob_grads = dot(back, two_diagonal(values, which, lane), 1, 1)
            probs = []
            score_grads = []
            for head in range(2):
                at = 4 * p + 2 * which + head
                level = jnp.sum(jnp.where(lane == at, lse_ref[...], 0.0), axis=-1, keepdims=True)
                span = slice(head * rows, (head + 1) * rows)
                prob = jnp.exp(scores[:, span] + bias_s[...] - level)
                prob_grad = prob_grads[:, span]
                row_dot = jnp.sum(prob * prob_grad, axis=-1, keepdims=True)
                probs.append(prob.astype(jnp.bfloat16))
                score_grads.append((prob * (prob_grad - row_dot)).astype(jnp.bfloat16))
            score_grads = jnp.concatenate(score_grads, axis=1)
            query_grad = dot(score_grads, key_two) * HEAD_DIM**-0.5
            proj_s[:, query_at] = turned(query_grad, cosine, -sine, front).astype(jnp.bfloat16)
            for grads, left, right in (
                (key_grads, score_grads, queries),
                (value_grads, jnp.concatenate(probs, axis=1), back),
            ):
                both = dot(left, right, 0, 0)
                first, last = both[:rows], both[rows:]
                if which == 0:
                    grads.append(first + pltpu.roll(last, HEAD_DIM, 1))
                else:
                    grads.append(pltpu.roll(first, HEAD_DIM, 1) + last)
        key_grad = jnp.where(low, key_grads[0], key_grads[1])
        proj_s[:, key_at] = turned(key_grad, cosine, -sine, front).astype(jnp.bfloat16)
        proj_s[:, value_at] = jnp.where(low, value_grads[0], value_grads[1]).astype(jnp.bfloat16)
        return carry

    lax.fori_loop(0, KV_HEADS // 2, pair_step, 0)
    dense_ref[:, :columns] = dot(normed_ref[...], proj_s[...], 0, 0).astype(jnp.bfloat16)
    normed_grad = dot(proj_s[...], qkv_w_ref[...], 1, 1)
    hidden = hidden_ref[...]
    inverse = lax.rsqrt(jnp.mean(hidden * hidden, axis=-1, keepdims=True) + EPS_NORM)
    gain_a = jnp.sum(normed_grad * hidden * inverse, axis=0, keepdims=True)
    weighted = normed_grad * gains[0:1, :]
    input_grad_ref[...] += inverse * weighted - hidden * (inverse * inverse * inverse) * jnp.mean(
        weighted * hidden, axis=-1, keepdims=True
    )
    both = jnp.concatenate([gain_a, gain_f, jnp.zeros((LANES - 2, width), jnp.float32)], axis=0)
    dense_ref[:, columns + width :] = both.T.astype(jnp.bfloat16)


def attend_back(hidden, out_grad, middle, parts, normed, qkv, attended, lse, ids, gains, qkv_w, out_w):
    rows, width = hidden.shape
    columns = qkv_w.shape[1] + width + LANES
    return pl.pallas_call(
        attend_back_kernel,
        out_shape=(
            jax.ShapeDtypeStruct((rows, width), jnp.float32),
            jax.ShapeDtypeStruct((width, columns), jnp.bfloat16),
        ),
        in_specs=[pl.BlockSpec(memory_space=pltpu.VMEM)] * 14,
        out_specs=[pl.BlockSpec(memory_space=pltpu.VMEM)] * 2,
        scratch_shapes=[
            pltpu.VMEM((rows, qkv_w.shape[1]), jnp.bfloat16),
            pltpu.VMEM((rows, rows), jnp.float32),
            pltpu.VMEM((rows, out_w.shape[0]), jnp.bfloat16),
        ],
        compiler_params=pltpu.CompilerParams(vmem_limit_bytes=VM),
        cost_estimate=pl.CostEstimate(
            flops=20 * rows * width * width, bytes_accessed=24 * width * width, transcendentals=HEADS * rows * rows
        ),
        name="attend_back",
    )(hidden, out_grad, middle, *parts, normed, qkv, attended, lse, ids, gains, qkv_w, out_w)


MESH = pl.DeviceIdType.MESH


def greet(peers):
    barrier = pltpu.get_barrier_semaphore()
    for peer in peers:
        pl.semaphore_signal(barrier, inc=1, device_id=peer, device_id_type=MESH)
    pl.semaphore_wait(barrier, len(peers))


def total_kernel(axis, count, mine_ref, out_ref, got_ref, send_sem, recv_sem):
    me = lax.axis_index(axis)
    after = [lax.rem(me + k, count) for k in range(count)]
    greet([{axis: after[k]} for k in range(1, count)])
    scatter = [
        pltpu.make_async_remote_copy(
            src_ref=mine_ref.at[after[k]],
            dst_ref=got_ref.at[k],
            send_sem=send_sem.at[0, k],
            recv_sem=recv_sem.at[0, k],
            device_id={axis: after[k]},
            device_id_type=MESH,
        )
        for k in range(1, count)
    ]
    for copy in scatter:
        copy.start()
    total = mine_ref[me]
    for k in range(1, count):
        scatter[k - 1].wait_recv()
        total = total + got_ref[k]
    out_ref[me] = total
    share = [
        pltpu.make_async_remote_copy(
            src_ref=out_ref.at[me],
            dst_ref=out_ref.at[me],
            send_sem=send_sem.at[1, k],
            recv_sem=recv_sem.at[1, k],
            device_id={axis: after[k]},
            device_id_type=MESH,
        )
        for k in range(1, count)
    ]
    for copy in share:
        copy.start()
    for copy in share:
        copy.wait_recv()
    for copy in scatter + share:
        copy.wait_send()


def total_over(values, axis, label):
    count = lax.axis_size(axis)
    rows = -(-values.shape[0] // (8 * 128 * count)) * 8
    padded = jnp.pad(values, (0, count * rows * 128 - values.shape[0])).reshape(count, rows, 128)
    out = pl.pallas_call(
        functools.partial(total_kernel, axis, count),
        out_shape=jax.ShapeDtypeStruct(padded.shape, jnp.float32),
        in_specs=[pl.BlockSpec(memory_space=pltpu.VMEM)],
        out_specs=pl.BlockSpec(memory_space=pltpu.VMEM),
        scratch_shapes=[
            pltpu.VMEM(padded.shape, jnp.float32),
            pltpu.SemaphoreType.DMA((2, count)),
            pltpu.SemaphoreType.DMA((2, count)),
        ],
        compiler_params=pltpu.CompilerParams(
            collective_id=label, has_side_effects=True, vmem_limit_bytes=16 * 1024 * 1024
        ),
        name="total_%d" % label,
    )(padded)
    return out.reshape(-1)[: values.shape[0]]


def collect_kernel(axis, count, mine_ref, out_ref, send_sem, recv_sem, local_sem):
    me = lax.axis_index(axis)
    after = [lax.rem(me + k, count) for k in range(count)]
    greet([{axis: after[k]} for k in range(1, count)])
    copies = [
        pltpu.make_async_remote_copy(
            src_ref=mine_ref,
            dst_ref=out_ref.at[me],
            send_sem=send_sem.at[k],
            recv_sem=recv_sem.at[k],
            device_id={axis: after[k]},
            device_id_type=MESH,
        )
        for k in range(1, count)
    ]
    for copy in copies:
        copy.start()
    out_ref[me] = mine_ref[...]
    for copy in copies:
        copy.wait()


def collect(values, axis, label):
    count = lax.axis_size(axis)
    return pl.pallas_call(
        functools.partial(collect_kernel, axis, count),
        out_shape=jax.ShapeDtypeStruct((count,) + values.shape, jnp.float32),
        in_specs=[pl.BlockSpec(memory_space=pltpu.VMEM)],
        out_specs=pl.BlockSpec(memory_space=pltpu.VMEM),
        scratch_shapes=[
            pltpu.SemaphoreType.DMA((count,)),
            pltpu.SemaphoreType.DMA((count,)),
            pltpu.SemaphoreType.DMA,
        ],
        compiler_params=pltpu.CompilerParams(
            collective_id=label, has_side_effects=True, vmem_limit_bytes=16 * 1024 * 1024
        ),
        name="collect_%d" % label,
    )(values)


def flipped(axis, mask):
    index = lax.axis_index(axis)
    bit = lax.rem(index // mask, 2)
    return bit, {axis: index + mask - 2 * mask * bit}


def dense_kernel(orders, spans, mine_ref, out_ref, sum_ref, *scratch):
    steps = len(orders[0])
    first_got = scratch[0]
    got = scratch[1 : 1 + steps]
    send_sem, recv_sem = scratch[1 + steps :]
    bits = len(mine_ref.shape) - 4
    core, core_peer = flipped("expert", 1)
    chip, chip_peer = flipped("expert", 2)
    links = [flipped("dp", 1 << b) for b in range(bits)] + [(chip, chip_peer)]
    greet([core_peer] + [peer for _, peer in links])
    whole = (slice(None),) * bits
    copies = []

    def send(src, dst, peer, part, step):
        copy = pltpu.make_async_remote_copy(
            src_ref=src,
            dst_ref=dst,
            send_sem=send_sem.at[part, step],
            recv_sem=recv_sem.at[part, step],
            device_id=peer,
            device_id_type=MESH,
        )
        copy.start()
        copies.append(copy)
        return copy

    def add(first, second):
        return (first.astype(jnp.float32) + second.astype(jnp.float32)).astype(jnp.bfloat16)

    flying = []
    for part, span in enumerate(spans):
        at = whole + (1 - core, slice(None), slice(None), span)
        flying.append(send(mine_ref.at[at], first_got.at[..., span], core_peer, part, 0))

    def place(chosen, span):
        return tuple(chosen.get(bits - 1 - i, slice(None)) for i in range(bits)) + (
            chosen.get(bits, slice(None)),
            slice(None),
            span,
        )

    chosen = [{} for _ in spans]
    for step in range(steps + 1):
        for part, span in enumerate(spans):
            flying[part].wait_recv()
            if step == 0:
                sum_ref[..., span] = add(
                    mine_ref[whole + (core, slice(None), slice(None), span)], first_got[..., span]
                )
            else:
                here = place(chosen[part], span)
                sum_ref[here] = add(sum_ref[here], got[step - 1][part_index(orders, part, step - 1) + (slice(None), span)])
            if step < steps:
                link = orders[part][step]
                bit, peer = links[link]
                away = place({**chosen[part], link: 1 - bit}, span)
                flying[part] = send(
                    sum_ref.at[away],
                    got[step].at[part_index(orders, part, step) + (slice(None), span)],
                    peer,
                    part,
                    1 + step,
                )
                chosen[part] = {**chosen[part], link: bit}
            else:
                out_ref[core, chip, :, span] = sum_ref[place(chosen[part], span)]
                mine = out_ref.at[core, chip, :, span]
                flying[part] = send(mine, mine, chip_peer, part, 1 + steps)
    for part, span in enumerate(spans):
        flying[part].wait_recv()
        mine = out_ref.at[core, :, :, span]
        flying[part] = send(mine, mine, core_peer, part, 2 + steps)
    for copy in flying:
        copy.wait_recv()
    for copy in copies:
        copy.wait_send()


def part_index(orders, part, step):
    return (slice(None),) * (len(orders[part]) - 1 - step)


def reduce_dense(dense, label):
    owners = lax.axis_size("dp")
    width, columns = dense.shape
    bits = owners.bit_length() - 1
    rows = width // owners // 4
    tiles = columns // 128
    parts = bits
    bounds = [128 * (tiles * i // parts) for i in range(parts + 1)]
    spans = [slice(a, b) for a, b in zip(bounds[:-1], bounds[1:])]
    all_links = list(range(bits + 1))
    starts = [bits, 0, 1] + list(range(2, bits))
    orders = [tuple(all_links[s:] + all_links[:s]) for s in starts[:parts]]
    shape = (2,) * bits + (2, 2, rows, columns)
    half = (2,) * bits + (2, rows, columns)
    out = pl.pallas_call(
        functools.partial(dense_kernel, orders, spans),
        out_shape=jax.ShapeDtypeStruct((2, 2, rows, columns), jnp.bfloat16),
        in_specs=[pl.BlockSpec(memory_space=pltpu.VMEM)],
        out_specs=pl.BlockSpec(memory_space=pltpu.VMEM),
        scratch_shapes=[pltpu.VMEM(half, jnp.bfloat16), pltpu.VMEM(half, jnp.bfloat16)]
        + [
            pltpu.VMEM((2,) * (bits - step) + (rows, columns), jnp.bfloat16)
            for step in range(bits + 1)
        ]
        + [pltpu.SemaphoreType.DMA((parts, bits + 4)), pltpu.SemaphoreType.DMA((parts, bits + 4))],
        compiler_params=pltpu.CompilerParams(
            collective_id=label, has_side_effects=True, vmem_limit_bytes=VM
        ),
        name="reduce_dense",
    )(dense.reshape(shape))
    return out.reshape(width // owners, columns)


D = 1024
FF = 512
TOP = 8
EPS_STAT = 1e-30
STAT_DECAY = 0.5
LEARN_RATE = 0.5
CLIP_LEVEL = 0.05


def swap(values, axis, mask):
    count = lax.axis_size(axis)
    return lax.ppermute(values, axis, [(i, i ^ mask) for i in range(count)])


def swap_pair(values):
    return swap(values, "dp", 1)


def swap_chip(values):
    return swap(values, "expert", 2)


def swap_core(values):
    return swap(values, "expert", 1)


def gather_group(shard):
    from_pair = swap_pair(shard)
    from_chip = swap_chip(shard)
    half = shard.shape[0] // 2
    from_both = jnp.concatenate([swap_chip(from_pair[:half]), swap_pair(from_chip[half:])], axis=0)
    return [(piece, swap_core(piece)) for piece in (shard, from_chip, from_pair, from_both)]


def plus(a, b):
    return (a.astype(jnp.float32) + b.astype(jnp.float32)).astype(jnp.bfloat16)


def scatter_group(partials):
    summed = [plus(mine, swap_core(theirs)) for mine, theirs in partials]
    half = summed[3].shape[0] // 2
    for_chip = jnp.concatenate(
        [plus(summed[1][:half], swap_pair(summed[3][:half])), summed[1][half:]], axis=0
    )
    for_pair = jnp.concatenate(
        [summed[2][:half], plus(summed[2][half:], swap_chip(summed[3][half:]))], axis=0
    )
    return summed[0], swap_chip(for_chip), swap_pair(for_pair)


def halve(blocks, axis, mask):
    bit = lax.rem(lax.axis_index(axis) // mask, 2)
    keep = lax.dynamic_index_in_dim(blocks, bit, 1, keepdims=False)
    give = lax.dynamic_index_in_dim(blocks, 1 - bit, 1, keepdims=False)
    return keep, swap(give, axis, mask)


def reduce_expert(keep, give):
    count = lax.axis_size("dp")
    rest = keep.shape[1:]
    blocks = plus(keep, swap(give, "dp", 2))
    low = 4
    while low < count:
        keep, got = halve(blocks.reshape((-1, 2, 2) + rest), "dp", low)
        blocks = plus(keep, got)
        low *= 2
    keep, got = halve(blocks.reshape((1, 2) + rest), "dp", 1)
    return keep[0], got[0]


def reduce_dense_far(blocks):
    count = lax.axis_size("dp")
    width, columns = blocks.shape
    rows = width // count
    blocks = blocks.reshape(count, 2, 2, rows // 4, columns)
    keep, got = halve(jnp.moveaxis(blocks, 2, 1), "expert", 1)
    keep, got = halve(plus(keep, got), "expert", 2)
    blocks = plus(keep, got)
    low = 1
    while low < count:
        keep, got = halve(blocks.reshape((-1, 2, 1) + blocks.shape[1:]), "dp", low)
        blocks = plus(keep, got).reshape((-1,) + blocks.shape[1:])
        low *= 2
    mine = blocks[0]
    chip = lax.axis_index("expert") // 2
    core = lax.rem(lax.axis_index("expert"), 2)
    other = swap_chip(mine)
    both = jnp.where(chip == 0, jnp.stack([mine, other]), jnp.stack([other, mine]))
    across = swap_core(both)
    all_four = jnp.where(core == 0, jnp.stack([both, across], 1), jnp.stack([across, both], 1))
    return all_four.reshape(rows, columns)


def own_share(matrix, along):
    count = lax.axis_size("dp")
    width = matrix.shape[along] // count
    return lax.dynamic_slice_in_dim(matrix, lax.axis_index("dp") * width, width, along)


def decayed(old, new):
    return STAT_DECAY * old + (1.0 - STAT_DECAY) * new


def factored(part, rows_old):
    square = part * part
    rows_new = decayed(rows_old, jnp.mean(square + EPS_STAT, axis=-1))
    return (
        rows_new,
        jnp.sum(square + EPS_STAT, axis=-2),
        jnp.sum(square / rows_new[..., None], axis=-2),
    )


def per_device(
    hidden_in,
    out_grad,
    segment_ids,
    parent_ids,
    positions,
    expert_ids,
    gate_weights,
    norm_gains,
    qkv_weight,
    out_weight,
    gate_up_weight,
    down_weight,
    gain_moment,
    qkv_rows,
    qkv_cols,
    out_rows,
    out_cols,
    gateup_rows,
    gateup_cols,
    down_rows,
    down_cols,
):
    rows_here = hidden_in.shape[0]
    dp_count = lax.axis_size("dp")
    groups = lax.axis_size("expert")
    experts_here = gate_up_weight.shape[0]
    total_experts = experts_here * groups
    capacity = 3 * rows_here * TOP // (2 * total_experts)
    half_experts = experts_here // 2
    dp_index = lax.axis_index("dp")
    pair_bit = lax.rem(dp_index, 2)
    z_bit = lax.rem(dp_index // 2, 2)
    first_local = pair_bit * half_experts
    first_expert = lax.axis_index("expert") * experts_here + first_local

    routing = jnp.concatenate([expert_ids.T.astype(jnp.float32), gate_weights.T], axis=0)
    routes = [r for pair in gather_group(routing) for r in pair]
    code, weight_of = route_slots(first_expert, routes, half_experts)
    grad_pairs = gather_group(out_grad.astype(jnp.bfloat16))
    arrived, scale = dispatch(code, weight_of, grad_pairs, capacity, True)

    ids = jnp.stack([segment_ids, parent_ids, positions])
    normed, qkv, attended, lse, middle, normed_ffn = attend(
        hidden_in, ids, norm_gains, qkv_weight, out_weight
    )
    (received,) = dispatch(code, weight_of, gather_group(normed_ffn), capacity, False)
    scalars = jnp.stack([first_local, z_bit])
    own_parts = []
    other_parts = []
    backs = []
    mixes = []
    for j in range(half_experts):
        keep, give, back, mix = run_expert(
            scalars, j, received, arrived, scale, gate_up_weight, down_weight, dp_count
        )
        own, other = reduce_expert(keep, give)
        own_parts.append(own)
        other_parts.append(other)
        backs.append(back)
        mixes.append(mix)
    places = (3, 1, 2, 0)
    back_parts = {i: combine(code, backs, i, capacity, "back") for i in places}
    grad_parts = scatter_group([back_parts[i] for i in range(4)])
    mix_parts = {i: combine(code, mixes, i, capacity, "mix") for i in places}
    block_out = middle + sum(
        part.astype(jnp.float32) for part in scatter_group([mix_parts[i] for i in range(4)])
    )
    input_grad, dense = attend_back(
        hidden_in, out_grad, middle, grad_parts, normed, qkv, attended, lse, ids, norm_gains, qkv_weight, out_weight
    )

    own = jnp.stack(own_parts).astype(jnp.float32)
    other = jnp.stack(other_parts).astype(jnp.float32)
    parts = jnp.where(pair_bit == 0, jnp.concatenate([own, other]), jnp.concatenate([other, own]))
    gateup_part = parts[:, : D // dp_count]
    down_part = parts[:, D // dp_count :]
    gateup_rows_new, gateup_square, gateup_scaled = factored(gateup_part, own_share(gateup_rows, 1))
    down_rows_new, down_square, down_scaled = factored(down_part, own_share(down_rows, 1))
    sizes = [gateup_square.size, gateup_scaled.size, down_square.size, down_scaled.size]
    summed = total_over(
        jnp.concatenate(
            [
                gateup_square.reshape(-1),
                gateup_scaled.reshape(-1),
                down_square.reshape(-1),
                down_scaled.reshape(-1),
                jnp.sum(gateup_rows_new, axis=1),
                jnp.sum(down_rows_new, axis=1),
            ]
        ),
        "dp",
        1,
    )
    pieces = jnp.split(summed, [sum(sizes[: i + 1]) for i in range(4)])
    gateup_square, gateup_scaled, down_square, down_scaled = [
        p.reshape(experts_here, D) for p in pieces[:4]
    ]
    gateup_row_mean = pieces[4][:experts_here] / D
    down_row_mean = pieces[4][experts_here:] / FF
    gateup_cols_new = decayed(gateup_cols, gateup_square / D)
    down_cols_new = decayed(down_cols, down_square / FF)
    expert_squares = jnp.stack(
        [
            jnp.sum(gateup_row_mean * jnp.sum(gateup_scaled / gateup_cols_new, axis=1)),
            jnp.sum(down_row_mean * jnp.sum(down_scaled / down_cols_new, axis=1)),
        ]
    )
    spread_squares = collect(
        jnp.zeros((8, 128), jnp.float32).at[0, :2].set(expert_squares), "expert", 2
    )
    expert_squares = jnp.sum(spread_squares[:, 0, :2], axis=0)

    qkv_columns = qkv_weight.shape[1]
    if D // dp_count % 64 == 0:
        dense_own = reduce_dense(dense, 3)
    else:
        dense_own = reduce_dense_far(dense)
    dense_own = dense_own.astype(jnp.float32)
    qkv_own = dense_own[:, :qkv_columns]
    out_own = dense_own[:, qkv_columns : qkv_columns + D]
    gains_own = dense_own[:, qkv_columns + D : qkv_columns + D + 2].T
    gain_moment_new = decayed(own_share(gain_moment, 1), gains_own * gains_own + EPS_STAT)
    gains_step = gains_own * lax.rsqrt(gain_moment_new)
    qkv_rows_new, qkv_square, qkv_scaled = factored(qkv_own, own_share(qkv_rows, 0))
    out_rows_new, out_square, out_scaled = factored(out_own, own_share(out_rows, 0))
    dense_sums = total_over(
        jnp.concatenate(
            [
                qkv_square,
                qkv_scaled,
                out_square,
                out_scaled,
                jnp.stack(
                    [jnp.sum(qkv_rows_new), jnp.sum(out_rows_new), jnp.sum(gains_step * gains_step)]
                ),
            ]
        ),
        "dp",
        4,
    )
    qkv_square, qkv_scaled, out_square, out_scaled, rest = jnp.split(
        dense_sums, [qkv_columns, 2 * qkv_columns, 2 * qkv_columns + D, 2 * qkv_columns + 2 * D]
    )
    qkv_row_mean = rest[0] / D
    out_row_mean = rest[1] / D
    qkv_cols_new = decayed(qkv_cols, qkv_square / D)
    out_cols_new = decayed(out_cols, out_square / D)
    squares = jnp.concatenate(
        [
            jnp.stack(
                [
                    rest[2],
                    qkv_row_mean * jnp.sum(qkv_scaled / qkv_cols_new),
                    out_row_mean * jnp.sum(out_scaled / out_cols_new),
                ]
            ),
            expert_squares,
        ]
    )
    element_counts = jnp.array(
        [2 * D, D * qkv_columns, D * D, total_experts * D * 2 * FF, total_experts * FF * D], jnp.float32
    )
    update_rms = jnp.sqrt(squares / element_counts)
    factors = LEARN_RATE / jnp.maximum(1.0, update_rms / CLIP_LEVEL)

    def stepped(weight, part, rows_new, row_mean, cols_new, factor):
        return weight.astype(jnp.float32) - part * (
            factor * lax.rsqrt(rows_new / row_mean[..., None])
        )[..., :, None] * lax.rsqrt(cols_new)[..., None, :]

    return (
        block_out,
        input_grad,
        update_rms,
        -factors[0] * gains_step,
        gain_moment_new,
        stepped(own_share(qkv_weight, 0), qkv_own, qkv_rows_new, qkv_row_mean, qkv_cols_new, factors[1]),
        qkv_rows_new,
        qkv_cols_new,
        stepped(own_share(out_weight, 0), out_own, out_rows_new, out_row_mean, out_cols_new, factors[2]),
        out_rows_new,
        out_cols_new,
        stepped(own_share(gate_up_weight, 1), gateup_part, gateup_rows_new, gateup_row_mean, gateup_cols_new, factors[3]),
        gateup_rows_new,
        gateup_cols_new,
        stepped(own_share(down_weight, 1), down_part, down_rows_new, down_row_mean, down_cols_new, factors[4]),
        down_rows_new,
        down_cols_new,
    )


def solution(mesh):
    placed = (
        P(("dp", "expert"), None),
        P(("dp", "expert"), None),
        P(("dp", "expert")),
        P(("dp", "expert")),
        P(("dp", "expert")),
        P(("dp", "expert"), None),
        P(("dp", "expert"), None),
        P(),
        P(),
        P(),
        P("expert", None, None),
        P("expert", None, None),
        P(),
        P(),
        P(),
        P(),
        P(),
        P("expert", None),
        P("expert", None),
        P("expert", None),
        P("expert", None),
    )
    return jax.shard_map(
        per_device,
        mesh=mesh,
        in_specs=placed,
        out_specs=(
            P(("dp", "expert"), None),
            P(("dp", "expert"), None),
            P(),
            P(None, "dp"),
            P(None, "dp"),
            P("dp", None),
            P("dp"),
            P(),
            P("dp", None),
            P("dp"),
            P(),
            P("expert", "dp", None),
            P("expert", "dp"),
            P("expert", None),
            P("expert", "dp", None),
            P("expert", "dp"),
            P("expert", None),
        ),
        check_vma=False,
    )
```

```python
import functools
import math

import jax
import jax.numpy as jnp
from jax import lax
from jax.experimental import pallas as pl
from jax.experimental.pallas import tpu as pltpu
from jax.sharding import PartitionSpec as P

VM = 60 * 1024 * 1024


def dot(a, b, ca=1, cb=0):
    return lax.dot_general(a, b, (((ca,), (cb,)), ((), ())), preferred_element_type=jnp.float32)


def one_hot(code, capacity):
    count, rows = code.shape
    place = lax.broadcasted_iota(jnp.int32, (capacity, rows), 0).astype(jnp.float32)
    return [place == code[j : j + 1, :] for j in range(count)]


def expert_kernel(owners, waits, s_ref, rec_ref, arr_ref, scale_ref, up_ref, down_ref, *refs):
    (keep_ref, give_ref, back_ref, mix_ref, act_s, gug_s, wg_s, wd_s) = refs[waits:]
    ff = down_ref.shape[1]
    rows, width = act_s.shape[0], up_ref.shape[1]
    tile = rows // 3
    up_w = up_ref[0]
    down_w = down_ref[0]
    received = rec_ref[0].reshape(rows, width)
    arrived = arr_ref[0].reshape(rows, width)
    scale = scale_ref[0].reshape(rows, 1)
    for t in range(3):
        at = slice(t * tile, (t + 1) * tile)
        gate_up = dot(received[at], up_w)
        act_grad = dot(arrived[at], down_w, 1, 1)
        gate = gate_up[:, :ff]
        up = gate_up[:, ff:]
        sig = 1.0 / (1.0 + jnp.exp(-gate))
        silu = gate * sig
        act_s[at, :] = (silu * up).astype(jnp.bfloat16)
        gug_s[at, :ff] = (act_grad * up * sig * (1.0 + gate * (1.0 - sig))).astype(jnp.bfloat16)
        gug_s[at, ff:] = (act_grad * silu).astype(jnp.bfloat16)
    wg_s[...] = dot(received, gug_s[...], 0, 0)
    wd_s[...] = dot(act_s[...], arrived, 0, 0)
    bit = s_ref[1]
    up_rows = width // owners
    down_rows = ff // owners
    for slot in range(owners // 2):
        high, low = slot // 2, slot % 2
        for ref, side in ((keep_ref, bit), (give_ref, 1 - bit)):
            owner = high * 4 + side * 2 + low
            ref[slot, :up_rows, :] = wg_s[
                pl.ds(pl.multiple_of(owner * up_rows, up_rows), up_rows), :
            ].astype(jnp.bfloat16)
            ref[slot, up_rows:, :] = wd_s[
                pl.ds(pl.multiple_of(owner * down_rows, down_rows), down_rows), :
            ].astype(jnp.bfloat16)
    for t in range(3):
        at = slice(t * tile, (t + 1) * tile)
        back = dot(gug_s[at, :], up_w, 1, 1).astype(jnp.bfloat16)
        mix = (dot(act_s[at, :], down_w) * scale[at]).astype(jnp.bfloat16)
        back_ref[at, :] = back
        mix_ref[at, :] = mix


def run_expert(scalars, j, received, arrived, scale, up_w, down_w, owners, after=()):
    count, sources, capacity, width = received.shape
    ff = down_w.shape[1]
    rows = sources * capacity
    share = (owners // 2, (width + ff) // owners, width)
    rows_spec = pl.BlockSpec((1, sources, capacity, width), lambda g, s: (j, 0, 0, 0))
    whole2 = lambda *shape: pl.BlockSpec(shape, lambda g, s: (0,) * len(shape))
    slots = jax.ShapeDtypeStruct((rows, width), jnp.bfloat16)
    parts = jax.ShapeDtypeStruct(share, jnp.bfloat16)
    return pl.pallas_call(
        functools.partial(expert_kernel, owners, len(after)),
        out_shape=(parts, parts, slots, slots),
        grid_spec=pltpu.PrefetchScalarGridSpec(
            num_scalar_prefetch=1,
            grid=(1,),
            in_specs=[
                rows_spec,
                rows_spec,
                pl.BlockSpec((1, sources, capacity, 1), lambda g, s: (j, 0, 0, 0)),
                pl.BlockSpec((1, width, 2 * ff), lambda g, s: (s[0] + j, 0, 0)),
                pl.BlockSpec((1, ff, width), lambda g, s: (s[0] + j, 0, 0)),
            ]
            + [pl.BlockSpec(memory_space=pl.ANY)] * len(after),
            out_specs=[whole2(*share), whole2(*share), whole2(rows, width), whole2(rows, width)],
            scratch_shapes=[
                pltpu.VMEM((rows, ff), jnp.bfloat16),
                pltpu.VMEM((rows, 2 * ff), jnp.bfloat16),
                pltpu.VMEM((width, 2 * ff), jnp.float32),
                pltpu.VMEM((ff, width), jnp.float32),
            ],
        ),
        compiler_params=pltpu.CompilerParams(vmem_limit_bytes=VM),
        name="expert_%d" % j,
    )(scalars, received, arrived, scale, up_w, down_w, *after)


HEADS = 16
KV_HEADS = 8
HEAD_DIM = 64
EPS_NORM = 1e-06
ROPE_BASE = 10000.0
MASKED = -1e30
LANES = 128


def spread(row):
    rows = row.shape[1]
    by_column = jnp.broadcast_to(row.astype(jnp.float32), (rows, rows))
    return by_column, by_column.T


def mask_and_angles(ids_ref):
    seg_k, seg_q = spread(ids_ref[0:1, :])
    par_k, par_q = spread(ids_ref[1:2, :])
    pos_k, pos_q = spread(ids_ref[2:3, :])
    seen = ((seg_k == seg_q) | (seg_k == par_q) | (seg_k == par_k)) & (pos_k <= pos_q)
    bias = jnp.where(seen, 0.0, MASKED)
    lane = lax.broadcasted_iota(jnp.int32, (seg_k.shape[0], LANES), 1)
    half = HEAD_DIM // 2
    place = lax.rem(lane, half).astype(jnp.float32)
    frequency = jnp.exp(place * (-2.0 * math.log(ROPE_BASE) / HEAD_DIM))
    angles = pos_q[:, :LANES] * frequency
    front = lax.rem(lane, HEAD_DIM) < half
    sine = jnp.sin(angles)
    return bias, jnp.cos(angles), jnp.where(front, -sine, sine), front, lane


def turned(block, cosine, sine, front):
    other = jnp.where(
        front,
        pltpu.roll(block, LANES - HEAD_DIM // 2, 1),
        pltpu.roll(block, HEAD_DIM // 2, 1),
    )
    return block * cosine + other * sine


def two_diagonal(pair, which, lane):
    rolled = pltpu.roll(pair, HEAD_DIM, 1)
    first, last = (pair, rolled) if which == 0 else (rolled, pair)
    low = lane < HEAD_DIM
    return jnp.concatenate(
        [jnp.where(low, first, 0.0), jnp.where(low, 0.0, last)], axis=0
    ).astype(jnp.bfloat16)


def column_block(index):
    return pl.ds(pl.multiple_of(index * LANES, LANES), LANES)


def attend_kernel(hidden_ref, ids_ref, gains_ref, qkv_w_ref, out_w_ref,
                  normed_ref, qkv_ref, attended_ref, lse_ref, middle_ref, normed_f_ref, proj_s, bias_s):
    rows = hidden_ref.shape[0]
    att = HEADS * HEAD_DIM
    kv = KV_HEADS * HEAD_DIM
    hidden = hidden_ref[...]
    gains = gains_ref[...].astype(jnp.float32)
    inverse = lax.rsqrt(jnp.mean(hidden * hidden, axis=-1, keepdims=True) + EPS_NORM)
    normed_ref[...] = (hidden * inverse * gains[0:1, :]).astype(jnp.bfloat16)
    proj_s[...] = dot(normed_ref[...], qkv_w_ref[...])
    bias, cosine, sine, front, lane = mask_and_angles(ids_ref)
    bias_s[...] = bias
    lse_ref[...] = jnp.zeros_like(lse_ref)

    def pair_step(p, carry):
        key_at = column_block(att // LANES + p)
        value_at = column_block((att + kv) // LANES + p)
        keys = turned(proj_s[:, key_at], cosine, sine, front).astype(jnp.bfloat16)
        values = proj_s[:, value_at].astype(jnp.bfloat16)
        qkv_ref[:, key_at] = keys
        qkv_ref[:, value_at] = values
        keys = keys.astype(jnp.float32)
        values = values.astype(jnp.float32)
        for which in range(2):
            query_at = column_block(2 * p + which)
            queries = turned(proj_s[:, query_at], cosine, sine, front).astype(jnp.bfloat16)
            queries = (queries.astype(jnp.float32) * HEAD_DIM**-0.5).astype(jnp.bfloat16)
            qkv_ref[:, query_at] = queries
            scores = dot(queries, two_diagonal(keys, which, lane), 1, 1)
            probs = []
            for head in range(2):
                part = scores[:, head * rows : (head + 1) * rows] + bias_s[...]
                top = jnp.max(part, axis=-1, keepdims=True)
                part = jnp.exp(part - top)
                total = jnp.sum(part, axis=-1, keepdims=True)
                probs.append((part * (1.0 / total)).astype(jnp.bfloat16))
                at = 4 * p + 2 * which + head
                lse_ref[...] = jnp.where(lane == at, top + jnp.log(total), lse_ref[...])
            attended_ref[:, query_at] = dot(
                jnp.concatenate(probs, axis=1), two_diagonal(values, which, lane)
            ).astype(jnp.bfloat16)
        return carry

    lax.fori_loop(0, KV_HEADS // 2, pair_step, 0)
    middle = hidden + dot(attended_ref[...], out_w_ref[...])
    middle_ref[...] = middle
    inverse_f = lax.rsqrt(jnp.mean(middle * middle, axis=-1, keepdims=True) + EPS_NORM)
    normed_f_ref[...] = (middle * inverse_f * gains[1:2, :]).astype(jnp.bfloat16)


def attend(hidden, ids, gains, qkv_w, out_w):
    rows, width = hidden.shape
    shape = jax.ShapeDtypeStruct
    return pl.pallas_call(
        attend_kernel,
        out_shape=(
            shape((rows, width), jnp.bfloat16),
            shape((rows, qkv_w.shape[1]), jnp.bfloat16),
            shape((rows, out_w.shape[0]), jnp.bfloat16),
            shape((rows, LANES), jnp.float32),
            shape((rows, width), jnp.float32),
            shape((rows, width), jnp.bfloat16),
        ),
        in_specs=[pl.BlockSpec(memory_space=pltpu.VMEM)] * 5,
        out_specs=[pl.BlockSpec(memory_space=pltpu.VMEM)] * 6,
        scratch_shapes=[
            pltpu.VMEM((rows, qkv_w.shape[1]), jnp.float32),
            pltpu.VMEM((rows, rows), jnp.float32),
        ],
        compiler_params=pltpu.CompilerParams(vmem_limit_bytes=VM),
        name="attend",
    )(hidden, ids, gains, qkv_w, out_w)


def attend_back_kernel(hidden_ref, grad_ref, middle_ref, normed_grad_ref, normed_ref, qkv_ref, attended_ref, lse_ref,
                       ids_ref, gains_ref, qkv_w_ref, out_w_ref, *refs):
    input_grad_ref, dense_ref, proj_s, bias_s, back_s = refs[-5:]
    rows, width = hidden_ref.shape
    att = HEADS * HEAD_DIM
    kv = KV_HEADS * HEAD_DIM
    gains = gains_ref[...].astype(jnp.float32)
    normed_grad = normed_grad_ref[...]
    middle = middle_ref[...]
    inverse_f = lax.rsqrt(jnp.mean(middle * middle, axis=-1, keepdims=True) + EPS_NORM)
    gain_f = jnp.sum(normed_grad * middle * inverse_f, axis=0, keepdims=True)
    weighted = normed_grad * gains[1:2, :]
    middle_grad = grad_ref[...] + (
        inverse_f * weighted
        - middle * (inverse_f * inverse_f * inverse_f)
        * jnp.mean(weighted * middle, axis=-1, keepdims=True)
    )
    input_grad_ref[...] = middle_grad
    branch = middle_grad.astype(jnp.bfloat16)
    columns = att + 2 * kv
    dense_ref[:, columns : columns + width] = dot(attended_ref[...], branch, 0, 0).astype(jnp.bfloat16)
    back_s[...] = dot(branch, out_w_ref[...], 1, 1).astype(jnp.bfloat16)
    bias, cosine, sine, front, lane = mask_and_angles(ids_ref)
    bias_s[...] = bias
    low = lane < HEAD_DIM

    def pair_step(p, carry):
        key_at = column_block(att // LANES + p)
        value_at = column_block((att + kv) // LANES + p)
        keys = qkv_ref[:, key_at].astype(jnp.float32)
        values = qkv_ref[:, value_at].astype(jnp.float32)
        key_grads = []
        value_grads = []
        for which in range(2):
            query_at = column_block(2 * p + which)
            queries = qkv_ref[:, query_at]
            back = back_s[:, query_at]
            key_two = two_diagonal(keys, which, lane)
            scores = dot(queries, key_two, 1, 1)
            prob_grads = dot(back, two_diagonal(values, which, lane), 1, 1)
            probs = []
            score_grads = []
            for head in range(2):
                at = 4 * p + 2 * which + head
                level = jnp.sum(jnp.where(lane == at, lse_ref[...], 0.0), axis=-1, keepdims=True)
                span = slice(head * rows, (head + 1) * rows)
                prob = jnp.exp(scores[:, span] + bias_s[...] - level)
                prob_grad = prob_grads[:, span]
                row_dot = jnp.sum(prob * prob_grad, axis=-1, keepdims=True)
                probs.append(prob.astype(jnp.bfloat16))
                score_grads.append((prob * (prob_grad - row_dot)).astype(jnp.bfloat16))
            score_grads = jnp.concatenate(score_grads, axis=1)
            query_grad = dot(score_grads, key_two) * HEAD_DIM**-0.5
            proj_s[:, query_at] = turned(query_grad, cosine, -sine, front).astype(jnp.bfloat16)
            for grads, left, right in (
                (key_grads, score_grads, queries),
                (value_grads, jnp.concatenate(probs, axis=1), back),
            ):
                both = dot(left, right, 0, 0)
                first, last = both[:rows], both[rows:]
                if which == 0:
                    grads.append(first + pltpu.roll(last, HEAD_DIM, 1))
                else:
                    grads.append(pltpu.roll(first, HEAD_DIM, 1) + last)
        key_grad = jnp.where(low, key_grads[0], key_grads[1])
        proj_s[:, key_at] = turned(key_grad, cosine, -sine, front).astype(jnp.bfloat16)
        proj_s[:, value_at] = jnp.where(low, value_grads[0], value_grads[1]).astype(jnp.bfloat16)
        return carry

    lax.fori_loop(0, KV_HEADS // 2, pair_step, 0)
    dense_ref[:, :columns] = dot(normed_ref[...], proj_s[...], 0, 0).astype(jnp.bfloat16)
    normed_grad = dot(proj_s[...], qkv_w_ref[...], 1, 1)
    hidden = hidden_ref[...]
    inverse = lax.rsqrt(jnp.mean(hidden * hidden, axis=-1, keepdims=True) + EPS_NORM)
    gain_a = jnp.sum(normed_grad * hidden * inverse, axis=0, keepdims=True)
    weighted = normed_grad * gains[0:1, :]
    input_grad_ref[...] += inverse * weighted - hidden * (inverse * inverse * inverse) * jnp.mean(
        weighted * hidden, axis=-1, keepdims=True
    )
    both = jnp.concatenate([gain_a, gain_f, jnp.zeros((LANES - 2, width), jnp.float32)], axis=0)
    dense_ref[:, columns + width :] = both.T.astype(jnp.bfloat16)


def attend_back(hidden, out_grad, middle, normed_f_grad, normed, qkv, attended, lse, ids, gains, qkv_w, out_w, after=()):
    rows, width = hidden.shape
    columns = qkv_w.shape[1] + width + LANES
    return pl.pallas_call(
        attend_back_kernel,
        out_shape=(
            jax.ShapeDtypeStruct((rows, width), jnp.float32),
            jax.ShapeDtypeStruct((width, columns), jnp.bfloat16),
        ),
        in_specs=[pl.BlockSpec(memory_space=pltpu.VMEM)] * 12
        + [pl.BlockSpec(memory_space=pl.ANY)] * len(after),
        out_specs=[pl.BlockSpec(memory_space=pltpu.VMEM)] * 2,
        scratch_shapes=[
            pltpu.VMEM((rows, qkv_w.shape[1]), jnp.bfloat16),
            pltpu.VMEM((rows, rows), jnp.float32),
            pltpu.VMEM((rows, out_w.shape[0]), jnp.bfloat16),
        ],
        compiler_params=pltpu.CompilerParams(vmem_limit_bytes=VM),
        name="attend_back",
    )(hidden, out_grad, middle, normed_f_grad, normed, qkv, attended, lse, ids, gains, qkv_w, out_w, *after)


MESH = pl.DeviceIdType.MESH


def greet(peers):
    barrier = pltpu.get_barrier_semaphore()
    for peer in peers:
        pl.semaphore_signal(barrier, inc=1, device_id=peer, device_id_type=MESH)
    pl.semaphore_wait(barrier, len(peers))


def total_kernel(axis, count, mine_ref, out_ref, got_ref, send_sem, recv_sem):
    me = lax.axis_index(axis)
    after = [lax.rem(me + k, count) for k in range(count)]
    greet([{axis: after[k]} for k in range(1, count)])
    scatter = [
        pltpu.make_async_remote_copy(
            src_ref=mine_ref.at[after[k]],
            dst_ref=got_ref.at[k],
            send_sem=send_sem.at[0, k],
            recv_sem=recv_sem.at[0, k],
            device_id={axis: after[k]},
            device_id_type=MESH,
        )
        for k in range(1, count)
    ]
    for copy in scatter:
        copy.start()
    total = mine_ref[me]
    for k in range(1, count):
        scatter[k - 1].wait_recv()
        total = total + got_ref[k]
    out_ref[me] = total
    share = [
        pltpu.make_async_remote_copy(
            src_ref=out_ref.at[me],
            dst_ref=out_ref.at[me],
            send_sem=send_sem.at[1, k],
            recv_sem=recv_sem.at[1, k],
            device_id={axis: after[k]},
            device_id_type=MESH,
        )
        for k in range(1, count)
    ]
    for copy in share:
        copy.start()
    for copy in share:
        copy.wait_recv()
    for copy in scatter + share:
        copy.wait_send()


def total_over(values, axis, label):
    count = lax.axis_size(axis)
    rows = -(-values.shape[0] // (8 * 128 * count)) * 8
    padded = jnp.pad(values, (0, count * rows * 128 - values.shape[0])).reshape(count, rows, 128)
    out = pl.pallas_call(
        functools.partial(total_kernel, axis, count),
        out_shape=jax.ShapeDtypeStruct(padded.shape, jnp.float32),
        in_specs=[pl.BlockSpec(memory_space=pltpu.VMEM)],
        out_specs=pl.BlockSpec(memory_space=pltpu.VMEM),
        scratch_shapes=[
            pltpu.VMEM(padded.shape, jnp.float32),
            pltpu.SemaphoreType.DMA((2, count)),
            pltpu.SemaphoreType.DMA((2, count)),
        ],
        compiler_params=pltpu.CompilerParams(
            collective_id=label, has_side_effects=True, vmem_limit_bytes=16 * 1024 * 1024
        ),
        name="total_%d" % label,
    )(padded)
    return out.reshape(-1)[: values.shape[0]]


def collect_kernel(axis, count, mine_ref, out_ref, send_sem, recv_sem, local_sem):
    me = lax.axis_index(axis)
    after = [lax.rem(me + k, count) for k in range(count)]
    greet([{axis: after[k]} for k in range(1, count)])
    copies = [
        pltpu.make_async_remote_copy(
            src_ref=mine_ref,
            dst_ref=out_ref.at[me],
            send_sem=send_sem.at[k],
            recv_sem=recv_sem.at[k],
            device_id={axis: after[k]},
            device_id_type=MESH,
        )
        for k in range(1, count)
    ]
    for copy in copies:
        copy.start()
    out_ref[me] = mine_ref[...]
    for copy in copies:
        copy.wait()


def collect(values, axis, label):
    count = lax.axis_size(axis)
    return pl.pallas_call(
        functools.partial(collect_kernel, axis, count),
        out_shape=jax.ShapeDtypeStruct((count,) + values.shape, jnp.float32),
        in_specs=[pl.BlockSpec(memory_space=pltpu.VMEM)],
        out_specs=pl.BlockSpec(memory_space=pltpu.VMEM),
        scratch_shapes=[
            pltpu.SemaphoreType.DMA((count,)),
            pltpu.SemaphoreType.DMA((count,)),
            pltpu.SemaphoreType.DMA,
        ],
        compiler_params=pltpu.CompilerParams(
            collective_id=label, has_side_effects=True, vmem_limit_bytes=16 * 1024 * 1024
        ),
        name="collect_%d" % label,
    )(values)


def flipped(axis, mask):
    index = lax.axis_index(axis)
    bit = lax.rem(index // mask, 2)
    return bit, {axis: index + mask - 2 * mask * bit}


def dense_kernel(orders, spans, waits, mine_ref, *refs):
    steps = len(orders[0])
    (out_ref, sum_ref), scratch = refs[waits : waits + 2], refs[waits + 2 :]
    first_got = scratch[0]
    got = scratch[1 : 1 + steps]
    send_sem, recv_sem = scratch[1 + steps :]
    bits = len(mine_ref.shape) - 4
    core, core_peer = flipped("expert", 1)
    chip, chip_peer = flipped("expert", 2)
    links = [flipped("dp", 1 << b) for b in range(bits)] + [(chip, chip_peer)]
    greet([core_peer] + [peer for _, peer in links])
    whole = (slice(None),) * bits
    copies = []

    def send(src, dst, peer, part, step):
        copy = pltpu.make_async_remote_copy(
            src_ref=src,
            dst_ref=dst,
            send_sem=send_sem.at[part, step],
            recv_sem=recv_sem.at[part, step],
            device_id=peer,
            device_id_type=MESH,
        )
        copy.start()
        copies.append(copy)
        return copy

    def add(first, second):
        return (first.astype(jnp.float32) + second.astype(jnp.float32)).astype(jnp.bfloat16)

    flying = []
    for part, span in enumerate(spans):
        at = whole + (1 - core, slice(None), slice(None), span)
        flying.append(send(mine_ref.at[at], first_got.at[..., span], core_peer, part, 0))

    def place(chosen, span):
        return tuple(chosen.get(bits - 1 - i, slice(None)) for i in range(bits)) + (
            chosen.get(bits, slice(None)),
            slice(None),
            span,
        )

    chosen = [{} for _ in spans]
    for step in range(steps + 1):
        for part, span in enumerate(spans):
            flying[part].wait_recv()
            if step == 0:
                sum_ref[..., span] = add(
                    mine_ref[whole + (core, slice(None), slice(None), span)], first_got[..., span]
                )
            else:
                here = place(chosen[part], span)
                sum_ref[here] = add(sum_ref[here], got[step - 1][part_index(orders, part, step - 1) + (slice(None), span)])
            if step < steps:
                link = orders[part][step]
                bit, peer = links[link]
                away = place({**chosen[part], link: 1 - bit}, span)
                flying[part] = send(
                    sum_ref.at[away],
                    got[step].at[part_index(orders, part, step) + (slice(None), span)],
                    peer,
                    part,
                    1 + step,
                )
                chosen[part] = {**chosen[part], link: bit}
            else:
                out_ref[core, chip, :, span] = sum_ref[place(chosen[part], span)]
                mine = out_ref.at[core, chip, :, span]
                flying[part] = send(mine, mine, chip_peer, part, 1 + steps)
    for part, span in enumerate(spans):
        flying[part].wait_recv()
        mine = out_ref.at[core, :, :, span]
        flying[part] = send(mine, mine, core_peer, part, 2 + steps)
    for copy in flying:
        copy.wait_recv()
    for copy in copies:
        copy.wait_send()


def part_index(orders, part, step):
    return (slice(None),) * (len(orders[part]) - 1 - step)


def reduce_dense(dense, label, after=()):
    owners = lax.axis_size("dp")
    width, columns = dense.shape
    bits = owners.bit_length() - 1
    rows = width // owners // 4
    tiles = columns // 128
    parts = bits
    bounds = [128 * (tiles * i // parts) for i in range(parts + 1)]
    spans = [slice(a, b) for a, b in zip(bounds[:-1], bounds[1:])]
    all_links = list(range(bits + 1))
    starts = [bits, 0, 1] + list(range(2, bits))
    orders = [tuple(all_links[s:] + all_links[:s]) for s in starts[:parts]]
    shape = (2,) * bits + (2, 2, rows, columns)
    half = (2,) * bits + (2, rows, columns)
    out = pl.pallas_call(
        functools.partial(dense_kernel, orders, spans, len(after)),
        out_shape=jax.ShapeDtypeStruct((2, 2, rows, columns), jnp.bfloat16),
        in_specs=[pl.BlockSpec(memory_space=pltpu.VMEM)] + [pl.BlockSpec(memory_space=pl.ANY)] * len(after),
        out_specs=pl.BlockSpec(memory_space=pltpu.VMEM),
        scratch_shapes=[pltpu.VMEM(half, jnp.bfloat16), pltpu.VMEM(half, jnp.bfloat16)]
        + [
            pltpu.VMEM((2,) * (bits - step) + (rows, columns), jnp.bfloat16)
            for step in range(bits + 1)
        ]
        + [pltpu.SemaphoreType.DMA((parts, bits + 4)), pltpu.SemaphoreType.DMA((parts, bits + 4))],
        compiler_params=pltpu.CompilerParams(
            collective_id=label, has_side_effects=True, vmem_limit_bytes=VM
        ),
        name="reduce_dense",
    )(dense.reshape(shape), *after)
    return out.reshape(width // owners, columns)


PAIR = 1
ROUTE_ROWS = 32


class Pusher:
    def __init__(self, send_sem, recv_sem):
        self.send_sem, self.recv_sem, self.copies = send_sem, recv_sem, []

    def __call__(self, src, dst, peer):
        at = len(self.copies)
        copy = pltpu.make_async_remote_copy(
            src_ref=src,
            dst_ref=dst,
            send_sem=self.send_sem.at[at],
            recv_sem=self.recv_sem.at[at],
            device_id=peer,
            device_id_type=MESH,
        )
        copy.start()
        self.copies.append(copy)
        return copy

    def finish(self):
        for copy in self.copies:
            copy.wait_send()


def picked(code, capacity):
    return jnp.concatenate(
        [c.astype(jnp.float32) for c in one_hot(code, capacity)], axis=0
    ).astype(jnp.bfloat16)


def gather_kernel(capacity, experts_here, half_experts, top, token_ref, grad_ref, chip_grad_ref, pair_grad_ref,
                  rec_ref, arr_ref, scale_ref, code_ref, tokens, grads, weight_s, stage, send_sem, recv_sem, local_sem):
    rows = token_ref.shape[0]
    half = rows // 2
    first = lax.axis_index("expert") * experts_here + lax.rem(lax.axis_index("dp") // PAIR, 2) * half_experts
    _, core = flipped("expert", 1)
    _, chip = flipped("expert", 2)
    _, pair = flipped("dp", PAIR)
    greet([core, chip, pair])
    push = Pusher(send_sem, recv_sem)
    everything, routing = slice(None), slice(rows, rows + ROUTE_ROWS)
    to_chip = push(token_ref, tokens.at[2], chip)
    to_pair = push(token_ref, tokens.at[4], pair)
    route_both = push(pair_grad_ref.at[routing], grads.at[6, routing], chip)
    to_core = push(token_ref, tokens.at[1], core)
    grad_core = push(grad_ref, grads.at[1], core)
    grad_chip_core = push(chip_grad_ref, grads.at[3], core)
    grad_pair_core = push(pair_grad_ref, grads.at[5], core)

    earlier = lax.broadcasted_iota(jnp.int32, (rows, rows), 0)
    later = lax.broadcasted_iota(jnp.int32, (rows, rows), 1)
    before = jnp.where(earlier < later, 1.0, 0.0).astype(jnp.bfloat16)

    def route(r, table):
        table = table.astype(jnp.float32)
        ids = table[:top]
        gates = table[top : 2 * top] + table[2 * top : 3 * top]
        hits = [ids == (first + j).astype(jnp.float32) for j in range(half_experts)]
        named = jnp.concatenate(
            [jnp.max(jnp.where(hit, 1.0, 0.0), axis=0, keepdims=True) for hit in hits], axis=0
        )
        weight_s[r] = jnp.concatenate(
            [jnp.sum(jnp.where(hit, gates, 0.0), axis=0, keepdims=True) for hit in hits], axis=0
        )
        code_ref[r] = jnp.where(named > 0.0, dot(named.astype(jnp.bfloat16), before), -1.0)

    leaving = []

    def select(r, source, out_ref, weighted):
        slot = len(leaving) % stage.shape[0]
        if len(leaving) >= stage.shape[0]:
            leaving[len(leaving) - stage.shape[0]].wait()
        chosen = one_hot(code_ref[r], capacity)
        pick = jnp.concatenate([c.astype(jnp.float32) for c in chosen], axis=0).astype(jnp.bfloat16)
        made = dot(pick, source)
        for j in range(half_experts):
            part = made[j * capacity : (j + 1) * capacity]
            if weighted:
                scale = jnp.sum(
                    jnp.where(chosen[j], weight_s[r, j : j + 1, :], 0.0), axis=1, keepdims=True
                )
                scale_ref[j, r] = scale
                part = part * scale
            stage[slot, j] = part.astype(jnp.bfloat16)
        copy = pltpu.make_async_copy(stage.at[slot], out_ref.at[:, r], local_sem.at[slot])
        copy.start()
        leaving.append(copy)

    def select_grad(r, ref):
        route(r, ref[rows:, :rows])
        select(r, ref[:rows, :], arr_ref, True)

    select_grad(0, grad_ref)
    select(0, token_ref[...], rec_ref, False)
    select_grad(2, chip_grad_ref)
    select_grad(4, pair_grad_ref)
    for r, copy in ((1, grad_core), (3, grad_chip_core), (5, grad_pair_core)):
        copy.wait_recv()
        select_grad(r, grads.at[r])
    to_core.wait_recv()
    select(1, tokens[1], rec_ref, False)
    route_both.wait_recv()
    route_core = push(grads.at[6, routing], grads.at[7, routing], core)
    to_chip.wait_recv()
    both_low = push(tokens.at[2, half:rows], tokens.at[6, half:rows], pair)
    chip_core = push(tokens.at[2], tokens.at[3], core)
    to_pair.wait_recv()
    both_high = push(tokens.at[4, 0:half], tokens.at[6, 0:half], chip)
    pair_core = push(tokens.at[4], tokens.at[5], core)
    grad_low = push(chip_grad_ref.at[half:rows], grads.at[6, half:rows], pair)
    grad_high = push(pair_grad_ref.at[0:half], grads.at[6, 0:half], chip)
    select(2, tokens[2], rec_ref, False)
    select(4, tokens[4], rec_ref, False)
    route(6, grads[6, rows:, :rows])
    route_core.wait_recv()
    route(7, grads[7, rows:, :rows])
    chip_core.wait_recv()
    select(3, tokens[3], rec_ref, False)
    pair_core.wait_recv()
    select(5, tokens[5], rec_ref, False)
    both_low.wait_recv()
    both_high.wait_recv()
    both_core = push(tokens.at[6], tokens.at[7], core)
    select(6, tokens[6], rec_ref, False)
    both_core.wait_recv()
    select(7, tokens[7], rec_ref, False)
    grad_low.wait_recv()
    grad_high.wait_recv()
    grad_both_core = push(grads.at[6, 0:rows], grads.at[7, 0:rows], core)
    select(6, grads[6, :rows], arr_ref, True)
    grad_both_core.wait_recv()
    select(7, grads[7, :rows], arr_ref, True)
    for copy in leaving[-stage.shape[0] :]:
        copy.wait()
    push.finish()


def gather_and_select(token, grad, chip_grad, pair_grad, capacity, experts_here, half_experts, top, label):
    rows, width = token.shape
    vmem = pl.BlockSpec(memory_space=pltpu.VMEM)
    anywhere = pl.BlockSpec(memory_space=pl.ANY)
    slots = jax.ShapeDtypeStruct((half_experts, 8, capacity, width), jnp.bfloat16)
    return pl.pallas_call(
        functools.partial(gather_kernel, capacity, experts_here, half_experts, top),
        out_shape=(
            slots,
            slots,
            jax.ShapeDtypeStruct((half_experts, 8, capacity, 1), jnp.float32),
            jax.ShapeDtypeStruct((8, half_experts, rows), jnp.float32),
        ),
        in_specs=[vmem] * 4,
        out_specs=[anywhere, anywhere, vmem, vmem],
        scratch_shapes=[
            pltpu.VMEM((8, rows, width), jnp.bfloat16),
            pltpu.VMEM((8, rows + ROUTE_ROWS, width), jnp.bfloat16),
            pltpu.VMEM((8, half_experts, rows), jnp.float32),
            pltpu.VMEM((4, half_experts, capacity, width), jnp.bfloat16),
            pltpu.SemaphoreType.DMA((18,)),
            pltpu.SemaphoreType.DMA((18,)),
            pltpu.SemaphoreType.DMA((4,)),
        ],
        compiler_params=pltpu.CompilerParams(
            collective_id=label, has_side_effects=True, vmem_limit_bytes=VM
        ),
        name="gather_and_select",
    )(token, grad, chip_grad, pair_grad)


def return_kernel(capacity, count, code_ref, *refs):
    backs, mixes = refs[:count], refs[count : 2 * count]
    out_ref, mix_ref = refs[2 * count : 2 * count + 2]
    (fetched, theirs, core_got, own, theirs_mix, core_got_mix, half_pair, half_chip, from_chip, from_pair,
     send_sem, recv_sem, local_sem) = refs[2 * count + 2 :]
    rows = out_ref.shape[0]
    half = rows // 2
    _, core = flipped("expert", 1)
    _, chip = flipped("expert", 2)
    _, pair = flipped("dp", PAIR)
    greet([core, chip, pair])
    push = Pusher(send_sem, recv_sem)
    order = [(backs, r) for r in (7, 6, 3, 2, 5, 4, 1, 0)] + [(mixes, r) for r in (7, 6, 3, 2, 5, 4, 1, 0)]
    depth = fetched.shape[0]
    fetching = []

    def fetch():
        n = len(fetching)
        if n < len(order):
            slots, r = order[n]
            fetching.append(
                [
                    pltpu.make_async_copy(
                        ref.at[r * capacity : (r + 1) * capacity],
                        fetched.at[n % depth, j * capacity : (j + 1) * capacity],
                        local_sem.at[n % depth, j],
                    )
                    for j, ref in enumerate(slots)
                ]
            )
            for copy in fetching[-1]:
                copy.start()

    done = []

    def combined():
        n = len(done)
        for copy in fetching[n]:
            copy.wait()
        made = dot(picked(code_ref[order[n][1]], capacity), fetched[n % depth], 0, 0)
        done.append(n)
        return made

    for _ in range(depth - 1):
        fetch()

    def next_sum():
        fetch()
        return combined()

    def plus(a, b):
        return (a + b.astype(jnp.float32)).astype(jnp.bfloat16)

    def sums(i, theirs, core_got):
        theirs[i] = next_sum().astype(jnp.bfloat16)
        copy = push(theirs.at[i], core_got.at[i], core)
        return next_sum(), copy

    mine, copy = sums(3, theirs, core_got)
    copy.wait_recv()
    own[3] = plus(mine, core_got[3])
    at_pair = push(own.at[3, 0:half], half_pair, pair)
    at_chip = push(own.at[3, half:rows], half_chip, chip)
    mine, copy = sums(1, theirs, core_got)
    copy.wait_recv()
    own[1] = plus(mine, core_got[1])
    low_chip = push(own.at[1, half:rows], from_chip.at[half:rows], chip)
    mine, copy = sums(2, theirs, core_got)
    copy.wait_recv()
    own[2] = plus(mine, core_got[2])
    high_pair = push(own.at[2, 0:half], from_pair.at[0:half], pair)
    mine, copy = sums(0, theirs, core_got)
    copy.wait_recv()
    out_ref[...] = mine + core_got[0].astype(jnp.float32)
    mine, copy = sums(3, theirs_mix, core_got_mix)
    copy.wait_recv()
    mix_ref[3] = plus(mine, core_got_mix[3])
    at_pair.wait_recv()
    own[1, :half] = plus(own[1, :half].astype(jnp.float32), half_pair[...])
    high_chip = push(own.at[1, 0:half], from_chip.at[0:half], chip)
    at_chip.wait_recv()
    own[2, half:] = plus(own[2, half:].astype(jnp.float32), half_chip[...])
    low_pair = push(own.at[2, half:rows], from_pair.at[half:rows], pair)
    for i in (1, 2, 0):
        mine, copy = sums(i, theirs_mix, core_got_mix)
        copy.wait_recv()
        mix_ref[i] = plus(mine, core_got_mix[i])
    low_chip.wait_recv()
    high_pair.wait_recv()
    high_chip.wait_recv()
    low_pair.wait_recv()
    out_ref[...] += from_chip[...].astype(jnp.float32) + from_pair[...].astype(jnp.float32)
    push.finish()


def combine_and_return(code, backs, mixes, capacity, label):
    _, count, rows = code.shape
    width = backs[0].shape[1]
    vmem = pl.BlockSpec(memory_space=pltpu.VMEM)
    anywhere = pl.BlockSpec(memory_space=pl.ANY)
    four = pltpu.VMEM((4, rows, width), jnp.bfloat16)
    return pl.pallas_call(
        functools.partial(return_kernel, capacity, count),
        out_shape=(
            jax.ShapeDtypeStruct((rows, width), jnp.float32),
            jax.ShapeDtypeStruct((4, rows, width), jnp.bfloat16),
        ),
        in_specs=[vmem] + [anywhere] * (2 * count),
        out_specs=[vmem, vmem],
        scratch_shapes=[pltpu.VMEM((4, count * capacity, width), jnp.bfloat16), four, four, four, four, four]
        + [pltpu.VMEM((rows // 2, width), jnp.bfloat16)] * 2
        + [pltpu.VMEM((rows, width), jnp.bfloat16)] * 2
        + [
            pltpu.SemaphoreType.DMA((14,)),
            pltpu.SemaphoreType.DMA((14,)),
            pltpu.SemaphoreType.DMA((4, count)),
        ],
        compiler_params=pltpu.CompilerParams(
            collective_id=label, has_side_effects=True, vmem_limit_bytes=VM
        ),
        name="combine_and_return",
    )(code, *backs, *mixes)


D = 1024
FF = 512
TOP = 8
EPS_STAT = 1e-30
STAT_DECAY = 0.5
LEARN_RATE = 0.5
CLIP_LEVEL = 0.05


def swap(values, axis, mask):
    count = lax.axis_size(axis)
    return lax.ppermute(values, axis, [(i, i ^ mask) for i in range(count)])


def swap_pair(values):
    return swap(values, "dp", 1)


def swap_chip(values):
    return swap(values, "expert", 2)


def swap_core(values):
    return swap(values, "expert", 1)


def plus(a, b):
    return (a.astype(jnp.float32) + b.astype(jnp.float32)).astype(jnp.bfloat16)


def return_to_owners(summed):
    half = summed[3].shape[0] // 2
    for_chip = jnp.concatenate(
        [plus(summed[1][:half], swap_pair(summed[3][:half])), summed[1][half:]], axis=0
    )
    for_pair = jnp.concatenate(
        [summed[2][:half], plus(summed[2][half:], swap_chip(summed[3][half:]))], axis=0
    )
    return summed[0], swap_chip(for_chip), swap_pair(for_pair)


def halve(blocks, axis, mask):
    bit = lax.rem(lax.axis_index(axis) // mask, 2)
    keep = lax.dynamic_index_in_dim(blocks, bit, 1, keepdims=False)
    give = lax.dynamic_index_in_dim(blocks, 1 - bit, 1, keepdims=False)
    return keep, swap(give, axis, mask)


def far_sum(blocks):
    count = lax.axis_size("dp")
    rest = blocks.shape[1:]
    low = 4
    while low < count:
        keep, got = halve(blocks.reshape((-1, 2, 2) + rest), "dp", low)
        blocks = plus(keep, got)
        low *= 2
    keep, got = halve(blocks.reshape((1, 2) + rest), "dp", 1)
    return keep[0], got[0]


def reduce_dense_far(blocks):
    count = lax.axis_size("dp")
    width, columns = blocks.shape
    rows = width // count
    blocks = blocks.reshape(count, 2, 2, rows // 4, columns)
    keep, got = halve(jnp.moveaxis(blocks, 2, 1), "expert", 1)
    keep, got = halve(plus(keep, got), "expert", 2)
    blocks = plus(keep, got)
    low = 1
    while low < count:
        keep, got = halve(blocks.reshape((-1, 2, 1) + blocks.shape[1:]), "dp", low)
        blocks = plus(keep, got).reshape((-1,) + blocks.shape[1:])
        low *= 2
    mine = blocks[0]
    chip = lax.axis_index("expert") // 2
    core = lax.rem(lax.axis_index("expert"), 2)
    other = swap_chip(mine)
    both = jnp.where(chip == 0, jnp.stack([mine, other]), jnp.stack([other, mine]))
    across = swap_core(both)
    all_four = jnp.where(core == 0, jnp.stack([both, across], 1), jnp.stack([across, both], 1))
    return all_four.reshape(rows, columns)


def own_share(matrix, along):
    count = lax.axis_size("dp")
    width = matrix.shape[along] // count
    return lax.dynamic_slice_in_dim(matrix, lax.axis_index("dp") * width, width, along)


def decayed(old, new):
    return STAT_DECAY * old + (1.0 - STAT_DECAY) * new


def factored(part, rows_old):
    square = part * part
    rows_new = decayed(rows_old, jnp.mean(square + EPS_STAT, axis=-1))
    return (
        rows_new,
        jnp.sum(square + EPS_STAT, axis=-2),
        jnp.sum(square / rows_new[..., None], axis=-2),
    )


def per_device(
    hidden_in,
    out_grad,
    segment_ids,
    parent_ids,
    positions,
    expert_ids,
    gate_weights,
    norm_gains,
    qkv_weight,
    out_weight,
    gate_up_weight,
    down_weight,
    gain_moment,
    qkv_rows,
    qkv_cols,
    out_rows,
    out_cols,
    gateup_rows,
    gateup_cols,
    down_rows,
    down_cols,
):
    rows_here = hidden_in.shape[0]
    dp_count = lax.axis_size("dp")
    groups = lax.axis_size("expert")
    experts_here = gate_up_weight.shape[0]
    total_experts = experts_here * groups
    capacity = 3 * rows_here * TOP // (2 * total_experts)
    half_experts = experts_here // 2
    dp_index = lax.axis_index("dp")
    pair_bit = lax.rem(dp_index, 2)
    z_bit = lax.rem(dp_index // 2, 2)
    first_local = pair_bit * half_experts
    first_expert = lax.axis_index("expert") * experts_here + first_local

    weight_high = gate_weights.astype(jnp.bfloat16)
    weight_low = (gate_weights - weight_high.astype(jnp.float32)).astype(jnp.bfloat16)
    routing = jnp.concatenate([expert_ids.astype(jnp.bfloat16), weight_high, weight_low], axis=1).T
    routing = jnp.pad(routing, ((0, ROUTE_ROWS - routing.shape[0]), (0, D - rows_here)))
    grad_rows = jnp.concatenate([out_grad.astype(jnp.bfloat16), routing], axis=0)
    chip_grad_rows = swap_chip(grad_rows)
    pair_grad_rows = swap_pair(grad_rows)
    ids = jnp.stack([segment_ids, parent_ids, positions])
    normed, qkv, attended, lse, middle, normed_ffn = attend(
        hidden_in, ids, norm_gains, qkv_weight, out_weight
    )
    received, arrived, scale, code = gather_and_select(
        normed_ffn, grad_rows, chip_grad_rows, pair_grad_rows, capacity, experts_here, half_experts, TOP, 5
    )
    scalars = jnp.stack([first_local, z_bit])
    experts = []
    near = []

    def near_sum(j):
        keep, give = experts[j][:2]
        near.append(plus(keep, swap(give, "dp", 2)))

    for j in range(half_experts):
        after = [experts[-1][2]] if experts else []
        if j == 3:
            near_sum(0)
            after.append(near[0])
        experts.append(
            run_expert(
                scalars, j, received, arrived, scale, gate_up_weight, down_weight, dp_count, after
            )
        )
    normed_f_grad, mix_sums = combine_and_return(
        code, [e[2] for e in experts], [e[3] for e in experts], capacity, 6
    )
    mix_parts = return_to_owners(mix_sums)
    block_out = middle + sum(part.astype(jnp.float32) for part in mix_parts)
    near_sum(1)
    input_grad, dense = attend_back(
        hidden_in, out_grad, middle, normed_f_grad, normed, qkv, attended, lse, ids, norm_gains, qkv_weight,
        out_weight, [near[1]]
    )
    for j in range(2, half_experts):
        near_sum(j)
    far = [far_sum(blocks) for blocks in near]
    own_parts = [own for own, _ in far]
    other_parts = [other for _, other in far]

    own = jnp.stack(own_parts).astype(jnp.float32)
    other = jnp.stack(other_parts).astype(jnp.float32)
    parts = jnp.where(pair_bit == 0, jnp.concatenate([own, other]), jnp.concatenate([other, own]))
    gateup_part = parts[:, : D // dp_count]
    down_part = parts[:, D // dp_count :]
    gateup_rows_new, gateup_square, gateup_scaled = factored(gateup_part, own_share(gateup_rows, 1))
    down_rows_new, down_square, down_scaled = factored(down_part, own_share(down_rows, 1))
    sizes = [gateup_square.size, gateup_scaled.size, down_square.size, down_scaled.size]
    summed = total_over(
        jnp.concatenate(
            [
                gateup_square.reshape(-1),
                gateup_scaled.reshape(-1),
                down_square.reshape(-1),
                down_scaled.reshape(-1),
                jnp.sum(gateup_rows_new, axis=1),
                jnp.sum(down_rows_new, axis=1),
            ]
        ),
        "dp",
        1,
    )
    pieces = jnp.split(summed, [sum(sizes[: i + 1]) for i in range(4)])
    gateup_square, gateup_scaled, down_square, down_scaled = [
        p.reshape(experts_here, D) for p in pieces[:4]
    ]
    gateup_row_mean = pieces[4][:experts_here] / D
    down_row_mean = pieces[4][experts_here:] / FF
    gateup_cols_new = decayed(gateup_cols, gateup_square / D)
    down_cols_new = decayed(down_cols, down_square / FF)
    expert_squares = jnp.stack(
        [
            jnp.sum(gateup_row_mean * jnp.sum(gateup_scaled / gateup_cols_new, axis=1)),
            jnp.sum(down_row_mean * jnp.sum(down_scaled / down_cols_new, axis=1)),
        ]
    )
    spread_squares = collect(
        jnp.zeros((8, 128), jnp.float32).at[0, :2].set(expert_squares), "expert", 2
    )
    expert_squares = jnp.sum(spread_squares[:, 0, :2], axis=0)

    qkv_columns = qkv_weight.shape[1]
    if D // dp_count % 64 == 0:
        dense_own = reduce_dense(dense, 3, [near[2]])
    else:
        dense_own = reduce_dense_far(dense)
    dense_own = dense_own.astype(jnp.float32)
    qkv_own = dense_own[:, :qkv_columns]
    out_own = dense_own[:, qkv_columns : qkv_columns + D]
    gains_own = dense_own[:, qkv_columns + D : qkv_columns + D + 2].T
    gain_moment_new = decayed(own_share(gain_moment, 1), gains_own * gains_own + EPS_STAT)
    gains_step = gains_own * lax.rsqrt(gain_moment_new)
    qkv_rows_new, qkv_square, qkv_scaled = factored(qkv_own, own_share(qkv_rows, 0))
    out_rows_new, out_square, out_scaled = factored(out_own, own_share(out_rows, 0))
    dense_sums = total_over(
        jnp.concatenate(
            [
                qkv_square,
                qkv_scaled,
                out_square,
                out_scaled,
                jnp.stack(
                    [jnp.sum(qkv_rows_new), jnp.sum(out_rows_new), jnp.sum(gains_step * gains_step)]
                ),
            ]
        ),
        "dp",
        4,
    )
    qkv_square, qkv_scaled, out_square, out_scaled, rest = jnp.split(
        dense_sums, [qkv_columns, 2 * qkv_columns, 2 * qkv_columns + D, 2 * qkv_columns + 2 * D]
    )
    qkv_row_mean = rest[0] / D
    out_row_mean = rest[1] / D
    qkv_cols_new = decayed(qkv_cols, qkv_square / D)
    out_cols_new = decayed(out_cols, out_square / D)
    squares = jnp.concatenate(
        [
            jnp.stack(
                [
                    rest[2],
                    qkv_row_mean * jnp.sum(qkv_scaled / qkv_cols_new),
                    out_row_mean * jnp.sum(out_scaled / out_cols_new),
                ]
            ),
            expert_squares,
        ]
    )
    element_counts = jnp.array(
        [2 * D, D * qkv_columns, D * D, total_experts * D * 2 * FF, total_experts * FF * D], jnp.float32
    )
    update_rms = jnp.sqrt(squares / element_counts)
    factors = LEARN_RATE / jnp.maximum(1.0, update_rms / CLIP_LEVEL)

    def stepped(weight, part, rows_new, row_mean, cols_new, factor):
        return weight.astype(jnp.float32) - part * (
            factor * lax.rsqrt(rows_new / row_mean[..., None])
        )[..., :, None] * lax.rsqrt(cols_new)[..., None, :]

    return (
        block_out,
        input_grad,
        update_rms,
        -factors[0] * gains_step,
        gain_moment_new,
        stepped(own_share(qkv_weight, 0), qkv_own, qkv_rows_new, qkv_row_mean, qkv_cols_new, factors[1]),
        qkv_rows_new,
        qkv_cols_new,
        stepped(own_share(out_weight, 0), out_own, out_rows_new, out_row_mean, out_cols_new, factors[2]),
        out_rows_new,
        out_cols_new,
        stepped(own_share(gate_up_weight, 1), gateup_part, gateup_rows_new, gateup_row_mean, gateup_cols_new, factors[3]),
        gateup_rows_new,
        gateup_cols_new,
        stepped(own_share(down_weight, 1), down_part, down_rows_new, down_row_mean, down_cols_new, factors[4]),
        down_rows_new,
        down_cols_new,
    )


def solution(mesh):
    placed = (
        P(("dp", "expert"), None),
        P(("dp", "expert"), None),
        P(("dp", "expert")),
        P(("dp", "expert")),
        P(("dp", "expert")),
        P(("dp", "expert"), None),
        P(("dp", "expert"), None),
        P(),
        P(),
        P(),
        P("expert", None, None),
        P("expert", None, None),
        P(),
        P(),
        P(),
        P(),
        P(),
        P("expert", None),
        P("expert", None),
        P("expert", None),
        P("expert", None),
    )
    return jax.shard_map(
        per_device,
        mesh=mesh,
        in_specs=placed,
        out_specs=(
            P(("dp", "expert"), None),
            P(("dp", "expert"), None),
            P(),
            P(None, "dp"),
            P(None, "dp"),
            P("dp", None),
            P("dp"),
            P(),
            P("dp", None),
            P("dp"),
            P(),
            P("expert", "dp", None),
            P("expert", "dp"),
            P("expert", None),
            P("expert", "dp", None),
            P("expert", "dp"),
            P("expert", None),
        ),
        check_vma=False,
    )
```

```python
import functools
import math

import jax
import jax.numpy as jnp
from jax import lax
from jax.experimental import pallas as pl
from jax.experimental.pallas import tpu as pltpu
from jax.sharding import PartitionSpec as P

VM = 60 * 1024 * 1024
SCALE = 1e6


def lasts(microseconds):
    return pl.CostEstimate(
        flops=int(microseconds * SCALE), bytes_accessed=1024, transcendentals=0
    )


def dot(a, b, ca=1, cb=0):
    return lax.dot_general(a, b, (((ca,), (cb,)), ((), ())), preferred_element_type=jnp.float32)


def one_hot(code, capacity):
    count, rows = code.shape
    place = lax.broadcasted_iota(jnp.int32, (capacity, rows), 0).astype(jnp.float32)
    return [place == code[j : j + 1, :] for j in range(count)]


def expert_kernel(owners, waits, s_ref, rec_ref, arr_ref, scale_ref, up_ref, down_ref, *refs):
    (keep_ref, give_ref, back_ref, mix_ref, act_s, gug_s, wg_s, wd_s) = refs[waits:]
    ff = down_ref.shape[1]
    rows, width = act_s.shape[0], up_ref.shape[1]
    tile = rows // 3
    up_w = up_ref[0]
    down_w = down_ref[0]
    received = rec_ref[0].reshape(rows, width)
    arrived = arr_ref[0].reshape(rows, width)
    scale = scale_ref[0].reshape(rows, 1)
    for t in range(3):
        at = slice(t * tile, (t + 1) * tile)
        gate_up = dot(received[at], up_w)
        act_grad = dot(arrived[at], down_w, 1, 1)
        gate = gate_up[:, :ff]
        up = gate_up[:, ff:]
        sig = 1.0 / (1.0 + jnp.exp(-gate))
        silu = gate * sig
        act_s[at, :] = (silu * up).astype(jnp.bfloat16)
        gug_s[at, :ff] = (act_grad * up * sig * (1.0 + gate * (1.0 - sig))).astype(jnp.bfloat16)
        gug_s[at, ff:] = (act_grad * silu).astype(jnp.bfloat16)
    wg_s[...] = dot(received, gug_s[...], 0, 0)
    wd_s[...] = dot(act_s[...], arrived, 0, 0)
    bit = s_ref[1]
    up_rows = width // owners
    down_rows = ff // owners
    for slot in range(owners // 2):
        for ref, side in ((keep_ref, bit), (give_ref, 1 - bit)):
            owner = 2 * slot + side
            ref[slot, :up_rows, :] = wg_s[
                pl.ds(pl.multiple_of(owner * up_rows, up_rows), up_rows), :
            ].astype(jnp.bfloat16)
            ref[slot, up_rows:, :] = wd_s[
                pl.ds(pl.multiple_of(owner * down_rows, down_rows), down_rows), :
            ].astype(jnp.bfloat16)
    for t in range(3):
        at = slice(t * tile, (t + 1) * tile)
        back = dot(gug_s[at, :], up_w, 1, 1).astype(jnp.bfloat16)
        mix = (dot(act_s[at, :], down_w) * scale[at]).astype(jnp.bfloat16)
        back_ref[at, :] = back
        mix_ref[at, :] = mix


def run_expert(scalars, j, received, arrived, scale, up_w, down_w, owners, after=()):
    count, sources, capacity, width = received.shape
    ff = down_w.shape[1]
    rows = sources * capacity
    share = (owners // 2, (width + ff) // owners, width)
    rows_spec = pl.BlockSpec((1, sources, capacity, width), lambda g, s: (j, 0, 0, 0))
    whole2 = lambda *shape: pl.BlockSpec(shape, lambda g, s: (0,) * len(shape))
    slots = jax.ShapeDtypeStruct((rows, width), jnp.bfloat16)
    parts = jax.ShapeDtypeStruct(share, jnp.bfloat16)
    return pl.pallas_call(
        functools.partial(expert_kernel, owners, len(after)),
        out_shape=(parts, parts, slots, slots),
        grid_spec=pltpu.PrefetchScalarGridSpec(
            num_scalar_prefetch=1,
            grid=(1,),
            in_specs=[
                rows_spec,
                rows_spec,
                pl.BlockSpec((1, sources, capacity, 1), lambda g, s: (j, 0, 0, 0)),
                pl.BlockSpec((1, width, 2 * ff), lambda g, s: (s[0] + j, 0, 0)),
                pl.BlockSpec((1, ff, width), lambda g, s: (s[0] + j, 0, 0)),
            ]
            + [pl.BlockSpec(memory_space=pl.ANY)] * len(after),
            out_specs=[whole2(*share), whole2(*share), whole2(rows, width), whole2(rows, width)],
            scratch_shapes=[
                pltpu.VMEM((rows, ff), jnp.bfloat16),
                pltpu.VMEM((rows, 2 * ff), jnp.bfloat16),
                pltpu.VMEM((width, 2 * ff), jnp.float32),
                pltpu.VMEM((ff, width), jnp.float32),
            ],
        ),
        compiler_params=pltpu.CompilerParams(vmem_limit_bytes=VM),
        cost_estimate=lasts(18),
        name="expert_%d" % j,
    )(scalars, received, arrived, scale, up_w, down_w, *after)


HEADS = 16
KV_HEADS = 8
HEAD_DIM = 64
EPS_NORM = 1e-06
ROPE_BASE = 10000.0
MASKED = -1e30
LANES = 128


def spread(row):
    rows = row.shape[1]
    by_column = jnp.broadcast_to(row.astype(jnp.float32), (rows, rows))
    return by_column, by_column.T


def mask_and_angles(ids_ref):
    seg_k, seg_q = spread(ids_ref[0:1, :])
    par_k, par_q = spread(ids_ref[1:2, :])
    pos_k, pos_q = spread(ids_ref[2:3, :])
    seen = ((seg_k == seg_q) | (seg_k == par_q) | (seg_k == par_k)) & (pos_k <= pos_q)
    bias = jnp.where(seen, 0.0, MASKED)
    lane = lax.broadcasted_iota(jnp.int32, (seg_k.shape[0], LANES), 1)
    half = HEAD_DIM // 2
    place = lax.rem(lane, half).astype(jnp.float32)
    frequency = jnp.exp(place * (-2.0 * math.log(ROPE_BASE) / HEAD_DIM))
    angles = pos_q[:, :LANES] * frequency
    front = lax.rem(lane, HEAD_DIM) < half
    sine = jnp.sin(angles)
    return bias, jnp.cos(angles), jnp.where(front, -sine, sine), front, lane


def turned(block, cosine, sine, front):
    other = jnp.where(
        front,
        pltpu.roll(block, LANES - HEAD_DIM // 2, 1),
        pltpu.roll(block, HEAD_DIM // 2, 1),
    )
    return block * cosine + other * sine


def two_diagonal(pair, which, lane):
    rolled = pltpu.roll(pair, HEAD_DIM, 1)
    first, last = (pair, rolled) if which == 0 else (rolled, pair)
    low = lane < HEAD_DIM
    return jnp.concatenate(
        [jnp.where(low, first, 0.0), jnp.where(low, 0.0, last)], axis=0
    ).astype(jnp.bfloat16)


def column_block(index):
    return pl.ds(pl.multiple_of(index * LANES, LANES), LANES)


def attend_kernel(hidden_ref, ids_ref, gains_ref, qkv_w_ref, out_w_ref,
                  normed_ref, qkv_ref, attended_ref, lse_ref, middle_ref, normed_f_ref, proj_s, bias_s):
    rows = hidden_ref.shape[0]
    att = HEADS * HEAD_DIM
    kv = KV_HEADS * HEAD_DIM
    hidden = hidden_ref[...]
    gains = gains_ref[...].astype(jnp.float32)
    inverse = lax.rsqrt(jnp.mean(hidden * hidden, axis=-1, keepdims=True) + EPS_NORM)
    normed_ref[...] = (hidden * inverse * gains[0:1, :]).astype(jnp.bfloat16)
    proj_s[...] = dot(normed_ref[...], qkv_w_ref[...])
    bias, cosine, sine, front, lane = mask_and_angles(ids_ref)
    bias_s[...] = bias
    lse_ref[...] = jnp.zeros_like(lse_ref)

    def pair_step(p, carry):
        key_at = column_block(att // LANES + p)
        value_at = column_block((att + kv) // LANES + p)
        keys = turned(proj_s[:, key_at], cosine, sine, front).astype(jnp.bfloat16)
        values = proj_s[:, value_at].astype(jnp.bfloat16)
        qkv_ref[:, key_at] = keys
        qkv_ref[:, value_at] = values
        keys = keys.astype(jnp.float32)
        values = values.astype(jnp.float32)
        for which in range(2):
            query_at = column_block(2 * p + which)
            queries = turned(proj_s[:, query_at], cosine, sine, front).astype(jnp.bfloat16)
            queries = (queries.astype(jnp.float32) * HEAD_DIM**-0.5).astype(jnp.bfloat16)
            qkv_ref[:, query_at] = queries
            scores = dot(queries, two_diagonal(keys, which, lane), 1, 1)
            probs = []
            for head in range(2):
                part = scores[:, head * rows : (head + 1) * rows] + bias_s[...]
                top = jnp.max(part, axis=-1, keepdims=True)
                part = jnp.exp(part - top)
                total = jnp.sum(part, axis=-1, keepdims=True)
                probs.append((part * (1.0 / total)).astype(jnp.bfloat16))
                at = 4 * p + 2 * which + head
                lse_ref[...] = jnp.where(lane == at, top + jnp.log(total), lse_ref[...])
            attended_ref[:, query_at] = dot(
                jnp.concatenate(probs, axis=1), two_diagonal(values, which, lane)
            ).astype(jnp.bfloat16)
        return carry

    lax.fori_loop(0, KV_HEADS // 2, pair_step, 0)
    middle = hidden + dot(attended_ref[...], out_w_ref[...])
    middle_ref[...] = middle
    inverse_f = lax.rsqrt(jnp.mean(middle * middle, axis=-1, keepdims=True) + EPS_NORM)
    normed_f_ref[...] = (middle * inverse_f * gains[1:2, :]).astype(jnp.bfloat16)


def attend(hidden, ids, gains, qkv_w, out_w):
    rows, width = hidden.shape
    shape = jax.ShapeDtypeStruct
    return pl.pallas_call(
        attend_kernel,
        out_shape=(
            shape((rows, width), jnp.bfloat16),
            shape((rows, qkv_w.shape[1]), jnp.bfloat16),
            shape((rows, out_w.shape[0]), jnp.bfloat16),
            shape((rows, LANES), jnp.float32),
            shape((rows, width), jnp.float32),
            shape((rows, width), jnp.bfloat16),
        ),
        in_specs=[pl.BlockSpec(memory_space=pltpu.VMEM)] * 5,
        out_specs=[pl.BlockSpec(memory_space=pltpu.VMEM)] * 6,
        scratch_shapes=[
            pltpu.VMEM((rows, qkv_w.shape[1]), jnp.float32),
            pltpu.VMEM((rows, rows), jnp.float32),
        ],
        compiler_params=pltpu.CompilerParams(vmem_limit_bytes=VM),
        cost_estimate=lasts(18),
        name="attend",
    )(hidden, ids, gains, qkv_w, out_w)


def attend_back_kernel(hidden_ref, grad_ref, middle_ref, normed_grad_ref, normed_ref, qkv_ref, attended_ref, lse_ref,
                       ids_ref, gains_ref, qkv_w_ref, out_w_ref, *refs):
    input_grad_ref, dense_ref, proj_s, bias_s, back_s = refs[-5:]
    rows, width = hidden_ref.shape
    att = HEADS * HEAD_DIM
    kv = KV_HEADS * HEAD_DIM
    gains = gains_ref[...].astype(jnp.float32)
    normed_grad = normed_grad_ref[...]
    middle = middle_ref[...]
    inverse_f = lax.rsqrt(jnp.mean(middle * middle, axis=-1, keepdims=True) + EPS_NORM)
    gain_f = jnp.sum(normed_grad * middle * inverse_f, axis=0, keepdims=True)
    weighted = normed_grad * gains[1:2, :]
    middle_grad = grad_ref[...] + (
        inverse_f * weighted
        - middle * (inverse_f * inverse_f * inverse_f)
        * jnp.mean(weighted * middle, axis=-1, keepdims=True)
    )
    input_grad_ref[...] = middle_grad
    branch = middle_grad.astype(jnp.bfloat16)
    columns = att + 2 * kv
    dense_ref[:, columns : columns + width] = dot(attended_ref[...], branch, 0, 0).astype(jnp.bfloat16)
    back_s[...] = dot(branch, out_w_ref[...], 1, 1).astype(jnp.bfloat16)
    bias, cosine, sine, front, lane = mask_and_angles(ids_ref)
    bias_s[...] = bias
    low = lane < HEAD_DIM

    def pair_step(p, carry):
        key_at = column_block(att // LANES + p)
        value_at = column_block((att + kv) // LANES + p)
        keys = qkv_ref[:, key_at].astype(jnp.float32)
        values = qkv_ref[:, value_at].astype(jnp.float32)
        key_grads = []
        value_grads = []
        for which in range(2):
            query_at = column_block(2 * p + which)
            queries = qkv_ref[:, query_at]
            back = back_s[:, query_at]
            key_two = two_diagonal(keys, which, lane)
            scores = dot(queries, key_two, 1, 1)
            prob_grads = dot(back, two_diagonal(values, which, lane), 1, 1)
            probs = []
            score_grads = []
            for head in range(2):
                at = 4 * p + 2 * which + head
                level = jnp.sum(jnp.where(lane == at, lse_ref[...], 0.0), axis=-1, keepdims=True)
                span = slice(head * rows, (head + 1) * rows)
                prob = jnp.exp(scores[:, span] + bias_s[...] - level)
                prob_grad = prob_grads[:, span]
                row_dot = jnp.sum(prob * prob_grad, axis=-1, keepdims=True)
                probs.append(prob.astype(jnp.bfloat16))
                score_grads.append((prob * (prob_grad - row_dot)).astype(jnp.bfloat16))
            score_grads = jnp.concatenate(score_grads, axis=1)
            query_grad = dot(score_grads, key_two) * HEAD_DIM**-0.5
            proj_s[:, query_at] = turned(query_grad, cosine, -sine, front).astype(jnp.bfloat16)
            for grads, left, right in (
                (key_grads, score_grads, queries),
                (value_grads, jnp.concatenate(probs, axis=1), back),
            ):
                both = dot(left, right, 0, 0)
                first, last = both[:rows], both[rows:]
                if which == 0:
                    grads.append(first + pltpu.roll(last, HEAD_DIM, 1))
                else:
                    grads.append(pltpu.roll(first, HEAD_DIM, 1) + last)
        key_grad = jnp.where(low, key_grads[0], key_grads[1])
        proj_s[:, key_at] = turned(key_grad, cosine, -sine, front).astype(jnp.bfloat16)
        proj_s[:, value_at] = jnp.where(low, value_grads[0], value_grads[1]).astype(jnp.bfloat16)
        return carry

    lax.fori_loop(0, KV_HEADS // 2, pair_step, 0)
    dense_ref[:, :columns] = dot(normed_ref[...], proj_s[...], 0, 0).astype(jnp.bfloat16)
    normed_grad = dot(proj_s[...], qkv_w_ref[...], 1, 1)
    hidden = hidden_ref[...]
    inverse = lax.rsqrt(jnp.mean(hidden * hidden, axis=-1, keepdims=True) + EPS_NORM)
    gain_a = jnp.sum(normed_grad * hidden * inverse, axis=0, keepdims=True)
    weighted = normed_grad * gains[0:1, :]
    input_grad_ref[...] += inverse * weighted - hidden * (inverse * inverse * inverse) * jnp.mean(
        weighted * hidden, axis=-1, keepdims=True
    )
    both = jnp.concatenate([gain_a, gain_f, jnp.zeros((LANES - 2, width), jnp.float32)], axis=0)
    dense_ref[:, columns + width :] = both.T.astype(jnp.bfloat16)


def attend_back(hidden, out_grad, middle, normed_f_grad, normed, qkv, attended, lse, ids, gains, qkv_w, out_w, after=()):
    rows, width = hidden.shape
    columns = qkv_w.shape[1] + width + LANES
    return pl.pallas_call(
        attend_back_kernel,
        out_shape=(
            jax.ShapeDtypeStruct((rows, width), jnp.float32),
            jax.ShapeDtypeStruct((width, columns), jnp.bfloat16),
        ),
        in_specs=[pl.BlockSpec(memory_space=pltpu.VMEM)] * 12
        + [pl.BlockSpec(memory_space=pl.ANY)] * len(after),
        out_specs=[pl.BlockSpec(memory_space=pltpu.VMEM)] * 2,
        scratch_shapes=[
            pltpu.VMEM((rows, qkv_w.shape[1]), jnp.bfloat16),
            pltpu.VMEM((rows, rows), jnp.float32),
            pltpu.VMEM((rows, out_w.shape[0]), jnp.bfloat16),
        ],
        compiler_params=pltpu.CompilerParams(vmem_limit_bytes=VM),
        cost_estimate=lasts(26),
        name="attend_back",
    )(hidden, out_grad, middle, normed_f_grad, normed, qkv, attended, lse, ids, gains, qkv_w, out_w, *after)


MESH = pl.DeviceIdType.MESH


def greet(peers):
    barrier = pltpu.get_barrier_semaphore()
    for peer in peers:
        pl.semaphore_signal(barrier, inc=1, device_id=peer, device_id_type=MESH)
    pl.semaphore_wait(barrier, len(peers))


def total_kernel(axis, count, mine_ref, *refs):
    out_ref, got_ref, send_sem, recv_sem = refs[-4:]
    me = lax.axis_index(axis)
    after = [lax.rem(me + k, count) for k in range(count)]
    greet([{axis: after[k]} for k in range(1, count)])
    scatter = [
        pltpu.make_async_remote_copy(
            src_ref=mine_ref.at[after[k]],
            dst_ref=got_ref.at[k],
            send_sem=send_sem.at[0, k],
            recv_sem=recv_sem.at[0, k],
            device_id={axis: after[k]},
            device_id_type=MESH,
        )
        for k in range(1, count)
    ]
    for copy in scatter:
        copy.start()
    total = mine_ref[me]
    for k in range(1, count):
        scatter[k - 1].wait_recv()
        total = total + got_ref[k]
    out_ref[me] = total
    share = [
        pltpu.make_async_remote_copy(
            src_ref=out_ref.at[me],
            dst_ref=out_ref.at[me],
            send_sem=send_sem.at[1, k],
            recv_sem=recv_sem.at[1, k],
            device_id={axis: after[k]},
            device_id_type=MESH,
        )
        for k in range(1, count)
    ]
    for copy in share:
        copy.start()
    for copy in share:
        copy.wait_recv()
    for copy in scatter + share:
        copy.wait_send()


def total_over(values, axis, label, after=()):
    count = lax.axis_size(axis)
    rows = -(-values.shape[0] // (8 * 128 * count)) * 8
    padded = jnp.pad(values, (0, count * rows * 128 - values.shape[0])).reshape(count, rows, 128)
    out = pl.pallas_call(
        functools.partial(total_kernel, axis, count),
        out_shape=jax.ShapeDtypeStruct(padded.shape, jnp.float32),
        in_specs=[pl.BlockSpec(memory_space=pltpu.VMEM)] + [pl.BlockSpec(memory_space=pl.ANY)] * len(after),
        out_specs=pl.BlockSpec(memory_space=pltpu.VMEM),
        scratch_shapes=[
            pltpu.VMEM(padded.shape, jnp.float32),
            pltpu.SemaphoreType.DMA((2, count)),
            pltpu.SemaphoreType.DMA((2, count)),
        ],
        compiler_params=pltpu.CompilerParams(
            collective_id=label, has_side_effects=True, vmem_limit_bytes=16 * 1024 * 1024
        ),
        cost_estimate=lasts(12),
        name="total_%d" % label,
    )(padded, *after)
    return out.reshape(-1)[: values.shape[0]]


def collect_kernel(axis, count, mine_ref, out_ref, send_sem, recv_sem, local_sem):
    me = lax.axis_index(axis)
    after = [lax.rem(me + k, count) for k in range(count)]
    greet([{axis: after[k]} for k in range(1, count)])
    copies = [
        pltpu.make_async_remote_copy(
            src_ref=mine_ref,
            dst_ref=out_ref.at[me],
            send_sem=send_sem.at[k],
            recv_sem=recv_sem.at[k],
            device_id={axis: after[k]},
            device_id_type=MESH,
        )
        for k in range(1, count)
    ]
    for copy in copies:
        copy.start()
    out_ref[me] = mine_ref[...]
    for copy in copies:
        copy.wait()


def collect(values, axis, label):
    count = lax.axis_size(axis)
    return pl.pallas_call(
        functools.partial(collect_kernel, axis, count),
        out_shape=jax.ShapeDtypeStruct((count,) + values.shape, jnp.float32),
        in_specs=[pl.BlockSpec(memory_space=pltpu.VMEM)],
        out_specs=pl.BlockSpec(memory_space=pltpu.VMEM),
        scratch_shapes=[
            pltpu.SemaphoreType.DMA((count,)),
            pltpu.SemaphoreType.DMA((count,)),
            pltpu.SemaphoreType.DMA,
        ],
        compiler_params=pltpu.CompilerParams(
            collective_id=label, has_side_effects=True, vmem_limit_bytes=16 * 1024 * 1024
        ),
        cost_estimate=lasts(4),
        name="collect_%d" % label,
    )(values)


def flipped(axis, mask):
    index = lax.axis_index(axis)
    bit = lax.rem(index // mask, 2)
    return bit, {axis: index + mask - 2 * mask * bit}


def dense_kernel(orders, spans, waits, far_bit, mine_ref, go_ref, *refs):
    steps = len(orders[0])
    (out_ref, come_ref, sum_ref), scratch = refs[waits : waits + 3], refs[waits + 3 :]
    first_got = scratch[0]
    got = scratch[1 : 1 + steps]
    send_sem, recv_sem = scratch[1 + steps :]
    bits = len(mine_ref.shape) - 4
    core, core_peer = flipped("expert", 1)
    chip, chip_peer = flipped("expert", 2)
    links = [flipped("dp", 1 << b) for b in range(bits)] + [(chip, chip_peer)]
    greet([core_peer] + [peer for _, peer in links])
    whole = (slice(None),) * bits
    copies = []

    def send(src, dst, peer, part, step):
        copy = pltpu.make_async_remote_copy(
            src_ref=src,
            dst_ref=dst,
            send_sem=send_sem.at[part, step],
            recv_sem=recv_sem.at[part, step],
            device_id=peer,
            device_id_type=MESH,
        )
        copy.start()
        copies.append(copy)
        return copy

    def add(first, second):
        return (first.astype(jnp.float32) + second.astype(jnp.float32)).astype(jnp.bfloat16)

    flying = []
    beside = send(go_ref, come_ref, links[far_bit][1], 0, 3 + steps)
    for part, span in enumerate(spans):
        at = whole + (1 - core, slice(None), slice(None), span)
        flying.append(send(mine_ref.at[at], first_got.at[..., span], core_peer, part, 0))

    def place(chosen, span):
        return tuple(chosen.get(bits - 1 - i, slice(None)) for i in range(bits)) + (
            chosen.get(bits, slice(None)),
            slice(None),
            span,
        )

    chosen = [{} for _ in spans]
    for step in range(steps + 1):
        for part, span in enumerate(spans):
            flying[part].wait_recv()
            if step == 0:
                sum_ref[..., span] = add(
                    mine_ref[whole + (core, slice(None), slice(None), span)], first_got[..., span]
                )
            else:
                here = place(chosen[part], span)
                sum_ref[here] = add(sum_ref[here], got[step - 1][part_index(orders, part, step - 1) + (slice(None), span)])
            if step < steps:
                link = orders[part][step]
                bit, peer = links[link]
                away = place({**chosen[part], link: 1 - bit}, span)
                flying[part] = send(
                    sum_ref.at[away],
                    got[step].at[part_index(orders, part, step) + (slice(None), span)],
                    peer,
                    part,
                    1 + step,
                )
                chosen[part] = {**chosen[part], link: bit}
            else:
                out_ref[core, chip, :, span] = sum_ref[place(chosen[part], span)]
                mine = out_ref.at[core, chip, :, span]
                flying[part] = send(mine, mine, chip_peer, part, 1 + steps)
    for part, span in enumerate(spans):
        flying[part].wait_recv()
        mine = out_ref.at[core, :, :, span]
        flying[part] = send(mine, mine, core_peer, part, 2 + steps)
    for copy in flying + [beside]:
        copy.wait_recv()
    for copy in copies:
        copy.wait_send()


def part_index(orders, part, step):
    return (slice(None),) * (len(orders[part]) - 1 - step)


def reduce_dense(dense, go, far_mask, label, after=()):
    owners = lax.axis_size("dp")
    width, columns = dense.shape
    bits = owners.bit_length() - 1
    rows = width // owners // 4
    tiles = columns // 128
    parts = bits
    bounds = [128 * (tiles * i // parts) for i in range(parts + 1)]
    spans = [slice(a, b) for a, b in zip(bounds[:-1], bounds[1:])]
    all_links = list(range(bits + 1))
    starts = [bits, 0, 1] + list(range(2, bits))
    orders = [tuple(all_links[s:] + all_links[:s]) for s in starts[:parts]]
    shape = (2,) * bits + (2, 2, rows, columns)
    half = (2,) * bits + (2, rows, columns)
    out, come = pl.pallas_call(
        functools.partial(dense_kernel, orders, spans, len(after), far_mask.bit_length() - 1),
        out_shape=(
            jax.ShapeDtypeStruct((2, 2, rows, columns), jnp.bfloat16),
            jax.ShapeDtypeStruct(go.shape, jnp.bfloat16),
        ),
        in_specs=[pl.BlockSpec(memory_space=pltpu.VMEM)]
        + [pl.BlockSpec(memory_space=pl.ANY)] * (1 + len(after)),
        out_specs=[pl.BlockSpec(memory_space=pltpu.VMEM), pl.BlockSpec(memory_space=pl.ANY)],
        scratch_shapes=[pltpu.VMEM(half, jnp.bfloat16), pltpu.VMEM(half, jnp.bfloat16)]
        + [
            pltpu.VMEM((2,) * (bits - step) + (rows, columns), jnp.bfloat16)
            for step in range(bits + 1)
        ]
        + [pltpu.SemaphoreType.DMA((parts, bits + 5)), pltpu.SemaphoreType.DMA((parts, bits + 5))],
        compiler_params=pltpu.CompilerParams(
            collective_id=label, has_side_effects=True, vmem_limit_bytes=VM
        ),
        cost_estimate=lasts(50),
        name="reduce_dense",
    )(dense.reshape(shape), go, *after)
    return out.reshape(width // owners, columns), come


PAIR = 2
ROUTE_ROWS = 32


class Pusher:
    def __init__(self, send_sem, recv_sem):
        self.send_sem, self.recv_sem, self.copies = send_sem, recv_sem, []

    def __call__(self, src, dst, peer):
        at = len(self.copies)
        copy = pltpu.make_async_remote_copy(
            src_ref=src,
            dst_ref=dst,
            send_sem=self.send_sem.at[at],
            recv_sem=self.recv_sem.at[at],
            device_id=peer,
            device_id_type=MESH,
        )
        copy.start()
        self.copies.append(copy)
        return copy

    def finish(self):
        for copy in self.copies:
            copy.wait_send()


def picked(code, capacity):
    return jnp.concatenate(
        [c.astype(jnp.float32) for c in one_hot(code, capacity)], axis=0
    ).astype(jnp.bfloat16)


def gather_kernel(capacity, experts_here, half_experts, top, token_ref, grad_ref, chip_grad_ref, pair_grad_ref,
                  rec_ref, arr_ref, scale_ref, code_ref, tokens, grads, weight_s, stage, send_sem, recv_sem, local_sem):
    rows = token_ref.shape[0]
    half = rows // 2
    first = lax.axis_index("expert") * experts_here + lax.rem(lax.axis_index("dp") // PAIR, 2) * half_experts
    _, core = flipped("expert", 1)
    _, chip = flipped("expert", 2)
    _, pair = flipped("dp", PAIR)
    greet([core, chip, pair])
    push = Pusher(send_sem, recv_sem)
    everything, routing = slice(None), slice(rows, rows + ROUTE_ROWS)
    to_chip = push(token_ref, tokens.at[2], chip)
    to_pair = push(token_ref, tokens.at[4], pair)
    route_both = push(pair_grad_ref.at[routing], grads.at[6, routing], chip)
    to_core = push(token_ref, tokens.at[1], core)
    grad_core = push(grad_ref, grads.at[1], core)
    grad_chip_core = push(chip_grad_ref, grads.at[3], core)
    grad_pair_core = push(pair_grad_ref, grads.at[5], core)

    earlier = lax.broadcasted_iota(jnp.int32, (rows, rows), 0)
    later = lax.broadcasted_iota(jnp.int32, (rows, rows), 1)
    before = jnp.where(earlier < later, 1.0, 0.0).astype(jnp.bfloat16)

    def route(r, table):
        table = table.astype(jnp.float32)
        ids = table[:top]
        gates = table[top : 2 * top] + table[2 * top : 3 * top]
        hits = [ids == (first + j).astype(jnp.float32) for j in range(half_experts)]
        named = jnp.concatenate(
            [jnp.max(jnp.where(hit, 1.0, 0.0), axis=0, keepdims=True) for hit in hits], axis=0
        )
        weight_s[r] = jnp.concatenate(
            [jnp.sum(jnp.where(hit, gates, 0.0), axis=0, keepdims=True) for hit in hits], axis=0
        )
        code_ref[r] = jnp.where(named > 0.0, dot(named.astype(jnp.bfloat16), before), -1.0)

    leaving = []

    def select(r, source, out_ref, weighted):
        slot = len(leaving) % stage.shape[0]
        if len(leaving) >= stage.shape[0]:
            leaving[len(leaving) - stage.shape[0]].wait()
        chosen = one_hot(code_ref[r], capacity)
        pick = jnp.concatenate([c.astype(jnp.float32) for c in chosen], axis=0).astype(jnp.bfloat16)
        made = dot(pick, source)
        for j in range(half_experts):
            part = made[j * capacity : (j + 1) * capacity]
            if weighted:
                scale = jnp.sum(
                    jnp.where(chosen[j], weight_s[r, j : j + 1, :], 0.0), axis=1, keepdims=True
                )
                scale_ref[j, r] = scale
                part = part * scale
            stage[slot, j] = part.astype(jnp.bfloat16)
        copy = pltpu.make_async_copy(stage.at[slot], out_ref.at[:, r], local_sem.at[slot])
        copy.start()
        leaving.append(copy)

    def select_grad(r, ref):
        route(r, ref[rows:, :rows])
        select(r, ref[:rows, :], arr_ref, True)

    select_grad(0, grad_ref)
    select(0, token_ref[...], rec_ref, False)
    select_grad(2, chip_grad_ref)
    select_grad(4, pair_grad_ref)
    for r, copy in ((1, grad_core), (3, grad_chip_core), (5, grad_pair_core)):
        copy.wait_recv()
        select_grad(r, grads.at[r])
    to_core.wait_recv()
    select(1, tokens[1], rec_ref, False)
    route_both.wait_recv()
    route_core = push(grads.at[6, routing], grads.at[7, routing], core)
    to_chip.wait_recv()
    both_low = push(tokens.at[2, half:rows], tokens.at[6, half:rows], pair)
    chip_core = push(tokens.at[2], tokens.at[3], core)
    to_pair.wait_recv()
    both_high = push(tokens.at[4, 0:half], tokens.at[6, 0:half], chip)
    pair_core = push(tokens.at[4], tokens.at[5], core)
    grad_low = push(chip_grad_ref.at[half:rows], grads.at[6, half:rows], pair)
    grad_high = push(pair_grad_ref.at[0:half], grads.at[6, 0:half], chip)
    select(2, tokens[2], rec_ref, False)
    select(4, tokens[4], rec_ref, False)
    route(6, grads[6, rows:, :rows])
    route_core.wait_recv()
    route(7, grads[7, rows:, :rows])
    chip_core.wait_recv()
    select(3, tokens[3], rec_ref, False)
    pair_core.wait_recv()
    select(5, tokens[5], rec_ref, False)
    both_low.wait_recv()
    both_high.wait_recv()
    both_core = push(tokens.at[6], tokens.at[7], core)
    select(6, tokens[6], rec_ref, False)
    both_core.wait_recv()
    select(7, tokens[7], rec_ref, False)
    grad_low.wait_recv()
    grad_high.wait_recv()
    grad_both_core = push(grads.at[6, 0:rows], grads.at[7, 0:rows], core)
    select(6, grads[6, :rows], arr_ref, True)
    grad_both_core.wait_recv()
    select(7, grads[7, :rows], arr_ref, True)
    for copy in leaving[-stage.shape[0] :]:
        copy.wait()
    push.finish()


def gather_and_select(token, grad, chip_grad, pair_grad, capacity, experts_here, half_experts, top, label):
    rows, width = token.shape
    vmem = pl.BlockSpec(memory_space=pltpu.VMEM)
    anywhere = pl.BlockSpec(memory_space=pl.ANY)
    slots = jax.ShapeDtypeStruct((half_experts, 8, capacity, width), jnp.bfloat16)
    return pl.pallas_call(
        functools.partial(gather_kernel, capacity, experts_here, half_experts, top),
        out_shape=(
            slots,
            slots,
            jax.ShapeDtypeStruct((half_experts, 8, capacity, 1), jnp.float32),
            jax.ShapeDtypeStruct((8, half_experts, rows), jnp.float32),
        ),
        in_specs=[vmem] * 4,
        out_specs=[anywhere, anywhere, vmem, vmem],
        scratch_shapes=[
            pltpu.VMEM((8, rows, width), jnp.bfloat16),
            pltpu.VMEM((8, rows + ROUTE_ROWS, width), jnp.bfloat16),
            pltpu.VMEM((8, half_experts, rows), jnp.float32),
            pltpu.VMEM((4, half_experts, capacity, width), jnp.bfloat16),
            pltpu.SemaphoreType.DMA((18,)),
            pltpu.SemaphoreType.DMA((18,)),
            pltpu.SemaphoreType.DMA((4,)),
        ],
        compiler_params=pltpu.CompilerParams(
            collective_id=label, has_side_effects=True, vmem_limit_bytes=VM
        ),
        cost_estimate=lasts(44),
        name="gather_and_select",
    )(token, grad, chip_grad, pair_grad)


def return_kernel(capacity, count, far_mask, code_ref, *refs):
    backs, mixes = refs[:count], refs[count : 2 * count]
    go_ref, out_ref, near_ref, far_ref, come_ref = refs[2 * count : 2 * count + 5]
    (fetched, theirs, core_got, own, theirs_mix, core_got_mix, half_pair, half_chip, from_chip, from_pair,
     send_sem, recv_sem, local_sem) = refs[2 * count + 5 :]
    rows = out_ref.shape[0]
    half = rows // 2
    _, core = flipped("expert", 1)
    _, chip = flipped("expert", 2)
    _, pair = flipped("dp", PAIR)
    _, far = flipped("dp", far_mask)
    greet([core, chip, pair, far])
    push = Pusher(send_sem, recv_sem)
    beside = push(go_ref, come_ref, far)
    order = [(backs, r) for r in (7, 6, 3, 2, 5, 4, 1, 0)] + [(mixes, r) for r in (7, 6, 3, 2, 5, 4, 1, 0)]
    depth = fetched.shape[0]
    fetching = []

    def fetch():
        n = len(fetching)
        if n < len(order):
            slots, r = order[n]
            fetching.append(
                [
                    pltpu.make_async_copy(
                        ref.at[r * capacity : (r + 1) * capacity],
                        fetched.at[n % depth, j * capacity : (j + 1) * capacity],
                        local_sem.at[n % depth, j],
                    )
                    for j, ref in enumerate(slots)
                ]
            )
            for copy in fetching[-1]:
                copy.start()

    done = []

    def combined():
        n = len(done)
        for copy in fetching[n]:
            copy.wait()
        made = dot(picked(code_ref[order[n][1]], capacity), fetched[n % depth], 0, 0)
        done.append(n)
        return made

    for _ in range(depth - 1):
        fetch()

    def next_sum():
        fetch()
        return combined()

    def plus(a, b):
        return (a + b.astype(jnp.float32)).astype(jnp.bfloat16)

    def sums(i, theirs, core_got):
        theirs[i] = next_sum().astype(jnp.bfloat16)
        copy = push(theirs.at[i], core_got.at[i], core)
        return next_sum(), copy

    mine, copy = sums(3, theirs, core_got)
    copy.wait_recv()
    own[3] = plus(mine, core_got[3])
    at_pair = push(own.at[3, 0:half], half_pair, pair)
    at_chip = push(own.at[3, half:rows], half_chip, chip)
    mine, copy = sums(1, theirs, core_got)
    copy.wait_recv()
    own[1] = plus(mine, core_got[1])
    low_chip = push(own.at[1, half:rows], from_chip.at[half:rows], chip)
    mine, copy = sums(2, theirs, core_got)
    copy.wait_recv()
    own[2] = plus(mine, core_got[2])
    high_pair = push(own.at[2, 0:half], from_pair.at[0:half], pair)
    mine, copy = sums(0, theirs, core_got)
    copy.wait_recv()
    out_ref[...] = mine + core_got[0].astype(jnp.float32)
    mine, copy = sums(3, theirs_mix, core_got_mix)
    copy.wait_recv()
    far_ref[1] = plus(mine, core_got_mix[3])
    at_pair.wait_recv()
    own[1, :half] = plus(own[1, :half].astype(jnp.float32), half_pair[...])
    high_chip = push(own.at[1, 0:half], from_chip.at[0:half], chip)
    at_chip.wait_recv()
    own[2, half:] = plus(own[2, half:].astype(jnp.float32), half_chip[...])
    low_pair = push(own.at[2, half:rows], from_pair.at[half:rows], pair)
    for i in (1, 2, 0):
        mine, copy = sums(i, theirs_mix, core_got_mix)
        copy.wait_recv()
        (far_ref if i > 1 else near_ref)[i % 2] = plus(mine, core_got_mix[i])
    low_chip.wait_recv()
    high_pair.wait_recv()
    high_chip.wait_recv()
    low_pair.wait_recv()
    out_ref[...] += from_chip[...].astype(jnp.float32) + from_pair[...].astype(jnp.float32)
    beside.wait_recv()
    push.finish()


def combine_and_return(code, backs, mixes, capacity, go, far_mask, label):
    _, count, rows = code.shape
    width = backs[0].shape[1]
    vmem = pl.BlockSpec(memory_space=pltpu.VMEM)
    anywhere = pl.BlockSpec(memory_space=pl.ANY)
    four = pltpu.VMEM((4, rows, width), jnp.bfloat16)
    return pl.pallas_call(
        functools.partial(return_kernel, capacity, count, far_mask),
        out_shape=(
            jax.ShapeDtypeStruct((rows, width), jnp.float32),
            jax.ShapeDtypeStruct((2, rows, width), jnp.bfloat16),
            jax.ShapeDtypeStruct((2, rows, width), jnp.bfloat16),
            jax.ShapeDtypeStruct(go.shape, jnp.bfloat16),
        ),
        in_specs=[vmem] + [anywhere] * (2 * count + 1),
        out_specs=[vmem, vmem, vmem, anywhere],
        scratch_shapes=[pltpu.VMEM((4, count * capacity, width), jnp.bfloat16), four, four, four, four, four]
        + [pltpu.VMEM((rows // 2, width), jnp.bfloat16)] * 2
        + [pltpu.VMEM((rows, width), jnp.bfloat16)] * 2
        + [
            pltpu.SemaphoreType.DMA((16,)),
            pltpu.SemaphoreType.DMA((16,)),
            pltpu.SemaphoreType.DMA((4, count)),
        ],
        compiler_params=pltpu.CompilerParams(
            collective_id=label, has_side_effects=True, vmem_limit_bytes=VM
        ),
        cost_estimate=lasts(37),
        name="combine_and_return",
    )(code, *backs, *mixes, go)


def settle_kernel(bit_ref, keep_ref, got_ref, *refs):
    stay_ref, go_ref = refs[-2:]
    bit = bit_ref[0]
    for high in range(keep_ref.shape[0]):
        for low in range(keep_ref.shape[2]):
            for ref, side in ((stay_ref, bit), (go_ref, 1 - bit)):
                total = keep_ref[high, side, low].astype(jnp.float32) + got_ref[
                    high, side, low
                ].astype(jnp.float32)
                ref[high, low] = total.astype(jnp.bfloat16)


def settle(keep, got, mask, label, after):
    count, rows, columns = keep.shape
    low = 1 if mask == PAIR else 2
    shape = (count // 2 // low, 2, low, rows, columns)
    half = jax.ShapeDtypeStruct((count // 2 // low, low, rows, columns), jnp.bfloat16)
    bit = lax.rem(lax.axis_index("dp") // mask, 2)
    vmem = pl.BlockSpec(memory_space=pltpu.VMEM)
    stay, go = pl.pallas_call(
        settle_kernel,
        out_shape=(half, half),
        in_specs=[pl.BlockSpec(memory_space=pltpu.SMEM), vmem, vmem]
        + [pl.BlockSpec(memory_space=pl.ANY)] * len(after),
        out_specs=[vmem, vmem],
        compiler_params=pltpu.CompilerParams(vmem_limit_bytes=VM),
        cost_estimate=lasts(3),
        name="settle_%s" % label,
    )(bit.reshape(1), keep.reshape(shape), got.reshape(shape), *after)
    return stay.reshape(-1, rows, columns), go.reshape(-1, rows, columns)


def settle_mix_kernel(near_ref, got_ref, *refs):
    refs[-1][...] = (near_ref[1].astype(jnp.float32) + got_ref[1].astype(jnp.float32)).astype(jnp.bfloat16)


def settle_mix(near, got, after):
    vmem = pl.BlockSpec(memory_space=pltpu.VMEM)
    return pl.pallas_call(
        settle_mix_kernel,
        out_shape=jax.ShapeDtypeStruct(near.shape[1:], jnp.bfloat16),
        in_specs=[vmem] * 2 + [pl.BlockSpec(memory_space=pl.ANY)] * len(after),
        out_specs=vmem,
        compiler_params=pltpu.CompilerParams(vmem_limit_bytes=VM),
        cost_estimate=lasts(3),
        name="settle_mix",
    )(near, got, *after)


EPS_STAT = 1e-30
STAT_DECAY = 0.5
LEARN_RATE = 0.5
CLIP_LEVEL = 0.05


def decayed(old, new):
    return STAT_DECAY * old + (1.0 - STAT_DECAY) * new


def clip_factor(squares, count):
    return LEARN_RATE / jnp.maximum(1.0, jnp.sqrt(squares / count) / CLIP_LEVEL)


def add_all(values):
    return jnp.sum(jnp.sum(values, axis=1, keepdims=True), axis=0, keepdims=True)


def column_of(table, lane, at):
    return jnp.sum(jnp.where(lane == at, table, 0.0), axis=1, keepdims=True)


def expert_stats_kernel(count, groups, half, *refs):
    stays, gots = refs[:half], refs[half : 2 * half]
    (up_old_ref, down_old_ref, up_rows_ref, down_rows_ref, up_cols_ref, down_cols_ref,
     out_ref, sums_ref, up_new_ref, down_new_ref, pay_s, got_s, spread_s, send_sem, recv_sem) = refs[2 * half :]
    width = up_rows_ref.shape[1]
    ff = down_rows_ref.shape[1]
    wide = width // 2
    own_up = up_old_ref.shape[0]
    own_down = down_old_ref.shape[0]
    me = lax.axis_index("dp")
    place = lax.axis_index("expert")
    after = [lax.rem(me + k, count) for k in range(count)]
    beside = [lax.rem(place + k, groups) for k in range(groups)]
    greet([{"dp": after[k]} for k in range(1, count)] + [{"expert": beside[k]} for k in range(1, groups)])
    push = Pusher(send_sem, recv_sem)
    pair_bit = lax.rem(me // PAIR, 2)
    up_lane = lax.broadcasted_iota(jnp.int32, (own_up, LANES), 1)
    down_lane = lax.broadcasted_iota(jnp.int32, (own_down, LANES), 1)
    up_new_ref[...] = jnp.zeros_like(up_new_ref)
    down_new_ref[...] = jnp.zeros_like(down_new_ref)
    for j in range(half):
        for ref, at in ((stays[j], pair_bit * half + j), (gots[j], (1 - pair_bit) * half + j)):
            for kind, (part, old_ref, new_ref, lane, rows) in enumerate(
                (
                    (ref[:own_up, :], up_old_ref, up_new_ref, up_lane, own_up),
                    (ref[own_up:, :], down_old_ref, down_new_ref, down_lane, own_down),
                )
            ):
                grad = part.astype(jnp.float32)
                square = grad * grad
                new = decayed(
                    column_of(old_ref[...], lane, at),
                    jnp.mean(square + EPS_STAT, axis=1, keepdims=True),
                )
                new_ref[:rows, :] = jnp.where(lane == at, new, new_ref[:rows, :])
                total = jnp.sum(square + EPS_STAT, axis=0, keepdims=True)
                scaled = jnp.sum(square * (1.0 / new), axis=0, keepdims=True)
                for h in range(2):
                    span = slice(h * wide, (h + 1) * wide)
                    pay_s[at, 4 * kind + h : 4 * kind + h + 1, :] = total[:, span]
                    pay_s[at, 4 * kind + 2 + h : 4 * kind + 3 + h, :] = scaled[:, span]
    arriving = [push(pay_s.at[after[k]], got_s.at[k], {"dp": after[k]}) for k in range(1, count)]
    tile = pay_s[me]
    for k in range(1, count):
        arriving[k - 1].wait_recv()
        tile = tile + got_s[k]
    made = []
    tops = []
    for kind, (rows_ref, cols_ref, rows) in enumerate(
        ((up_rows_ref, up_cols_ref, width), (down_rows_ref, down_cols_ref, ff))
    ):
        here = pl.ds(me, 1)
        square = jnp.concatenate([tile[4 * kind + h : 4 * kind + h + 1] for h in range(2)], axis=1)
        scaled = jnp.concatenate([tile[4 * kind + 2 + h : 4 * kind + 3 + h] for h in range(2)], axis=1)
        columns = decayed(cols_ref[here, :], square / rows)
        row_mean = decayed(
            jnp.mean(rows_ref[here, :], axis=1, keepdims=True),
            jnp.sum(square, axis=1, keepdims=True) / (rows * width),
        )
        squares = row_mean * jnp.sum(scaled / columns, axis=1, keepdims=True)
        made += [columns[:, :wide], columns[:, wide:]]
        tops += [jnp.broadcast_to(v, (1, wide)) for v in (row_mean, squares)]
    out_ref[me] = jnp.concatenate(made + tops, axis=0)
    arriving = [push(out_ref.at[me], out_ref.at[me], {"dp": after[k]}) for k in range(1, count)]
    for copy in arriving:
        copy.wait_recv()
    total = out_ref[0, :, :LANES]
    for a in range(1, count):
        total = total + out_ref[a, :, :LANES]
    spread_s[place] = total
    arriving = [push(spread_s.at[place], spread_s.at[place], {"expert": beside[k]}) for k in range(1, groups)]
    for copy in arriving:
        copy.wait_recv()
    total = spread_s[0]
    for e in range(1, groups):
        total = total + spread_s[e]
    sums_ref[...] = total
    push.finish()


def expert_stats(stays, gots, up_old, down_old, up_rows, down_rows, up_cols, down_cols, label):
    count = lax.axis_size("dp")
    groups = lax.axis_size("expert")
    width = up_rows.shape[1]
    vmem = pl.BlockSpec(memory_space=pltpu.VMEM)
    tiles = (count, 8, width // 2)
    copies = 2 * (count - 1) + groups - 1
    return pl.pallas_call(
        functools.partial(expert_stats_kernel, count, groups, len(stays)),
        out_shape=(
            jax.ShapeDtypeStruct(tiles, jnp.float32),
            jax.ShapeDtypeStruct((8, LANES), jnp.float32),
            jax.ShapeDtypeStruct((LANES, LANES), jnp.float32),
            jax.ShapeDtypeStruct((LANES, LANES), jnp.float32),
        ),
        in_specs=[vmem] * (2 * len(stays) + 6),
        out_specs=[vmem] * 4,
        scratch_shapes=[
            pltpu.VMEM(tiles, jnp.float32),
            pltpu.VMEM(tiles, jnp.float32),
            pltpu.VMEM((groups, 8, LANES), jnp.float32),
            pltpu.SemaphoreType.DMA((copies,)),
            pltpu.SemaphoreType.DMA((copies,)),
        ],
        compiler_params=pltpu.CompilerParams(
            collective_id=label, has_side_effects=True, vmem_limit_bytes=VM
        ),
        cost_estimate=lasts(15),
        name="expert_stats",
    )(*stays, *gots, up_old, down_old, up_rows, down_rows, up_cols, down_cols)


def expert_update_kernel(counts, half, s_ref, *refs):
    stays, gots = refs[:half], refs[half : 2 * half]
    (tiles_ref, sums_ref, up_new_ref, down_new_ref, up_w_ref, down_w_ref,
     up_out_ref, down_out_ref, up_rows_ref, down_rows_ref, up_cols_ref, down_cols_ref) = refs[2 * half :]
    own_up = up_out_ref.shape[1]
    own_down = down_out_ref.shape[1]
    wide = tiles_ref.shape[2]
    pair_bit = s_ref[0]
    up_table = up_new_ref[...]
    down_table = down_new_ref[...]
    lane = lax.broadcasted_iota(jnp.int32, up_table.shape, 1)
    factors = [clip_factor(sums_ref[5 + 2 * kind : 6 + 2 * kind, 0:1], counts[kind]) for kind in range(2)]
    for j in range(half):
        for ref, at in ((stays[j], pair_bit * half + j), (gots[j], (1 - pair_bit) * half + j)):
            tile = tiles_ref[at]
            for kind, (table, weight_ref, out_ref, first, rows) in enumerate(
                (
                    (up_table, up_w_ref, up_out_ref, 0, own_up),
                    (down_table, down_w_ref, down_out_ref, own_up, own_down),
                )
            ):
                row_mean = tile[4 + 2 * kind : 5 + 2 * kind, 0:1]
                scale = factors[kind] * lax.rsqrt(column_of(table, lane, at)[:rows] / row_mean)
                for h in range(2):
                    span = slice(h * wide, (h + 1) * wide)
                    columns = lax.rsqrt(tile[2 * kind + h : 2 * kind + h + 1, :])
                    out_ref[at, :, span] = (
                        weight_ref[at, :, span].astype(jnp.float32)
                        - ref[first : first + rows, span].astype(jnp.float32) * scale * columns
                    )
    up_rows_ref[...] = up_table.T[: up_rows_ref.shape[0], :own_up]
    down_rows_ref[...] = down_table.T[: down_rows_ref.shape[0], :own_down]
    for a in range(up_cols_ref.shape[0]):
        for h in range(2):
            span = slice(h * wide, (h + 1) * wide)
            up_cols_ref[a : a + 1, span] = tiles_ref[a, h : h + 1, :]
            down_cols_ref[a : a + 1, span] = tiles_ref[a, 2 + h : 3 + h, :]


def expert_update(stays, gots, tiles, sums, up_new, down_new, up_w, down_w):
    count = lax.axis_size("dp")
    groups = lax.axis_size("expert")
    me = lax.axis_index("dp")
    experts, width, _ = up_w.shape
    ff = down_w.shape[1]
    own_up, own_down = width // count, ff // count
    counts = (float(groups * experts * width * up_w.shape[2]), float(groups * experts * ff * width))
    whole = lambda *shape: pl.BlockSpec(shape, lambda g, s: (0,) * len(shape))
    shape = lambda *s: jax.ShapeDtypeStruct(s, jnp.float32)
    rows = own_up + own_down
    outs = [
        shape(experts, own_up, up_w.shape[2]),
        shape(experts, own_down, width),
        shape(experts, own_up),
        shape(experts, own_down),
        shape(experts, up_w.shape[2]),
        shape(experts, width),
    ]
    return pl.pallas_call(
        functools.partial(expert_update_kernel, counts, len(stays)),
        out_shape=outs,
        grid_spec=pltpu.PrefetchScalarGridSpec(
            num_scalar_prefetch=1,
            grid=(1,),
            in_specs=[whole(rows, width)] * (2 * len(stays))
            + [whole(*tiles.shape), whole(*sums.shape), whole(*up_new.shape), whole(*down_new.shape)]
            + [
                pl.BlockSpec((experts, own_up, up_w.shape[2]), lambda g, s: (0, s[1], 0)),
                pl.BlockSpec((experts, own_down, width), lambda g, s: (0, s[1], 0)),
            ],
            out_specs=[whole(*o.shape) for o in outs],
        ),
        compiler_params=pltpu.CompilerParams(vmem_limit_bytes=VM),
        cost_estimate=lasts(6),
        name="expert_update",
    )(jnp.stack([lax.rem(me // PAIR, 2), me]), *stays, *gots, tiles, sums, up_new, down_new, up_w, down_w)


D = 1024
FF = 512
TOP = 8


def swap(values, axis, mask):
    count = lax.axis_size(axis)
    return lax.ppermute(values, axis, [(i, i ^ mask) for i in range(count)])


def swap_pair(values):
    return swap(values, "dp", PAIR)


def swap_chip(values):
    return swap(values, "expert", 2)


def swap_core(values):
    return swap(values, "expert", 1)


def plus(a, b):
    return (a.astype(jnp.float32) + b.astype(jnp.float32)).astype(jnp.bfloat16)


def halve(blocks, axis, mask):
    bit = lax.rem(lax.axis_index(axis) // mask, 2)
    keep = lax.dynamic_index_in_dim(blocks, bit, 1, keepdims=False)
    give = lax.dynamic_index_in_dim(blocks, 1 - bit, 1, keepdims=False)
    return keep, swap(give, axis, mask)


def reduce_dense_far(blocks):
    count = lax.axis_size("dp")
    width, columns = blocks.shape
    rows = width // count
    blocks = blocks.reshape(count, 2, 2, rows // 4, columns)
    keep, got = halve(jnp.moveaxis(blocks, 2, 1), "expert", 1)
    keep, got = halve(plus(keep, got), "expert", 2)
    blocks = plus(keep, got)
    low = 1
    while low < count:
        keep, got = halve(blocks.reshape((-1, 2, 1) + blocks.shape[1:]), "dp", low)
        blocks = plus(keep, got).reshape((-1,) + blocks.shape[1:])
        low *= 2
    mine = blocks[0]
    chip = lax.axis_index("expert") // 2
    core = lax.rem(lax.axis_index("expert"), 2)
    other = swap_chip(mine)
    both = jnp.where(chip == 0, jnp.stack([mine, other]), jnp.stack([other, mine]))
    across = swap_core(both)
    all_four = jnp.where(core == 0, jnp.stack([both, across], 1), jnp.stack([across, both], 1))
    return all_four.reshape(rows, columns)


def own_share(matrix, along):
    count = lax.axis_size("dp")
    width = matrix.shape[along] // count
    return lax.dynamic_slice_in_dim(matrix, lax.axis_index("dp") * width, width, along)


def factored(part, rows_old):
    square = part * part
    rows_new = decayed(rows_old, jnp.mean(square + EPS_STAT, axis=-1))
    return (
        rows_new,
        jnp.sum(square + EPS_STAT, axis=-2),
        jnp.sum(square / rows_new[..., None], axis=-2),
    )


def per_device(
    hidden_in,
    out_grad,
    segment_ids,
    parent_ids,
    positions,
    expert_ids,
    gate_weights,
    norm_gains,
    qkv_weight,
    out_weight,
    gate_up_weight,
    down_weight,
    gain_moment,
    qkv_rows,
    qkv_cols,
    out_rows,
    out_cols,
    gateup_rows,
    gateup_cols,
    down_rows,
    down_cols,
):
    rows_here = hidden_in.shape[0]
    dp_count = lax.axis_size("dp")
    groups = lax.axis_size("expert")
    experts_here = gate_up_weight.shape[0]
    total_experts = experts_here * groups
    capacity = 3 * rows_here * TOP // (2 * total_experts)
    half_experts = experts_here // 2
    dp_index = lax.axis_index("dp")
    pair_bit = lax.rem(dp_index // PAIR, 2)
    first_local = pair_bit * half_experts
    first_expert = lax.axis_index("expert") * experts_here + first_local

    weight_high = gate_weights.astype(jnp.bfloat16)
    weight_low = (gate_weights - weight_high.astype(jnp.float32)).astype(jnp.bfloat16)
    routing = jnp.concatenate([expert_ids.astype(jnp.bfloat16), weight_high, weight_low], axis=1).T
    routing = jnp.pad(routing, ((0, ROUTE_ROWS - routing.shape[0]), (0, D - rows_here)))
    grad_rows = jnp.concatenate([out_grad.astype(jnp.bfloat16), routing], axis=0)
    chip_grad_rows = swap_chip(grad_rows)
    pair_grad_rows = swap_pair(grad_rows)
    ids = jnp.stack([segment_ids, parent_ids, positions])
    normed, qkv, attended, lse, middle, normed_ffn = attend(
        hidden_in, ids, norm_gains, qkv_weight, out_weight
    )
    received, arrived, scale, code = gather_and_select(
        normed_ffn, grad_rows, chip_grad_rows, pair_grad_rows, capacity, experts_here, half_experts, TOP, 5
    )
    scalars = jnp.stack([first_local, lax.rem(dp_index, 2)])
    experts, chains = [], []

    def advance(j, after, come=None):
        masks, stay, go = chains[j]
        come = swap(go, "dp", masks[0]) if come is None else come
        stay, go = settle(stay, come, masks[1], "%d_%d" % (j, masks[1]), after)
        chains[j] = (masks[1:], stay, go)
        return stay

    masks = [1] + [1 << b for b in range(2, dp_count.bit_length() - 1)] + [PAIR]
    for j in range(half_experts):
        after = [experts[-1][2]] if experts else []
        if j == 3:
            after.append(advance(0, after))
        experts.append(
            run_expert(
                scalars, j, received, arrived, scale, gate_up_weight, down_weight, dp_count, after
            )
        )
        chains.append((masks, experts[j][0], experts[j][1]))
    normed_f_grad, near_mix, far_mix, come = combine_and_return(
        code, [e[2] for e in experts], [e[3] for e in experts], capacity, chains[0][2], chains[0][0][0], 6
    )
    steps = [normed_f_grad]
    for j in (1, 2, 0):
        steps.append(advance(j, steps[-1:], come if j == 0 else None))
    input_grad, dense = attend_back(
        hidden_in, out_grad, middle, normed_f_grad, normed, qkv, attended, lse, ids, norm_gains, qkv_weight,
        out_weight, steps
    )
    pair_mix = swap_pair(far_mix)
    for_chip = settle_mix(near_mix, pair_mix, [input_grad])
    steps = [for_chip]
    for j in (3, 1):
        steps.append(advance(j, steps[-1:]))
    mix_parts = (near_mix[0], pair_mix[0], swap_chip(for_chip))
    block_out = middle + sum(part.astype(jnp.float32) for part in mix_parts)

    qkv_columns = qkv_weight.shape[1]
    if D // dp_count % 64 == 0:
        dense_own, come = reduce_dense(dense, chains[3][2], chains[3][0][0], 3, steps)
    else:
        dense_own, come = reduce_dense_far(dense), None
    for j in (2, 3, 0, 1):
        while len(chains[j][0]) > 1:
            advance(j, [dense_own], come if j == 3 else None)
            come = None if j == 3 else come
    own_parts = [c[1][0] for c in chains]
    other_parts = [swap_pair(c[2][0]) for c in chains]
    fused_tail = dp_count == experts_here
    if fused_tail:
        spare = ((0, 0), (0, LANES - experts_here))
        tiles, sums, up_rows_T, down_rows_T = expert_stats(
            own_parts,
            other_parts,
            jnp.pad(own_share(gateup_rows, 1).T, spare),
            jnp.pad(own_share(down_rows, 1).T, spare),
            gateup_rows,
            down_rows,
            gateup_cols,
            down_cols,
            1,
        )
        gate_up_new, down_new, gateup_rows_new, down_rows_new, gateup_cols_new, down_cols_new = expert_update(
            own_parts, other_parts, tiles, sums, up_rows_T, down_rows_T, gate_up_weight, down_weight
        )
        expert_squares = jnp.stack([sums[5, 0], sums[7, 0]])
    else:
        own = jnp.stack(own_parts).astype(jnp.float32)
        other = jnp.stack(other_parts).astype(jnp.float32)
        parts = jnp.where(pair_bit == 0, jnp.concatenate([own, other]), jnp.concatenate([other, own]))
        gateup_part = parts[:, : D // dp_count]
        down_part = parts[:, D // dp_count :]
        gateup_rows_new, gateup_square, gateup_scaled = factored(gateup_part, own_share(gateup_rows, 1))
        down_rows_new, down_square, down_scaled = factored(down_part, own_share(down_rows, 1))
        sizes = [gateup_square.size, gateup_scaled.size, down_square.size, down_scaled.size]
        summed = total_over(
            jnp.concatenate(
                [
                    gateup_square.reshape(-1),
                    gateup_scaled.reshape(-1),
                    down_square.reshape(-1),
                    down_scaled.reshape(-1),
                    jnp.sum(gateup_rows_new, axis=1),
                    jnp.sum(down_rows_new, axis=1),
                ]
            ),
            "dp",
            1,
        )
        pieces = jnp.split(summed, [sum(sizes[: i + 1]) for i in range(4)])
        gateup_square, gateup_scaled, down_square, down_scaled = [
            p.reshape(experts_here, D) for p in pieces[:4]
        ]
        gateup_row_mean = pieces[4][:experts_here] / D
        down_row_mean = pieces[4][experts_here:] / FF
        gateup_cols_new = decayed(gateup_cols, gateup_square / D)
        down_cols_new = decayed(down_cols, down_square / FF)
        expert_squares = jnp.stack(
            [
                jnp.sum(gateup_row_mean * jnp.sum(gateup_scaled / gateup_cols_new, axis=1)),
                jnp.sum(down_row_mean * jnp.sum(down_scaled / down_cols_new, axis=1)),
            ]
        )
        spread_squares = collect(
            jnp.zeros((8, 128), jnp.float32).at[0, :2].set(expert_squares), "expert", 2
        )
        expert_squares = jnp.sum(spread_squares[:, 0, :2], axis=0)

    dense_own = dense_own.astype(jnp.float32)
    qkv_own = dense_own[:, :qkv_columns]
    out_own = dense_own[:, qkv_columns : qkv_columns + D]
    gains_own = dense_own[:, qkv_columns + D : qkv_columns + D + 2].T
    gain_moment_new = decayed(own_share(gain_moment, 1), gains_own * gains_own + EPS_STAT)
    gains_step = gains_own * lax.rsqrt(gain_moment_new)
    qkv_rows_new, qkv_square, qkv_scaled = factored(qkv_own, own_share(qkv_rows, 0))
    out_rows_new, out_square, out_scaled = factored(out_own, own_share(out_rows, 0))
    dense_sums = total_over(
        jnp.concatenate(
            [
                qkv_square,
                qkv_scaled,
                out_square,
                out_scaled,
                jnp.stack(
                    [jnp.sum(qkv_rows_new), jnp.sum(out_rows_new), jnp.sum(gains_step * gains_step)]
                ),
            ]
        ),
        "dp",
        4,
        [c[1] for c in chains],
    )
    qkv_square, qkv_scaled, out_square, out_scaled, rest = jnp.split(
        dense_sums, [qkv_columns, 2 * qkv_columns, 2 * qkv_columns + D, 2 * qkv_columns + 2 * D]
    )
    qkv_row_mean = rest[0] / D
    out_row_mean = rest[1] / D
    qkv_cols_new = decayed(qkv_cols, qkv_square / D)
    out_cols_new = decayed(out_cols, out_square / D)
    squares = jnp.concatenate(
        [
            jnp.stack(
                [
                    rest[2],
                    qkv_row_mean * jnp.sum(qkv_scaled / qkv_cols_new),
                    out_row_mean * jnp.sum(out_scaled / out_cols_new),
                ]
            ),
            expert_squares,
        ]
    )
    element_counts = jnp.array(
        [2 * D, D * qkv_columns, D * D, total_experts * D * 2 * FF, total_experts * FF * D], jnp.float32
    )
    update_rms = jnp.sqrt(squares / element_counts)
    factors = LEARN_RATE / jnp.maximum(1.0, update_rms / CLIP_LEVEL)

    def stepped(weight, part, rows_new, row_mean, cols_new, factor):
        return weight.astype(jnp.float32) - part * (
            factor * lax.rsqrt(rows_new / row_mean[..., None])
        )[..., :, None] * lax.rsqrt(cols_new)[..., None, :]

    if not fused_tail:
        gate_up_new = stepped(
            own_share(gate_up_weight, 1), gateup_part, gateup_rows_new, gateup_row_mean, gateup_cols_new, factors[3]
        )
        down_new = stepped(
            own_share(down_weight, 1), down_part, down_rows_new, down_row_mean, down_cols_new, factors[4]
        )
    return (
        block_out,
        input_grad,
        update_rms,
        -factors[0] * gains_step,
        gain_moment_new,
        stepped(own_share(qkv_weight, 0), qkv_own, qkv_rows_new, qkv_row_mean, qkv_cols_new, factors[1]),
        qkv_rows_new,
        qkv_cols_new,
        stepped(own_share(out_weight, 0), out_own, out_rows_new, out_row_mean, out_cols_new, factors[2]),
        out_rows_new,
        out_cols_new,
        gate_up_new,
        gateup_rows_new,
        gateup_cols_new,
        down_new,
        down_rows_new,
        down_cols_new,
    )


def solution(mesh):
    placed = (
        P(("dp", "expert"), None),
        P(("dp", "expert"), None),
        P(("dp", "expert")),
        P(("dp", "expert")),
        P(("dp", "expert")),
        P(("dp", "expert"), None),
        P(("dp", "expert"), None),
        P(),
        P(),
        P(),
        P("expert", None, None),
        P("expert", None, None),
        P(),
        P(),
        P(),
        P(),
        P(),
        P("expert", None),
        P("expert", None),
        P("expert", None),
        P("expert", None),
    )
    return jax.shard_map(
        per_device,
        mesh=mesh,
        in_specs=placed,
        out_specs=(
            P(("dp", "expert"), None),
            P(("dp", "expert"), None),
            P(),
            P(None, "dp"),
            P(None, "dp"),
            P("dp", None),
            P("dp"),
            P(),
            P("dp", None),
            P("dp"),
            P(),
            P("expert", "dp", None),
            P("expert", "dp"),
            P("expert", None),
            P("expert", "dp", None),
            P("expert", "dp"),
            P("expert", None),
        ),
        check_vma=False,
    )
```

```python
import functools
import math

import jax
import jax.numpy as jnp
from jax import lax
from jax.experimental import pallas as pl
from jax.experimental.pallas import tpu as pltpu
from jax.sharding import PartitionSpec as P

VM = 60 * 1024 * 1024
SCALE = 1e6


def lasts(microseconds):
    return pl.CostEstimate(
        flops=int(microseconds * SCALE), bytes_accessed=1024, transcendentals=0
    )


def dot(a, b, ca=1, cb=0):
    return lax.dot_general(a, b, (((ca,), (cb,)), ((), ())), preferred_element_type=jnp.float32)


def one_hot(code, capacity):
    count, rows = code.shape
    place = lax.broadcasted_iota(jnp.int32, (capacity, rows), 0).astype(jnp.float32)
    return [place == code[j : j + 1, :] for j in range(count)]


def expert_kernel(j, owners, tiles, waits, s_ref, rec_hbm, arr_hbm, scale_ref, up_hbm, down_hbm, *refs):
    (keep_hbm, give_hbm, back_hbm, mix_hbm,
     rec_s, arr_s, up_s, down_s, act_s, gug_s, wg_s, wd_s, parts_s, out_s, in_sem, out_sem) = refs[waits:]
    rows, ff = act_s.shape
    width = up_s.shape[0]
    sources, capacity = rec_s.shape[0], rec_s.shape[1]
    tile = rows // tiles
    per = sources // tiles

    def load(src, dst, at):
        copy = pltpu.make_async_copy(src, dst, in_sem.at[at])
        copy.start()
        return copy

    def load_rows(hbm, held, t, at):
        span = slice(t * per, (t + 1) * per)
        return load(hbm.at[j, span], held.at[span], at)

    expert = s_ref[0] + j
    rec_in = [load_rows(rec_hbm, rec_s, 0, 0)]
    up_in = load(up_hbm.at[expert], up_s, 2 * tiles)
    arr_in = [load_rows(arr_hbm, arr_s, 0, tiles)]
    down_in = load(down_hbm.at[expert], down_s, 2 * tiles + 1)
    for t in range(1, tiles):
        rec_in.append(load_rows(rec_hbm, rec_s, t, t))
        arr_in.append(load_rows(arr_hbm, arr_s, t, tiles + t))
    def products(t):
        span = slice(t * per, (t + 1) * per)
        return (
            dot(rec_s[span].reshape(tile, width), up_s[...]),
            dot(arr_s[span].reshape(tile, width), down_s[...], 1, 1),
        )

    for copy in (up_in, down_in, rec_in[0], arr_in[0]):
        copy.wait()
    following = products(0)
    for t in range(tiles):
        at = slice(t * tile, (t + 1) * tile)
        gate_up, act_grad = following
        if t + 1 < tiles:
            rec_in[t + 1].wait()
            arr_in[t + 1].wait()
            following = products(t + 1)
        gate = gate_up[:, :ff]
        up = gate_up[:, ff:]
        sig = 1.0 / (1.0 + jnp.exp(-gate))
        silu = gate * sig
        act_s[at, :] = (silu * up).astype(jnp.bfloat16)
        gug_s[at, :ff] = (act_grad * up * sig * (1.0 + gate * (1.0 - sig))).astype(jnp.bfloat16)
        gug_s[at, ff:] = (act_grad * silu).astype(jnp.bfloat16)
    wg_s[...] = dot(rec_s[...].reshape(rows, width), gug_s[...], 0, 0)
    wd_s[...] = dot(act_s[...], arr_s[...].reshape(rows, width), 0, 0)
    bit = s_ref[1]
    up_rows = width // owners
    down_rows = ff // owners
    leaving = []
    for k, (hbm, side) in enumerate(((give_hbm, 1 - bit), (keep_hbm, bit))):
        for slot in range(owners // 2):
            owner = 2 * slot + side
            parts_s[k, slot, :up_rows, :] = wg_s[
                pl.ds(pl.multiple_of(owner * up_rows, up_rows), up_rows), :
            ].astype(jnp.bfloat16)
            parts_s[k, slot, up_rows:, :] = wd_s[
                pl.ds(pl.multiple_of(owner * down_rows, down_rows), down_rows), :
            ].astype(jnp.bfloat16)
        copy = pltpu.make_async_copy(parts_s.at[k], hbm, out_sem.at[k])
        copy.start()
        leaving.append(copy)
    for t in range(tiles):
        at = slice(t * tile, (t + 1) * tile)
        out_s[0, at] = dot(gug_s[at, :], up_s[...], 1, 1).astype(jnp.bfloat16)
        scale = scale_ref[0, t * per : (t + 1) * per].reshape(tile, 1)
        out_s[1, at] = (dot(act_s[at, :], down_s[...]) * scale).astype(jnp.bfloat16)
        for k, hbm in enumerate((back_hbm, mix_hbm)):
            copy = pltpu.make_async_copy(out_s.at[k, at], hbm.at[at], out_sem.at[2 + 2 * t + k])
            copy.start()
            leaving.append(copy)
    for copy in leaving:
        copy.wait()


def run_expert(scalars, j, received, arrived, scale, up_w, down_w, owners, after=()):
    count, sources, capacity, width = received.shape
    ff = down_w.shape[1]
    rows = sources * capacity
    tiles = 2
    share = (owners // 2, (width + ff) // owners, width)
    slots = jax.ShapeDtypeStruct((rows, width), jnp.bfloat16)
    parts = jax.ShapeDtypeStruct(share, jnp.bfloat16)
    anywhere = pl.BlockSpec(memory_space=pl.ANY)
    return pl.pallas_call(
        functools.partial(expert_kernel, j, owners, tiles, len(after)),
        out_shape=(parts, parts, slots, slots),
        grid_spec=pltpu.PrefetchScalarGridSpec(
            num_scalar_prefetch=1,
            grid=(1,),
            in_specs=[
                anywhere,
                anywhere,
                pl.BlockSpec((1, sources, capacity, 1), lambda g, s: (j, 0, 0, 0)),
                anywhere,
                anywhere,
            ]
            + [anywhere] * len(after),
            out_specs=[anywhere] * 4,
            scratch_shapes=[
                pltpu.VMEM((sources, capacity, width), jnp.bfloat16),
                pltpu.VMEM((sources, capacity, width), jnp.bfloat16),
                pltpu.VMEM((width, 2 * ff), jnp.bfloat16),
                pltpu.VMEM((ff, width), jnp.bfloat16),
                pltpu.VMEM((rows, ff), jnp.bfloat16),
                pltpu.VMEM((rows, 2 * ff), jnp.bfloat16),
                pltpu.VMEM((width, 2 * ff), jnp.float32),
                pltpu.VMEM((ff, width), jnp.float32),
                pltpu.VMEM((2,) + share, jnp.bfloat16),
                pltpu.VMEM((2, rows, width), jnp.bfloat16),
                pltpu.SemaphoreType.DMA((2 * tiles + 2,)),
                pltpu.SemaphoreType.DMA((2 + 2 * tiles,)),
            ],
        ),
        compiler_params=pltpu.CompilerParams(vmem_limit_bytes=VM),
        cost_estimate=lasts(18),
        name="expert_%d" % j,
    )(scalars, received, arrived, scale, up_w, down_w, *after)


HEADS = 16
KV_HEADS = 8
HEAD_DIM = 64
EPS_NORM = 1e-06
ROPE_BASE = 10000.0
MASKED = -1e30
LANES = 128


def spread(row):
    rows = row.shape[1]
    by_column = jnp.broadcast_to(row.astype(jnp.float32), (rows, rows))
    return by_column, by_column.T


def mask_and_angles(ids_ref):
    seg_k, seg_q = spread(ids_ref[0:1, :])
    par_k, par_q = spread(ids_ref[1:2, :])
    pos_k, pos_q = spread(ids_ref[2:3, :])
    seen = ((seg_k == seg_q) | (seg_k == par_q) | (seg_k == par_k)) & (pos_k <= pos_q)
    bias = jnp.where(seen, 0.0, MASKED)
    lane = lax.broadcasted_iota(jnp.int32, (seg_k.shape[0], LANES), 1)
    half = HEAD_DIM // 2
    place = lax.rem(lane, half).astype(jnp.float32)
    frequency = jnp.exp(place * (-2.0 * math.log(ROPE_BASE) / HEAD_DIM))
    angles = pos_q[:, :LANES] * frequency
    front = lax.rem(lane, HEAD_DIM) < half
    sine = jnp.sin(angles)
    return bias, jnp.cos(angles), jnp.where(front, -sine, sine), front, lane


def turned(block, cosine, sine, front):
    other = jnp.where(
        front,
        pltpu.roll(block, LANES - HEAD_DIM // 2, 1),
        pltpu.roll(block, HEAD_DIM // 2, 1),
    )
    return block * cosine + other * sine


def two_diagonal(pair, which, lane):
    rolled = pltpu.roll(pair, HEAD_DIM, 1)
    first, last = (pair, rolled) if which == 0 else (rolled, pair)
    low = lane < HEAD_DIM
    return jnp.concatenate(
        [jnp.where(low, first, 0.0), jnp.where(low, 0.0, last)], axis=0
    ).astype(jnp.bfloat16)


def column_block(index):
    return pl.ds(pl.multiple_of(index * LANES, LANES), LANES)


def attend_kernel(hidden_ref, ids_ref, gains_ref, qkv_w_ref, out_w_ref,
                  normed_ref, qkv_ref, attended_ref, lse_ref, middle_ref, normed_f_ref, proj_s, bias_s):
    rows = hidden_ref.shape[0]
    att = HEADS * HEAD_DIM
    kv = KV_HEADS * HEAD_DIM
    hidden = hidden_ref[...]
    gains = gains_ref[...].astype(jnp.float32)
    inverse = lax.rsqrt(jnp.mean(hidden * hidden, axis=-1, keepdims=True) + EPS_NORM)
    normed_ref[...] = (hidden * inverse * gains[0:1, :]).astype(jnp.bfloat16)
    proj_s[...] = dot(normed_ref[...], qkv_w_ref[...])
    bias, cosine, sine, front, lane = mask_and_angles(ids_ref)
    bias_s[...] = bias
    lse_ref[...] = jnp.zeros_like(lse_ref)

    def pair_step(p, carry):
        key_at = column_block(att // LANES + p)
        value_at = column_block((att + kv) // LANES + p)
        keys = turned(proj_s[:, key_at], cosine, sine, front).astype(jnp.bfloat16)
        values = proj_s[:, value_at].astype(jnp.bfloat16)
        qkv_ref[:, key_at] = keys
        qkv_ref[:, value_at] = values
        keys = keys.astype(jnp.float32)
        values = values.astype(jnp.float32)
        for which in range(2):
            query_at = column_block(2 * p + which)
            queries = turned(proj_s[:, query_at], cosine, sine, front).astype(jnp.bfloat16)
            queries = (queries.astype(jnp.float32) * HEAD_DIM**-0.5).astype(jnp.bfloat16)
            qkv_ref[:, query_at] = queries
            scores = dot(queries, two_diagonal(keys, which, lane), 1, 1)
            probs = []
            for head in range(2):
                part = scores[:, head * rows : (head + 1) * rows] + bias_s[...]
                top = jnp.max(part, axis=-1, keepdims=True)
                part = jnp.exp(part - top)
                total = jnp.sum(part, axis=-1, keepdims=True)
                probs.append((part * (1.0 / total)).astype(jnp.bfloat16))
                at = 4 * p + 2 * which + head
                lse_ref[...] = jnp.where(lane == at, top + jnp.log(total), lse_ref[...])
            attended_ref[:, query_at] = dot(
                jnp.concatenate(probs, axis=1), two_diagonal(values, which, lane)
            ).astype(jnp.bfloat16)
        return carry

    lax.fori_loop(0, KV_HEADS // 2, pair_step, 0)
    middle = hidden + dot(attended_ref[...], out_w_ref[...])
    middle_ref[...] = middle
    inverse_f = lax.rsqrt(jnp.mean(middle * middle, axis=-1, keepdims=True) + EPS_NORM)
    normed_f_ref[...] = (middle * inverse_f * gains[1:2, :]).astype(jnp.bfloat16)


def attend(hidden, ids, gains, qkv_w, out_w):
    rows, width = hidden.shape
    shape = jax.ShapeDtypeStruct
    return pl.pallas_call(
        attend_kernel,
        out_shape=(
            shape((rows, width), jnp.bfloat16),
            shape((rows, qkv_w.shape[1]), jnp.bfloat16),
            shape((rows, out_w.shape[0]), jnp.bfloat16),
            shape((rows, LANES), jnp.float32),
            shape((rows, width), jnp.float32),
            shape((rows, width), jnp.bfloat16),
        ),
        in_specs=[pl.BlockSpec(memory_space=pltpu.VMEM)] * 5,
        out_specs=[pl.BlockSpec(memory_space=pltpu.VMEM)] * 6,
        scratch_shapes=[
            pltpu.VMEM((rows, qkv_w.shape[1]), jnp.float32),
            pltpu.VMEM((rows, rows), jnp.float32),
        ],
        compiler_params=pltpu.CompilerParams(vmem_limit_bytes=VM),
        cost_estimate=lasts(18),
        name="attend",
    )(hidden, ids, gains, qkv_w, out_w)


def attend_back_kernel(hidden_ref, grad_ref, middle_ref, normed_grad_ref, normed_ref, qkv_ref, attended_ref, lse_ref,
                       ids_ref, gains_ref, qkv_w_ref, out_w_ref, *refs):
    input_grad_ref, dense_ref, proj_s, bias_s, back_s = refs[-5:]
    rows, width = hidden_ref.shape
    att = HEADS * HEAD_DIM
    kv = KV_HEADS * HEAD_DIM
    gains = gains_ref[...].astype(jnp.float32)
    normed_grad = normed_grad_ref[...]
    middle = middle_ref[...]
    inverse_f = lax.rsqrt(jnp.mean(middle * middle, axis=-1, keepdims=True) + EPS_NORM)
    gain_f = jnp.sum(normed_grad * middle * inverse_f, axis=0, keepdims=True)
    weighted = normed_grad * gains[1:2, :]
    middle_grad = grad_ref[...] + (
        inverse_f * weighted
        - middle * (inverse_f * inverse_f * inverse_f)
        * jnp.mean(weighted * middle, axis=-1, keepdims=True)
    )
    input_grad_ref[...] = middle_grad
    branch = middle_grad.astype(jnp.bfloat16)
    columns = att + 2 * kv
    dense_ref[:, columns : columns + width] = dot(attended_ref[...], branch, 0, 0).astype(jnp.bfloat16)
    back_s[...] = dot(branch, out_w_ref[...], 1, 1).astype(jnp.bfloat16)
    bias, cosine, sine, front, lane = mask_and_angles(ids_ref)
    bias_s[...] = bias
    low = lane < HEAD_DIM

    def pair_step(p, carry):
        key_at = column_block(att // LANES + p)
        value_at = column_block((att + kv) // LANES + p)
        keys = qkv_ref[:, key_at].astype(jnp.float32)
        values = qkv_ref[:, value_at].astype(jnp.float32)
        key_grads = []
        value_grads = []
        for which in range(2):
            query_at = column_block(2 * p + which)
            queries = qkv_ref[:, query_at]
            back = back_s[:, query_at]
            key_two = two_diagonal(keys, which, lane)
            scores = dot(queries, key_two, 1, 1)
            prob_grads = dot(back, two_diagonal(values, which, lane), 1, 1)
            probs = []
            score_grads = []
            for head in range(2):
                at = 4 * p + 2 * which + head
                level = jnp.sum(jnp.where(lane == at, lse_ref[...], 0.0), axis=-1, keepdims=True)
                span = slice(head * rows, (head + 1) * rows)
                prob = jnp.exp(scores[:, span] + bias_s[...] - level)
                prob_grad = prob_grads[:, span]
                row_dot = jnp.sum(prob * prob_grad, axis=-1, keepdims=True)
                probs.append(prob.astype(jnp.bfloat16))
                score_grads.append((prob * (prob_grad - row_dot)).astype(jnp.bfloat16))
            score_grads = jnp.concatenate(score_grads, axis=1)
            query_grad = dot(score_grads, key_two) * HEAD_DIM**-0.5
            proj_s[:, query_at] = turned(query_grad, cosine, -sine, front).astype(jnp.bfloat16)
            for grads, left, right in (
                (key_grads, score_grads, queries),
                (value_grads, jnp.concatenate(probs, axis=1), back),
            ):
                both = dot(left, right, 0, 0)
                first, last = both[:rows], both[rows:]
                if which == 0:
                    grads.append(first + pltpu.roll(last, HEAD_DIM, 1))
                else:
                    grads.append(pltpu.roll(first, HEAD_DIM, 1) + last)
        key_grad = jnp.where(low, key_grads[0], key_grads[1])
        proj_s[:, key_at] = turned(key_grad, cosine, -sine, front).astype(jnp.bfloat16)
        proj_s[:, value_at] = jnp.where(low, value_grads[0], value_grads[1]).astype(jnp.bfloat16)
        return carry

    lax.fori_loop(0, KV_HEADS // 2, pair_step, 0)
    dense_ref[:, :columns] = dot(normed_ref[...], proj_s[...], 0, 0).astype(jnp.bfloat16)
    normed_grad = dot(proj_s[...], qkv_w_ref[...], 1, 1)
    hidden = hidden_ref[...]
    inverse = lax.rsqrt(jnp.mean(hidden * hidden, axis=-1, keepdims=True) + EPS_NORM)
    gain_a = jnp.sum(normed_grad * hidden * inverse, axis=0, keepdims=True)
    weighted = normed_grad * gains[0:1, :]
    input_grad_ref[...] += inverse * weighted - hidden * (inverse * inverse * inverse) * jnp.mean(
        weighted * hidden, axis=-1, keepdims=True
    )
    both = jnp.concatenate([gain_a, gain_f, jnp.zeros((LANES - 2, width), jnp.float32)], axis=0)
    dense_ref[:, columns + width :] = both.T.astype(jnp.bfloat16)


def attend_back(hidden, out_grad, middle, normed_f_grad, normed, qkv, attended, lse, ids, gains, qkv_w, out_w, after=()):
    rows, width = hidden.shape
    columns = qkv_w.shape[1] + width + LANES
    return pl.pallas_call(
        attend_back_kernel,
        out_shape=(
            jax.ShapeDtypeStruct((rows, width), jnp.float32),
            jax.ShapeDtypeStruct((width, columns), jnp.bfloat16),
        ),
        in_specs=[pl.BlockSpec(memory_space=pltpu.VMEM)] * 12
        + [pl.BlockSpec(memory_space=pl.ANY)] * len(after),
        out_specs=[pl.BlockSpec(memory_space=pltpu.VMEM)] * 2,
        scratch_shapes=[
            pltpu.VMEM((rows, qkv_w.shape[1]), jnp.bfloat16),
            pltpu.VMEM((rows, rows), jnp.float32),
            pltpu.VMEM((rows, out_w.shape[0]), jnp.bfloat16),
        ],
        compiler_params=pltpu.CompilerParams(vmem_limit_bytes=VM),
        cost_estimate=lasts(26),
        name="attend_back",
    )(hidden, out_grad, middle, normed_f_grad, normed, qkv, attended, lse, ids, gains, qkv_w, out_w, *after)


MESH = pl.DeviceIdType.MESH


def greet(peers):
    barrier = pltpu.get_barrier_semaphore()
    for peer in peers:
        pl.semaphore_signal(barrier, inc=1, device_id=peer, device_id_type=MESH)
    pl.semaphore_wait(barrier, len(peers))


def total_kernel(axis, count, mine_ref, *refs):
    out_ref, got_ref, send_sem, recv_sem = refs[-4:]
    me = lax.axis_index(axis)
    after = [lax.rem(me + k, count) for k in range(count)]
    greet([{axis: after[k]} for k in range(1, count)])
    scatter = [
        pltpu.make_async_remote_copy(
            src_ref=mine_ref.at[after[k]],
            dst_ref=got_ref.at[k],
            send_sem=send_sem.at[0, k],
            recv_sem=recv_sem.at[0, k],
            device_id={axis: after[k]},
            device_id_type=MESH,
        )
        for k in range(1, count)
    ]
    for copy in scatter:
        copy.start()
    total = mine_ref[me]
    for k in range(1, count):
        scatter[k - 1].wait_recv()
        total = total + got_ref[k]
    out_ref[me] = total
    share = [
        pltpu.make_async_remote_copy(
            src_ref=out_ref.at[me],
            dst_ref=out_ref.at[me],
            send_sem=send_sem.at[1, k],
            recv_sem=recv_sem.at[1, k],
            device_id={axis: after[k]},
            device_id_type=MESH,
        )
        for k in range(1, count)
    ]
    for copy in share:
        copy.start()
    for copy in share:
        copy.wait_recv()
    for copy in scatter + share:
        copy.wait_send()


def total_over(values, axis, label, after=()):
    count = lax.axis_size(axis)
    rows = -(-values.shape[0] // (8 * 128 * count)) * 8
    padded = jnp.pad(values, (0, count * rows * 128 - values.shape[0])).reshape(count, rows, 128)
    out = pl.pallas_call(
        functools.partial(total_kernel, axis, count),
        out_shape=jax.ShapeDtypeStruct(padded.shape, jnp.float32),
        in_specs=[pl.BlockSpec(memory_space=pltpu.VMEM)] + [pl.BlockSpec(memory_space=pl.ANY)] * len(after),
        out_specs=pl.BlockSpec(memory_space=pltpu.VMEM),
        scratch_shapes=[
            pltpu.VMEM(padded.shape, jnp.float32),
            pltpu.SemaphoreType.DMA((2, count)),
            pltpu.SemaphoreType.DMA((2, count)),
        ],
        compiler_params=pltpu.CompilerParams(
            collective_id=label, has_side_effects=True, vmem_limit_bytes=16 * 1024 * 1024
        ),
        cost_estimate=lasts(12),
        name="total_%d" % label,
    )(padded, *after)
    return out.reshape(-1)[: values.shape[0]]


def collect_kernel(axis, count, mine_ref, out_ref, send_sem, recv_sem, local_sem):
    me = lax.axis_index(axis)
    after = [lax.rem(me + k, count) for k in range(count)]
    greet([{axis: after[k]} for k in range(1, count)])
    copies = [
        pltpu.make_async_remote_copy(
            src_ref=mine_ref,
            dst_ref=out_ref.at[me],
            send_sem=send_sem.at[k],
            recv_sem=recv_sem.at[k],
            device_id={axis: after[k]},
            device_id_type=MESH,
        )
        for k in range(1, count)
    ]
    for copy in copies:
        copy.start()
    out_ref[me] = mine_ref[...]
    for copy in copies:
        copy.wait()


def collect(values, axis, label):
    count = lax.axis_size(axis)
    return pl.pallas_call(
        functools.partial(collect_kernel, axis, count),
        out_shape=jax.ShapeDtypeStruct((count,) + values.shape, jnp.float32),
        in_specs=[pl.BlockSpec(memory_space=pltpu.VMEM)],
        out_specs=pl.BlockSpec(memory_space=pltpu.VMEM),
        scratch_shapes=[
            pltpu.SemaphoreType.DMA((count,)),
            pltpu.SemaphoreType.DMA((count,)),
            pltpu.SemaphoreType.DMA,
        ],
        compiler_params=pltpu.CompilerParams(
            collective_id=label, has_side_effects=True, vmem_limit_bytes=16 * 1024 * 1024
        ),
        cost_estimate=lasts(4),
        name="collect_%d" % label,
    )(values)


def flipped(axis, mask):
    index = lax.axis_index(axis)
    bit = lax.rem(index // mask, 2)
    return bit, {axis: index + mask - 2 * mask * bit}


def dense_kernel(orders, spans, waits, carried, mine_ref, *refs):
    steps = len(orders[0])
    extra = len(carried)
    go_refs, out_ref, come_refs = refs[:extra], refs[extra + waits], refs[extra + waits + 1 : 2 * extra + waits + 1]
    sum_ref, scratch = refs[2 * extra + waits + 1], refs[2 * extra + waits + 2 :]
    first_got = scratch[0]
    got = scratch[1 : 1 + steps]
    send_sem, recv_sem = scratch[1 + steps :]
    bits = len(mine_ref.shape) - 4
    core, core_peer = flipped("expert", 1)
    chip, chip_peer = flipped("expert", 2)
    links = [flipped("dp", 1 << b) for b in range(bits)] + [(chip, chip_peer)]
    greet([core_peer] + [peer for _, peer in links])
    whole = (slice(None),) * bits
    copies = []

    def send(src, dst, peer, part, step):
        copy = pltpu.make_async_remote_copy(
            src_ref=src,
            dst_ref=dst,
            send_sem=send_sem.at[part, step],
            recv_sem=recv_sem.at[part, step],
            device_id=peer,
            device_id_type=MESH,
        )
        copy.start()
        copies.append(copy)
        return copy

    def add(first, second):
        return (first.astype(jnp.float32) + second.astype(jnp.float32)).astype(jnp.bfloat16)

    flying = []
    beside = [
        send(go, come, links[bit][1], i, 3 + steps)
        for i, (bit, go, come) in enumerate(zip(carried, go_refs, come_refs))
    ]
    for part, span in enumerate(spans):
        at = whole + (1 - core, slice(None), slice(None), span)
        flying.append(send(mine_ref.at[at], first_got.at[..., span], core_peer, part, 0))

    def place(chosen, span):
        return tuple(chosen.get(bits - 1 - i, slice(None)) for i in range(bits)) + (
            chosen.get(bits, slice(None)),
            slice(None),
            span,
        )

    chosen = [{} for _ in spans]
    for step in range(steps + 1):
        for part, span in enumerate(spans):
            flying[part].wait_recv()
            if step == 0:
                sum_ref[..., span] = add(
                    mine_ref[whole + (core, slice(None), slice(None), span)], first_got[..., span]
                )
            else:
                here = place(chosen[part], span)
                sum_ref[here] = add(sum_ref[here], got[step - 1][part_index(orders, part, step - 1) + (slice(None), span)])
            if step < steps:
                link = orders[part][step]
                bit, peer = links[link]
                away = place({**chosen[part], link: 1 - bit}, span)
                flying[part] = send(
                    sum_ref.at[away],
                    got[step].at[part_index(orders, part, step) + (slice(None), span)],
                    peer,
                    part,
                    1 + step,
                )
                chosen[part] = {**chosen[part], link: bit}
            else:
                out_ref[core, chip, :, span] = sum_ref[place(chosen[part], span)]
                mine = out_ref.at[core, chip, :, span]
                flying[part] = send(mine, mine, chip_peer, part, 1 + steps)
    for part, span in enumerate(spans):
        flying[part].wait_recv()
        mine = out_ref.at[core, :, :, span]
        flying[part] = send(mine, mine, core_peer, part, 2 + steps)
    for copy in flying + beside:
        copy.wait_recv()
    for copy in copies:
        copy.wait_send()


def part_index(orders, part, step):
    return (slice(None),) * (len(orders[part]) - 1 - step)


def reduce_dense(dense, carried, label, after=()):
    owners = lax.axis_size("dp")
    width, columns = dense.shape
    bits = owners.bit_length() - 1
    rows = width // owners // 4
    tiles = columns // 128
    parts = 6
    bounds = [128 * (tiles * i // parts) for i in range(parts + 1)]
    spans = [slice(a, b) for a, b in zip(bounds[:-1], bounds[1:])]
    last = tuple(range(1, bits))
    orders = [((bits, 0) if part % 2 == 0 else (0, bits)) + last for part in range(parts)]
    shape = (2,) * bits + (2, 2, rows, columns)
    half = (2,) * bits + (2, rows, columns)
    goes = [go for go, _ in carried]
    out, *comes = pl.pallas_call(
        functools.partial(
            dense_kernel, orders, spans, len(after), [mask.bit_length() - 1 for _, mask in carried]
        ),
        out_shape=[jax.ShapeDtypeStruct((2, 2, rows, columns), jnp.bfloat16)]
        + [jax.ShapeDtypeStruct(go.shape, jnp.bfloat16) for go in goes],
        in_specs=[pl.BlockSpec(memory_space=pltpu.VMEM)]
        + [pl.BlockSpec(memory_space=pl.ANY)] * (len(goes) + len(after)),
        out_specs=[pl.BlockSpec(memory_space=pltpu.VMEM)] + [pl.BlockSpec(memory_space=pl.ANY)] * len(goes),
        scratch_shapes=[pltpu.VMEM(half, jnp.bfloat16), pltpu.VMEM(half, jnp.bfloat16)]
        + [
            pltpu.VMEM((2,) * (bits - step) + (rows, columns), jnp.bfloat16)
            for step in range(bits + 1)
        ]
        + [pltpu.SemaphoreType.DMA((parts, bits + 5)), pltpu.SemaphoreType.DMA((parts, bits + 5))],
        compiler_params=pltpu.CompilerParams(
            collective_id=label, has_side_effects=True, vmem_limit_bytes=VM
        ),
        cost_estimate=lasts(50),
        name="reduce_dense",
    )(dense.reshape(shape), *goes, *after)
    return out.reshape(width // owners, columns), *comes


PAIR = 2
ROUTE_ROWS = 32


class Pusher:
    def __init__(self, send_sem, recv_sem):
        self.send_sem, self.recv_sem, self.copies = send_sem, recv_sem, []

    def __call__(self, src, dst, peer):
        at = len(self.copies)
        copy = pltpu.make_async_remote_copy(
            src_ref=src,
            dst_ref=dst,
            send_sem=self.send_sem.at[at],
            recv_sem=self.recv_sem.at[at],
            device_id=peer,
            device_id_type=MESH,
        )
        copy.start()
        self.copies.append(copy)
        return copy

    def finish(self):
        for copy in self.copies:
            copy.wait_send()


def picked(code, capacity):
    return jnp.concatenate(
        [c.astype(jnp.float32) for c in one_hot(code, capacity)], axis=0
    ).astype(jnp.bfloat16)


def gather_kernel(capacity, experts_here, half_experts, top, token_ref, grad_ref, chip_grad_ref, pair_grad_ref,
                  rec_ref, arr_ref, scale_ref, code_ref, tokens, grads, weight_s, stage, send_sem, recv_sem, local_sem):
    rows = token_ref.shape[0]
    half = rows // 2
    first = lax.axis_index("expert") * experts_here + lax.rem(lax.axis_index("dp") // PAIR, 2) * half_experts
    _, core = flipped("expert", 1)
    _, chip = flipped("expert", 2)
    _, pair = flipped("dp", PAIR)
    greet([core, chip, pair])
    push = Pusher(send_sem, recv_sem)
    everything, routing = slice(None), slice(rows, rows + ROUTE_ROWS)
    to_chip = push(token_ref, tokens.at[2], chip)
    to_pair = push(token_ref, tokens.at[4], pair)
    route_both = push(pair_grad_ref.at[routing], grads.at[6, routing], chip)
    to_core = push(token_ref, tokens.at[1], core)
    grad_core = push(grad_ref, grads.at[1], core)
    grad_chip_core = push(chip_grad_ref, grads.at[3], core)
    grad_pair_core = push(pair_grad_ref, grads.at[5], core)

    earlier = lax.broadcasted_iota(jnp.int32, (rows, rows), 0)
    later = lax.broadcasted_iota(jnp.int32, (rows, rows), 1)
    before = jnp.where(earlier < later, 1.0, 0.0).astype(jnp.bfloat16)

    def route(r, table):
        table = table.astype(jnp.float32)
        ids = table[:top]
        gates = table[top : 2 * top] + table[2 * top : 3 * top]
        hits = [ids == (first + j).astype(jnp.float32) for j in range(half_experts)]
        named = jnp.concatenate(
            [jnp.max(jnp.where(hit, 1.0, 0.0), axis=0, keepdims=True) for hit in hits], axis=0
        )
        weight_s[r] = jnp.concatenate(
            [jnp.sum(jnp.where(hit, gates, 0.0), axis=0, keepdims=True) for hit in hits], axis=0
        )
        code_ref[r] = jnp.where(named > 0.0, dot(named.astype(jnp.bfloat16), before), -1.0)

    leaving = []

    def select(r, source, out_ref, weighted):
        slot = len(leaving) % stage.shape[0]
        if len(leaving) >= stage.shape[0]:
            leaving[len(leaving) - stage.shape[0]].wait()
        chosen = one_hot(code_ref[r], capacity)
        pick = jnp.concatenate([c.astype(jnp.float32) for c in chosen], axis=0).astype(jnp.bfloat16)
        made = dot(pick, source)
        for j in range(half_experts):
            part = made[j * capacity : (j + 1) * capacity]
            if weighted:
                scale = jnp.sum(
                    jnp.where(chosen[j], weight_s[r, j : j + 1, :], 0.0), axis=1, keepdims=True
                )
                scale_ref[j, r] = scale
                part = part * scale
            stage[slot, j] = part.astype(jnp.bfloat16)
        copy = pltpu.make_async_copy(stage.at[slot], out_ref.at[:, r], local_sem.at[slot])
        copy.start()
        leaving.append(copy)

    def select_grad(r, ref):
        route(r, ref[rows:, :rows])
        select(r, ref[:rows, :], arr_ref, True)

    select_grad(0, grad_ref)
    select(0, token_ref[...], rec_ref, False)
    select_grad(2, chip_grad_ref)
    select_grad(4, pair_grad_ref)
    for r, copy in ((1, grad_core), (3, grad_chip_core), (5, grad_pair_core)):
        copy.wait_recv()
        select_grad(r, grads.at[r])
    to_core.wait_recv()
    select(1, tokens[1], rec_ref, False)
    route_both.wait_recv()
    route_core = push(grads.at[6, routing], grads.at[7, routing], core)
    to_chip.wait_recv()
    both_low = push(tokens.at[2, half:rows], tokens.at[6, half:rows], pair)
    chip_core = push(tokens.at[2], tokens.at[3], core)
    to_pair.wait_recv()
    both_high = push(tokens.at[4, 0:half], tokens.at[6, 0:half], chip)
    pair_core = push(tokens.at[4], tokens.at[5], core)
    grad_low = push(chip_grad_ref.at[half:rows], grads.at[6, half:rows], pair)
    grad_high = push(pair_grad_ref.at[0:half], grads.at[6, 0:half], chip)
    select(2, tokens[2], rec_ref, False)
    select(4, tokens[4], rec_ref, False)
    route(6, grads[6, rows:, :rows])
    route_core.wait_recv()
    route(7, grads[7, rows:, :rows])
    chip_core.wait_recv()
    select(3, tokens[3], rec_ref, False)
    pair_core.wait_recv()
    select(5, tokens[5], rec_ref, False)
    both_low.wait_recv()
    both_high.wait_recv()
    both_core = push(tokens.at[6], tokens.at[7], core)
    select(6, tokens[6], rec_ref, False)
    both_core.wait_recv()
    select(7, tokens[7], rec_ref, False)
    grad_low.wait_recv()
    grad_high.wait_recv()
    grad_both_core = push(grads.at[6, 0:rows], grads.at[7, 0:rows], core)
    select(6, grads[6, :rows], arr_ref, True)
    grad_both_core.wait_recv()
    select(7, grads[7, :rows], arr_ref, True)
    for copy in leaving[-stage.shape[0] :]:
        copy.wait()
    push.finish()


def gather_and_select(token, grad, chip_grad, pair_grad, capacity, experts_here, half_experts, top, label):
    rows, width = token.shape
    vmem = pl.BlockSpec(memory_space=pltpu.VMEM)
    anywhere = pl.BlockSpec(memory_space=pl.ANY)
    slots = jax.ShapeDtypeStruct((half_experts, 8, capacity, width), jnp.bfloat16)
    return pl.pallas_call(
        functools.partial(gather_kernel, capacity, experts_here, half_experts, top),
        out_shape=(
            slots,
            slots,
            jax.ShapeDtypeStruct((half_experts, 8, capacity, 1), jnp.float32),
            jax.ShapeDtypeStruct((8, half_experts, rows), jnp.float32),
        ),
        in_specs=[vmem] * 4,
        out_specs=[anywhere, anywhere, vmem, vmem],
        scratch_shapes=[
            pltpu.VMEM((8, rows, width), jnp.bfloat16),
            pltpu.VMEM((8, rows + ROUTE_ROWS, width), jnp.bfloat16),
            pltpu.VMEM((8, half_experts, rows), jnp.float32),
            pltpu.VMEM((4, half_experts, capacity, width), jnp.bfloat16),
            pltpu.SemaphoreType.DMA((18,)),
            pltpu.SemaphoreType.DMA((18,)),
            pltpu.SemaphoreType.DMA((4,)),
        ],
        compiler_params=pltpu.CompilerParams(
            collective_id=label, has_side_effects=True, vmem_limit_bytes=VM
        ),
        cost_estimate=lasts(44),
        name="gather_and_select",
    )(token, grad, chip_grad, pair_grad)


def fetcher(order, fetched, local_sem, capacity, code_ref):
    depth = fetched.shape[0]
    fetching = []
    done = []

    def fetch():
        n = len(fetching)
        if n < len(order):
            slots, r = order[n]
            fetching.append(
                [
                    pltpu.make_async_copy(
                        ref.at[r * capacity : (r + 1) * capacity],
                        fetched.at[n % depth, j * capacity : (j + 1) * capacity],
                        local_sem.at[n % depth, j],
                    )
                    for j, ref in enumerate(slots)
                ]
            )
            for copy in fetching[-1]:
                copy.start()

    for _ in range(depth - 1):
        fetch()

    def next_sum():
        fetch()
        n = len(done)
        for copy in fetching[n]:
            copy.wait()
        done.append(n)
        return dot(picked(code_ref[order[n][1]], capacity), fetched[n % depth], 0, 0)

    return next_sum


def combine_kernel(capacity, count, code_ref, *refs):
    slots = refs[:count]
    mine_ref, theirs_ref, fetched, local_sem = refs[-4:]
    order = [(slots, r) for r in (7, 6, 3, 2, 5, 4, 1, 0)]
    next_sum = fetcher(order, fetched, local_sem, capacity, code_ref)
    for _, r in order:
        (theirs_ref if r % 2 else mine_ref)[r // 2] = next_sum().astype(jnp.bfloat16)


def combine(code, slots, capacity, after):
    _, count, rows = code.shape
    width = slots[0].shape[1]
    vmem = pl.BlockSpec(memory_space=pltpu.VMEM)
    anywhere = pl.BlockSpec(memory_space=pl.ANY)
    four = jax.ShapeDtypeStruct((4, rows, width), jnp.bfloat16)
    return pl.pallas_call(
        functools.partial(combine_kernel, capacity, count),
        out_shape=(four, four),
        in_specs=[vmem] + [anywhere] * (count + len(after)),
        out_specs=[vmem, vmem],
        scratch_shapes=[
            pltpu.VMEM((4, count * capacity, width), jnp.bfloat16),
            pltpu.SemaphoreType.DMA((4, count)),
        ],
        compiler_params=pltpu.CompilerParams(vmem_limit_bytes=VM),
        cost_estimate=lasts(12),
        name="combine",
    )(code, *slots, *after)


def return_kernel(capacity, count, far_mask, code_ref, mine_ref, theirs_ref, go_ref, *refs):
    mixes = refs[:count]
    (out_ref, near_ref, far_ref, come_ref, fetched, core_got, own, theirs_mix, core_got_mix, half_pair, half_chip, from_chip,
     from_pair, send_sem, recv_sem, local_sem) = refs[-16:]
    rows = out_ref.shape[0]
    half = rows // 2
    _, core = flipped("expert", 1)
    _, chip = flipped("expert", 2)
    _, pair = flipped("dp", PAIR)
    _, far = flipped("dp", far_mask)
    greet([core, chip, pair, far])
    push = Pusher(send_sem, recv_sem)
    beside = push(go_ref, come_ref, far)
    crossing = {i: push(theirs_ref.at[i], core_got.at[i], core) for i in (3, 1, 2, 0)}
    order = [(mixes, r) for r in (7, 6, 3, 2, 5, 4, 1, 0)]
    next_sum = fetcher(order, fetched, local_sem, capacity, code_ref)

    def plus(a, b):
        return (a.astype(jnp.float32) + b.astype(jnp.float32)).astype(jnp.bfloat16)

    def mix(i, ref, at):
        theirs_mix[i] = next_sum().astype(jnp.bfloat16)
        copy = push(theirs_mix.at[i], core_got_mix.at[i], core)
        mine = next_sum()
        copy.wait_recv()
        ref[at] = plus(mine, core_got_mix[i])

    crossing[3].wait_recv()
    own[3] = plus(mine_ref[3], core_got[3])
    at_pair = push(own.at[3, 0:half], half_pair, pair)
    at_chip = push(own.at[3, half:rows], half_chip, chip)
    crossing[1].wait_recv()
    own[1] = plus(mine_ref[1], core_got[1])
    low_chip = push(own.at[1, half:rows], from_chip.at[half:rows], chip)
    crossing[2].wait_recv()
    own[2] = plus(mine_ref[2], core_got[2])
    high_pair = push(own.at[2, 0:half], from_pair.at[0:half], pair)
    crossing[0].wait_recv()
    out_ref[...] = mine_ref[0].astype(jnp.float32) + core_got[0].astype(jnp.float32)
    mix(3, far_ref, 1)
    mix(1, far_ref, 0)
    at_pair.wait_recv()
    own[1, :half] = plus(own[1, :half], half_pair[...])
    high_chip = push(own.at[1, 0:half], from_chip.at[0:half], chip)
    at_chip.wait_recv()
    own[2, half:] = plus(own[2, half:], half_chip[...])
    low_pair = push(own.at[2, half:rows], from_pair.at[half:rows], pair)
    mix(2, near_ref, 1)
    mix(0, near_ref, 0)
    low_chip.wait_recv()
    high_pair.wait_recv()
    high_chip.wait_recv()
    low_pair.wait_recv()
    out_ref[...] += from_chip[...].astype(jnp.float32) + from_pair[...].astype(jnp.float32)
    beside.wait_recv()
    push.finish()


def return_sums(code, mine, theirs, mixes, capacity, go, far_mask, label, after):
    _, count, rows = code.shape
    width = mine.shape[2]
    vmem = pl.BlockSpec(memory_space=pltpu.VMEM)
    anywhere = pl.BlockSpec(memory_space=pl.ANY)
    four = pltpu.VMEM((4, rows, width), jnp.bfloat16)
    two = jax.ShapeDtypeStruct((2, rows, width), jnp.bfloat16)
    return pl.pallas_call(
        functools.partial(return_kernel, capacity, count, far_mask),
        out_shape=(
            jax.ShapeDtypeStruct((rows, width), jnp.float32),
            two,
            two,
            jax.ShapeDtypeStruct(go.shape, jnp.bfloat16),
        ),
        in_specs=[vmem] * 3 + [anywhere] * (1 + count + len(after)),
        out_specs=[vmem] * 3 + [anywhere],
        scratch_shapes=[pltpu.VMEM((4, count * capacity, width), jnp.bfloat16), four, four, four, four]
        + [pltpu.VMEM((rows // 2, width), jnp.bfloat16)] * 2
        + [pltpu.VMEM((rows, width), jnp.bfloat16)] * 2
        + [
            pltpu.SemaphoreType.DMA((15,)),
            pltpu.SemaphoreType.DMA((15,)),
            pltpu.SemaphoreType.DMA((4, count)),
        ],
        compiler_params=pltpu.CompilerParams(
            collective_id=label, has_side_effects=True, vmem_limit_bytes=VM
        ),
        cost_estimate=lasts(37),
        name="return_sums",
    )(code, mine, theirs, go, *mixes, *after)


def settle_kernel(waits, bit_ref, keep_ref, got_ref, *refs):
    stay_ref, go_ref = refs[waits : waits + 2]
    bit = bit_ref[0]
    for high in range(keep_ref.shape[0]):
        for low in range(keep_ref.shape[2]):
            for ref, side in ((stay_ref, bit), (go_ref, 1 - bit)):
                total = keep_ref[high, side, low].astype(jnp.float32) + got_ref[
                    high, side, low
                ].astype(jnp.float32)
                ref[high, low] = total.astype(jnp.bfloat16)


def settle(keep, got, mask, label, after, passed=()):
    count, rows, columns = keep.shape
    low = 1 if mask == PAIR else 2
    shape = (count // 2 // low, 2, low, rows, columns)
    half = jax.ShapeDtypeStruct((count // 2 // low, low, rows, columns), jnp.bfloat16)
    bit = lax.rem(lax.axis_index("dp") // mask, 2)
    vmem = pl.BlockSpec(memory_space=pltpu.VMEM)
    anywhere = pl.BlockSpec(memory_space=pl.ANY)
    stay, go, *passed = pl.pallas_call(
        functools.partial(settle_kernel, len(after) + len(passed)),
        out_shape=[half, half] + [jax.ShapeDtypeStruct(p.shape, p.dtype) for p in passed],
        in_specs=[pl.BlockSpec(memory_space=pltpu.SMEM), vmem, vmem] + [anywhere] * (len(after) + len(passed)),
        out_specs=[vmem, vmem] + [anywhere] * len(passed),
        input_output_aliases={3 + len(after) + i: 2 + i for i in range(len(passed))},
        compiler_params=pltpu.CompilerParams(vmem_limit_bytes=VM),
        cost_estimate=lasts(3),
        name="settle_%s" % label,
    )(bit.reshape(1), keep.reshape(shape), got.reshape(shape), *after, *passed)
    return stay.reshape(-1, rows, columns), go.reshape(-1, rows, columns), *passed


def settle_mix_kernel(near_ref, got_ref, *refs):
    refs[-1][...] = (near_ref[1].astype(jnp.float32) + got_ref[1].astype(jnp.float32)).astype(jnp.bfloat16)


def settle_mix(near, got, after):
    vmem = pl.BlockSpec(memory_space=pltpu.VMEM)
    return pl.pallas_call(
        settle_mix_kernel,
        out_shape=jax.ShapeDtypeStruct(near.shape[1:], jnp.bfloat16),
        in_specs=[vmem] * 2 + [pl.BlockSpec(memory_space=pl.ANY)] * len(after),
        out_specs=vmem,
        compiler_params=pltpu.CompilerParams(vmem_limit_bytes=VM),
        cost_estimate=lasts(3),
        name="settle_mix",
    )(near, got, *after)


EPS_STAT = 1e-30
STAT_DECAY = 0.5
LEARN_RATE = 0.5
CLIP_LEVEL = 0.05


def decayed(old, new):
    return STAT_DECAY * old + (1.0 - STAT_DECAY) * new


def final_stats_kernel(count, groups, half, early, *refs):
    late = half - early
    owns, gots = refs[:early], refs[early : 2 * early]
    stays, comes = refs[2 * early : 2 * early + late], refs[2 * early + late : 2 * half]
    (dense_ref, up_old_ref, down_old_ref, up_rows_ref, down_rows_ref, up_cols_ref, down_cols_ref, dense_old_ref,
     dense_cols_ref, ends_ref, out_ref, sums_ref, up_new_ref, down_new_ref, dense_out_ref, dense_new_ref,
     go_s, pay_s, got_s, dense_pay_s, dense_got_s, spread_s, send_sem, recv_sem) = refs[2 * half :]
    width = up_rows_ref.shape[1]
    ff = down_rows_ref.shape[1]
    wide = width // 2
    own_up = up_old_ref.shape[0]
    own_down = down_old_ref.shape[0]
    me = lax.axis_index("dp")
    place = lax.axis_index("expert")
    after = [lax.rem(me + k, count) for k in range(count)]
    beside = [lax.rem(place + k, groups) for k in range(groups)]
    pair_bit, pair = flipped("dp", PAIR)
    greet([{"dp": after[k]} for k in range(1, count)] + [{"expert": beside[k]} for k in range(1, groups)])
    push = Pusher(send_sem, recv_sem)

    def summed(j, side):
        return (
            stays[j][side].astype(jnp.float32) + comes[j][side].astype(jnp.float32)
        ).astype(jnp.bfloat16)

    crossing = []
    for j in range(late):
        go_s[j] = summed(j, 1 - pair_bit)
        crossing.append(push(go_s.at[j], ends_ref.at[late + j], pair))

    def column_of(table_ref, lane, at):
        return jnp.sum(jnp.where(lane == at, table_ref[...], 0.0), axis=1, keepdims=True)

    up_lane = lax.broadcasted_iota(jnp.int32, (own_up, LANES), 1)
    down_lane = lax.broadcasted_iota(jnp.int32, (own_down, LANES), 1)
    up_new_ref[...] = jnp.zeros_like(up_new_ref)
    down_new_ref[...] = jnp.zeros_like(down_new_ref)

    def factored(grad, old):
        square = grad * grad
        new = decayed(old, jnp.mean(square + EPS_STAT, axis=1, keepdims=True))
        return (
            new,
            jnp.sum(square + EPS_STAT, axis=0, keepdims=True),
            jnp.sum(square * (1.0 / new), axis=0, keepdims=True),
        )

    def expert(values, at):
        for kind, (part, old_ref, new_ref, lane, rows) in enumerate(
            (
                (values[:own_up, :], up_old_ref, up_new_ref, up_lane, own_up),
                (values[own_up:, :], down_old_ref, down_new_ref, down_lane, own_down),
            )
        ):
            new, total, scaled = factored(part.astype(jnp.float32), column_of(old_ref, lane, at))
            new_ref[:rows, :] = jnp.where(lane == at, new, new_ref[:rows, :])
            for h in range(2):
                span = slice(h * wide, (h + 1) * wide)
                pay_s[at, 4 * kind + h : 4 * kind + h + 1, :] = total[:, span]
                pay_s[at, 4 * kind + 2 + h : 4 * kind + 3 + h, :] = scaled[:, span]

    own_at, got_at = pair_bit * half, (1 - pair_bit) * half
    for j in range(late):
        ends_ref[j] = summed(j, pair_bit)
        expert(ends_ref[j], own_at + early + j)
    for j in range(early):
        expert(owns[j][...], own_at + j)
        expert(gots[j][...], got_at + j)

    columns = count * dense_cols_ref.shape[2]
    piece = dense_cols_ref.shape[2]
    dense_lane = lax.broadcasted_iota(jnp.int32, dense_new_ref.shape, 1)
    old = dense_old_ref[...]
    qkv_columns = columns - width
    totals, scaleds, rows_new = [], [], []
    for at, span in enumerate((slice(0, qkv_columns), slice(qkv_columns, columns))):
        new, total, scaled = factored(
            dense_ref[:, span].astype(jnp.float32), column_of(dense_old_ref, dense_lane, at)
        )
        rows_new.append(new)
        totals.append(total)
        scaleds.append(scaled)
    gain_lanes = (dense_lane == 2) | (dense_lane == 3)
    gains = pltpu.roll(dense_ref[:, columns:].astype(jnp.float32), 2, 1)
    moments = jnp.where(gain_lanes, decayed(old, gains * gains + EPS_STAT), 1.0)
    gain_steps = jnp.where(gain_lanes, gains * lax.rsqrt(moments), 0.0)
    dense_new_ref[...] = jnp.where(
        dense_lane == 0,
        rows_new[0],
        jnp.where(dense_lane == 1, rows_new[1], jnp.where(gain_lanes, gain_steps, pltpu.roll(moments, 2, 1))),
    )
    gain_squares = jnp.sum(jnp.sum(gain_steps * gain_steps, axis=1, keepdims=True), axis=0, keepdims=True)
    total = jnp.concatenate(totals, axis=1)
    scaled = jnp.concatenate(scaleds, axis=1)
    for d in range(count):
        span = slice(d * piece, (d + 1) * piece)
        dense_pay_s[d] = jnp.concatenate(
            [total[:, span], scaled[:, span], jnp.broadcast_to(gain_squares, (1, piece)), jnp.zeros((5, piece), jnp.float32)],
            axis=0,
        )
    dense_arriving = [push(dense_pay_s.at[after[k]], dense_got_s.at[k], {"dp": after[k]}) for k in range(1, count)]
    for j in range(late):
        crossing[j].wait_recv()
        expert(ends_ref[late + j], got_at + early + j)
    arriving = [push(pay_s.at[after[k]], got_s.at[k], {"dp": after[k]}) for k in range(1, count)]

    tile = dense_pay_s[me]
    for k in range(1, count):
        dense_arriving[k - 1].wait_recv()
        tile = tile + dense_got_s[k]
    new_columns = decayed(dense_cols_ref[me], tile[0:1] / width)
    is_qkv = lax.broadcasted_iota(jnp.int32, (1, piece), 1) + me * piece < qkv_columns
    ratio = tile[1:2] / new_columns
    sums = [
        jnp.sum(jnp.where(chosen, row, 0.0), axis=1, keepdims=True)
        for row in (ratio, tile[0:1])
        for chosen in (is_qkv, ~is_qkv)
    ]
    dense_out_ref[me] = jnp.concatenate(
        [new_columns]
        + [jnp.broadcast_to(v, (1, piece)) for v in sums]
        + [tile[2:3], jnp.zeros((2, piece), jnp.float32)],
        axis=0,
    )
    dense_arriving = [push(dense_out_ref.at[me], dense_out_ref.at[me], {"dp": after[k]}) for k in range(1, count)]

    tile = pay_s[me]
    for k in range(1, count):
        arriving[k - 1].wait_recv()
        tile = tile + got_s[k]
    made = []
    tops = []
    for kind, (rows_ref, cols_ref, rows) in enumerate(
        ((up_rows_ref, up_cols_ref, width), (down_rows_ref, down_cols_ref, ff))
    ):
        here = pl.ds(me, 1)
        square = jnp.concatenate([tile[4 * kind + h : 4 * kind + h + 1] for h in range(2)], axis=1)
        scaled = jnp.concatenate([tile[4 * kind + 2 + h : 4 * kind + 3 + h] for h in range(2)], axis=1)
        new_columns = decayed(cols_ref[here, :], square / rows)
        row_mean = decayed(
            jnp.mean(rows_ref[here, :], axis=1, keepdims=True),
            jnp.sum(square, axis=1, keepdims=True) / (rows * width),
        )
        squares = row_mean * jnp.sum(scaled / new_columns, axis=1, keepdims=True)
        made += [new_columns[:, :wide], new_columns[:, wide:]]
        tops += [jnp.broadcast_to(v, (1, wide)) for v in (row_mean, squares)]
    out_ref[me] = jnp.concatenate(made + tops, axis=0)
    arriving = [push(out_ref.at[me], out_ref.at[me], {"dp": after[k]}) for k in range(1, count)]
    for copy in arriving:
        copy.wait_recv()
    total = out_ref[0, :, :LANES]
    for a in range(1, count):
        total = total + out_ref[a, :, :LANES]
    spread_s[place] = total
    arriving = [push(spread_s.at[place], spread_s.at[place], {"expert": beside[k]}) for k in range(1, groups)]
    for copy in arriving + dense_arriving:
        copy.wait_recv()
    total = spread_s[0]
    for e in range(1, groups):
        total = total + spread_s[e]
    sums_ref[...] = total
    push.finish()


def final_stats(owns, gots, stays, comes, dense, olds, all_rows, all_columns, dense_old, dense_columns, label):
    count = lax.axis_size("dp")
    groups = lax.axis_size("expert")
    width = all_rows[0].shape[1]
    rows = olds[0].shape[0] + olds[1].shape[0]
    piece = dense_columns.shape[2]
    vmem = pl.BlockSpec(memory_space=pltpu.VMEM)
    tiles = (count, 8, width // 2)
    dense_tiles = (count, 8, piece)
    late = len(stays)
    copies = 4 * (count - 1) + groups - 1 + late
    shape = lambda *s: jax.ShapeDtypeStruct(s, jnp.float32)
    outs = (
        jax.ShapeDtypeStruct((2 * late, rows, width), jnp.bfloat16),
        shape(*tiles),
        shape(8, LANES),
        shape(LANES, LANES),
        shape(LANES, LANES),
        shape(*dense_tiles),
        shape(dense.shape[0], LANES),
    )
    args = (*owns, *gots, *stays, *comes, dense, *olds, *all_rows, *all_columns, dense_old, dense_columns)
    return pl.pallas_call(
        functools.partial(final_stats_kernel, count, groups, len(owns) + late, len(owns)),
        out_shape=outs,
        in_specs=[vmem] * len(args),
        out_specs=[vmem] * len(outs),
        scratch_shapes=[
            pltpu.VMEM((late, rows, width), jnp.bfloat16),
            pltpu.VMEM(tiles, jnp.float32),
            pltpu.VMEM(tiles, jnp.float32),
            pltpu.VMEM(dense_tiles, jnp.float32),
            pltpu.VMEM(dense_tiles, jnp.float32),
            pltpu.VMEM((groups, 8, LANES), jnp.float32),
            pltpu.SemaphoreType.DMA((copies,)),
            pltpu.SemaphoreType.DMA((copies,)),
        ],
        compiler_params=pltpu.CompilerParams(
            collective_id=label, has_side_effects=True, vmem_limit_bytes=VM
        ),
        cost_estimate=lasts(15),
        name="final_stats",
    )(*args)


def update_kernel(counts, half, early, s_ref, *refs):
    owns, gots = refs[:early], refs[early : 2 * early]
    (ends_ref, tiles_ref, sums_ref, up_new_ref, down_new_ref, dense_tiles_ref, dense_new_ref, dense_ref, dense_rows_ref,
     up_w_ref, down_w_ref, qkv_w_ref, out_w_ref,
     up_out_ref, down_out_ref, up_rows_ref, down_rows_ref, up_cols_ref, down_cols_ref,
     qkv_out_ref, out_out_ref, qkv_cols_ref, out_cols_ref, turned_ref, gains_ref, rms_ref) = refs[2 * early :]
    late = half - early
    own_up = up_out_ref.shape[1]
    own_down = down_out_ref.shape[1]
    wide = tiles_ref.shape[2]
    pair_bit = s_ref[0]
    count = dense_tiles_ref.shape[0]
    dense_sums = dense_tiles_ref[0, :, 0:1]
    for a in range(1, count):
        dense_sums = dense_sums + dense_tiles_ref[a, :, 0:1]
    width = dense_rows_ref.shape[1]
    qkv_columns = qkv_out_ref.shape[1]
    row_means = []
    squares = [dense_tiles_ref[0, 5:6, 0:1]]
    for at, columns in enumerate((qkv_columns, width)):
        row_means.append(
            decayed(
                jnp.mean(dense_rows_ref[at : at + 1, :], axis=1, keepdims=True),
                dense_sums[3 + at : 4 + at] / (width * columns),
            )
        )
        squares.append(row_means[-1] * dense_sums[1 + at : 2 + at])
    squares += [sums_ref[5:6, 0:1], sums_ref[7:8, 0:1]]
    roots = [jnp.sqrt(square / number) for square, number in zip(squares, counts)]
    factors = [LEARN_RATE / jnp.maximum(1.0, root / CLIP_LEVEL) for root in roots]
    rms_ref[...] = jnp.concatenate(
        [jnp.broadcast_to(root, (1, LANES)) for root in roots] + [jnp.zeros((3, LANES), jnp.float32)], axis=0
    )

    up_table = up_new_ref[...]
    down_table = down_new_ref[...]
    lane = lax.broadcasted_iota(jnp.int32, up_table.shape, 1)

    def expert(ref, at):
        tile = tiles_ref[at]
        for kind, (table, weight_ref, out_ref, first, rows) in enumerate(
            (
                (up_table, up_w_ref, up_out_ref, 0, own_up),
                (down_table, down_w_ref, down_out_ref, own_up, own_down),
            )
        ):
            row_mean = tile[4 + 2 * kind : 5 + 2 * kind, 0:1]
            column = jnp.sum(jnp.where(lane == at, table, 0.0), axis=1, keepdims=True)[:rows]
            scale = factors[3 + kind] * lax.rsqrt(column / row_mean)
            for h in range(2):
                span = slice(h * wide, (h + 1) * wide)
                columns = lax.rsqrt(tile[2 * kind + h : 2 * kind + h + 1, :])
                out_ref[at, :, span] = (
                    weight_ref[at, :, span].astype(jnp.float32)
                    - ref[first : first + rows, span].astype(jnp.float32) * scale * columns
                )

    own_at, got_at = pair_bit * half, (1 - pair_bit) * half
    for j in range(early):
        expert(owns[j], own_at + j)
        expert(gots[j], got_at + j)
    for j in range(late):
        expert(ends_ref.at[j], own_at + early + j)
        expert(ends_ref.at[late + j], got_at + early + j)
    up_rows_ref[...] = up_table.T[: up_rows_ref.shape[0], :own_up]
    down_rows_ref[...] = down_table.T[: down_rows_ref.shape[0], :own_down]
    for a in range(up_cols_ref.shape[0]):
        for h in range(2):
            span = slice(h * wide, (h + 1) * wide)
            up_cols_ref[a : a + 1, span] = tiles_ref[a, h : h + 1, :]
            down_cols_ref[a : a + 1, span] = tiles_ref[a, 2 + h : 3 + h, :]

    table = dense_new_ref[...]
    scales = [
        factors[1 + at] * lax.rsqrt(table[:, at : at + 1] / row_means[at]) for at in range(2)
    ]
    piece = dense_tiles_ref.shape[2]
    for first in range(0, qkv_columns + width, LANES):
        at = 0 if first < qkv_columns else 1
        weight_ref, out_ref, cols_ref = (
            (qkv_w_ref, qkv_out_ref, qkv_cols_ref) if at == 0 else (out_w_ref, out_out_ref, out_cols_ref)
        )
        here = slice(first - at * qkv_columns, first - at * qkv_columns + LANES)
        within = first % piece
        columns = dense_tiles_ref[first // piece, 0:1, within : within + LANES]
        cols_ref[:, here] = columns
        out_ref[:, here] = weight_ref[:, here].astype(jnp.float32) - dense_ref[
            :, first : first + LANES
        ].astype(jnp.float32) * scales[at] * lax.rsqrt(columns)
    turned = table.T[:8]
    turned_ref[...] = turned
    gains_ref[...] = -factors[0] * turned


def update(owns, gots, stats, dense, dense_rows, up_w, down_w, qkv_w, out_w):
    count = lax.axis_size("dp")
    groups = lax.axis_size("expert")
    me = lax.axis_index("dp")
    experts, width, up_columns = up_w.shape
    ff = down_w.shape[1]
    qkv_columns = qkv_w.shape[1]
    own_up, own_down = width // count, ff // count
    counts = (
        float(2 * width),
        float(width * qkv_columns),
        float(width * width),
        float(groups * experts * width * up_columns),
        float(groups * experts * ff * width),
    )
    ends = stats[0]
    early = len(owns)
    whole = lambda *shape: pl.BlockSpec(shape, lambda g, s: (0,) * len(shape))
    shape = lambda *s: jax.ShapeDtypeStruct(s, jnp.float32)
    rows = own_up + own_down
    outs = [
        shape(experts, own_up, up_columns),
        shape(experts, own_down, width),
        shape(experts, own_up),
        shape(experts, own_down),
        shape(experts, up_columns),
        shape(experts, width),
        shape(own_up, qkv_columns),
        shape(own_up, width),
        shape(1, qkv_columns),
        shape(1, width),
        shape(8, LANES),
        shape(8, LANES),
        shape(8, LANES),
    ]
    return pl.pallas_call(
        functools.partial(update_kernel, counts, early + ends.shape[0] // 2, early),
        out_shape=outs,
        grid_spec=pltpu.PrefetchScalarGridSpec(
            num_scalar_prefetch=1,
            grid=(1,),
            in_specs=[whole(rows, width)] * (2 * early)
            + [whole(*s.shape) for s in stats]
            + [whole(*dense.shape), whole(*dense_rows.shape)]
            + [
                pl.BlockSpec((experts, own_up, up_columns), lambda g, s: (0, s[1], 0)),
                pl.BlockSpec((experts, own_down, width), lambda g, s: (0, s[1], 0)),
                pl.BlockSpec((own_up, qkv_columns), lambda g, s: (s[1], 0)),
                pl.BlockSpec((own_up, width), lambda g, s: (s[1], 0)),
            ],
            out_specs=[whole(*o.shape) for o in outs],
        ),
        compiler_params=pltpu.CompilerParams(vmem_limit_bytes=VM),
        cost_estimate=lasts(6),
        name="update",
    )(
        jnp.stack([lax.rem(me // PAIR, 2), me]),
        *owns, *gots, *stats, dense, dense_rows, up_w, down_w, qkv_w, out_w,
    )


D = 1024
FF = 512
TOP = 8


def swap(values, axis, mask):
    count = lax.axis_size(axis)
    return lax.ppermute(values, axis, [(i, i ^ mask) for i in range(count)])


def swap_pair(values):
    return swap(values, "dp", PAIR)


def swap_chip(values):
    return swap(values, "expert", 2)


def swap_core(values):
    return swap(values, "expert", 1)


def plus(a, b):
    return (a.astype(jnp.float32) + b.astype(jnp.float32)).astype(jnp.bfloat16)


def halve(blocks, axis, mask):
    bit = lax.rem(lax.axis_index(axis) // mask, 2)
    keep = lax.dynamic_index_in_dim(blocks, bit, 1, keepdims=False)
    give = lax.dynamic_index_in_dim(blocks, 1 - bit, 1, keepdims=False)
    return keep, swap(give, axis, mask)


def reduce_dense_far(blocks):
    count = lax.axis_size("dp")
    width, columns = blocks.shape
    rows = width // count
    blocks = blocks.reshape(count, 2, 2, rows // 4, columns)
    keep, got = halve(jnp.moveaxis(blocks, 2, 1), "expert", 1)
    keep, got = halve(plus(keep, got), "expert", 2)
    blocks = plus(keep, got)
    low = 1
    while low < count:
        keep, got = halve(blocks.reshape((-1, 2, 1) + blocks.shape[1:]), "dp", low)
        blocks = plus(keep, got).reshape((-1,) + blocks.shape[1:])
        low *= 2
    mine = blocks[0]
    chip = lax.axis_index("expert") // 2
    core = lax.rem(lax.axis_index("expert"), 2)
    other = swap_chip(mine)
    both = jnp.where(chip == 0, jnp.stack([mine, other]), jnp.stack([other, mine]))
    across = swap_core(both)
    all_four = jnp.where(core == 0, jnp.stack([both, across], 1), jnp.stack([across, both], 1))
    return all_four.reshape(rows, columns)


def own_share(matrix, along):
    count = lax.axis_size("dp")
    width = matrix.shape[along] // count
    return lax.dynamic_slice_in_dim(matrix, lax.axis_index("dp") * width, width, along)


def factored(part, rows_old):
    square = part * part
    rows_new = decayed(rows_old, jnp.mean(square + EPS_STAT, axis=-1))
    return (
        rows_new,
        jnp.sum(square + EPS_STAT, axis=-2),
        jnp.sum(square / rows_new[..., None], axis=-2),
    )


def per_device(
    hidden_in,
    out_grad,
    segment_ids,
    parent_ids,
    positions,
    expert_ids,
    gate_weights,
    norm_gains,
    qkv_weight,
    out_weight,
    gate_up_weight,
    down_weight,
    gain_moment,
    qkv_rows,
    qkv_cols,
    out_rows,
    out_cols,
    gateup_rows,
    gateup_cols,
    down_rows,
    down_cols,
):
    rows_here = hidden_in.shape[0]
    dp_count = lax.axis_size("dp")
    groups = lax.axis_size("expert")
    experts_here = gate_up_weight.shape[0]
    total_experts = experts_here * groups
    capacity = 3 * rows_here * TOP // (2 * total_experts)
    half_experts = experts_here // 2
    dp_index = lax.axis_index("dp")
    pair_bit = lax.rem(dp_index // PAIR, 2)
    first_local = pair_bit * half_experts
    first_expert = lax.axis_index("expert") * experts_here + first_local

    weight_high = gate_weights.astype(jnp.bfloat16)
    weight_low = (gate_weights - weight_high.astype(jnp.float32)).astype(jnp.bfloat16)
    routing = jnp.concatenate([expert_ids.astype(jnp.bfloat16), weight_high, weight_low], axis=1).T
    routing = jnp.pad(routing, ((0, ROUTE_ROWS - routing.shape[0]), (0, D - rows_here)))
    grad_rows = jnp.concatenate([out_grad.astype(jnp.bfloat16), routing], axis=0)
    chip_grad_rows = swap_chip(grad_rows)
    pair_grad_rows = swap_pair(grad_rows)
    ids = jnp.stack([segment_ids, parent_ids, positions])
    normed, qkv, attended, lse, middle, normed_ffn = attend(
        hidden_in, ids, norm_gains, qkv_weight, out_weight
    )
    received, arrived, scale, code = gather_and_select(
        normed_ffn, grad_rows, chip_grad_rows, pair_grad_rows, capacity, experts_here, half_experts, TOP, 5
    )
    scalars = jnp.stack([first_local, lax.rem(dp_index, 2)])
    experts, chains = [], []

    def advance(j, after, come=None, passed=()):
        masks, stay, go = chains[j]
        come = swap(go, "dp", masks[0]) if come is None else come
        stay, go, *passed = settle(stay, come, masks[1], "%d_%d" % (j, masks[1]), after, passed)
        chains[j] = (masks[1:], stay, go)
        return (stay, *passed) if passed else stay

    masks = [1] + [1 << b for b in range(2, dp_count.bit_length() - 1)] + [PAIR]
    for j in range(half_experts):
        after = [experts[-1][2]] if experts else []
        if j == 3:
            after.append(advance(0, after))
        experts.append(
            run_expert(
                scalars, j, received, arrived, scale, gate_up_weight, down_weight, dp_count, after
            )
        )
        chains.append((masks, experts[j][0], experts[j][1]))
    mine, theirs = combine(code, [e[2] for e in experts], capacity, [])
    steps = [advance(1, [mine])]
    normed_f_grad, near_mix, far_mix, come = return_sums(
        code, mine, theirs, [e[3] for e in experts], capacity, chains[1][2], chains[1][0][0], 6, steps
    )
    steps = [normed_f_grad]
    steps.append(advance(0, steps))
    stay, far_mix = advance(2, steps[-1:], None, [far_mix])
    steps.append(stay)
    steps.append(advance(1, steps[-1:], come))
    input_grad, dense = attend_back(
        hidden_in, out_grad, middle, normed_f_grad, normed, qkv, attended, lse, ids, norm_gains, qkv_weight,
        out_weight, steps
    )
    got_mix = swap_chip(far_mix)
    steps = [input_grad]
    steps.append(advance(3, steps[-1:]))
    for_pair = settle_mix(near_mix, got_mix, steps[-1:])
    steps.append(for_pair)
    qkv_columns = qkv_weight.shape[1]
    fast_tail = dp_count == experts_here and D // dp_count % 64 == 0
    if fast_tail:
        dense_own, come = reduce_dense(dense, [(chains[3][2], chains[3][0][0])], 3, steps)
    else:
        dense_own = reduce_dense_far(dense)
    mix_parts = (near_mix[0], got_mix[0], swap_pair(for_pair))
    block_out = middle + sum(part.astype(jnp.float32) for part in mix_parts)
    if fast_tail:
        spare = ((0, 0), (0, LANES - experts_here))
        owns = [chains[j][1][0] for j in (0, 1)]
        gots = [swap_pair(chains[j][2][0]) for j in (0, 1)]
        dense_rows = jnp.stack([qkv_rows, out_rows])
        dense_old = jnp.pad(
            jnp.concatenate([own_share(dense_rows, 1), own_share(gain_moment, 1)], axis=0).T,
            ((0, 0), (0, LANES - 4)),
        )
        stats = final_stats(
            owns,
            gots,
            [chains[j][1] for j in (2, 3)],
            [swap(chains[2][2], "dp", chains[2][0][0]), come],
            dense_own,
            [jnp.pad(own_share(old, 1).T, spare) for old in (gateup_rows, down_rows)],
            (gateup_rows, down_rows),
            (gateup_cols, down_cols),
            dense_old,
            jnp.concatenate([qkv_cols, out_cols]).reshape(dp_count, 1, -1),
            1,
        )
        (
            gate_up_new,
            down_new,
            gateup_rows_new,
            down_rows_new,
            gateup_cols_new,
            down_cols_new,
            qkv_new,
            out_new,
            qkv_cols_new,
            out_cols_new,
            turned,
            gains,
            roots,
        ) = update(owns, gots, stats, dense_own, dense_rows, gate_up_weight, down_weight, qkv_weight, out_weight)
        qkv_cols_new, out_cols_new = qkv_cols_new[0], out_cols_new[0]
        qkv_rows_new, out_rows_new = turned[0], turned[1]
        gains_update, gain_moment_new = gains[2:4], turned[4:6]
        update_rms = roots[:5, 0]
    else:
        for j in range(half_experts):
            while len(chains[j][0]) > 1:
                advance(j, [dense_own])
        own_parts = [c[1][0] for c in chains]
        other_parts = [swap_pair(c[2][0]) for c in chains]
        own = jnp.stack(own_parts).astype(jnp.float32)
        other = jnp.stack(other_parts).astype(jnp.float32)
        parts = jnp.where(pair_bit == 0, jnp.concatenate([own, other]), jnp.concatenate([other, own]))
        gateup_part = parts[:, : D // dp_count]
        down_part = parts[:, D // dp_count :]
        gateup_rows_new, gateup_square, gateup_scaled = factored(gateup_part, own_share(gateup_rows, 1))
        down_rows_new, down_square, down_scaled = factored(down_part, own_share(down_rows, 1))
        sizes = [gateup_square.size, gateup_scaled.size, down_square.size, down_scaled.size]
        summed = total_over(
            jnp.concatenate(
                [
                    gateup_square.reshape(-1),
                    gateup_scaled.reshape(-1),
                    down_square.reshape(-1),
                    down_scaled.reshape(-1),
                    jnp.sum(gateup_rows_new, axis=1),
                    jnp.sum(down_rows_new, axis=1),
                ]
            ),
            "dp",
            1,
        )
        pieces = jnp.split(summed, [sum(sizes[: i + 1]) for i in range(4)])
        gateup_square, gateup_scaled, down_square, down_scaled = [
            p.reshape(experts_here, D) for p in pieces[:4]
        ]
        gateup_row_mean = pieces[4][:experts_here] / D
        down_row_mean = pieces[4][experts_here:] / FF
        gateup_cols_new = decayed(gateup_cols, gateup_square / D)
        down_cols_new = decayed(down_cols, down_square / FF)
        expert_squares = jnp.stack(
            [
                jnp.sum(gateup_row_mean * jnp.sum(gateup_scaled / gateup_cols_new, axis=1)),
                jnp.sum(down_row_mean * jnp.sum(down_scaled / down_cols_new, axis=1)),
            ]
        )
        spread_squares = collect(
            jnp.zeros((8, 128), jnp.float32).at[0, :2].set(expert_squares), "expert", 2
        )
        expert_squares = jnp.sum(spread_squares[:, 0, :2], axis=0)
        dense_own = dense_own.astype(jnp.float32)
        qkv_own = dense_own[:, :qkv_columns]
        out_own = dense_own[:, qkv_columns : qkv_columns + D]
        gains_own = dense_own[:, qkv_columns + D : qkv_columns + D + 2].T
        gain_moment_new = decayed(own_share(gain_moment, 1), gains_own * gains_own + EPS_STAT)
        gains_step = gains_own * lax.rsqrt(gain_moment_new)
        qkv_rows_new, qkv_square, qkv_scaled = factored(qkv_own, own_share(qkv_rows, 0))
        out_rows_new, out_square, out_scaled = factored(out_own, own_share(out_rows, 0))
        dense_sums = total_over(
            jnp.concatenate(
                [
                    qkv_square,
                    qkv_scaled,
                    out_square,
                    out_scaled,
                    jnp.stack(
                        [jnp.sum(qkv_rows_new), jnp.sum(out_rows_new), jnp.sum(gains_step * gains_step)]
                    ),
                ]
            ),
            "dp",
            4,
        )
        qkv_square, qkv_scaled, out_square, out_scaled, rest = jnp.split(
            dense_sums, [qkv_columns, 2 * qkv_columns, 2 * qkv_columns + D, 2 * qkv_columns + 2 * D]
        )
        qkv_row_mean = rest[0] / D
        out_row_mean = rest[1] / D
        qkv_cols_new = decayed(qkv_cols, qkv_square / D)
        out_cols_new = decayed(out_cols, out_square / D)
        squares = jnp.concatenate(
            [
                jnp.stack(
                    [
                        rest[2],
                        qkv_row_mean * jnp.sum(qkv_scaled / qkv_cols_new),
                        out_row_mean * jnp.sum(out_scaled / out_cols_new),
                    ]
                ),
                expert_squares,
            ]
        )
        element_counts = jnp.array(
            [2 * D, D * qkv_columns, D * D, total_experts * D * 2 * FF, total_experts * FF * D], jnp.float32
        )
        update_rms = jnp.sqrt(squares / element_counts)
        factors = LEARN_RATE / jnp.maximum(1.0, update_rms / CLIP_LEVEL)

        def stepped(weight, part, rows_new, row_mean, cols_new, factor):
            return weight.astype(jnp.float32) - part * (
                factor * lax.rsqrt(rows_new / row_mean[..., None])
            )[..., :, None] * lax.rsqrt(cols_new)[..., None, :]

        gains_update = -factors[0] * gains_step
        qkv_new = stepped(own_share(qkv_weight, 0), qkv_own, qkv_rows_new, qkv_row_mean, qkv_cols_new, factors[1])
        out_new = stepped(own_share(out_weight, 0), out_own, out_rows_new, out_row_mean, out_cols_new, factors[2])
        gate_up_new = stepped(
            own_share(gate_up_weight, 1), gateup_part, gateup_rows_new, gateup_row_mean, gateup_cols_new, factors[3]
        )
        down_new = stepped(
            own_share(down_weight, 1), down_part, down_rows_new, down_row_mean, down_cols_new, factors[4]
        )
    return (
        block_out,
        input_grad,
        update_rms,
        gains_update,
        gain_moment_new,
        qkv_new,
        qkv_rows_new,
        qkv_cols_new,
        out_new,
        out_rows_new,
        out_cols_new,
        gate_up_new,
        gateup_rows_new,
        gateup_cols_new,
        down_new,
        down_rows_new,
        down_cols_new,
    )


def solution(mesh):
    placed = (
        P(("dp", "expert"), None),
        P(("dp", "expert"), None),
        P(("dp", "expert")),
        P(("dp", "expert")),
        P(("dp", "expert")),
        P(("dp", "expert"), None),
        P(("dp", "expert"), None),
        P(),
        P(),
        P(),
        P("expert", None, None),
        P("expert", None, None),
        P(),
        P(),
        P(),
        P(),
        P(),
        P("expert", None),
        P("expert", None),
        P("expert", None),
        P("expert", None),
    )
    return jax.shard_map(
        per_device,
        mesh=mesh,
        in_specs=placed,
        out_specs=(
            P(("dp", "expert"), None),
            P(("dp", "expert"), None),
            P(),
            P(None, "dp"),
            P(None, "dp"),
            P("dp", None),
            P("dp"),
            P(),
            P("dp", None),
            P("dp"),
            P(),
            P("expert", "dp", None),
            P("expert", "dp"),
            P("expert", None),
            P("expert", "dp", None),
            P("expert", "dp"),
            P("expert", None),
        ),
        check_vma=False,
    )
```

```python
import functools
import math

import jax
import jax.numpy as jnp
from jax import lax
from jax.experimental import pallas as pl
from jax.experimental.pallas import tpu as pltpu
from jax.sharding import PartitionSpec as P

VM = 60 * 1024 * 1024
SCALE = 1e6


def lasts(microseconds):
    return pl.CostEstimate(
        flops=int(microseconds * SCALE), bytes_accessed=1024, transcendentals=0
    )


def dot(a, b, ca=1, cb=0):
    return lax.dot_general(a, b, (((ca,), (cb,)), ((), ())), preferred_element_type=jnp.float32)


def one_hot(code, capacity):
    count, rows = code.shape
    place = lax.broadcasted_iota(jnp.int32, (capacity, rows), 0).astype(jnp.float32)
    return [place == code[j : j + 1, :] for j in range(count)]


def expert_kernel(j, owners, tiles, waits, s_ref, rec_hbm, arr_hbm, scale_ref, up_hbm, down_hbm, *refs):
    (keep_hbm, give_hbm, back_hbm, mix_hbm,
     rec_s, arr_s, up_s, down_s, act_s, gug_s, wg_s, wd_s, parts_s, out_s, in_sem, out_sem) = refs[waits:]
    rows, ff = act_s.shape
    width = up_s.shape[0]
    sources, capacity = rec_s.shape[0], rec_s.shape[1]
    tile = rows // tiles
    per = sources // tiles

    def load(src, dst, at):
        copy = pltpu.make_async_copy(src, dst, in_sem.at[at])
        copy.start()
        return copy

    def load_rows(hbm, held, t, at):
        span = slice(t * per, (t + 1) * per)
        return load(hbm.at[j, span], held.at[span], at)

    expert = s_ref[0] + j
    rec_in = [load_rows(rec_hbm, rec_s, 0, 0)]
    up_in = load(up_hbm.at[expert], up_s, 2 * tiles)
    arr_in = [load_rows(arr_hbm, arr_s, 0, tiles)]
    down_in = load(down_hbm.at[expert], down_s, 2 * tiles + 1)
    for t in range(1, tiles):
        rec_in.append(load_rows(rec_hbm, rec_s, t, t))
        arr_in.append(load_rows(arr_hbm, arr_s, t, tiles + t))
    def products(t):
        span = slice(t * per, (t + 1) * per)
        return (
            dot(rec_s[span].reshape(tile, width), up_s[...]),
            dot(arr_s[span].reshape(tile, width), down_s[...], 1, 1),
        )

    for copy in (up_in, down_in, rec_in[0], arr_in[0]):
        copy.wait()
    following = products(0)
    for t in range(tiles):
        at = slice(t * tile, (t + 1) * tile)
        gate_up, act_grad = following
        if t + 1 < tiles:
            rec_in[t + 1].wait()
            arr_in[t + 1].wait()
            following = products(t + 1)
        gate = gate_up[:, :ff]
        up = gate_up[:, ff:]
        sig = 1.0 / (1.0 + jnp.exp(-gate))
        silu = gate * sig
        act_s[at, :] = (silu * up).astype(jnp.bfloat16)
        gug_s[at, :ff] = (act_grad * up * sig * (1.0 + gate * (1.0 - sig))).astype(jnp.bfloat16)
        gug_s[at, ff:] = (act_grad * silu).astype(jnp.bfloat16)
    wg_s[...] = dot(rec_s[...].reshape(rows, width), gug_s[...], 0, 0)
    wd_s[...] = dot(act_s[...], arr_s[...].reshape(rows, width), 0, 0)
    bit = s_ref[1]
    up_rows = width // owners
    down_rows = ff // owners
    leaving = []
    for k, (hbm, side) in enumerate(((give_hbm, 1 - bit), (keep_hbm, bit))):
        for slot in range(owners // 2):
            owner = 2 * slot + side
            parts_s[k, slot, :up_rows, :] = wg_s[
                pl.ds(pl.multiple_of(owner * up_rows, up_rows), up_rows), :
            ].astype(jnp.bfloat16)
            parts_s[k, slot, up_rows:, :] = wd_s[
                pl.ds(pl.multiple_of(owner * down_rows, down_rows), down_rows), :
            ].astype(jnp.bfloat16)
        copy = pltpu.make_async_copy(parts_s.at[k], hbm, out_sem.at[k])
        copy.start()
        leaving.append(copy)
    for t in range(tiles):
        at = slice(t * tile, (t + 1) * tile)
        out_s[0, at] = dot(gug_s[at, :], up_s[...], 1, 1).astype(jnp.bfloat16)
        scale = scale_ref[0, t * per : (t + 1) * per].reshape(tile, 1)
        out_s[1, at] = (dot(act_s[at, :], down_s[...]) * scale).astype(jnp.bfloat16)
        for k, hbm in enumerate((back_hbm, mix_hbm)):
            copy = pltpu.make_async_copy(out_s.at[k, at], hbm.at[at], out_sem.at[2 + 2 * t + k])
            copy.start()
            leaving.append(copy)
    for copy in leaving:
        copy.wait()


def run_expert(scalars, j, received, arrived, scale, up_w, down_w, owners, after=()):
    count, sources, capacity, width = received.shape
    ff = down_w.shape[1]
    rows = sources * capacity
    tiles = 2
    share = (owners // 2, (width + ff) // owners, width)
    slots = jax.ShapeDtypeStruct((rows, width), jnp.bfloat16)
    parts = jax.ShapeDtypeStruct(share, jnp.bfloat16)
    anywhere = pl.BlockSpec(memory_space=pl.ANY)
    return pl.pallas_call(
        functools.partial(expert_kernel, j, owners, tiles, len(after)),
        out_shape=(parts, parts, slots, slots),
        grid_spec=pltpu.PrefetchScalarGridSpec(
            num_scalar_prefetch=1,
            grid=(1,),
            in_specs=[
                anywhere,
                anywhere,
                pl.BlockSpec((1, sources, capacity, 1), lambda g, s: (j, 0, 0, 0)),
                anywhere,
                anywhere,
            ]
            + [anywhere] * len(after),
            out_specs=[anywhere] * 4,
            scratch_shapes=[
                pltpu.VMEM((sources, capacity, width), jnp.bfloat16),
                pltpu.VMEM((sources, capacity, width), jnp.bfloat16),
                pltpu.VMEM((width, 2 * ff), jnp.bfloat16),
                pltpu.VMEM((ff, width), jnp.bfloat16),
                pltpu.VMEM((rows, ff), jnp.bfloat16),
                pltpu.VMEM((rows, 2 * ff), jnp.bfloat16),
                pltpu.VMEM((width, 2 * ff), jnp.float32),
                pltpu.VMEM((ff, width), jnp.float32),
                pltpu.VMEM((2,) + share, jnp.bfloat16),
                pltpu.VMEM((2, rows, width), jnp.bfloat16),
                pltpu.SemaphoreType.DMA((2 * tiles + 2,)),
                pltpu.SemaphoreType.DMA((2 + 2 * tiles,)),
            ],
        ),
        compiler_params=pltpu.CompilerParams(vmem_limit_bytes=VM),
        cost_estimate=lasts(18),
        name="expert_%d" % j,
    )(scalars, received, arrived, scale, up_w, down_w, *after)


HEADS = 16
KV_HEADS = 8
HEAD_DIM = 64
EPS_NORM = 1e-06
ROPE_BASE = 10000.0
MASKED = -1e30
LANES = 128


def spread(row):
    rows = row.shape[1]
    by_column = jnp.broadcast_to(row.astype(jnp.float32), (rows, rows))
    return by_column, by_column.T


def mask_and_angles(ids_ref):
    seg_k, seg_q = spread(ids_ref[0:1, :])
    par_k, par_q = spread(ids_ref[1:2, :])
    pos_k, pos_q = spread(ids_ref[2:3, :])
    seen = ((seg_k == seg_q) | (seg_k == par_q) | (seg_k == par_k)) & (pos_k <= pos_q)
    bias = jnp.where(seen, 0.0, MASKED)
    lane = lax.broadcasted_iota(jnp.int32, (seg_k.shape[0], LANES), 1)
    half = HEAD_DIM // 2
    place = lax.rem(lane, half).astype(jnp.float32)
    frequency = jnp.exp(place * (-2.0 * math.log(ROPE_BASE) / HEAD_DIM))
    angles = pos_q[:, :LANES] * frequency
    front = lax.rem(lane, HEAD_DIM) < half
    sine = jnp.sin(angles)
    return bias, jnp.cos(angles), jnp.where(front, -sine, sine), front, lane


def turned(block, cosine, sine, front):
    other = jnp.where(
        front,
        pltpu.roll(block, LANES - HEAD_DIM // 2, 1),
        pltpu.roll(block, HEAD_DIM // 2, 1),
    )
    return block * cosine + other * sine


def two_diagonal(pair, which, lane):
    rolled = pltpu.roll(pair, HEAD_DIM, 1)
    first, last = (pair, rolled) if which == 0 else (rolled, pair)
    low = lane < HEAD_DIM
    return jnp.concatenate(
        [jnp.where(low, first, 0.0), jnp.where(low, 0.0, last)], axis=0
    ).astype(jnp.bfloat16)


def column_block(index):
    return pl.ds(pl.multiple_of(index * LANES, LANES), LANES)


def attend_kernel(hidden_ref, ids_ref, gains_ref, qkv_w_hbm, out_w_hbm,
                  normed_hbm, qkv_hbm, attended_hbm, lse_ref, middle_ref, normed_f_ref,
                  normed_ref, qkv_ref, attended_ref, qkv_w_ref, out_w_ref, proj_s, bias_s, sem):
    moving = [
        pltpu.make_async_copy(src, dst, sem.at[i])
        for i, (src, dst) in enumerate(
            (
                (qkv_w_hbm, qkv_w_ref),
                (out_w_hbm, out_w_ref),
                (normed_ref, normed_hbm),
                (qkv_ref, qkv_hbm),
                (attended_ref, attended_hbm),
            )
        )
    ]
    moving[0].start()
    moving[1].start()
    rows = hidden_ref.shape[0]
    att = HEADS * HEAD_DIM
    kv = KV_HEADS * HEAD_DIM
    hidden = hidden_ref[...]
    gains = gains_ref[...].astype(jnp.float32)
    inverse = lax.rsqrt(jnp.mean(hidden * hidden, axis=-1, keepdims=True) + EPS_NORM)
    normed_ref[...] = (hidden * inverse * gains[0:1, :]).astype(jnp.bfloat16)
    moving[2].start()
    bias, cosine, sine, front, lane = mask_and_angles(ids_ref)
    bias_s[...] = bias
    moving[0].wait()
    proj_s[...] = dot(normed_ref[...], qkv_w_ref[...])
    lse_ref[...] = jnp.zeros_like(lse_ref)

    def pair_step(p, carry):
        key_at = column_block(att // LANES + p)
        value_at = column_block((att + kv) // LANES + p)
        keys = turned(proj_s[:, key_at], cosine, sine, front).astype(jnp.bfloat16)
        values = proj_s[:, value_at].astype(jnp.bfloat16)
        qkv_ref[:, key_at] = keys
        qkv_ref[:, value_at] = values
        keys = keys.astype(jnp.float32)
        values = values.astype(jnp.float32)
        for which in range(2):
            query_at = column_block(2 * p + which)
            queries = turned(proj_s[:, query_at], cosine, sine, front).astype(jnp.bfloat16)
            queries = (queries.astype(jnp.float32) * HEAD_DIM**-0.5).astype(jnp.bfloat16)
            qkv_ref[:, query_at] = queries
            scores = dot(queries, two_diagonal(keys, which, lane), 1, 1)
            probs = []
            for head in range(2):
                part = scores[:, head * rows : (head + 1) * rows] + bias_s[...]
                top = jnp.max(part, axis=-1, keepdims=True)
                part = jnp.exp(part - top)
                total = jnp.sum(part, axis=-1, keepdims=True)
                probs.append((part * (1.0 / total)).astype(jnp.bfloat16))
                at = 4 * p + 2 * which + head
                lse_ref[...] = jnp.where(lane == at, top + jnp.log(total), lse_ref[...])
            attended_ref[:, query_at] = dot(
                jnp.concatenate(probs, axis=1), two_diagonal(values, which, lane)
            ).astype(jnp.bfloat16)
        return carry

    lax.fori_loop(0, KV_HEADS // 2, pair_step, 0)
    moving[3].start()
    moving[4].start()
    moving[1].wait()
    middle = hidden + dot(attended_ref[...], out_w_ref[...])
    middle_ref[...] = middle
    inverse_f = lax.rsqrt(jnp.mean(middle * middle, axis=-1, keepdims=True) + EPS_NORM)
    normed_f_ref[...] = (middle * inverse_f * gains[1:2, :]).astype(jnp.bfloat16)
    for copy in moving[2:]:
        copy.wait()


def attend(hidden, ids, gains, qkv_w, out_w):
    rows, width = hidden.shape
    shape = jax.ShapeDtypeStruct
    return pl.pallas_call(
        attend_kernel,
        out_shape=(
            shape((rows, width), jnp.bfloat16),
            shape((rows, qkv_w.shape[1]), jnp.bfloat16),
            shape((rows, out_w.shape[0]), jnp.bfloat16),
            shape((rows, LANES), jnp.float32),
            shape((rows, width), jnp.float32),
            shape((rows, width), jnp.bfloat16),
        ),
        in_specs=[pl.BlockSpec(memory_space=pltpu.VMEM)] * 3 + [pl.BlockSpec(memory_space=pl.ANY)] * 2,
        out_specs=[pl.BlockSpec(memory_space=pl.ANY)] * 3 + [pl.BlockSpec(memory_space=pltpu.VMEM)] * 3,
        scratch_shapes=[
            pltpu.VMEM((rows, width), jnp.bfloat16),
            pltpu.VMEM((rows, qkv_w.shape[1]), jnp.bfloat16),
            pltpu.VMEM((rows, out_w.shape[0]), jnp.bfloat16),
            pltpu.VMEM(qkv_w.shape, jnp.bfloat16),
            pltpu.VMEM(out_w.shape, jnp.bfloat16),
            pltpu.VMEM((rows, qkv_w.shape[1]), jnp.float32),
            pltpu.VMEM((rows, rows), jnp.float32),
            pltpu.SemaphoreType.DMA((5,)),
        ],
        compiler_params=pltpu.CompilerParams(vmem_limit_bytes=VM),
        cost_estimate=lasts(18),
        name="attend",
    )(hidden, ids, gains, qkv_w, out_w)


def attend_back_kernel(waits, grad_ref, middle_ref, normed_grad_ref, lse_ref, ids_ref, gains_ref,
                       hidden_hbm, normed_hbm, qkv_hbm, attended_hbm, qkv_w_hbm, out_w_hbm, *refs):
    (input_grad_ref, dense_hbm, dense_ref, hidden_ref, normed_ref, qkv_ref, attended_ref, qkv_w_ref, out_w_ref,
     proj_s, bias_s, back_s, sem) = refs[waits:]
    rows, width = hidden_ref.shape
    incoming = {
        name: pltpu.make_async_copy(src, dst, sem.at[i])
        for i, (name, src, dst) in enumerate(
            (
                ("attended", attended_hbm, attended_ref),
                ("out_w", out_w_hbm, out_w_ref),
                ("qkv", qkv_hbm, qkv_ref),
                ("normed", normed_hbm, normed_ref),
                ("qkv_w", qkv_w_hbm, qkv_w_ref),
                ("hidden", hidden_hbm, hidden_ref),
            )
        )
    }
    for copy in incoming.values():
        copy.start()
    leaving = []

    def leave(span):
        copy = pltpu.make_async_copy(dense_ref.at[:, span], dense_hbm.at[:, span], sem.at[6 + len(leaving)])
        copy.start()
        leaving.append(copy)

    att = HEADS * HEAD_DIM
    kv = KV_HEADS * HEAD_DIM
    gains = gains_ref[...].astype(jnp.float32)
    normed_grad = normed_grad_ref[...]
    middle = middle_ref[...]
    inverse_f = lax.rsqrt(jnp.mean(middle * middle, axis=-1, keepdims=True) + EPS_NORM)
    gain_f = jnp.sum(normed_grad * middle * inverse_f, axis=0, keepdims=True)
    weighted = normed_grad * gains[1:2, :]
    middle_grad = grad_ref[...] + (
        inverse_f * weighted
        - middle * (inverse_f * inverse_f * inverse_f)
        * jnp.mean(weighted * middle, axis=-1, keepdims=True)
    )
    input_grad_ref[...] = middle_grad
    branch = middle_grad.astype(jnp.bfloat16)
    columns = att + 2 * kv
    incoming["attended"].wait()
    dense_ref[:, columns : columns + width] = dot(attended_ref[...], branch, 0, 0).astype(jnp.bfloat16)
    leave(slice(columns, columns + width))
    incoming["out_w"].wait()
    back_s[...] = dot(branch, out_w_ref[...], 1, 1).astype(jnp.bfloat16)
    bias, cosine, sine, front, lane = mask_and_angles(ids_ref)
    bias_s[...] = bias
    low = lane < HEAD_DIM
    incoming["qkv"].wait()

    def pair_step(p, carry):
        key_at = column_block(att // LANES + p)
        value_at = column_block((att + kv) // LANES + p)
        keys = qkv_ref[:, key_at].astype(jnp.float32)
        values = qkv_ref[:, value_at].astype(jnp.float32)
        key_grads = []
        value_grads = []
        for which in range(2):
            query_at = column_block(2 * p + which)
            queries = qkv_ref[:, query_at]
            back = back_s[:, query_at]
            key_two = two_diagonal(keys, which, lane)
            scores = dot(queries, key_two, 1, 1)
            prob_grads = dot(back, two_diagonal(values, which, lane), 1, 1)
            probs = []
            score_grads = []
            for head in range(2):
                at = 4 * p + 2 * which + head
                level = jnp.sum(jnp.where(lane == at, lse_ref[...], 0.0), axis=-1, keepdims=True)
                span = slice(head * rows, (head + 1) * rows)
                prob = jnp.exp(scores[:, span] + bias_s[...] - level)
                prob_grad = prob_grads[:, span]
                row_dot = jnp.sum(prob * prob_grad, axis=-1, keepdims=True)
                probs.append(prob.astype(jnp.bfloat16))
                score_grads.append((prob * (prob_grad - row_dot)).astype(jnp.bfloat16))
            score_grads = jnp.concatenate(score_grads, axis=1)
            query_grad = dot(score_grads, key_two) * HEAD_DIM**-0.5
            proj_s[:, query_at] = turned(query_grad, cosine, -sine, front).astype(jnp.bfloat16)
            for grads, left, right in (
                (key_grads, score_grads, queries),
                (value_grads, jnp.concatenate(probs, axis=1), back),
            ):
                both = dot(left, right, 0, 0)
                first, last = both[:rows], both[rows:]
                if which == 0:
                    grads.append(first + pltpu.roll(last, HEAD_DIM, 1))
                else:
                    grads.append(pltpu.roll(first, HEAD_DIM, 1) + last)
        key_grad = jnp.where(low, key_grads[0], key_grads[1])
        proj_s[:, key_at] = turned(key_grad, cosine, -sine, front).astype(jnp.bfloat16)
        proj_s[:, value_at] = jnp.where(low, value_grads[0], value_grads[1]).astype(jnp.bfloat16)
        return carry

    lax.fori_loop(0, KV_HEADS // 2, pair_step, 0)
    for name in ("normed", "qkv_w", "hidden"):
        incoming[name].wait()
    for first in range(0, columns, columns // 2):
        span = slice(first, first + columns // 2)
        dense_ref[:, span] = dot(normed_ref[...], proj_s[:, span], 0, 0).astype(jnp.bfloat16)
        leave(span)
    normed_grad = dot(proj_s[...], qkv_w_ref[...], 1, 1)
    hidden = hidden_ref[...]
    inverse = lax.rsqrt(jnp.mean(hidden * hidden, axis=-1, keepdims=True) + EPS_NORM)
    gain_a = jnp.sum(normed_grad * hidden * inverse, axis=0, keepdims=True)
    weighted = normed_grad * gains[0:1, :]
    input_grad_ref[...] += inverse * weighted - hidden * (inverse * inverse * inverse) * jnp.mean(
        weighted * hidden, axis=-1, keepdims=True
    )
    both = jnp.concatenate([gain_a, gain_f, jnp.zeros((LANES - 2, width), jnp.float32)], axis=0)
    dense_ref[:, columns + width :] = both.T.astype(jnp.bfloat16)
    leave(slice(columns + width, columns + width + LANES))
    for copy in leaving:
        copy.wait()


def attend_back(hidden, out_grad, middle, normed_f_grad, normed, qkv, attended, lse, ids, gains, qkv_w, out_w, after=()):
    rows, width = hidden.shape
    columns = qkv_w.shape[1] + width + LANES
    return pl.pallas_call(
        functools.partial(attend_back_kernel, len(after)),
        out_shape=(
            jax.ShapeDtypeStruct((rows, width), jnp.float32),
            jax.ShapeDtypeStruct((width, columns), jnp.bfloat16),
        ),
        in_specs=[pl.BlockSpec(memory_space=pltpu.VMEM)] * 6
        + [pl.BlockSpec(memory_space=pl.ANY)] * (6 + len(after)),
        out_specs=[pl.BlockSpec(memory_space=pltpu.VMEM), pl.BlockSpec(memory_space=pl.ANY)],
        scratch_shapes=[
            pltpu.VMEM((width, columns), jnp.bfloat16),
            pltpu.VMEM((rows, width), jnp.float32),
            pltpu.VMEM((rows, width), jnp.bfloat16),
            pltpu.VMEM((rows, qkv_w.shape[1]), jnp.bfloat16),
            pltpu.VMEM((rows, out_w.shape[0]), jnp.bfloat16),
            pltpu.VMEM(qkv_w.shape, jnp.bfloat16),
            pltpu.VMEM(out_w.shape, jnp.bfloat16),
            pltpu.VMEM((rows, qkv_w.shape[1]), jnp.bfloat16),
            pltpu.VMEM((rows, rows), jnp.float32),
            pltpu.VMEM((rows, out_w.shape[0]), jnp.bfloat16),
            pltpu.SemaphoreType.DMA((10,)),
        ],
        compiler_params=pltpu.CompilerParams(vmem_limit_bytes=VM),
        cost_estimate=lasts(26),
        name="attend_back",
    )(out_grad, middle, normed_f_grad, lse, ids, gains, hidden, normed, qkv, attended, qkv_w, out_w, *after)


MESH = pl.DeviceIdType.MESH


def greet(peers):
    barrier = pltpu.get_barrier_semaphore()
    for peer in peers:
        pl.semaphore_signal(barrier, inc=1, device_id=peer, device_id_type=MESH)
    pl.semaphore_wait(barrier, len(peers))


def total_kernel(axis, count, mine_ref, *refs):
    out_ref, got_ref, send_sem, recv_sem = refs[-4:]
    me = lax.axis_index(axis)
    after = [lax.rem(me + k, count) for k in range(count)]
    greet([{axis: after[k]} for k in range(1, count)])
    scatter = [
        pltpu.make_async_remote_copy(
            src_ref=mine_ref.at[after[k]],
            dst_ref=got_ref.at[k],
            send_sem=send_sem.at[0, k],
            recv_sem=recv_sem.at[0, k],
            device_id={axis: after[k]},
            device_id_type=MESH,
        )
        for k in range(1, count)
    ]
    for copy in scatter:
        copy.start()
    total = mine_ref[me]
    for k in range(1, count):
        scatter[k - 1].wait_recv()
        total = total + got_ref[k]
    out_ref[me] = total
    share = [
        pltpu.make_async_remote_copy(
            src_ref=out_ref.at[me],
            dst_ref=out_ref.at[me],
            send_sem=send_sem.at[1, k],
            recv_sem=recv_sem.at[1, k],
            device_id={axis: after[k]},
            device_id_type=MESH,
        )
        for k in range(1, count)
    ]
    for copy in share:
        copy.start()
    for copy in share:
        copy.wait_recv()
    for copy in scatter + share:
        copy.wait_send()


def total_over(values, axis, label, after=()):
    count = lax.axis_size(axis)
    rows = -(-values.shape[0] // (8 * 128 * count)) * 8
    padded = jnp.pad(values, (0, count * rows * 128 - values.shape[0])).reshape(count, rows, 128)
    out = pl.pallas_call(
        functools.partial(total_kernel, axis, count),
        out_shape=jax.ShapeDtypeStruct(padded.shape, jnp.float32),
        in_specs=[pl.BlockSpec(memory_space=pltpu.VMEM)] + [pl.BlockSpec(memory_space=pl.ANY)] * len(after),
        out_specs=pl.BlockSpec(memory_space=pltpu.VMEM),
        scratch_shapes=[
            pltpu.VMEM(padded.shape, jnp.float32),
            pltpu.SemaphoreType.DMA((2, count)),
            pltpu.SemaphoreType.DMA((2, count)),
        ],
        compiler_params=pltpu.CompilerParams(
            collective_id=label, has_side_effects=True, vmem_limit_bytes=16 * 1024 * 1024
        ),
        cost_estimate=lasts(12),
        name="total_%d" % label,
    )(padded, *after)
    return out.reshape(-1)[: values.shape[0]]


def collect_kernel(axis, count, mine_ref, out_ref, send_sem, recv_sem, local_sem):
    me = lax.axis_index(axis)
    after = [lax.rem(me + k, count) for k in range(count)]
    greet([{axis: after[k]} for k in range(1, count)])
    copies = [
        pltpu.make_async_remote_copy(
            src_ref=mine_ref,
            dst_ref=out_ref.at[me],
            send_sem=send_sem.at[k],
            recv_sem=recv_sem.at[k],
            device_id={axis: after[k]},
            device_id_type=MESH,
        )
        for k in range(1, count)
    ]
    for copy in copies:
        copy.start()
    out_ref[me] = mine_ref[...]
    for copy in copies:
        copy.wait()


def collect(values, axis, label):
    count = lax.axis_size(axis)
    return pl.pallas_call(
        functools.partial(collect_kernel, axis, count),
        out_shape=jax.ShapeDtypeStruct((count,) + values.shape, jnp.float32),
        in_specs=[pl.BlockSpec(memory_space=pltpu.VMEM)],
        out_specs=pl.BlockSpec(memory_space=pltpu.VMEM),
        scratch_shapes=[
            pltpu.SemaphoreType.DMA((count,)),
            pltpu.SemaphoreType.DMA((count,)),
            pltpu.SemaphoreType.DMA,
        ],
        compiler_params=pltpu.CompilerParams(
            collective_id=label, has_side_effects=True, vmem_limit_bytes=16 * 1024 * 1024
        ),
        cost_estimate=lasts(4),
        name="collect_%d" % label,
    )(values)


def flipped(axis, mask):
    index = lax.axis_index(axis)
    bit = lax.rem(index // mask, 2)
    return bit, {axis: index + mask - 2 * mask * bit}


PAIR = 2
ROUTE_ROWS = 32


class Pusher:
    def __init__(self, send_sem, recv_sem):
        self.send_sem, self.recv_sem, self.copies = send_sem, recv_sem, []

    def __call__(self, src, dst, peer):
        at = len(self.copies)
        copy = pltpu.make_async_remote_copy(
            src_ref=src,
            dst_ref=dst,
            send_sem=self.send_sem.at[at],
            recv_sem=self.recv_sem.at[at],
            device_id=peer,
            device_id_type=MESH,
        )
        copy.start()
        self.copies.append(copy)
        return copy

    def finish(self):
        for copy in self.copies:
            copy.wait_send()


def picked(code, capacity):
    return jnp.concatenate(
        [c.astype(jnp.float32) for c in one_hot(code, capacity)], axis=0
    ).astype(jnp.bfloat16)


def gather_kernel(capacity, experts_here, half_experts, top, token_ref, grad_ref, chip_grad_ref, pair_grad_ref,
                  rec_ref, arr_ref, scale_ref, code_ref, tokens, grads, weight_s, stage, send_sem, recv_sem, local_sem):
    rows = token_ref.shape[0]
    half = rows // 2
    first = lax.axis_index("expert") * experts_here + lax.rem(lax.axis_index("dp") // PAIR, 2) * half_experts
    _, core = flipped("expert", 1)
    _, chip = flipped("expert", 2)
    _, pair = flipped("dp", PAIR)
    greet([core, chip, pair])
    push = Pusher(send_sem, recv_sem)
    everything, routing = slice(None), slice(rows, rows + ROUTE_ROWS)
    to_chip = push(token_ref, tokens.at[2], chip)
    to_pair = push(token_ref, tokens.at[4], pair)
    route_both = push(pair_grad_ref.at[routing], grads.at[6, routing], chip)
    to_core = push(token_ref, tokens.at[1], core)
    grad_core = push(grad_ref, grads.at[1], core)
    grad_chip_core = push(chip_grad_ref, grads.at[3], core)
    grad_pair_core = push(pair_grad_ref, grads.at[5], core)

    earlier = lax.broadcasted_iota(jnp.int32, (rows, rows), 0)
    later = lax.broadcasted_iota(jnp.int32, (rows, rows), 1)
    before = jnp.where(earlier < later, 1.0, 0.0).astype(jnp.bfloat16)

    def route(r, table):
        table = table.astype(jnp.float32)
        ids = table[:top]
        gates = table[top : 2 * top] + table[2 * top : 3 * top]
        hits = [ids == (first + j).astype(jnp.float32) for j in range(half_experts)]
        named = jnp.concatenate(
            [jnp.max(jnp.where(hit, 1.0, 0.0), axis=0, keepdims=True) for hit in hits], axis=0
        )
        weight_s[r] = jnp.concatenate(
            [jnp.sum(jnp.where(hit, gates, 0.0), axis=0, keepdims=True) for hit in hits], axis=0
        )
        code_ref[r] = jnp.where(named > 0.0, dot(named.astype(jnp.bfloat16), before), -1.0)

    leaving = []

    def select(r, source, out_ref, weighted):
        slot = len(leaving) % stage.shape[0]
        if len(leaving) >= stage.shape[0]:
            leaving[len(leaving) - stage.shape[0]].wait()
        chosen = one_hot(code_ref[r], capacity)
        pick = jnp.concatenate([c.astype(jnp.float32) for c in chosen], axis=0).astype(jnp.bfloat16)
        made = dot(pick, source)
        for j in range(half_experts):
            part = made[j * capacity : (j + 1) * capacity]
            if weighted:
                scale = jnp.sum(
                    jnp.where(chosen[j], weight_s[r, j : j + 1, :], 0.0), axis=1, keepdims=True
                )
                scale_ref[j, r] = scale
                part = part * scale
            stage[slot, j] = part.astype(jnp.bfloat16)
        copy = pltpu.make_async_copy(stage.at[slot], out_ref.at[:, r], local_sem.at[slot])
        copy.start()
        leaving.append(copy)

    def select_grad(r, ref):
        route(r, ref[rows:, :rows])
        select(r, ref[:rows, :], arr_ref, True)

    select_grad(0, grad_ref)
    select(0, token_ref[...], rec_ref, False)
    select_grad(2, chip_grad_ref)
    select_grad(4, pair_grad_ref)
    for r, copy in ((1, grad_core), (3, grad_chip_core), (5, grad_pair_core)):
        copy.wait_recv()
        select_grad(r, grads.at[r])
    to_core.wait_recv()
    select(1, tokens[1], rec_ref, False)
    route_both.wait_recv()
    route_core = push(grads.at[6, routing], grads.at[7, routing], core)
    to_chip.wait_recv()
    both_low = push(tokens.at[2, half:rows], tokens.at[6, half:rows], pair)
    chip_core = push(tokens.at[2], tokens.at[3], core)
    to_pair.wait_recv()
    both_high = push(tokens.at[4, 0:half], tokens.at[6, 0:half], chip)
    pair_core = push(tokens.at[4], tokens.at[5], core)
    grad_low = push(chip_grad_ref.at[half:rows], grads.at[6, half:rows], pair)
    grad_high = push(pair_grad_ref.at[0:half], grads.at[6, 0:half], chip)
    select(2, tokens[2], rec_ref, False)
    select(4, tokens[4], rec_ref, False)
    route(6, grads[6, rows:, :rows])
    route_core.wait_recv()
    route(7, grads[7, rows:, :rows])
    chip_core.wait_recv()
    select(3, tokens[3], rec_ref, False)
    pair_core.wait_recv()
    select(5, tokens[5], rec_ref, False)
    both_low.wait_recv()
    both_high.wait_recv()
    both_core = push(tokens.at[6], tokens.at[7], core)
    select(6, tokens[6], rec_ref, False)
    both_core.wait_recv()
    select(7, tokens[7], rec_ref, False)
    grad_low.wait_recv()
    grad_high.wait_recv()
    grad_both_core = push(grads.at[6, 0:rows], grads.at[7, 0:rows], core)
    select(6, grads[6, :rows], arr_ref, True)
    grad_both_core.wait_recv()
    select(7, grads[7, :rows], arr_ref, True)
    for copy in leaving[-stage.shape[0] :]:
        copy.wait()
    push.finish()


def gather_and_select(token, grad, chip_grad, pair_grad, capacity, experts_here, half_experts, top, label):
    rows, width = token.shape
    vmem = pl.BlockSpec(memory_space=pltpu.VMEM)
    anywhere = pl.BlockSpec(memory_space=pl.ANY)
    slots = jax.ShapeDtypeStruct((half_experts, 8, capacity, width), jnp.bfloat16)
    return pl.pallas_call(
        functools.partial(gather_kernel, capacity, experts_here, half_experts, top),
        out_shape=(
            slots,
            slots,
            jax.ShapeDtypeStruct((half_experts, 8, capacity, 1), jnp.float32),
            jax.ShapeDtypeStruct((8, half_experts, rows), jnp.float32),
        ),
        in_specs=[vmem] * 4,
        out_specs=[anywhere, anywhere, vmem, vmem],
        scratch_shapes=[
            pltpu.VMEM((8, rows, width), jnp.bfloat16),
            pltpu.VMEM((8, rows + ROUTE_ROWS, width), jnp.bfloat16),
            pltpu.VMEM((8, half_experts, rows), jnp.float32),
            pltpu.VMEM((4, half_experts, capacity, width), jnp.bfloat16),
            pltpu.SemaphoreType.DMA((18,)),
            pltpu.SemaphoreType.DMA((18,)),
            pltpu.SemaphoreType.DMA((4,)),
        ],
        compiler_params=pltpu.CompilerParams(
            collective_id=label, has_side_effects=True, vmem_limit_bytes=VM
        ),
        cost_estimate=lasts(44),
        name="gather_and_select",
    )(token, grad, chip_grad, pair_grad)


def fetcher(order, fetched, local_sem, capacity, code_ref):
    depth = fetched.shape[0]
    fetching = []
    done = []

    def fetch():
        n = len(fetching)
        if n < len(order):
            slots, r = order[n]
            fetching.append(
                [
                    pltpu.make_async_copy(
                        ref.at[r * capacity : (r + 1) * capacity],
                        fetched.at[n % depth, j * capacity : (j + 1) * capacity],
                        local_sem.at[n % depth, j],
                    )
                    for j, ref in enumerate(slots)
                ]
            )
            for copy in fetching[-1]:
                copy.start()

    for _ in range(depth - 1):
        fetch()

    def next_sum():
        fetch()
        n = len(done)
        for copy in fetching[n]:
            copy.wait()
        done.append(n)
        return dot(picked(code_ref[order[n][1]], capacity), fetched[n % depth], 0, 0)

    return next_sum


def combine_kernel(capacity, count, code_ref, *refs):
    slots = refs[:count]
    mine_ref, theirs_ref, fetched, local_sem = refs[-4:]
    order = [(slots, r) for r in (7, 6, 3, 2, 5, 4, 1, 0)]
    next_sum = fetcher(order, fetched, local_sem, capacity, code_ref)
    for _, r in order:
        (theirs_ref if r % 2 else mine_ref)[r // 2] = next_sum().astype(jnp.bfloat16)


def combine(code, slots, capacity, after):
    _, count, rows = code.shape
    width = slots[0].shape[1]
    vmem = pl.BlockSpec(memory_space=pltpu.VMEM)
    anywhere = pl.BlockSpec(memory_space=pl.ANY)
    four = jax.ShapeDtypeStruct((4, rows, width), jnp.bfloat16)
    return pl.pallas_call(
        functools.partial(combine_kernel, capacity, count),
        out_shape=(four, four),
        in_specs=[vmem] + [anywhere] * (count + len(after)),
        out_specs=[vmem, vmem],
        scratch_shapes=[
            pltpu.VMEM((4, count * capacity, width), jnp.bfloat16),
            pltpu.SemaphoreType.DMA((4, count)),
        ],
        compiler_params=pltpu.CompilerParams(vmem_limit_bytes=VM),
        cost_estimate=lasts(12),
        name="combine",
    )(code, *slots, *after)


def return_kernel(capacity, count, far_mask, code_ref, mine_ref, theirs_ref, go_ref, *refs):
    mixes = refs[:count]
    (out_ref, near_ref, far_ref, come_ref, fetched, core_got, own, theirs_mix, core_got_mix, half_pair, half_chip, from_chip,
     from_pair, send_sem, recv_sem, local_sem) = refs[-16:]
    rows = out_ref.shape[0]
    half = rows // 2
    _, core = flipped("expert", 1)
    _, chip = flipped("expert", 2)
    _, pair = flipped("dp", PAIR)
    _, far = flipped("dp", far_mask)
    greet([core, chip, pair, far])
    push = Pusher(send_sem, recv_sem)
    beside = push(go_ref, come_ref, far)
    crossing = {i: push(theirs_ref.at[i], core_got.at[i], core) for i in (3, 1, 2, 0)}
    order = [(mixes, r) for r in (7, 6, 3, 2, 5, 4, 1, 0)]
    next_sum = fetcher(order, fetched, local_sem, capacity, code_ref)

    def plus(a, b):
        return (a.astype(jnp.float32) + b.astype(jnp.float32)).astype(jnp.bfloat16)

    def mix(i, ref, at):
        theirs_mix[i] = next_sum().astype(jnp.bfloat16)
        copy = push(theirs_mix.at[i], core_got_mix.at[i], core)
        mine = next_sum()
        copy.wait_recv()
        ref[at] = plus(mine, core_got_mix[i])

    crossing[3].wait_recv()
    own[3] = plus(mine_ref[3], core_got[3])
    at_pair = push(own.at[3, 0:half], half_pair, pair)
    at_chip = push(own.at[3, half:rows], half_chip, chip)
    crossing[1].wait_recv()
    own[1] = plus(mine_ref[1], core_got[1])
    low_chip = push(own.at[1, half:rows], from_chip.at[half:rows], chip)
    crossing[2].wait_recv()
    own[2] = plus(mine_ref[2], core_got[2])
    high_pair = push(own.at[2, 0:half], from_pair.at[0:half], pair)
    crossing[0].wait_recv()
    out_ref[...] = mine_ref[0].astype(jnp.float32) + core_got[0].astype(jnp.float32)
    mix(3, far_ref, 1)
    mix(1, far_ref, 0)
    at_pair.wait_recv()
    own[1, :half] = plus(own[1, :half], half_pair[...])
    high_chip = push(own.at[1, 0:half], from_chip.at[0:half], chip)
    at_chip.wait_recv()
    own[2, half:] = plus(own[2, half:], half_chip[...])
    low_pair = push(own.at[2, half:rows], from_pair.at[half:rows], pair)
    mix(2, near_ref, 1)
    mix(0, near_ref, 0)
    low_chip.wait_recv()
    high_pair.wait_recv()
    high_chip.wait_recv()
    low_pair.wait_recv()
    out_ref[...] += from_chip[...].astype(jnp.float32) + from_pair[...].astype(jnp.float32)
    beside.wait_recv()
    push.finish()


def return_sums(code, mine, theirs, mixes, capacity, go, far_mask, label, after):
    _, count, rows = code.shape
    width = mine.shape[2]
    vmem = pl.BlockSpec(memory_space=pltpu.VMEM)
    anywhere = pl.BlockSpec(memory_space=pl.ANY)
    four = pltpu.VMEM((4, rows, width), jnp.bfloat16)
    two = jax.ShapeDtypeStruct((2, rows, width), jnp.bfloat16)
    return pl.pallas_call(
        functools.partial(return_kernel, capacity, count, far_mask),
        out_shape=(
            jax.ShapeDtypeStruct((rows, width), jnp.float32),
            two,
            two,
            jax.ShapeDtypeStruct(go.shape, jnp.bfloat16),
        ),
        in_specs=[vmem] * 3 + [anywhere] * (1 + count + len(after)),
        out_specs=[vmem] * 3 + [anywhere],
        scratch_shapes=[pltpu.VMEM((4, count * capacity, width), jnp.bfloat16), four, four, four, four]
        + [pltpu.VMEM((rows // 2, width), jnp.bfloat16)] * 2
        + [pltpu.VMEM((rows, width), jnp.bfloat16)] * 2
        + [
            pltpu.SemaphoreType.DMA((15,)),
            pltpu.SemaphoreType.DMA((15,)),
            pltpu.SemaphoreType.DMA((4, count)),
        ],
        compiler_params=pltpu.CompilerParams(
            collective_id=label, has_side_effects=True, vmem_limit_bytes=VM
        ),
        cost_estimate=lasts(37),
        name="return_sums",
    )(code, mine, theirs, go, *mixes, *after)


def settle_kernel(waits, bit_ref, keep_ref, got_ref, *refs):
    stay_ref, go_ref = refs[waits : waits + 2]
    bit = bit_ref[0]
    for high in range(keep_ref.shape[0]):
        for low in range(keep_ref.shape[2]):
            for ref, side in ((stay_ref, bit), (go_ref, 1 - bit)):
                total = keep_ref[high, side, low].astype(jnp.float32) + got_ref[
                    high, side, low
                ].astype(jnp.float32)
                ref[high, low] = total.astype(jnp.bfloat16)


def settle(keep, got, mask, label, after, passed=()):
    count, rows, columns = keep.shape
    low = 1 if mask == PAIR else 2
    shape = (count // 2 // low, 2, low, rows, columns)
    half = jax.ShapeDtypeStruct((count // 2 // low, low, rows, columns), jnp.bfloat16)
    bit = lax.rem(lax.axis_index("dp") // mask, 2)
    vmem = pl.BlockSpec(memory_space=pltpu.VMEM)
    anywhere = pl.BlockSpec(memory_space=pl.ANY)
    stay, go, *passed = pl.pallas_call(
        functools.partial(settle_kernel, len(after) + len(passed)),
        out_shape=[half, half] + [jax.ShapeDtypeStruct(p.shape, p.dtype) for p in passed],
        in_specs=[pl.BlockSpec(memory_space=pltpu.SMEM), vmem, vmem] + [anywhere] * (len(after) + len(passed)),
        out_specs=[vmem, vmem] + [anywhere] * len(passed),
        input_output_aliases={3 + len(after) + i: 2 + i for i in range(len(passed))},
        compiler_params=pltpu.CompilerParams(vmem_limit_bytes=VM),
        cost_estimate=lasts(3),
        name="settle_%s" % label,
    )(bit.reshape(1), keep.reshape(shape), got.reshape(shape), *after, *passed)
    return stay.reshape(-1, rows, columns), go.reshape(-1, rows, columns), *passed


def settle_mix_kernel(near_ref, got_ref, *refs):
    refs[-1][...] = (near_ref[1].astype(jnp.float32) + got_ref[1].astype(jnp.float32)).astype(jnp.bfloat16)


def settle_mix(near, got, after):
    vmem = pl.BlockSpec(memory_space=pltpu.VMEM)
    return pl.pallas_call(
        settle_mix_kernel,
        out_shape=jax.ShapeDtypeStruct(near.shape[1:], jnp.bfloat16),
        in_specs=[vmem] * 2 + [pl.BlockSpec(memory_space=pl.ANY)] * len(after),
        out_specs=vmem,
        compiler_params=pltpu.CompilerParams(vmem_limit_bytes=VM),
        cost_estimate=lasts(3),
        name="settle_mix",
    )(near, got, *after)


EPS_STAT = 1e-30
STAT_DECAY = 0.5
LEARN_RATE = 0.5
CLIP_LEVEL = 0.05


def decayed(old, new):
    return STAT_DECAY * old + (1.0 - STAT_DECAY) * new


def finish_kernel(count, groups, half, orders, spans, *refs):
    bits = count.bit_length() - 1
    steps = len(orders[0])
    (mine_hbm, own_0, own_1, got_0, got_1, stay_2, come_2, keep_3, come_3, near_mix_ref, got_mix_ref,
     up_old_ref, down_old_ref, up_rows_ref, down_rows_ref, up_cols_ref, down_cols_ref, dense_old_ref,
     dense_cols_ref) = refs[:19]
    (dense_ref, ends_ref, pair_mix_ref, out_ref, sums_ref, up_new_ref, down_new_ref, dense_out_ref,
     dense_new_ref) = refs[19:28]
    sum_ref, first_got, *got = refs[28 : 30 + steps]
    (mine_ref, load_sem, go_s, far_go_s, far_stay_s, far_got_s, mix_s, pay_s, got_s, dense_pay_s, dense_got_s, spread_s,
     send_sem, recv_sem) = refs[30 + steps :]
    width = up_rows_ref.shape[1]
    ff = down_rows_ref.shape[1]
    wide = width // 2
    own_up = up_old_ref.shape[0]
    own_down = down_old_ref.shape[0]
    me = lax.axis_index("dp")
    place = lax.axis_index("expert")
    after = [lax.rem(me + k, count) for k in range(count)]
    beside = [lax.rem(place + k, groups) for k in range(groups)]
    pair_bit, pair = flipped("dp", PAIR)
    far_bit, far = flipped("dp", FAR)
    core, core_peer = flipped("expert", 1)
    chip, chip_peer = flipped("expert", 2)
    links = [flipped("dp", 1 << b) for b in range(bits)] + [(chip, chip_peer)]
    whole = (slice(None),) * bits
    loading = pltpu.make_async_copy(mine_hbm.at[whole + (core,)], mine_ref, load_sem)
    loading.start()
    greet([{"dp": after[k]} for k in range(1, count)] + [{"expert": beside[k]} for k in range(1, groups)])
    push = Pusher(send_sem, recv_sem)

    def plus(a, b):
        return (a.astype(jnp.float32) + b.astype(jnp.float32)).astype(jnp.bfloat16)

    flying = [
        push(mine_hbm.at[whole + (1 - core, slice(None), slice(None), span)], first_got.at[..., span], core_peer)
        for span in spans
    ]
    for low in range(2):
        far_go_s[low] = plus(keep_3[1 - far_bit, low], come_3[1 - far_bit, low])
    far_exchange = push(far_go_s, far_got_s, far)
    go_s[0] = plus(stay_2[1 - pair_bit], come_2[1 - pair_bit])
    cross_2 = push(go_s.at[0], ends_ref.at[2], pair)
    mix_s[...] = plus(near_mix_ref[1], got_mix_ref[1])
    cross_mix = push(mix_s, pair_mix_ref, pair)
    ends_ref[0] = plus(stay_2[pair_bit], come_2[pair_bit])
    for low in range(2):
        far_stay_s[low] = plus(keep_3[far_bit, low], come_3[far_bit, low])

    def column_of(table_ref, lane, at):
        return jnp.sum(jnp.where(lane == at, table_ref[...], 0.0), axis=1, keepdims=True)

    up_lane = lax.broadcasted_iota(jnp.int32, (own_up, LANES), 1)
    down_lane = lax.broadcasted_iota(jnp.int32, (own_down, LANES), 1)
    up_new_ref[...] = jnp.zeros_like(up_new_ref)
    down_new_ref[...] = jnp.zeros_like(down_new_ref)

    def factored(grad, old):
        square = grad * grad
        new = decayed(old, jnp.mean(square + EPS_STAT, axis=1, keepdims=True))
        return (
            new,
            jnp.sum(square + EPS_STAT, axis=0, keepdims=True),
            jnp.sum(square * (1.0 / new), axis=0, keepdims=True),
        )

    def expert(values, at):
        for kind, (part, old_ref, new_ref, lane, rows) in enumerate(
            (
                (values[:own_up, :], up_old_ref, up_new_ref, up_lane, own_up),
                (values[own_up:, :], down_old_ref, down_new_ref, down_lane, own_down),
            )
        ):
            new, total, scaled = factored(part.astype(jnp.float32), column_of(old_ref, lane, at))
            new_ref[:rows, :] = jnp.where(lane == at, new, new_ref[:rows, :])
            for h in range(2):
                span = slice(h * wide, (h + 1) * wide)
                pay_s[at, 4 * kind + h : 4 * kind + h + 1, :] = total[:, span]
                pay_s[at, 4 * kind + 2 + h : 4 * kind + 3 + h, :] = scaled[:, span]

    own_at, got_at = pair_bit * half, (1 - pair_bit) * half

    def at_place(chosen, span):
        return tuple(chosen.get(bits - 1 - i, slice(None)) for i in range(bits)) + (
            chosen.get(bits, slice(None)),
            slice(None),
            span,
        )

    def got_place(step, span):
        return (slice(None),) * (steps - 1 - step) + (slice(None), span)

    loading.wait()
    chosen = [{} for _ in spans]
    for step in range(steps + 1):
        for part, span in enumerate(spans):
            flying[part].wait_recv()
            if step == 0:
                sum_ref[..., span] = plus(mine_ref[..., span], first_got[..., span])
            else:
                here = at_place(chosen[part], span)
                sum_ref[here] = plus(sum_ref[here], got[step - 1][got_place(step - 1, span)])
            if step < steps:
                link = orders[part][step]
                bit, peer = links[link]
                away = at_place({**chosen[part], link: 1 - bit}, span)
                flying[part] = push(sum_ref.at[away], got[step].at[got_place(step, span)], peer)
                chosen[part] = {**chosen[part], link: bit}
            else:
                dense_ref[core, chip, :, span] = sum_ref[at_place(chosen[part], span)]
                block = dense_ref.at[core, chip, :, span]
                flying[part] = push(block, block, chip_peer)
        if step == 0:
            expert(own_0, own_at)
            expert(got_0, got_at)
            expert(own_1, own_at + 1)
            expert(got_1, got_at + 1)
        elif step == 1:
            expert(ends_ref[0], own_at + 2)
        elif step == steps - 1:
            cross_2.wait_recv()
            expert(ends_ref[2], got_at + 2)
            far_exchange.wait_recv()
            go_s[1] = plus(far_stay_s[1 - pair_bit], far_got_s[1 - pair_bit])
            cross_3 = push(go_s.at[1], ends_ref.at[3], pair)
            ends_ref[1] = plus(far_stay_s[pair_bit], far_got_s[pair_bit])
            expert(ends_ref[1], own_at + 3)
    for part, span in enumerate(spans):
        flying[part].wait_recv()
        block = dense_ref.at[core, :, :, span]
        flying[part] = push(block, block, core_peer)
    cross_3.wait_recv()
    expert(ends_ref[3], got_at + 3)
    arriving = [push(pay_s.at[after[k]], got_s.at[k], {"dp": after[k]}) for k in range(1, count)]
    for copy in flying:
        copy.wait_recv()

    columns = count * dense_cols_ref.shape[2]
    piece = dense_cols_ref.shape[2]
    dense = dense_ref[...].reshape(own_up, dense_ref.shape[3])
    dense_lane = lax.broadcasted_iota(jnp.int32, dense_new_ref.shape, 1)
    old = dense_old_ref[...]
    qkv_columns = columns - width
    totals, scaleds, rows_new = [], [], []
    for at, span in enumerate((slice(0, qkv_columns), slice(qkv_columns, columns))):
        new, total, scaled = factored(
            dense[:, span].astype(jnp.float32), column_of(dense_old_ref, dense_lane, at)
        )
        rows_new.append(new)
        totals.append(total)
        scaleds.append(scaled)
    gain_lanes = (dense_lane == 2) | (dense_lane == 3)
    gains = pltpu.roll(dense[:, columns:].astype(jnp.float32), 2, 1)
    moments = jnp.where(gain_lanes, decayed(old, gains * gains + EPS_STAT), 1.0)
    gain_steps = jnp.where(gain_lanes, gains * lax.rsqrt(moments), 0.0)
    dense_new_ref[...] = jnp.where(
        dense_lane == 0,
        rows_new[0],
        jnp.where(dense_lane == 1, rows_new[1], jnp.where(gain_lanes, gain_steps, pltpu.roll(moments, 2, 1))),
    )
    gain_squares = jnp.sum(jnp.sum(gain_steps * gain_steps, axis=1, keepdims=True), axis=0, keepdims=True)
    total = jnp.concatenate(totals, axis=1)
    scaled = jnp.concatenate(scaleds, axis=1)
    for d in range(count):
        span = slice(d * piece, (d + 1) * piece)
        dense_pay_s[d] = jnp.concatenate(
            [total[:, span], scaled[:, span], jnp.broadcast_to(gain_squares, (1, piece)), jnp.zeros((5, piece), jnp.float32)],
            axis=0,
        )
    dense_arriving = [push(dense_pay_s.at[after[k]], dense_got_s.at[k], {"dp": after[k]}) for k in range(1, count)]

    tile = pay_s[me]
    for k in range(1, count):
        arriving[k - 1].wait_recv()
        tile = tile + got_s[k]
    made = []
    tops = []
    for kind, (rows_ref, cols_ref, rows) in enumerate(
        ((up_rows_ref, up_cols_ref, width), (down_rows_ref, down_cols_ref, ff))
    ):
        here = pl.ds(me, 1)
        square = jnp.concatenate([tile[4 * kind + h : 4 * kind + h + 1] for h in range(2)], axis=1)
        scaled = jnp.concatenate([tile[4 * kind + 2 + h : 4 * kind + 3 + h] for h in range(2)], axis=1)
        new_columns = decayed(cols_ref[here, :], square / rows)
        row_mean = decayed(
            jnp.mean(rows_ref[here, :], axis=1, keepdims=True),
            jnp.sum(square, axis=1, keepdims=True) / (rows * width),
        )
        squares = row_mean * jnp.sum(scaled / new_columns, axis=1, keepdims=True)
        made += [new_columns[:, :wide], new_columns[:, wide:]]
        tops += [jnp.broadcast_to(v, (1, wide)) for v in (row_mean, squares)]
    out_ref[me] = jnp.concatenate(made + tops, axis=0)
    arriving = [push(out_ref.at[me], out_ref.at[me], {"dp": after[k]}) for k in range(1, count)]

    tile = dense_pay_s[me]
    for k in range(1, count):
        dense_arriving[k - 1].wait_recv()
        tile = tile + dense_got_s[k]
    new_columns = decayed(dense_cols_ref[me], tile[0:1] / width)
    is_qkv = lax.broadcasted_iota(jnp.int32, (1, piece), 1) + me * piece < qkv_columns
    ratio = tile[1:2] / new_columns
    sums = [
        jnp.sum(jnp.where(chosen_columns, row, 0.0), axis=1, keepdims=True)
        for row in (ratio, tile[0:1])
        for chosen_columns in (is_qkv, ~is_qkv)
    ]
    dense_out_ref[me] = jnp.concatenate(
        [new_columns]
        + [jnp.broadcast_to(v, (1, piece)) for v in sums]
        + [tile[2:3], jnp.zeros((2, piece), jnp.float32)],
        axis=0,
    )
    dense_arriving = [push(dense_out_ref.at[me], dense_out_ref.at[me], {"dp": after[k]}) for k in range(1, count)]

    for copy in arriving:
        copy.wait_recv()
    total = out_ref[0, :, :LANES]
    for a in range(1, count):
        total = total + out_ref[a, :, :LANES]
    spread_s[place] = total
    arriving = [push(spread_s.at[place], spread_s.at[place], {"expert": beside[k]}) for k in range(1, groups)]
    for copy in arriving + dense_arriving + [cross_mix]:
        copy.wait_recv()
    total = spread_s[0]
    for e in range(1, groups):
        total = total + spread_s[e]
    sums_ref[...] = total
    push.finish()


FAR = 4


def finish(dense, owns, gots, settling, mixes, olds, all_rows, all_columns, dense_old, dense_columns, label):
    count = lax.axis_size("dp")
    groups = lax.axis_size("expert")
    width, dense_width = dense.shape
    bits = count.bit_length() - 1
    quarter = width // count // 4
    parts = 6
    tiles = dense_width // LANES
    bounds = [LANES * (tiles * i // parts) for i in range(parts + 1)]
    spans = [slice(a, b) for a, b in zip(bounds[:-1], bounds[1:])]
    last = tuple(range(1, bits))
    orders = [((bits, 0) if part % 2 == 0 else (0, bits)) + last for part in range(parts)]
    half = (2,) * bits + (2, quarter, dense_width)
    rows = olds[0].shape[0] + olds[1].shape[0]
    piece = dense_columns.shape[2]
    vmem = pl.BlockSpec(memory_space=pltpu.VMEM)
    stat_tiles = (count, 8, width // 2)
    dense_tiles = (count, 8, piece)
    copies = parts * (bits + 4) + 4 * (count - 1) + groups - 1 + 4
    shape = lambda *s: jax.ShapeDtypeStruct(s, jnp.float32)
    low = lambda *s: jax.ShapeDtypeStruct(s, jnp.bfloat16)
    held = lambda *s: pltpu.VMEM(s, jnp.bfloat16)
    outs = (
        low(2, 2, quarter, dense_width),
        low(4, rows, width),
        low(*mixes[0].shape[1:]),
        shape(*stat_tiles),
        shape(8, LANES),
        shape(LANES, LANES),
        shape(LANES, LANES),
        shape(*dense_tiles),
        shape(width // count, LANES),
    )
    args = (
        dense.reshape((2,) * bits + (2, 2, quarter, dense_width)),
        *owns, *gots, *settling, *mixes, *olds, *all_rows, *all_columns, dense_old, dense_columns,
    )
    own, *rest = pl.pallas_call(
        functools.partial(finish_kernel, count, groups, 4, orders, spans),
        out_shape=outs,
        in_specs=[pl.BlockSpec(memory_space=pl.ANY)] + [vmem] * (len(args) - 1),
        out_specs=[vmem] * len(outs),
        scratch_shapes=[held(*half), held(*half)]
        + [held(*((2,) * (bits - step)), quarter, dense_width) for step in range(bits + 1)]
        + [
            held(*half),
            pltpu.SemaphoreType.DMA,
            held(2, rows, width),
            held(2, rows, width),
            held(2, rows, width),
            held(2, rows, width),
            held(*mixes[0].shape[1:]),
            pltpu.VMEM(stat_tiles, jnp.float32),
            pltpu.VMEM(stat_tiles, jnp.float32),
            pltpu.VMEM(dense_tiles, jnp.float32),
            pltpu.VMEM(dense_tiles, jnp.float32),
            pltpu.VMEM((groups, 8, LANES), jnp.float32),
            pltpu.SemaphoreType.DMA((copies,)),
            pltpu.SemaphoreType.DMA((copies,)),
        ],
        compiler_params=pltpu.CompilerParams(
            collective_id=label, has_side_effects=True, vmem_limit_bytes=VM
        ),
        cost_estimate=lasts(75),
        name="finish",
    )(*args)
    return own.reshape(width // count, dense_width), *rest


def update_kernel(counts, half, early, s_ref, *refs):
    owns, gots = refs[:early], refs[early : 2 * early]
    (dense_ref, ends_ref, pair_mix_ref, tiles_ref, sums_ref, up_new_ref, down_new_ref, dense_tiles_ref, dense_new_ref,
     dense_rows_ref, middle_ref, near_mix_ref, got_mix_ref, up_w_ref, down_w_ref, qkv_w_ref, out_w_ref,
     block_ref, up_out_ref, down_out_ref, up_rows_ref, down_rows_ref, up_cols_ref, down_cols_ref,
     qkv_out_ref, out_out_ref, qkv_cols_ref, out_cols_ref, qkv_rows_ref, out_rows_ref, gains_ref, moments_ref,
     rms_ref) = refs[2 * early :]
    block_ref[...] = middle_ref[...] + (
        near_mix_ref[0].astype(jnp.float32)
        + got_mix_ref[0].astype(jnp.float32)
        + pair_mix_ref[...].astype(jnp.float32)
    )
    late = half - early
    own_up = up_out_ref.shape[1]
    own_down = down_out_ref.shape[1]
    wide = tiles_ref.shape[2]
    pair_bit = s_ref[0]
    count = dense_tiles_ref.shape[0]
    dense_sums = dense_tiles_ref[0, :, 0:1]
    for a in range(1, count):
        dense_sums = dense_sums + dense_tiles_ref[a, :, 0:1]
    width = dense_rows_ref.shape[1]
    qkv_columns = qkv_out_ref.shape[1]
    row_means = []
    squares = [dense_tiles_ref[0, 5:6, 0:1]]
    for at, columns in enumerate((qkv_columns, width)):
        row_means.append(
            decayed(
                jnp.mean(dense_rows_ref[at : at + 1, :], axis=1, keepdims=True),
                dense_sums[3 + at : 4 + at] / (width * columns),
            )
        )
        squares.append(row_means[-1] * dense_sums[1 + at : 2 + at])
    squares += [sums_ref[5:6, 0:1], sums_ref[7:8, 0:1]]
    roots = [jnp.sqrt(square / number) for square, number in zip(squares, counts)]
    factors = [LEARN_RATE / jnp.maximum(1.0, root / CLIP_LEVEL) for root in roots]
    rms_ref[...] = jnp.concatenate(
        [jnp.broadcast_to(root, (1, LANES)) for root in roots] + [jnp.zeros((3, LANES), jnp.float32)], axis=0
    )

    up_table = up_new_ref[...]
    down_table = down_new_ref[...]
    lane = lax.broadcasted_iota(jnp.int32, up_table.shape, 1)

    def expert(ref, at):
        tile = tiles_ref[at]
        for kind, (table, weight_ref, out_ref, first, rows) in enumerate(
            (
                (up_table, up_w_ref, up_out_ref, 0, own_up),
                (down_table, down_w_ref, down_out_ref, own_up, own_down),
            )
        ):
            row_mean = tile[4 + 2 * kind : 5 + 2 * kind, 0:1]
            column = jnp.sum(jnp.where(lane == at, table, 0.0), axis=1, keepdims=True)[:rows]
            scale = factors[3 + kind] * lax.rsqrt(column / row_mean)
            for h in range(2):
                span = slice(h * wide, (h + 1) * wide)
                columns = lax.rsqrt(tile[2 * kind + h : 2 * kind + h + 1, :])
                out_ref[at, :, span] = (
                    weight_ref[at, :, span].astype(jnp.float32)
                    - ref[first : first + rows, span].astype(jnp.float32) * scale * columns
                )

    own_at, got_at = pair_bit * half, (1 - pair_bit) * half
    for j in range(early):
        expert(owns[j], own_at + j)
        expert(gots[j], got_at + j)
    for j in range(late):
        expert(ends_ref.at[j], own_at + early + j)
        expert(ends_ref.at[late + j], got_at + early + j)
    up_rows_ref[...] = up_table.T[: up_rows_ref.shape[0], :own_up]
    down_rows_ref[...] = down_table.T[: down_rows_ref.shape[0], :own_down]
    for a in range(up_cols_ref.shape[0]):
        for h in range(2):
            span = slice(h * wide, (h + 1) * wide)
            up_cols_ref[a : a + 1, span] = tiles_ref[a, h : h + 1, :]
            down_cols_ref[a : a + 1, span] = tiles_ref[a, 2 + h : 3 + h, :]

    table = dense_new_ref[...]
    scales = [
        factors[1 + at] * lax.rsqrt(table[:, at : at + 1] / row_means[at]) for at in range(2)
    ]
    piece = dense_tiles_ref.shape[2]
    for first in range(0, qkv_columns + width, LANES):
        at = 0 if first < qkv_columns else 1
        weight_ref, out_ref, cols_ref = (
            (qkv_w_ref, qkv_out_ref, qkv_cols_ref) if at == 0 else (out_w_ref, out_out_ref, out_cols_ref)
        )
        here = slice(first - at * qkv_columns, first - at * qkv_columns + LANES)
        within = first % piece
        columns = dense_tiles_ref[first // piece, 0:1, within : within + LANES]
        cols_ref[:, here] = columns
        out_ref[:, here] = weight_ref[:, here].astype(jnp.float32) - dense_ref[
            :, first : first + LANES
        ].astype(jnp.float32) * scales[at] * lax.rsqrt(columns)
    turned = table.T
    qkv_rows_ref[...] = turned[0:1]
    out_rows_ref[...] = turned[1:2]
    gains_ref[...] = -factors[0] * turned[2:4]
    moments_ref[...] = turned[4:6]


def update(owns, gots, finished, dense_rows, middle, mixes, up_w, down_w, qkv_w, out_w):
    count = lax.axis_size("dp")
    groups = lax.axis_size("expert")
    me = lax.axis_index("dp")
    experts, width, up_columns = up_w.shape
    ff = down_w.shape[1]
    qkv_columns = qkv_w.shape[1]
    own_up, own_down = width // count, ff // count
    counts = (
        float(2 * width),
        float(width * qkv_columns),
        float(width * width),
        float(groups * experts * width * up_columns),
        float(groups * experts * ff * width),
    )
    ends = finished[1]
    early = len(owns)
    whole = lambda *shape: pl.BlockSpec(shape, lambda g, s: (0,) * len(shape))
    shape = lambda *s: jax.ShapeDtypeStruct(s, jnp.float32)
    rows = own_up + own_down
    outs = [
        shape(*middle.shape),
        shape(experts, own_up, up_columns),
        shape(experts, own_down, width),
        shape(experts, own_up),
        shape(experts, own_down),
        shape(experts, up_columns),
        shape(experts, width),
        shape(own_up, qkv_columns),
        shape(own_up, width),
        shape(1, qkv_columns),
        shape(1, width),
        shape(1, own_up),
        shape(1, own_up),
        shape(2, own_up),
        shape(2, own_up),
        shape(8, LANES),
    ]
    return pl.pallas_call(
        functools.partial(update_kernel, counts, early + ends.shape[0] // 2, early),
        out_shape=outs,
        grid_spec=pltpu.PrefetchScalarGridSpec(
            num_scalar_prefetch=1,
            grid=(1,),
            in_specs=[whole(rows, width)] * (2 * early)
            + [whole(*a.shape) for a in (*finished, dense_rows, middle, *mixes)]
            + [
                pl.BlockSpec((experts, own_up, up_columns), lambda g, s: (0, s[1], 0)),
                pl.BlockSpec((experts, own_down, width), lambda g, s: (0, s[1], 0)),
                pl.BlockSpec((own_up, qkv_columns), lambda g, s: (s[1], 0)),
                pl.BlockSpec((own_up, width), lambda g, s: (s[1], 0)),
            ],
            out_specs=[whole(*o.shape) for o in outs],
        ),
        compiler_params=pltpu.CompilerParams(vmem_limit_bytes=VM),
        cost_estimate=lasts(6),
        name="update",
    )(
        jnp.stack([lax.rem(me // PAIR, 2), me]),
        *owns, *gots, *finished, dense_rows, middle, *mixes, up_w, down_w, qkv_w, out_w,
    )


D = 1024
FF = 512
TOP = 8


def swap(values, axis, mask):
    count = lax.axis_size(axis)
    return lax.ppermute(values, axis, [(i, i ^ mask) for i in range(count)])


def swap_pair(values):
    return swap(values, "dp", PAIR)


def swap_chip(values):
    return swap(values, "expert", 2)


def swap_core(values):
    return swap(values, "expert", 1)


def plus(a, b):
    return (a.astype(jnp.float32) + b.astype(jnp.float32)).astype(jnp.bfloat16)


def halve(blocks, axis, mask):
    bit = lax.rem(lax.axis_index(axis) // mask, 2)
    keep = lax.dynamic_index_in_dim(blocks, bit, 1, keepdims=False)
    give = lax.dynamic_index_in_dim(blocks, 1 - bit, 1, keepdims=False)
    return keep, swap(give, axis, mask)


def reduce_dense_far(blocks):
    count = lax.axis_size("dp")
    width, columns = blocks.shape
    rows = width // count
    blocks = blocks.reshape(count, 2, 2, rows // 4, columns)
    keep, got = halve(jnp.moveaxis(blocks, 2, 1), "expert", 1)
    keep, got = halve(plus(keep, got), "expert", 2)
    blocks = plus(keep, got)
    low = 1
    while low < count:
        keep, got = halve(blocks.reshape((-1, 2, 1) + blocks.shape[1:]), "dp", low)
        blocks = plus(keep, got).reshape((-1,) + blocks.shape[1:])
        low *= 2
    mine = blocks[0]
    chip = lax.axis_index("expert") // 2
    core = lax.rem(lax.axis_index("expert"), 2)
    other = swap_chip(mine)
    both = jnp.where(chip == 0, jnp.stack([mine, other]), jnp.stack([other, mine]))
    across = swap_core(both)
    all_four = jnp.where(core == 0, jnp.stack([both, across], 1), jnp.stack([across, both], 1))
    return all_four.reshape(rows, columns)


def own_share(matrix, along):
    count = lax.axis_size("dp")
    width = matrix.shape[along] // count
    return lax.dynamic_slice_in_dim(matrix, lax.axis_index("dp") * width, width, along)


def factored(part, rows_old):
    square = part * part
    rows_new = decayed(rows_old, jnp.mean(square + EPS_STAT, axis=-1))
    return (
        rows_new,
        jnp.sum(square + EPS_STAT, axis=-2),
        jnp.sum(square / rows_new[..., None], axis=-2),
    )


def per_device(
    hidden_in,
    out_grad,
    segment_ids,
    parent_ids,
    positions,
    expert_ids,
    gate_weights,
    norm_gains,
    qkv_weight,
    out_weight,
    gate_up_weight,
    down_weight,
    gain_moment,
    qkv_rows,
    qkv_cols,
    out_rows,
    out_cols,
    gateup_rows,
    gateup_cols,
    down_rows,
    down_cols,
):
    rows_here = hidden_in.shape[0]
    dp_count = lax.axis_size("dp")
    groups = lax.axis_size("expert")
    experts_here = gate_up_weight.shape[0]
    total_experts = experts_here * groups
    capacity = 3 * rows_here * TOP // (2 * total_experts)
    half_experts = experts_here // 2
    dp_index = lax.axis_index("dp")
    pair_bit = lax.rem(dp_index // PAIR, 2)
    first_local = pair_bit * half_experts
    first_expert = lax.axis_index("expert") * experts_here + first_local

    weight_high = gate_weights.astype(jnp.bfloat16)
    weight_low = (gate_weights - weight_high.astype(jnp.float32)).astype(jnp.bfloat16)
    routing = jnp.concatenate([expert_ids.astype(jnp.bfloat16), weight_high, weight_low], axis=1).T
    routing = jnp.pad(routing, ((0, ROUTE_ROWS - routing.shape[0]), (0, D - rows_here)))
    grad_rows = jnp.concatenate([out_grad.astype(jnp.bfloat16), routing], axis=0)
    chip_grad_rows = swap_chip(grad_rows)
    pair_grad_rows = swap_pair(grad_rows)
    ids = jnp.stack([segment_ids, parent_ids, positions])
    normed, qkv, attended, lse, middle, normed_ffn = attend(
        hidden_in, ids, norm_gains, qkv_weight, out_weight
    )
    received, arrived, scale, code = gather_and_select(
        normed_ffn, grad_rows, chip_grad_rows, pair_grad_rows, capacity, experts_here, half_experts, TOP, 5
    )
    scalars = jnp.stack([first_local, lax.rem(dp_index, 2)])
    experts, chains = [], []

    def advance(j, after, come=None, passed=()):
        masks, stay, go = chains[j]
        come = swap(go, "dp", masks[0]) if come is None else come
        stay, go, *passed = settle(stay, come, masks[1], "%d_%d" % (j, masks[1]), after, passed)
        chains[j] = (masks[1:], stay, go)
        return (stay, *passed) if passed else stay

    masks = [1] + [1 << b for b in range(2, dp_count.bit_length() - 1)] + [PAIR]
    for j in range(half_experts):
        after = [experts[-1][2]] if experts else []
        if j == 3:
            after.append(advance(0, after))
        experts.append(
            run_expert(
                scalars, j, received, arrived, scale, gate_up_weight, down_weight, dp_count, after
            )
        )
        chains.append((masks, experts[j][0], experts[j][1]))
    mine, theirs = combine(code, [e[2] for e in experts], capacity, [])
    steps = [advance(1, [mine])]
    normed_f_grad, near_mix, far_mix, come = return_sums(
        code, mine, theirs, [e[3] for e in experts], capacity, chains[1][2], chains[1][0][0], 6, steps
    )
    steps = [normed_f_grad]
    steps.append(advance(0, steps))
    stay, far_mix = advance(2, steps[-1:], None, [far_mix])
    steps.append(stay)
    steps.append(advance(1, steps[-1:], come))
    input_grad, dense = attend_back(
        hidden_in, out_grad, middle, normed_f_grad, normed, qkv, attended, lse, ids, norm_gains, qkv_weight,
        out_weight, steps
    )
    got_mix = swap_chip(far_mix)
    qkv_columns = qkv_weight.shape[1]
    fast_tail = dp_count == experts_here and D // dp_count % 64 == 0
    if fast_tail:
        spare = ((0, 0), (0, LANES - experts_here))
        owns = [chains[j][1][0] for j in (0, 1)]
        gots = [swap_pair(chains[j][2][0]) for j in (0, 1)]
        settling = []
        for j in (2, 3):
            masks, stay, go = chains[j]
            settling += [stay, swap(go, "dp", masks[0])]
        settling[2:] = [x.reshape((2, 2) + x.shape[1:]) for x in settling[2:]]
        dense_rows = jnp.stack([qkv_rows, out_rows])
        dense_old = jnp.pad(
            jnp.concatenate([own_share(dense_rows, 1), own_share(gain_moment, 1)], axis=0).T,
            ((0, 0), (0, LANES - 4)),
        )
        finished = finish(
            dense,
            owns,
            gots,
            settling,
            (near_mix, got_mix),
            [jnp.pad(own_share(old, 1).T, spare) for old in (gateup_rows, down_rows)],
            (gateup_rows, down_rows),
            (gateup_cols, down_cols),
            dense_old,
            jnp.concatenate([qkv_cols, out_cols]).reshape(dp_count, 1, -1),
            1,
        )
        (
            block_out,
            gate_up_new,
            down_new,
            gateup_rows_new,
            down_rows_new,
            gateup_cols_new,
            down_cols_new,
            qkv_new,
            out_new,
            qkv_cols_new,
            out_cols_new,
            qkv_rows_new,
            out_rows_new,
            gains_update,
            gain_moment_new,
            roots,
        ) = update(
            owns,
            gots,
            finished,
            dense_rows,
            middle,
            (near_mix, got_mix),
            gate_up_weight,
            down_weight,
            qkv_weight,
            out_weight,
        )
        qkv_cols_new, out_cols_new = qkv_cols_new[0], out_cols_new[0]
        qkv_rows_new, out_rows_new = qkv_rows_new[0], out_rows_new[0]
        update_rms = roots[:5, 0]
    else:
        for_pair = settle_mix(near_mix, got_mix, [input_grad])
        mix_parts = (near_mix[0], got_mix[0], swap_pair(for_pair))
        block_out = middle + sum(part.astype(jnp.float32) for part in mix_parts)
        dense_own = reduce_dense_far(dense)
        for j in range(half_experts):
            while len(chains[j][0]) > 1:
                advance(j, [dense_own])
        own_parts = [c[1][0] for c in chains]
        other_parts = [swap_pair(c[2][0]) for c in chains]
        own = jnp.stack(own_parts).astype(jnp.float32)
        other = jnp.stack(other_parts).astype(jnp.float32)
        parts = jnp.where(pair_bit == 0, jnp.concatenate([own, other]), jnp.concatenate([other, own]))
        gateup_part = parts[:, : D // dp_count]
        down_part = parts[:, D // dp_count :]
        gateup_rows_new, gateup_square, gateup_scaled = factored(gateup_part, own_share(gateup_rows, 1))
        down_rows_new, down_square, down_scaled = factored(down_part, own_share(down_rows, 1))
        sizes = [gateup_square.size, gateup_scaled.size, down_square.size, down_scaled.size]
        summed = total_over(
            jnp.concatenate(
                [
                    gateup_square.reshape(-1),
                    gateup_scaled.reshape(-1),
                    down_square.reshape(-1),
                    down_scaled.reshape(-1),
                    jnp.sum(gateup_rows_new, axis=1),
                    jnp.sum(down_rows_new, axis=1),
                ]
            ),
            "dp",
            1,
        )
        pieces = jnp.split(summed, [sum(sizes[: i + 1]) for i in range(4)])
        gateup_square, gateup_scaled, down_square, down_scaled = [
            p.reshape(experts_here, D) for p in pieces[:4]
        ]
        gateup_row_mean = pieces[4][:experts_here] / D
        down_row_mean = pieces[4][experts_here:] / FF
        gateup_cols_new = decayed(gateup_cols, gateup_square / D)
        down_cols_new = decayed(down_cols, down_square / FF)
        expert_squares = jnp.stack(
            [
                jnp.sum(gateup_row_mean * jnp.sum(gateup_scaled / gateup_cols_new, axis=1)),
                jnp.sum(down_row_mean * jnp.sum(down_scaled / down_cols_new, axis=1)),
            ]
        )
        spread_squares = collect(
            jnp.zeros((8, 128), jnp.float32).at[0, :2].set(expert_squares), "expert", 2
        )
        expert_squares = jnp.sum(spread_squares[:, 0, :2], axis=0)
        dense_own = dense_own.astype(jnp.float32)
        qkv_own = dense_own[:, :qkv_columns]
        out_own = dense_own[:, qkv_columns : qkv_columns + D]
        gains_own = dense_own[:, qkv_columns + D : qkv_columns + D + 2].T
        gain_moment_new = decayed(own_share(gain_moment, 1), gains_own * gains_own + EPS_STAT)
        gains_step = gains_own * lax.rsqrt(gain_moment_new)
        qkv_rows_new, qkv_square, qkv_scaled = factored(qkv_own, own_share(qkv_rows, 0))
        out_rows_new, out_square, out_scaled = factored(out_own, own_share(out_rows, 0))
        dense_sums = total_over(
            jnp.concatenate(
                [
                    qkv_square,
                    qkv_scaled,
                    out_square,
                    out_scaled,
                    jnp.stack(
                        [jnp.sum(qkv_rows_new), jnp.sum(out_rows_new), jnp.sum(gains_step * gains_step)]
                    ),
                ]
            ),
            "dp",
            4,
        )
        qkv_square, qkv_scaled, out_square, out_scaled, rest = jnp.split(
            dense_sums, [qkv_columns, 2 * qkv_columns, 2 * qkv_columns + D, 2 * qkv_columns + 2 * D]
        )
        qkv_row_mean = rest[0] / D
        out_row_mean = rest[1] / D
        qkv_cols_new = decayed(qkv_cols, qkv_square / D)
        out_cols_new = decayed(out_cols, out_square / D)
        squares = jnp.concatenate(
            [
                jnp.stack(
                    [
                        rest[2],
                        qkv_row_mean * jnp.sum(qkv_scaled / qkv_cols_new),
                        out_row_mean * jnp.sum(out_scaled / out_cols_new),
                    ]
                ),
                expert_squares,
            ]
        )
        element_counts = jnp.array(
            [2 * D, D * qkv_columns, D * D, total_experts * D * 2 * FF, total_experts * FF * D], jnp.float32
        )
        update_rms = jnp.sqrt(squares / element_counts)
        factors = LEARN_RATE / jnp.maximum(1.0, update_rms / CLIP_LEVEL)

        def stepped(weight, part, rows_new, row_mean, cols_new, factor):
            return weight.astype(jnp.float32) - part * (
                factor * lax.rsqrt(rows_new / row_mean[..., None])
            )[..., :, None] * lax.rsqrt(cols_new)[..., None, :]

        gains_update = -factors[0] * gains_step
        qkv_new = stepped(own_share(qkv_weight, 0), qkv_own, qkv_rows_new, qkv_row_mean, qkv_cols_new, factors[1])
        out_new = stepped(own_share(out_weight, 0), out_own, out_rows_new, out_row_mean, out_cols_new, factors[2])
        gate_up_new = stepped(
            own_share(gate_up_weight, 1), gateup_part, gateup_rows_new, gateup_row_mean, gateup_cols_new, factors[3]
        )
        down_new = stepped(
            own_share(down_weight, 1), down_part, down_rows_new, down_row_mean, down_cols_new, factors[4]
        )
    return (
        block_out,
        input_grad,
        update_rms,
        gains_update,
        gain_moment_new,
        qkv_new,
        qkv_rows_new,
        qkv_cols_new,
        out_new,
        out_rows_new,
        out_cols_new,
        gate_up_new,
        gateup_rows_new,
        gateup_cols_new,
        down_new,
        down_rows_new,
        down_cols_new,
    )


def solution(mesh):
    placed = (
        P(("dp", "expert"), None),
        P(("dp", "expert"), None),
        P(("dp", "expert")),
        P(("dp", "expert")),
        P(("dp", "expert")),
        P(("dp", "expert"), None),
        P(("dp", "expert"), None),
        P(),
        P(),
        P(),
        P("expert", None, None),
        P("expert", None, None),
        P(),
        P(),
        P(),
        P(),
        P(),
        P("expert", None),
        P("expert", None),
        P("expert", None),
        P("expert", None),
    )
    return jax.shard_map(
        per_device,
        mesh=mesh,
        in_specs=placed,
        out_specs=(
            P(("dp", "expert"), None),
            P(("dp", "expert"), None),
            P(),
            P(None, "dp"),
            P(None, "dp"),
            P("dp", None),
            P("dp"),
            P(),
            P("dp", None),
            P("dp"),
            P(),
            P("expert", "dp", None),
            P("expert", "dp"),
            P("expert", None),
            P("expert", "dp", None),
            P("expert", "dp"),
            P("expert", None),
        ),
        check_vma=False,
    )
```

```python
import functools
import math

import jax
import jax.numpy as jnp
from jax import lax
from jax.experimental import pallas as pl
from jax.experimental.pallas import tpu as pltpu
from jax.sharding import PartitionSpec as P

VM = 60 * 1024 * 1024
SCALE = 1e6


def lasts(microseconds):
    return pl.CostEstimate(
        flops=int(microseconds * SCALE), bytes_accessed=1024, transcendentals=0
    )


def dot(a, b, ca=1, cb=0):
    return lax.dot_general(a, b, (((ca,), (cb,)), ((), ())), preferred_element_type=jnp.float32)


def one_hot(code, capacity):
    count, rows = code.shape
    place = lax.broadcasted_iota(jnp.int32, (capacity, rows), 0).astype(jnp.float32)
    return [place == code[j : j + 1, :] for j in range(count)]


def expert_kernel(j, owners, tiles, waits, s_ref, rec_hbm, arr_hbm, scale_ref, up_hbm, down_hbm, *refs):
    (keep_hbm, give_hbm, back_hbm, mix_hbm,
     rec_s, arr_s, up_s, down_s, act_s, gug_s, wg_s, wd_s, parts_s, out_s, in_sem, out_sem) = refs[waits:]
    rows, ff = act_s.shape
    width = up_s.shape[0]
    sources, capacity = rec_s.shape[0], rec_s.shape[1]
    tile = rows // tiles
    per = sources // tiles

    def load(src, dst, at):
        copy = pltpu.make_async_copy(src, dst, in_sem.at[at])
        copy.start()
        return copy

    def load_rows(hbm, held, t, at):
        span = slice(t * per, (t + 1) * per)
        return load(hbm.at[j, span], held.at[span], at)

    expert = s_ref[0] + j
    rec_in = [load_rows(rec_hbm, rec_s, 0, 0)]
    up_in = load(up_hbm.at[expert], up_s, 2 * tiles)
    arr_in = [load_rows(arr_hbm, arr_s, 0, tiles)]
    down_in = load(down_hbm.at[expert], down_s, 2 * tiles + 1)
    for t in range(1, tiles):
        rec_in.append(load_rows(rec_hbm, rec_s, t, t))
        arr_in.append(load_rows(arr_hbm, arr_s, t, tiles + t))
    def products(t):
        span = slice(t * per, (t + 1) * per)
        return (
            dot(rec_s[span].reshape(tile, width), up_s[...]),
            dot(arr_s[span].reshape(tile, width), down_s[...], 1, 1),
        )

    for copy in (up_in, down_in, rec_in[0], arr_in[0]):
        copy.wait()
    following = products(0)
    for t in range(tiles):
        at = slice(t * tile, (t + 1) * tile)
        gate_up, act_grad = following
        if t + 1 < tiles:
            rec_in[t + 1].wait()
            arr_in[t + 1].wait()
            following = products(t + 1)
        gate = gate_up[:, :ff]
        up = gate_up[:, ff:]
        sig = 1.0 / (1.0 + jnp.exp(-gate))
        silu = gate * sig
        act_s[at, :] = (silu * up).astype(jnp.bfloat16)
        gug_s[at, :ff] = (act_grad * up * sig * (1.0 + gate * (1.0 - sig))).astype(jnp.bfloat16)
        gug_s[at, ff:] = (act_grad * silu).astype(jnp.bfloat16)
    wg_s[...] = dot(rec_s[...].reshape(rows, width), gug_s[...], 0, 0)
    wd_s[...] = dot(act_s[...], arr_s[...].reshape(rows, width), 0, 0)
    bit = s_ref[1]
    up_rows = width // owners
    down_rows = ff // owners
    leaving = []
    for k, (hbm, side) in enumerate(((give_hbm, 1 - bit), (keep_hbm, bit))):
        for slot in range(owners // 2):
            owner = 2 * slot + side
            parts_s[k, slot, :up_rows, :] = wg_s[
                pl.ds(pl.multiple_of(owner * up_rows, up_rows), up_rows), :
            ].astype(jnp.bfloat16)
            parts_s[k, slot, up_rows:, :] = wd_s[
                pl.ds(pl.multiple_of(owner * down_rows, down_rows), down_rows), :
            ].astype(jnp.bfloat16)
        copy = pltpu.make_async_copy(parts_s.at[k], hbm, out_sem.at[k])
        copy.start()
        leaving.append(copy)
    for t in range(tiles):
        at = slice(t * tile, (t + 1) * tile)
        out_s[0, at] = dot(gug_s[at, :], up_s[...], 1, 1).astype(jnp.bfloat16)
        scale = scale_ref[0, t * per : (t + 1) * per].reshape(tile, 1)
        out_s[1, at] = (dot(act_s[at, :], down_s[...]) * scale).astype(jnp.bfloat16)
        for k, hbm in enumerate((back_hbm, mix_hbm)):
            copy = pltpu.make_async_copy(out_s.at[k, at], hbm.at[at], out_sem.at[2 + 2 * t + k])
            copy.start()
            leaving.append(copy)
    for copy in leaving:
        copy.wait()


def run_expert(scalars, j, received, arrived, scale, up_w, down_w, owners, after=()):
    count, sources, capacity, width = received.shape
    ff = down_w.shape[1]
    rows = sources * capacity
    tiles = 2
    share = (owners // 2, (width + ff) // owners, width)
    slots = jax.ShapeDtypeStruct((rows, width), jnp.bfloat16)
    parts = jax.ShapeDtypeStruct(share, jnp.bfloat16)
    anywhere = pl.BlockSpec(memory_space=pl.ANY)
    return pl.pallas_call(
        functools.partial(expert_kernel, j, owners, tiles, len(after)),
        out_shape=(parts, parts, slots, slots),
        grid_spec=pltpu.PrefetchScalarGridSpec(
            num_scalar_prefetch=1,
            grid=(1,),
            in_specs=[
                anywhere,
                anywhere,
                pl.BlockSpec((1, sources, capacity, 1), lambda g, s: (j, 0, 0, 0)),
                anywhere,
                anywhere,
            ]
            + [anywhere] * len(after),
            out_specs=[anywhere] * 4,
            scratch_shapes=[
                pltpu.VMEM((sources, capacity, width), jnp.bfloat16),
                pltpu.VMEM((sources, capacity, width), jnp.bfloat16),
                pltpu.VMEM((width, 2 * ff), jnp.bfloat16),
                pltpu.VMEM((ff, width), jnp.bfloat16),
                pltpu.VMEM((rows, ff), jnp.bfloat16),
                pltpu.VMEM((rows, 2 * ff), jnp.bfloat16),
                pltpu.VMEM((width, 2 * ff), jnp.float32),
                pltpu.VMEM((ff, width), jnp.float32),
                pltpu.VMEM((2,) + share, jnp.bfloat16),
                pltpu.VMEM((2, rows, width), jnp.bfloat16),
                pltpu.SemaphoreType.DMA((2 * tiles + 2,)),
                pltpu.SemaphoreType.DMA((2 + 2 * tiles,)),
            ],
        ),
        compiler_params=pltpu.CompilerParams(vmem_limit_bytes=VM),
        cost_estimate=lasts(18),
        name="expert_%d" % j,
    )(scalars, received, arrived, scale, up_w, down_w, *after)


HEADS = 16
KV_HEADS = 8
HEAD_DIM = 64
EPS_NORM = 1e-06
ROPE_BASE = 10000.0
MASKED = -1e30
LANES = 128


def spread(row):
    rows = row.shape[1]
    by_column = jnp.broadcast_to(row.astype(jnp.float32), (rows, rows))
    return by_column, by_column.T


def mask_and_angles(ids_ref):
    seg_k, seg_q = spread(ids_ref[0:1, :])
    par_k, par_q = spread(ids_ref[1:2, :])
    pos_k, pos_q = spread(ids_ref[2:3, :])
    seen = ((seg_k == seg_q) | (seg_k == par_q) | (seg_k == par_k)) & (pos_k <= pos_q)
    bias = jnp.where(seen, 0.0, MASKED)
    lane = lax.broadcasted_iota(jnp.int32, (seg_k.shape[0], LANES), 1)
    half = HEAD_DIM // 2
    place = lax.rem(lane, half).astype(jnp.float32)
    frequency = jnp.exp(place * (-2.0 * math.log(ROPE_BASE) / HEAD_DIM))
    angles = pos_q[:, :LANES] * frequency
    front = lax.rem(lane, HEAD_DIM) < half
    sine = jnp.sin(angles)
    return bias, jnp.cos(angles), jnp.where(front, -sine, sine), front, lane


def turned(block, cosine, sine, front):
    other = jnp.where(
        front,
        pltpu.roll(block, LANES - HEAD_DIM // 2, 1),
        pltpu.roll(block, HEAD_DIM // 2, 1),
    )
    return block * cosine + other * sine


def two_diagonal(pair, which, lane):
    rolled = pltpu.roll(pair, HEAD_DIM, 1)
    first, last = (pair, rolled) if which == 0 else (rolled, pair)
    low = lane < HEAD_DIM
    return jnp.concatenate(
        [jnp.where(low, first, 0.0), jnp.where(low, 0.0, last)], axis=0
    ).astype(jnp.bfloat16)


def column_block(index):
    return pl.ds(pl.multiple_of(index * LANES, LANES), LANES)


def attend_kernel(hidden_ref, ids_ref, gains_ref, qkv_w_hbm, out_w_hbm,
                  normed_hbm, qkv_hbm, attended_hbm, lse_ref, middle_ref, normed_f_ref,
                  normed_ref, qkv_ref, attended_ref, qkv_w_ref, out_w_ref, proj_s, bias_s, sem):
    moving = [
        pltpu.make_async_copy(src, dst, sem.at[i])
        for i, (src, dst) in enumerate(
            (
                (qkv_w_hbm, qkv_w_ref),
                (out_w_hbm, out_w_ref),
                (normed_ref, normed_hbm),
                (qkv_ref, qkv_hbm),
                (attended_ref, attended_hbm),
            )
        )
    ]
    moving[0].start()
    moving[1].start()
    rows = hidden_ref.shape[0]
    att = HEADS * HEAD_DIM
    kv = KV_HEADS * HEAD_DIM
    hidden = hidden_ref[...]
    gains = gains_ref[...].astype(jnp.float32)
    inverse = lax.rsqrt(jnp.mean(hidden * hidden, axis=-1, keepdims=True) + EPS_NORM)
    normed_ref[...] = (hidden * inverse * gains[0:1, :]).astype(jnp.bfloat16)
    moving[2].start()
    bias, cosine, sine, front, lane = mask_and_angles(ids_ref)
    bias_s[...] = bias
    moving[0].wait()
    proj_s[...] = dot(normed_ref[...], qkv_w_ref[...])
    lse_ref[...] = jnp.zeros_like(lse_ref)

    def pair_step(p, carry):
        key_at = column_block(att // LANES + p)
        value_at = column_block((att + kv) // LANES + p)
        keys = turned(proj_s[:, key_at], cosine, sine, front).astype(jnp.bfloat16)
        values = proj_s[:, value_at].astype(jnp.bfloat16)
        qkv_ref[:, key_at] = keys
        qkv_ref[:, value_at] = values
        keys = keys.astype(jnp.float32)
        values = values.astype(jnp.float32)
        for which in range(2):
            query_at = column_block(2 * p + which)
            queries = turned(proj_s[:, query_at], cosine, sine, front).astype(jnp.bfloat16)
            queries = (queries.astype(jnp.float32) * HEAD_DIM**-0.5).astype(jnp.bfloat16)
            qkv_ref[:, query_at] = queries
            scores = dot(queries, two_diagonal(keys, which, lane), 1, 1)
            probs = []
            for head in range(2):
                part = scores[:, head * rows : (head + 1) * rows] + bias_s[...]
                top = jnp.max(part, axis=-1, keepdims=True)
                part = jnp.exp(part - top)
                total = jnp.sum(part, axis=-1, keepdims=True)
                probs.append((part * (1.0 / total)).astype(jnp.bfloat16))
                at = 4 * p + 2 * which + head
                lse_ref[...] = jnp.where(lane == at, top + jnp.log(total), lse_ref[...])
            attended_ref[:, query_at] = dot(
                jnp.concatenate(probs, axis=1), two_diagonal(values, which, lane)
            ).astype(jnp.bfloat16)
        return carry

    lax.fori_loop(0, KV_HEADS // 2, pair_step, 0, unroll=True)
    moving[3].start()
    moving[4].start()
    moving[1].wait()
    middle = hidden + dot(attended_ref[...], out_w_ref[...])
    middle_ref[...] = middle
    inverse_f = lax.rsqrt(jnp.mean(middle * middle, axis=-1, keepdims=True) + EPS_NORM)
    normed_f_ref[...] = (middle * inverse_f * gains[1:2, :]).astype(jnp.bfloat16)
    for copy in moving[2:]:
        copy.wait()


def attend(hidden, ids, gains, qkv_w, out_w):
    rows, width = hidden.shape
    shape = jax.ShapeDtypeStruct
    return pl.pallas_call(
        attend_kernel,
        out_shape=(
            shape((rows, width), jnp.bfloat16),
            shape((rows, qkv_w.shape[1]), jnp.bfloat16),
            shape((rows, out_w.shape[0]), jnp.bfloat16),
            shape((rows, LANES), jnp.float32),
            shape((rows, width), jnp.float32),
            shape((rows, width), jnp.bfloat16),
        ),
        in_specs=[pl.BlockSpec(memory_space=pltpu.VMEM)] * 3 + [pl.BlockSpec(memory_space=pl.ANY)] * 2,
        out_specs=[pl.BlockSpec(memory_space=pl.ANY)] * 3 + [pl.BlockSpec(memory_space=pltpu.VMEM)] * 3,
        scratch_shapes=[
            pltpu.VMEM((rows, width), jnp.bfloat16),
            pltpu.VMEM((rows, qkv_w.shape[1]), jnp.bfloat16),
            pltpu.VMEM((rows, out_w.shape[0]), jnp.bfloat16),
            pltpu.VMEM(qkv_w.shape, jnp.bfloat16),
            pltpu.VMEM(out_w.shape, jnp.bfloat16),
            pltpu.VMEM((rows, qkv_w.shape[1]), jnp.float32),
            pltpu.VMEM((rows, rows), jnp.float32),
            pltpu.SemaphoreType.DMA((5,)),
        ],
        compiler_params=pltpu.CompilerParams(vmem_limit_bytes=VM),
        cost_estimate=lasts(18),
        name="attend",
    )(hidden, ids, gains, qkv_w, out_w)


def attend_back_kernel(waits, grad_ref, middle_ref, normed_grad_ref, lse_ref, ids_ref, gains_ref,
                       hidden_hbm, normed_hbm, qkv_hbm, attended_hbm, qkv_w_hbm, out_w_hbm, *refs):
    (input_grad_ref, dense_hbm, dense_ref, hidden_ref, normed_ref, qkv_ref, attended_ref, qkv_w_ref, out_w_ref,
     proj_s, bias_s, back_s, sem) = refs[waits:]
    rows, width = hidden_ref.shape
    incoming = {
        name: pltpu.make_async_copy(src, dst, sem.at[i])
        for i, (name, src, dst) in enumerate(
            (
                ("attended", attended_hbm, attended_ref),
                ("out_w", out_w_hbm, out_w_ref),
                ("qkv", qkv_hbm, qkv_ref),
                ("normed", normed_hbm, normed_ref),
                ("qkv_w", qkv_w_hbm, qkv_w_ref),
                ("hidden", hidden_hbm, hidden_ref),
            )
        )
    }
    for copy in incoming.values():
        copy.start()
    leaving = []

    def leave(span):
        copy = pltpu.make_async_copy(dense_ref.at[:, span], dense_hbm.at[:, span], sem.at[6 + len(leaving)])
        copy.start()
        leaving.append(copy)

    att = HEADS * HEAD_DIM
    kv = KV_HEADS * HEAD_DIM
    gains = gains_ref[...].astype(jnp.float32)
    normed_grad = normed_grad_ref[...]
    middle = middle_ref[...]
    inverse_f = lax.rsqrt(jnp.mean(middle * middle, axis=-1, keepdims=True) + EPS_NORM)
    gain_f = jnp.sum(normed_grad * middle * inverse_f, axis=0, keepdims=True)
    weighted = normed_grad * gains[1:2, :]
    middle_grad = grad_ref[...] + (
        inverse_f * weighted
        - middle * (inverse_f * inverse_f * inverse_f)
        * jnp.mean(weighted * middle, axis=-1, keepdims=True)
    )
    input_grad_ref[...] = middle_grad
    branch = middle_grad.astype(jnp.bfloat16)
    columns = att + 2 * kv
    incoming["attended"].wait()
    dense_ref[:, columns : columns + width] = dot(attended_ref[...], branch, 0, 0).astype(jnp.bfloat16)
    leave(slice(columns, columns + width))
    incoming["out_w"].wait()
    back_s[...] = dot(branch, out_w_ref[...], 1, 1).astype(jnp.bfloat16)
    bias, cosine, sine, front, lane = mask_and_angles(ids_ref)
    bias_s[...] = bias
    low = lane < HEAD_DIM
    incoming["qkv"].wait()

    def pair_step(p, carry):
        key_at = column_block(att // LANES + p)
        value_at = column_block((att + kv) // LANES + p)
        keys = qkv_ref[:, key_at].astype(jnp.float32)
        values = qkv_ref[:, value_at].astype(jnp.float32)
        key_grads = []
        value_grads = []
        for which in range(2):
            query_at = column_block(2 * p + which)
            queries = qkv_ref[:, query_at]
            back = back_s[:, query_at]
            key_two = two_diagonal(keys, which, lane)
            scores = dot(queries, key_two, 1, 1)
            prob_grads = dot(back, two_diagonal(values, which, lane), 1, 1)
            probs = []
            score_grads = []
            for head in range(2):
                at = 4 * p + 2 * which + head
                level = jnp.sum(jnp.where(lane == at, lse_ref[...], 0.0), axis=-1, keepdims=True)
                span = slice(head * rows, (head + 1) * rows)
                prob = jnp.exp(scores[:, span] + bias_s[...] - level)
                prob_grad = prob_grads[:, span]
                row_dot = jnp.sum(prob * prob_grad, axis=-1, keepdims=True)
                probs.append(prob.astype(jnp.bfloat16))
                score_grads.append((prob * (prob_grad - row_dot)).astype(jnp.bfloat16))
            score_grads = jnp.concatenate(score_grads, axis=1)
            query_grad = dot(score_grads, key_two) * HEAD_DIM**-0.5
            proj_s[:, query_at] = turned(query_grad, cosine, -sine, front).astype(jnp.bfloat16)
            for grads, left, right in (
                (key_grads, score_grads, queries),
                (value_grads, jnp.concatenate(probs, axis=1), back),
            ):
                both = dot(left, right, 0, 0)
                first, last = both[:rows], both[rows:]
                if which == 0:
                    grads.append(first + pltpu.roll(last, HEAD_DIM, 1))
                else:
                    grads.append(pltpu.roll(first, HEAD_DIM, 1) + last)
        key_grad = jnp.where(low, key_grads[0], key_grads[1])
        proj_s[:, key_at] = turned(key_grad, cosine, -sine, front).astype(jnp.bfloat16)
        proj_s[:, value_at] = jnp.where(low, value_grads[0], value_grads[1]).astype(jnp.bfloat16)
        return carry

    lax.fori_loop(0, KV_HEADS // 2, pair_step, 0)
    for name in ("normed", "qkv_w", "hidden"):
        incoming[name].wait()
    for first in range(0, columns, columns // 2):
        span = slice(first, first + columns // 2)
        dense_ref[:, span] = dot(normed_ref[...], proj_s[:, span], 0, 0).astype(jnp.bfloat16)
        leave(span)
    normed_grad = dot(proj_s[...], qkv_w_ref[...], 1, 1)
    hidden = hidden_ref[...]
    inverse = lax.rsqrt(jnp.mean(hidden * hidden, axis=-1, keepdims=True) + EPS_NORM)
    gain_a = jnp.sum(normed_grad * hidden * inverse, axis=0, keepdims=True)
    weighted = normed_grad * gains[0:1, :]
    input_grad_ref[...] += inverse * weighted - hidden * (inverse * inverse * inverse) * jnp.mean(
        weighted * hidden, axis=-1, keepdims=True
    )
    both = jnp.concatenate([gain_a, gain_f, jnp.zeros((LANES - 2, width), jnp.float32)], axis=0)
    dense_ref[:, columns + width :] = both.T.astype(jnp.bfloat16)
    leave(slice(columns + width, columns + width + LANES))
    for copy in leaving:
        copy.wait()


def attend_back(hidden, out_grad, middle, normed_f_grad, normed, qkv, attended, lse, ids, gains, qkv_w, out_w, after=()):
    rows, width = hidden.shape
    columns = qkv_w.shape[1] + width + LANES
    return pl.pallas_call(
        functools.partial(attend_back_kernel, len(after)),
        out_shape=(
            jax.ShapeDtypeStruct((rows, width), jnp.float32),
            jax.ShapeDtypeStruct((width, columns), jnp.bfloat16),
        ),
        in_specs=[pl.BlockSpec(memory_space=pltpu.VMEM)] * 6
        + [pl.BlockSpec(memory_space=pl.ANY)] * (6 + len(after)),
        out_specs=[pl.BlockSpec(memory_space=pltpu.VMEM), pl.BlockSpec(memory_space=pl.ANY)],
        scratch_shapes=[
            pltpu.VMEM((width, columns), jnp.bfloat16),
            pltpu.VMEM((rows, width), jnp.float32),
            pltpu.VMEM((rows, width), jnp.bfloat16),
            pltpu.VMEM((rows, qkv_w.shape[1]), jnp.bfloat16),
            pltpu.VMEM((rows, out_w.shape[0]), jnp.bfloat16),
            pltpu.VMEM(qkv_w.shape, jnp.bfloat16),
            pltpu.VMEM(out_w.shape, jnp.bfloat16),
            pltpu.VMEM((rows, qkv_w.shape[1]), jnp.bfloat16),
            pltpu.VMEM((rows, rows), jnp.float32),
            pltpu.VMEM((rows, out_w.shape[0]), jnp.bfloat16),
            pltpu.SemaphoreType.DMA((10,)),
        ],
        compiler_params=pltpu.CompilerParams(vmem_limit_bytes=VM),
        cost_estimate=lasts(26),
        name="attend_back",
    )(out_grad, middle, normed_f_grad, lse, ids, gains, hidden, normed, qkv, attended, qkv_w, out_w, *after)


MESH = pl.DeviceIdType.MESH


def greet(peers):
    barrier = pltpu.get_barrier_semaphore()
    for peer in peers:
        pl.semaphore_signal(barrier, inc=1, device_id=peer, device_id_type=MESH)
    pl.semaphore_wait(barrier, len(peers))


def total_kernel(axis, count, mine_ref, *refs):
    out_ref, got_ref, send_sem, recv_sem = refs[-4:]
    me = lax.axis_index(axis)
    after = [lax.rem(me + k, count) for k in range(count)]
    greet([{axis: after[k]} for k in range(1, count)])
    scatter = [
        pltpu.make_async_remote_copy(
            src_ref=mine_ref.at[after[k]],
            dst_ref=got_ref.at[k],
            send_sem=send_sem.at[0, k],
            recv_sem=recv_sem.at[0, k],
            device_id={axis: after[k]},
            device_id_type=MESH,
        )
        for k in range(1, count)
    ]
    for copy in scatter:
        copy.start()
    total = mine_ref[me]
    for k in range(1, count):
        scatter[k - 1].wait_recv()
        total = total + got_ref[k]
    out_ref[me] = total
    share = [
        pltpu.make_async_remote_copy(
            src_ref=out_ref.at[me],
            dst_ref=out_ref.at[me],
            send_sem=send_sem.at[1, k],
            recv_sem=recv_sem.at[1, k],
            device_id={axis: after[k]},
            device_id_type=MESH,
        )
        for k in range(1, count)
    ]
    for copy in share:
        copy.start()
    for copy in share:
        copy.wait_recv()
    for copy in scatter + share:
        copy.wait_send()


def total_over(values, axis, label, after=()):
    count = lax.axis_size(axis)
    rows = -(-values.shape[0] // (8 * 128 * count)) * 8
    padded = jnp.pad(values, (0, count * rows * 128 - values.shape[0])).reshape(count, rows, 128)
    out = pl.pallas_call(
        functools.partial(total_kernel, axis, count),
        out_shape=jax.ShapeDtypeStruct(padded.shape, jnp.float32),
        in_specs=[pl.BlockSpec(memory_space=pltpu.VMEM)] + [pl.BlockSpec(memory_space=pl.ANY)] * len(after),
        out_specs=pl.BlockSpec(memory_space=pltpu.VMEM),
        scratch_shapes=[
            pltpu.VMEM(padded.shape, jnp.float32),
            pltpu.SemaphoreType.DMA((2, count)),
            pltpu.SemaphoreType.DMA((2, count)),
        ],
        compiler_params=pltpu.CompilerParams(
            collective_id=label, has_side_effects=True, vmem_limit_bytes=16 * 1024 * 1024
        ),
        cost_estimate=lasts(12),
        name="total_%d" % label,
    )(padded, *after)
    return out.reshape(-1)[: values.shape[0]]


def collect_kernel(axis, count, mine_ref, out_ref, send_sem, recv_sem, local_sem):
    me = lax.axis_index(axis)
    after = [lax.rem(me + k, count) for k in range(count)]
    greet([{axis: after[k]} for k in range(1, count)])
    copies = [
        pltpu.make_async_remote_copy(
            src_ref=mine_ref,
            dst_ref=out_ref.at[me],
            send_sem=send_sem.at[k],
            recv_sem=recv_sem.at[k],
            device_id={axis: after[k]},
            device_id_type=MESH,
        )
        for k in range(1, count)
    ]
    for copy in copies:
        copy.start()
    out_ref[me] = mine_ref[...]
    for copy in copies:
        copy.wait()


def collect(values, axis, label):
    count = lax.axis_size(axis)
    return pl.pallas_call(
        functools.partial(collect_kernel, axis, count),
        out_shape=jax.ShapeDtypeStruct((count,) + values.shape, jnp.float32),
        in_specs=[pl.BlockSpec(memory_space=pltpu.VMEM)],
        out_specs=pl.BlockSpec(memory_space=pltpu.VMEM),
        scratch_shapes=[
            pltpu.SemaphoreType.DMA((count,)),
            pltpu.SemaphoreType.DMA((count,)),
            pltpu.SemaphoreType.DMA,
        ],
        compiler_params=pltpu.CompilerParams(
            collective_id=label, has_side_effects=True, vmem_limit_bytes=16 * 1024 * 1024
        ),
        cost_estimate=lasts(4),
        name="collect_%d" % label,
    )(values)


def flipped(axis, mask):
    index = lax.axis_index(axis)
    bit = lax.rem(index // mask, 2)
    return bit, {axis: index + mask - 2 * mask * bit}


PAIR = 2
ROUTE_ROWS = 32


class Pusher:
    def __init__(self, send_sem, recv_sem):
        self.send_sem, self.recv_sem, self.copies = send_sem, recv_sem, []

    def __call__(self, src, dst, peer):
        at = len(self.copies)
        copy = pltpu.make_async_remote_copy(
            src_ref=src,
            dst_ref=dst,
            send_sem=self.send_sem.at[at],
            recv_sem=self.recv_sem.at[at],
            device_id=peer,
            device_id_type=MESH,
        )
        copy.start()
        self.copies.append(copy)
        return copy

    def finish(self):
        for copy in self.copies:
            copy.wait_send()


def picked(code, capacity):
    return jnp.concatenate(
        [c.astype(jnp.float32) for c in one_hot(code, capacity)], axis=0
    ).astype(jnp.bfloat16)


def gather_kernel(capacity, experts_here, half_experts, top, token_ref, grad_ref, chip_grad_ref, pair_grad_ref,
                  rec_ref, arr_ref, scale_ref, code_ref, tokens, grads, weight_s, stage, send_sem, recv_sem, local_sem):
    rows = token_ref.shape[0]
    half = rows // 2
    first = lax.axis_index("expert") * experts_here + lax.rem(lax.axis_index("dp") // PAIR, 2) * half_experts
    _, core = flipped("expert", 1)
    _, chip = flipped("expert", 2)
    _, pair = flipped("dp", PAIR)
    greet([core, chip, pair])
    push = Pusher(send_sem, recv_sem)
    everything, routing = slice(None), slice(rows, rows + ROUTE_ROWS)
    to_chip = push(token_ref, tokens.at[2], chip)
    to_pair = push(token_ref, tokens.at[4], pair)
    route_both = push(pair_grad_ref.at[routing], grads.at[6, routing], chip)
    to_core = push(token_ref, tokens.at[1], core)
    grad_core = push(grad_ref, grads.at[1], core)
    grad_chip_core = push(chip_grad_ref, grads.at[3], core)
    grad_pair_core = push(pair_grad_ref, grads.at[5], core)

    earlier = lax.broadcasted_iota(jnp.int32, (rows, rows), 0)
    later = lax.broadcasted_iota(jnp.int32, (rows, rows), 1)
    before = jnp.where(earlier < later, 1.0, 0.0).astype(jnp.bfloat16)

    def route(r, table):
        table = table.astype(jnp.float32)
        ids = table[:top]
        gates = table[top : 2 * top] + table[2 * top : 3 * top]
        hits = [ids == (first + j).astype(jnp.float32) for j in range(half_experts)]
        named = jnp.concatenate(
            [jnp.max(jnp.where(hit, 1.0, 0.0), axis=0, keepdims=True) for hit in hits], axis=0
        )
        weight_s[r] = jnp.concatenate(
            [jnp.sum(jnp.where(hit, gates, 0.0), axis=0, keepdims=True) for hit in hits], axis=0
        )
        code_ref[r] = jnp.where(named > 0.0, dot(named.astype(jnp.bfloat16), before), -1.0)

    leaving = []

    def select(r, source, out_ref, weighted):
        slot = len(leaving) % stage.shape[0]
        if len(leaving) >= stage.shape[0]:
            leaving[len(leaving) - stage.shape[0]].wait()
        chosen = one_hot(code_ref[r], capacity)
        pick = jnp.concatenate([c.astype(jnp.float32) for c in chosen], axis=0).astype(jnp.bfloat16)
        made = dot(pick, source)
        for j in range(half_experts):
            part = made[j * capacity : (j + 1) * capacity]
            if weighted:
                scale = jnp.sum(
                    jnp.where(chosen[j], weight_s[r, j : j + 1, :], 0.0), axis=1, keepdims=True
                )
                scale_ref[j, r] = scale
                part = part * scale
            stage[slot, j] = part.astype(jnp.bfloat16)
        copy = pltpu.make_async_copy(stage.at[slot], out_ref.at[:, r], local_sem.at[slot])
        copy.start()
        leaving.append(copy)

    def select_grad(r, ref):
        route(r, ref[rows:, :rows])
        select(r, ref[:rows, :], arr_ref, True)

    select_grad(0, grad_ref)
    select(0, token_ref[...], rec_ref, False)
    select_grad(2, chip_grad_ref)
    select_grad(4, pair_grad_ref)
    for r, copy in ((1, grad_core), (3, grad_chip_core), (5, grad_pair_core)):
        copy.wait_recv()
        select_grad(r, grads.at[r])
    to_core.wait_recv()
    select(1, tokens[1], rec_ref, False)
    route_both.wait_recv()
    route_core = push(grads.at[6, routing], grads.at[7, routing], core)
    to_chip.wait_recv()
    both_low = push(tokens.at[2, half:rows], tokens.at[6, half:rows], pair)
    chip_core = push(tokens.at[2], tokens.at[3], core)
    to_pair.wait_recv()
    both_high = push(tokens.at[4, 0:half], tokens.at[6, 0:half], chip)
    pair_core = push(tokens.at[4], tokens.at[5], core)
    grad_low = push(chip_grad_ref.at[half:rows], grads.at[6, half:rows], pair)
    grad_high = push(pair_grad_ref.at[0:half], grads.at[6, 0:half], chip)
    select(2, tokens[2], rec_ref, False)
    select(4, tokens[4], rec_ref, False)
    route(6, grads[6, rows:, :rows])
    route_core.wait_recv()
    route(7, grads[7, rows:, :rows])
    chip_core.wait_recv()
    select(3, tokens[3], rec_ref, False)
    pair_core.wait_recv()
    select(5, tokens[5], rec_ref, False)
    both_low.wait_recv()
    both_high.wait_recv()
    both_core = push(tokens.at[6], tokens.at[7], core)
    select(6, tokens[6], rec_ref, False)
    both_core.wait_recv()
    select(7, tokens[7], rec_ref, False)
    grad_low.wait_recv()
    grad_high.wait_recv()
    grad_both_core = push(grads.at[6, 0:rows], grads.at[7, 0:rows], core)
    select(6, grads[6, :rows], arr_ref, True)
    grad_both_core.wait_recv()
    select(7, grads[7, :rows], arr_ref, True)
    for copy in leaving[-stage.shape[0] :]:
        copy.wait()
    push.finish()


def gather_and_select(token, grad, chip_grad, pair_grad, capacity, experts_here, half_experts, top, label):
    rows, width = token.shape
    vmem = pl.BlockSpec(memory_space=pltpu.VMEM)
    anywhere = pl.BlockSpec(memory_space=pl.ANY)
    slots = jax.ShapeDtypeStruct((half_experts, 8, capacity, width), jnp.bfloat16)
    return pl.pallas_call(
        functools.partial(gather_kernel, capacity, experts_here, half_experts, top),
        out_shape=(
            slots,
            slots,
            jax.ShapeDtypeStruct((half_experts, 8, capacity, 1), jnp.float32),
            jax.ShapeDtypeStruct((8, half_experts, rows), jnp.float32),
        ),
        in_specs=[vmem] * 4,
        out_specs=[anywhere, anywhere, vmem, vmem],
        scratch_shapes=[
            pltpu.VMEM((8, rows, width), jnp.bfloat16),
            pltpu.VMEM((8, rows + ROUTE_ROWS, width), jnp.bfloat16),
            pltpu.VMEM((8, half_experts, rows), jnp.float32),
            pltpu.VMEM((4, half_experts, capacity, width), jnp.bfloat16),
            pltpu.SemaphoreType.DMA((18,)),
            pltpu.SemaphoreType.DMA((18,)),
            pltpu.SemaphoreType.DMA((4,)),
        ],
        compiler_params=pltpu.CompilerParams(
            collective_id=label, has_side_effects=True, vmem_limit_bytes=VM
        ),
        cost_estimate=lasts(44),
        name="gather_and_select",
    )(token, grad, chip_grad, pair_grad)


def fetcher(order, fetched, local_sem, capacity, code_ref):
    depth = fetched.shape[0]
    fetching = []
    done = []

    def fetch():
        n = len(fetching)
        if n < len(order):
            slots, r = order[n]
            fetching.append(
                [
                    pltpu.make_async_copy(
                        ref.at[r * capacity : (r + 1) * capacity],
                        fetched.at[n % depth, j * capacity : (j + 1) * capacity],
                        local_sem.at[n % depth, j],
                    )
                    for j, ref in enumerate(slots)
                ]
            )
            for copy in fetching[-1]:
                copy.start()

    for _ in range(depth - 1):
        fetch()

    def next_sum():
        fetch()
        n = len(done)
        for copy in fetching[n]:
            copy.wait()
        done.append(n)
        return dot(picked(code_ref[order[n][1]], capacity), fetched[n % depth], 0, 0)

    return next_sum


def combine_kernel(capacity, count, code_ref, *refs):
    slots = refs[:count]
    mine_ref, theirs_ref, fetched, local_sem = refs[-4:]
    order = [(slots, r) for r in (7, 6, 3, 2, 5, 4, 1, 0)]
    next_sum = fetcher(order, fetched, local_sem, capacity, code_ref)
    for _, r in order:
        (theirs_ref if r % 2 else mine_ref)[r // 2] = next_sum().astype(jnp.bfloat16)


def combine(code, slots, capacity, after):
    _, count, rows = code.shape
    width = slots[0].shape[1]
    vmem = pl.BlockSpec(memory_space=pltpu.VMEM)
    anywhere = pl.BlockSpec(memory_space=pl.ANY)
    four = jax.ShapeDtypeStruct((4, rows, width), jnp.bfloat16)
    return pl.pallas_call(
        functools.partial(combine_kernel, capacity, count),
        out_shape=(four, four),
        in_specs=[vmem] + [anywhere] * (count + len(after)),
        out_specs=[vmem, vmem],
        scratch_shapes=[
            pltpu.VMEM((4, count * capacity, width), jnp.bfloat16),
            pltpu.SemaphoreType.DMA((4, count)),
        ],
        compiler_params=pltpu.CompilerParams(vmem_limit_bytes=VM),
        cost_estimate=lasts(12),
        name="combine",
    )(code, *slots, *after)


def return_kernel(capacity, count, far_mask, code_ref, mine_ref, theirs_ref, go_ref, *refs):
    mixes = refs[:count]
    (out_ref, near_ref, far_ref, come_ref, fetched, core_got, own, theirs_mix, core_got_mix, half_pair, half_chip, from_chip,
     from_pair, send_sem, recv_sem, local_sem) = refs[-16:]
    rows = out_ref.shape[0]
    half = rows // 2
    _, core = flipped("expert", 1)
    _, chip = flipped("expert", 2)
    _, pair = flipped("dp", PAIR)
    _, far = flipped("dp", far_mask)
    greet([core, chip, pair, far])
    push = Pusher(send_sem, recv_sem)
    beside = push(go_ref, come_ref, far)
    crossing = {i: push(theirs_ref.at[i], core_got.at[i], core) for i in (3, 1, 2, 0)}
    order = [(mixes, r) for r in (7, 6, 3, 2, 5, 4, 1, 0)]
    next_sum = fetcher(order, fetched, local_sem, capacity, code_ref)

    def plus(a, b):
        return (a.astype(jnp.float32) + b.astype(jnp.float32)).astype(jnp.bfloat16)

    def mix(i, ref, at):
        theirs_mix[i] = next_sum().astype(jnp.bfloat16)
        copy = push(theirs_mix.at[i], core_got_mix.at[i], core)
        mine = next_sum()
        copy.wait_recv()
        ref[at] = plus(mine, core_got_mix[i])

    crossing[3].wait_recv()
    own[3] = plus(mine_ref[3], core_got[3])
    at_pair = push(own.at[3, 0:half], half_pair, pair)
    at_chip = push(own.at[3, half:rows], half_chip, chip)
    crossing[1].wait_recv()
    own[1] = plus(mine_ref[1], core_got[1])
    low_chip = push(own.at[1, half:rows], from_chip.at[half:rows], chip)
    crossing[2].wait_recv()
    own[2] = plus(mine_ref[2], core_got[2])
    high_pair = push(own.at[2, 0:half], from_pair.at[0:half], pair)
    crossing[0].wait_recv()
    out_ref[...] = mine_ref[0].astype(jnp.float32) + core_got[0].astype(jnp.float32)
    mix(3, far_ref, 1)
    mix(1, far_ref, 0)
    at_pair.wait_recv()
    own[1, :half] = plus(own[1, :half], half_pair[...])
    high_chip = push(own.at[1, 0:half], from_chip.at[0:half], chip)
    at_chip.wait_recv()
    own[2, half:] = plus(own[2, half:], half_chip[...])
    low_pair = push(own.at[2, half:rows], from_pair.at[half:rows], pair)
    mix(2, near_ref, 1)
    mix(0, near_ref, 0)
    low_chip.wait_recv()
    high_pair.wait_recv()
    high_chip.wait_recv()
    low_pair.wait_recv()
    out_ref[...] += from_chip[...].astype(jnp.float32) + from_pair[...].astype(jnp.float32)
    beside.wait_recv()
    push.finish()


def return_sums(code, mine, theirs, mixes, capacity, go, far_mask, label, after):
    _, count, rows = code.shape
    width = mine.shape[2]
    vmem = pl.BlockSpec(memory_space=pltpu.VMEM)
    anywhere = pl.BlockSpec(memory_space=pl.ANY)
    four = pltpu.VMEM((4, rows, width), jnp.bfloat16)
    two = jax.ShapeDtypeStruct((2, rows, width), jnp.bfloat16)
    return pl.pallas_call(
        functools.partial(return_kernel, capacity, count, far_mask),
        out_shape=(
            jax.ShapeDtypeStruct((rows, width), jnp.float32),
            two,
            two,
            jax.ShapeDtypeStruct(go.shape, jnp.bfloat16),
        ),
        in_specs=[vmem] * 3 + [anywhere] * (1 + count + len(after)),
        out_specs=[vmem] * 3 + [anywhere],
        scratch_shapes=[pltpu.VMEM((4, count * capacity, width), jnp.bfloat16), four, four, four, four]
        + [pltpu.VMEM((rows // 2, width), jnp.bfloat16)] * 2
        + [pltpu.VMEM((rows, width), jnp.bfloat16)] * 2
        + [
            pltpu.SemaphoreType.DMA((15,)),
            pltpu.SemaphoreType.DMA((15,)),
            pltpu.SemaphoreType.DMA((4, count)),
        ],
        compiler_params=pltpu.CompilerParams(
            collective_id=label, has_side_effects=True, vmem_limit_bytes=VM
        ),
        cost_estimate=lasts(37),
        name="return_sums",
    )(code, mine, theirs, go, *mixes, *after)


def settle_kernel(waits, bit_ref, keep_hbm, got_hbm, *refs):
    stay_ref, go_ref = refs[waits : waits + 2]
    keep_ref, got_ref, sem = refs[-3:]
    arriving = [
        pltpu.make_async_copy(src, dst, sem.at[i])
        for i, (src, dst) in enumerate(((keep_hbm, keep_ref), (got_hbm, got_ref)))
    ]
    for copy in arriving:
        copy.start()
    for copy in arriving:
        copy.wait()
    bit = bit_ref[0]
    for high in range(keep_ref.shape[0]):
        for low in range(keep_ref.shape[2]):
            for ref, side in ((stay_ref, bit), (go_ref, 1 - bit)):
                total = keep_ref[high, side, low].astype(jnp.float32) + got_ref[
                    high, side, low
                ].astype(jnp.float32)
                ref[high, low] = total.astype(jnp.bfloat16)


def settle(keep, got, mask, label, after, passed=()):
    count, rows, columns = keep.shape
    low = 1 if mask == PAIR else 2
    shape = (count // 2 // low, 2, low, rows, columns)
    half = jax.ShapeDtypeStruct((count // 2 // low, low, rows, columns), jnp.bfloat16)
    bit = lax.rem(lax.axis_index("dp") // mask, 2)
    vmem = pl.BlockSpec(memory_space=pltpu.VMEM)
    anywhere = pl.BlockSpec(memory_space=pl.ANY)
    stay, go, *passed = pl.pallas_call(
        functools.partial(settle_kernel, len(after) + len(passed)),
        out_shape=[half, half] + [jax.ShapeDtypeStruct(p.shape, p.dtype) for p in passed],
        in_specs=[pl.BlockSpec(memory_space=pltpu.SMEM)] + [anywhere] * (2 + len(after) + len(passed)),
        scratch_shapes=[
            pltpu.VMEM(shape, jnp.bfloat16),
            pltpu.VMEM(shape, jnp.bfloat16),
            pltpu.SemaphoreType.DMA((2,)),
        ],
        out_specs=[vmem, vmem] + [anywhere] * len(passed),
        input_output_aliases={3 + len(after) + i: 2 + i for i in range(len(passed))},
        compiler_params=pltpu.CompilerParams(vmem_limit_bytes=VM),
        cost_estimate=lasts(3),
        name="settle_%s" % label,
    )(bit.reshape(1), keep.reshape(shape), got.reshape(shape), *after, *passed)
    return stay.reshape(-1, rows, columns), go.reshape(-1, rows, columns), *passed


def settle_mix_kernel(near_ref, got_ref, *refs):
    refs[-1][...] = (near_ref[1].astype(jnp.float32) + got_ref[1].astype(jnp.float32)).astype(jnp.bfloat16)


def settle_mix(near, got, after):
    vmem = pl.BlockSpec(memory_space=pltpu.VMEM)
    return pl.pallas_call(
        settle_mix_kernel,
        out_shape=jax.ShapeDtypeStruct(near.shape[1:], jnp.bfloat16),
        in_specs=[vmem] * 2 + [pl.BlockSpec(memory_space=pl.ANY)] * len(after),
        out_specs=vmem,
        compiler_params=pltpu.CompilerParams(vmem_limit_bytes=VM),
        cost_estimate=lasts(3),
        name="settle_mix",
    )(near, got, *after)


EPS_STAT = 1e-30
STAT_DECAY = 0.5
LEARN_RATE = 0.5
CLIP_LEVEL = 0.05


def decayed(old, new):
    return STAT_DECAY * old + (1.0 - STAT_DECAY) * new


def finish_kernel(count, groups, half, orders, spans, *refs):
    bits = count.bit_length() - 1
    steps = len(orders[0])
    (mine_hbm, own_0, own_1, got_0, got_1, stay_2, come_2, keep_3, come_3, near_mix_ref, got_mix_ref,
     up_rows_ref, down_rows_ref, up_cols_ref, down_cols_ref, qkv_rows_ref, out_rows_ref, moments_ref, qkv_cols_ref,
     out_cols_ref) = refs[:20]
    (dense_ref, ends_ref, pair_mix_ref, out_ref, sums_ref, up_new_ref, down_new_ref, dense_out_ref,
     dense_new_ref) = refs[20:29]
    sum_ref, first_got, *got = refs[29 : 31 + steps]
    (mine_ref, load_sem, go_s, far_go_s, far_stay_s, far_got_s, mix_s, pay_s, got_s, dense_pay_s, dense_got_s, spread_s,
     up_old_ref, down_old_ref, dense_old_ref, dense_cols_ref, send_sem, recv_sem) = refs[31 + steps :]
    width = up_rows_ref.shape[1]
    ff = down_rows_ref.shape[1]
    wide = width // 2
    own_up = width // count
    own_down = ff // count
    me = lax.axis_index("dp")
    place = lax.axis_index("expert")
    after = [lax.rem(me + k, count) for k in range(count)]
    beside = [lax.rem(place + k, groups) for k in range(groups)]
    pair_bit, pair = flipped("dp", PAIR)
    far_bit, far = flipped("dp", FAR)
    core, core_peer = flipped("expert", 1)
    chip, chip_peer = flipped("expert", 2)
    links = [flipped("dp", 1 << b) for b in range(bits)] + [(chip, chip_peer)]
    whole = (slice(None),) * bits
    loading = pltpu.make_async_copy(mine_hbm.at[whole + (core,)], mine_ref, load_sem)
    loading.start()
    greet([{"dp": after[k]} for k in range(1, count)] + [{"expert": beside[k]} for k in range(1, groups)])
    push = Pusher(send_sem, recv_sem)

    def plus(a, b):
        return (a.astype(jnp.float32) + b.astype(jnp.float32)).astype(jnp.bfloat16)

    flying = [
        push(mine_hbm.at[whole + (1 - core, slice(None), slice(None), span)], first_got.at[..., span], core_peer)
        for span in spans
    ]
    for low in range(2):
        far_go_s[low] = plus(keep_3[1 - far_bit, low], come_3[1 - far_bit, low])
    far_exchange = push(far_go_s, far_got_s, far)
    go_s[0] = plus(stay_2[1 - pair_bit], come_2[1 - pair_bit])
    cross_2 = push(go_s.at[0], ends_ref.at[2], pair)
    mix_s[...] = plus(near_mix_ref[1], got_mix_ref[1])
    cross_mix = push(mix_s, pair_mix_ref, pair)
    ends_ref[0] = plus(stay_2[pair_bit], come_2[pair_bit])
    for low in range(2):
        far_stay_s[low] = plus(keep_3[far_bit, low], come_3[far_bit, low])

    def own_columns(*tables):
        here = pl.ds(pl.multiple_of(me * LANES, LANES), LANES)
        rows = [table[:, here] for table in tables]
        return padded(jnp.concatenate(rows, axis=0)).T

    def padded(rows):
        return jnp.concatenate([rows, jnp.zeros((LANES - rows.shape[0], LANES), jnp.float32)], axis=0)

    up_old_ref[...] = own_columns(up_rows_ref)
    dense_old_ref[...] = own_columns(qkv_rows_ref, out_rows_ref, moments_ref)
    around = down_rows_ref[:, pl.ds(pl.multiple_of(me // 2 * LANES, LANES), LANES)]
    both_halves = padded(around).T
    down_old_ref[...] = jnp.where(lax.rem(me, 2) == 0, both_halves[:own_down], both_halves[own_down:])
    dense_cols_ref[:, : qkv_cols_ref.shape[1]] = qkv_cols_ref[...]
    dense_cols_ref[:, qkv_cols_ref.shape[1] :] = out_cols_ref[...]

    def column_of(table_ref, lane, at):
        return jnp.sum(jnp.where(lane == at, table_ref[...], 0.0), axis=1, keepdims=True)

    up_lane = lax.broadcasted_iota(jnp.int32, (own_up, LANES), 1)
    down_lane = lax.broadcasted_iota(jnp.int32, (own_down, LANES), 1)
    up_new_ref[...] = jnp.zeros_like(up_new_ref)
    down_new_ref[...] = jnp.zeros_like(down_new_ref)

    def factored(grad, old):
        square = grad * grad
        new = decayed(old, jnp.mean(square + EPS_STAT, axis=1, keepdims=True))
        return (
            new,
            jnp.sum(square + EPS_STAT, axis=0, keepdims=True),
            jnp.sum(square * (1.0 / new), axis=0, keepdims=True),
        )

    def expert(values, at):
        for kind, (part, old_ref, new_ref, lane, rows) in enumerate(
            (
                (values[:own_up, :], up_old_ref, up_new_ref, up_lane, own_up),
                (values[own_up:, :], down_old_ref, down_new_ref, down_lane, own_down),
            )
        ):
            new, total, scaled = factored(part.astype(jnp.float32), column_of(old_ref, lane, at))
            new_ref[:rows, :] = jnp.where(lane == at, new, new_ref[:rows, :])
            for h in range(2):
                span = slice(h * wide, (h + 1) * wide)
                pay_s[at, 4 * kind + h : 4 * kind + h + 1, :] = total[:, span]
                pay_s[at, 4 * kind + 2 + h : 4 * kind + 3 + h, :] = scaled[:, span]

    own_at, got_at = pair_bit * half, (1 - pair_bit) * half

    def at_place(chosen, span):
        return tuple(chosen.get(bits - 1 - i, slice(None)) for i in range(bits)) + (
            chosen.get(bits, slice(None)),
            slice(None),
            span,
        )

    def got_place(step, span):
        return (slice(None),) * (steps - 1 - step) + (slice(None), span)

    loading.wait()
    chosen = [{} for _ in spans]
    for step in range(steps + 1):
        for part, span in enumerate(spans):
            flying[part].wait_recv()
            if step == 0:
                sum_ref[..., span] = plus(mine_ref[..., span], first_got[..., span])
            else:
                here = at_place(chosen[part], span)
                sum_ref[here] = plus(sum_ref[here], got[step - 1][got_place(step - 1, span)])
            if step < steps:
                link = orders[part][step]
                bit, peer = links[link]
                away = at_place({**chosen[part], link: 1 - bit}, span)
                flying[part] = push(sum_ref.at[away], got[step].at[got_place(step, span)], peer)
                chosen[part] = {**chosen[part], link: bit}
            else:
                dense_ref[core, chip, :, span] = sum_ref[at_place(chosen[part], span)]
                block = dense_ref.at[core, chip, :, span]
                flying[part] = push(block, block, chip_peer)
        if step == 0:
            expert(own_0, own_at)
            expert(got_0, got_at)
            expert(own_1, own_at + 1)
            expert(got_1, got_at + 1)
        elif step == 1:
            expert(ends_ref[0], own_at + 2)
        elif step == steps - 1:
            cross_2.wait_recv()
            expert(ends_ref[2], got_at + 2)
            far_exchange.wait_recv()
            go_s[1] = plus(far_stay_s[1 - pair_bit], far_got_s[1 - pair_bit])
            cross_3 = push(go_s.at[1], ends_ref.at[3], pair)
            ends_ref[1] = plus(far_stay_s[pair_bit], far_got_s[pair_bit])
            expert(ends_ref[1], own_at + 3)
    for part, span in enumerate(spans):
        flying[part].wait_recv()
        block = dense_ref.at[core, :, :, span]
        flying[part] = push(block, block, core_peer)
    cross_3.wait_recv()
    expert(ends_ref[3], got_at + 3)
    arriving = [push(pay_s.at[after[k]], got_s.at[k], {"dp": after[k]}) for k in range(1, count)]
    for copy in flying:
        copy.wait_recv()

    columns = dense_cols_ref.shape[1]
    piece = columns // count
    dense = dense_ref[...].reshape(own_up, dense_ref.shape[3])
    dense_lane = lax.broadcasted_iota(jnp.int32, dense_new_ref.shape, 1)
    old = dense_old_ref[...]
    qkv_columns = columns - width
    totals, scaleds, rows_new = [], [], []
    for at, span in enumerate((slice(0, qkv_columns), slice(qkv_columns, columns))):
        new, total, scaled = factored(
            dense[:, span].astype(jnp.float32), column_of(dense_old_ref, dense_lane, at)
        )
        rows_new.append(new)
        totals.append(total)
        scaleds.append(scaled)
    gain_lanes = (dense_lane == 2) | (dense_lane == 3)
    gains = pltpu.roll(dense[:, columns:].astype(jnp.float32), 2, 1)
    moments = jnp.where(gain_lanes, decayed(old, gains * gains + EPS_STAT), 1.0)
    gain_steps = jnp.where(gain_lanes, gains * lax.rsqrt(moments), 0.0)
    dense_new_ref[...] = jnp.where(
        dense_lane == 0,
        rows_new[0],
        jnp.where(dense_lane == 1, rows_new[1], jnp.where(gain_lanes, gain_steps, pltpu.roll(moments, 2, 1))),
    )
    gain_squares = jnp.sum(jnp.sum(gain_steps * gain_steps, axis=1, keepdims=True), axis=0, keepdims=True)
    total = jnp.concatenate(totals, axis=1)
    scaled = jnp.concatenate(scaleds, axis=1)
    for d in range(count):
        span = slice(d * piece, (d + 1) * piece)
        dense_pay_s[d] = jnp.concatenate(
            [total[:, span], scaled[:, span], jnp.broadcast_to(gain_squares, (1, piece)), jnp.zeros((5, piece), jnp.float32)],
            axis=0,
        )
    dense_arriving = [push(dense_pay_s.at[after[k]], dense_got_s.at[k], {"dp": after[k]}) for k in range(1, count)]

    tile = pay_s[me]
    for k in range(1, count):
        arriving[k - 1].wait_recv()
        tile = tile + got_s[k]
    made = []
    tops = []
    for kind, (rows_ref, cols_ref, rows) in enumerate(
        ((up_rows_ref, up_cols_ref, width), (down_rows_ref, down_cols_ref, ff))
    ):
        here = pl.ds(me, 1)
        square = jnp.concatenate([tile[4 * kind + h : 4 * kind + h + 1] for h in range(2)], axis=1)
        scaled = jnp.concatenate([tile[4 * kind + 2 + h : 4 * kind + 3 + h] for h in range(2)], axis=1)
        new_columns = decayed(cols_ref[here, :], square / rows)
        row_mean = decayed(
            jnp.mean(rows_ref[here, :], axis=1, keepdims=True),
            jnp.sum(square, axis=1, keepdims=True) / (rows * width),
        )
        squares = row_mean * jnp.sum(scaled / new_columns, axis=1, keepdims=True)
        made += [new_columns[:, :wide], new_columns[:, wide:]]
        tops += [jnp.broadcast_to(v, (1, wide)) for v in (row_mean, squares)]
    out_ref[me] = jnp.concatenate(made + tops, axis=0)
    arriving = [push(out_ref.at[me], out_ref.at[me], {"dp": after[k]}) for k in range(1, count)]

    tile = dense_pay_s[me]
    for k in range(1, count):
        dense_arriving[k - 1].wait_recv()
        tile = tile + dense_got_s[k]
    own_piece = pl.ds(pl.multiple_of(me * piece, LANES), piece)
    new_columns = decayed(dense_cols_ref[:, own_piece], tile[0:1] / width)
    is_qkv = lax.broadcasted_iota(jnp.int32, (1, piece), 1) + me * piece < qkv_columns
    ratio = tile[1:2] / new_columns
    sums = [
        jnp.sum(jnp.where(chosen_columns, row, 0.0), axis=1, keepdims=True)
        for row in (ratio, tile[0:1])
        for chosen_columns in (is_qkv, ~is_qkv)
    ]
    dense_out_ref[me] = jnp.concatenate(
        [new_columns]
        + [jnp.broadcast_to(v, (1, piece)) for v in sums]
        + [tile[2:3], jnp.zeros((2, piece), jnp.float32)],
        axis=0,
    )
    dense_arriving = [push(dense_out_ref.at[me], dense_out_ref.at[me], {"dp": after[k]}) for k in range(1, count)]

    for copy in arriving:
        copy.wait_recv()
    total = out_ref[0, :, :LANES]
    for a in range(1, count):
        total = total + out_ref[a, :, :LANES]
    spread_s[place] = total
    arriving = [push(spread_s.at[place], spread_s.at[place], {"expert": beside[k]}) for k in range(1, groups)]
    for copy in arriving + dense_arriving + [cross_mix]:
        copy.wait_recv()
    total = spread_s[0]
    for e in range(1, groups):
        total = total + spread_s[e]
    sums_ref[...] = total
    push.finish()


FAR = 4


def finish(dense, owns, gots, settling, mixes, statistics, label):
    count = lax.axis_size("dp")
    groups = lax.axis_size("expert")
    width, dense_width = dense.shape
    bits = count.bit_length() - 1
    quarter = width // count // 4
    parts = 6
    tiles = dense_width // LANES
    bounds = [LANES * (tiles * i // parts) for i in range(parts + 1)]
    spans = [slice(a, b) for a, b in zip(bounds[:-1], bounds[1:])]
    last = tuple(range(1, bits))
    orders = [((bits, 0) if part % 2 == 0 else (0, bits)) + last for part in range(parts)]
    half = (2,) * bits + (2, quarter, dense_width)
    rows = owns[0].shape[0]
    own_up, own_down = width // count, rows - width // count
    dense_columns = dense_width - LANES
    piece = dense_columns // count
    vmem = pl.BlockSpec(memory_space=pltpu.VMEM)
    stat_tiles = (count, 8, width // 2)
    dense_tiles = (count, 8, piece)
    copies = parts * (bits + 4) + 4 * (count - 1) + groups - 1 + 4
    shape = lambda *s: jax.ShapeDtypeStruct(s, jnp.float32)
    low = lambda *s: jax.ShapeDtypeStruct(s, jnp.bfloat16)
    held = lambda *s: pltpu.VMEM(s, jnp.bfloat16)
    outs = (
        low(2, 2, quarter, dense_width),
        low(4, rows, width),
        low(*mixes[0].shape[1:]),
        shape(*stat_tiles),
        shape(8, LANES),
        shape(LANES, LANES),
        shape(LANES, LANES),
        shape(*dense_tiles),
        shape(width // count, LANES),
    )
    args = (
        dense.reshape((2,) * bits + (2, 2, quarter, dense_width)),
        *owns, *gots, *settling, *mixes, *statistics,
    )
    own, *rest = pl.pallas_call(
        functools.partial(finish_kernel, count, groups, 4, orders, spans),
        out_shape=outs,
        in_specs=[pl.BlockSpec(memory_space=pl.ANY)] + [vmem] * (len(args) - 1),
        out_specs=[vmem] * len(outs),
        scratch_shapes=[held(*half), held(*half)]
        + [held(*((2,) * (bits - step)), quarter, dense_width) for step in range(bits + 1)]
        + [
            held(*half),
            pltpu.SemaphoreType.DMA,
            held(2, rows, width),
            held(2, rows, width),
            held(2, rows, width),
            held(2, rows, width),
            held(*mixes[0].shape[1:]),
            pltpu.VMEM(stat_tiles, jnp.float32),
            pltpu.VMEM(stat_tiles, jnp.float32),
            pltpu.VMEM(dense_tiles, jnp.float32),
            pltpu.VMEM(dense_tiles, jnp.float32),
            pltpu.VMEM((groups, 8, LANES), jnp.float32),
            pltpu.VMEM((own_up, LANES), jnp.float32),
            pltpu.VMEM((own_down, LANES), jnp.float32),
            pltpu.VMEM((own_up, LANES), jnp.float32),
            pltpu.VMEM((1, dense_columns), jnp.float32),
            pltpu.SemaphoreType.DMA((copies,)),
            pltpu.SemaphoreType.DMA((copies,)),
        ],
        compiler_params=pltpu.CompilerParams(
            collective_id=label, has_side_effects=True, vmem_limit_bytes=VM
        ),
        cost_estimate=lasts(75),
        name="finish",
    )(*args)
    return own.reshape(width // count, dense_width), *rest


def update_kernel(counts, half, early, s_ref, *refs):
    owns, gots = refs[:early], refs[early : 2 * early]
    (dense_ref, ends_ref, pair_mix_ref, tiles_ref, sums_ref, up_new_ref, down_new_ref, dense_tiles_ref, dense_new_ref,
     qkv_old_ref, out_old_ref, middle_hbm, near_mix_hbm, got_mix_hbm, up_w_hbm, down_w_hbm, qkv_w_hbm, out_w_hbm,
     block_hbm, up_out_hbm, down_out_hbm, up_rows_ref, down_rows_ref, up_cols_ref, down_cols_ref,
     qkv_out_ref, out_out_ref, qkv_cols_ref, out_cols_ref, qkv_rows_ref, out_rows_ref, gains_ref, moments_ref,
     rms_ref, middle_ref, near_mix_ref, got_mix_ref, up_w_ref, down_w_ref, qkv_w_ref, out_w_ref,
     block_ref, up_out_ref, down_out_ref, in_sem, out_sem) = refs[2 * early :]
    me = s_ref[1]

    def rows_of(hbm, count, along=0):
        rows = pl.ds(pl.multiple_of(me * count, count), count)
        return hbm.at[:, rows] if along else hbm.at[rows]

    incoming = [
        pltpu.make_async_copy(src, dst, in_sem.at[i])
        for i, (src, dst) in enumerate(
            (
                (rows_of(up_w_hbm, up_w_ref.shape[1], 1), up_w_ref),
                (rows_of(down_w_hbm, down_w_ref.shape[1], 1), down_w_ref),
                (rows_of(qkv_w_hbm, qkv_w_ref.shape[0]), qkv_w_ref),
                (rows_of(out_w_hbm, out_w_ref.shape[0]), out_w_ref),
                (middle_hbm, middle_ref),
                (near_mix_hbm.at[0], near_mix_ref),
                (got_mix_hbm.at[0], got_mix_ref),
            )
        )
    ]
    for copy in incoming:
        copy.start()
    leaving = []

    def leave(src, dst):
        copy = pltpu.make_async_copy(src, dst, out_sem.at[len(leaving)])
        copy.start()
        leaving.append(copy)

    late = half - early
    own_up = up_out_ref.shape[1]
    own_down = down_out_ref.shape[1]
    wide = tiles_ref.shape[2]
    pair_bit = s_ref[0]
    count = dense_tiles_ref.shape[0]
    dense_sums = dense_tiles_ref[0, :, 0:1]
    for a in range(1, count):
        dense_sums = dense_sums + dense_tiles_ref[a, :, 0:1]
    width = qkv_old_ref.shape[1]
    qkv_columns = qkv_out_ref.shape[1]
    row_means = []
    squares = [dense_tiles_ref[0, 5:6, 0:1]]
    for at, (old_ref, columns) in enumerate(((qkv_old_ref, qkv_columns), (out_old_ref, width))):
        row_means.append(
            decayed(
                jnp.mean(old_ref[...], axis=1, keepdims=True),
                dense_sums[3 + at : 4 + at] / (width * columns),
            )
        )
        squares.append(row_means[-1] * dense_sums[1 + at : 2 + at])
    squares += [sums_ref[5:6, 0:1], sums_ref[7:8, 0:1]]
    roots = [jnp.sqrt(square / number) for square, number in zip(squares, counts)]
    factors = [LEARN_RATE / jnp.maximum(1.0, root / CLIP_LEVEL) for root in roots]
    for i, root in enumerate(roots):
        rms_ref[i] = root[0, 0]

    up_table = up_new_ref[...]
    down_table = down_new_ref[...]
    lane = lax.broadcasted_iota(jnp.int32, up_table.shape, 1)

    def expert(ref, at):
        tile = tiles_ref[at]
        for kind, (table, weight_ref, out_ref, first, rows) in enumerate(
            (
                (up_table, up_w_ref, up_out_ref, 0, own_up),
                (down_table, down_w_ref, down_out_ref, own_up, own_down),
            )
        ):
            row_mean = tile[4 + 2 * kind : 5 + 2 * kind, 0:1]
            column = jnp.sum(jnp.where(lane == at, table, 0.0), axis=1, keepdims=True)[:rows]
            scale = factors[3 + kind] * lax.rsqrt(column / row_mean)
            for h in range(2):
                span = slice(h * wide, (h + 1) * wide)
                columns = lax.rsqrt(tile[2 * kind + h : 2 * kind + h + 1, :])
                out_ref[at, :, span] = (
                    weight_ref[at, :, span].astype(jnp.float32)
                    - ref[first : first + rows, span].astype(jnp.float32) * scale * columns
                )
        leave(up_out_ref.at[at], up_out_hbm.at[at])
        leave(down_out_ref.at[at], down_out_hbm.at[at])

    own_at, got_at = pair_bit * half, (1 - pair_bit) * half
    incoming[0].wait()
    incoming[1].wait()
    for j in range(early):
        expert(owns[j], own_at + j)
        expert(gots[j], got_at + j)
    for j in range(late):
        expert(ends_ref.at[j], own_at + early + j)
        expert(ends_ref.at[late + j], got_at + early + j)
    for copy in incoming[2:]:
        copy.wait()
    block_ref[...] = middle_ref[...] + (
        near_mix_ref[...].astype(jnp.float32)
        + got_mix_ref[...].astype(jnp.float32)
        + pair_mix_ref[...].astype(jnp.float32)
    )
    leave(block_ref, block_hbm)
    up_rows_ref[...] = up_table.T[: up_rows_ref.shape[0], :own_up]
    down_rows_ref[...] = down_table.T[: down_rows_ref.shape[0], :own_down]
    for a in range(up_cols_ref.shape[0]):
        for h in range(2):
            span = slice(h * wide, (h + 1) * wide)
            up_cols_ref[a : a + 1, span] = tiles_ref[a, h : h + 1, :]
            down_cols_ref[a : a + 1, span] = tiles_ref[a, 2 + h : 3 + h, :]

    table = dense_new_ref[...]
    scales = [
        factors[1 + at] * lax.rsqrt(table[:, at : at + 1] / row_means[at]) for at in range(2)
    ]
    piece = dense_tiles_ref.shape[2]
    for first in range(0, qkv_columns + width, LANES):
        at = 0 if first < qkv_columns else 1
        weight_ref, out_ref, cols_ref = (
            (qkv_w_ref, qkv_out_ref, qkv_cols_ref) if at == 0 else (out_w_ref, out_out_ref, out_cols_ref)
        )
        here = slice(first - at * qkv_columns, first - at * qkv_columns + LANES)
        within = first % piece
        columns = dense_tiles_ref[first // piece, 0:1, within : within + LANES]
        cols_ref[:, here] = columns
        out_ref[:, here] = weight_ref[:, here].astype(jnp.float32) - dense_ref[
            :, first : first + LANES
        ].astype(jnp.float32) * scales[at] * lax.rsqrt(columns)
    turned = table.T
    qkv_rows_ref[...] = turned[0:1]
    out_rows_ref[...] = turned[1:2]
    gains_ref[...] = -factors[0] * turned[2:4]
    moments_ref[...] = turned[4:6]
    for copy in leaving:
        copy.wait()


def update(owns, gots, finished, row_statistics, middle, mixes, up_w, down_w, qkv_w, out_w):
    count = lax.axis_size("dp")
    groups = lax.axis_size("expert")
    me = lax.axis_index("dp")
    experts, width, up_columns = up_w.shape
    ff = down_w.shape[1]
    qkv_columns = qkv_w.shape[1]
    own_up, own_down = width // count, ff // count
    counts = (
        float(2 * width),
        float(width * qkv_columns),
        float(width * width),
        float(groups * experts * width * up_columns),
        float(groups * experts * ff * width),
    )
    ends = finished[1]
    early = len(owns)
    whole = lambda *shape: pl.BlockSpec(shape, lambda g, s: (0,) * len(shape))
    shape = lambda *s: jax.ShapeDtypeStruct(s, jnp.float32)
    rows = own_up + own_down
    outs = [
        shape(*middle.shape),
        shape(experts, own_up, up_columns),
        shape(experts, own_down, width),
        shape(experts, own_up),
        shape(experts, own_down),
        shape(experts, up_columns),
        shape(experts, width),
        shape(own_up, qkv_columns),
        shape(own_up, width),
        shape(1, qkv_columns),
        shape(1, width),
        shape(1, own_up),
        shape(1, own_up),
        shape(2, own_up),
        shape(2, own_up),
        shape(len(counts)),
    ]
    return pl.pallas_call(
        functools.partial(update_kernel, counts, early + ends.shape[0] // 2, early),
        out_shape=outs,
        grid_spec=pltpu.PrefetchScalarGridSpec(
            num_scalar_prefetch=1,
            grid=(1,),
            in_specs=[whole(rows, width)] * (2 * early)
            + [whole(*a.shape) for a in (*finished, *row_statistics)]
            + [pl.BlockSpec(memory_space=pl.ANY)] * 7,
            out_specs=[pl.BlockSpec(memory_space=pl.ANY)] * 3
            + [whole(*o.shape) for o in outs[3:-1]]
            + [pl.BlockSpec(memory_space=pltpu.SMEM)],
            scratch_shapes=[
                pltpu.VMEM(middle.shape, jnp.float32),
                pltpu.VMEM(middle.shape, jnp.bfloat16),
                pltpu.VMEM(middle.shape, jnp.bfloat16),
                pltpu.VMEM((experts, own_up, up_columns), jnp.bfloat16),
                pltpu.VMEM((experts, own_down, width), jnp.bfloat16),
                pltpu.VMEM((own_up, qkv_columns), jnp.bfloat16),
                pltpu.VMEM((own_up, width), jnp.bfloat16),
                pltpu.VMEM(middle.shape, jnp.float32),
                pltpu.VMEM((experts, own_up, up_columns), jnp.float32),
                pltpu.VMEM((experts, own_down, width), jnp.float32),
                pltpu.SemaphoreType.DMA((7,)),
                pltpu.SemaphoreType.DMA((2 * experts + 1,)),
            ],
        ),
        compiler_params=pltpu.CompilerParams(vmem_limit_bytes=VM),
        cost_estimate=lasts(6),
        name="update",
    )(
        jnp.stack([lax.rem(me // PAIR, 2), me]),
        *owns, *gots, *finished, *row_statistics, middle, *mixes, up_w, down_w, qkv_w, out_w,
    )


D = 1024
FF = 512
TOP = 8


def swap(values, axis, mask):
    count = lax.axis_size(axis)
    return lax.ppermute(values, axis, [(i, i ^ mask) for i in range(count)])


def swap_pair(values):
    return swap(values, "dp", PAIR)


def swap_chip(values):
    return swap(values, "expert", 2)


def swap_core(values):
    return swap(values, "expert", 1)


def plus(a, b):
    return (a.astype(jnp.float32) + b.astype(jnp.float32)).astype(jnp.bfloat16)


def halve(blocks, axis, mask):
    bit = lax.rem(lax.axis_index(axis) // mask, 2)
    keep = lax.dynamic_index_in_dim(blocks, bit, 1, keepdims=False)
    give = lax.dynamic_index_in_dim(blocks, 1 - bit, 1, keepdims=False)
    return keep, swap(give, axis, mask)


def reduce_dense_far(blocks):
    count = lax.axis_size("dp")
    width, columns = blocks.shape
    rows = width // count
    blocks = blocks.reshape(count, 2, 2, rows // 4, columns)
    keep, got = halve(jnp.moveaxis(blocks, 2, 1), "expert", 1)
    keep, got = halve(plus(keep, got), "expert", 2)
    blocks = plus(keep, got)
    low = 1
    while low < count:
        keep, got = halve(blocks.reshape((-1, 2, 1) + blocks.shape[1:]), "dp", low)
        blocks = plus(keep, got).reshape((-1,) + blocks.shape[1:])
        low *= 2
    mine = blocks[0]
    chip = lax.axis_index("expert") // 2
    core = lax.rem(lax.axis_index("expert"), 2)
    other = swap_chip(mine)
    both = jnp.where(chip == 0, jnp.stack([mine, other]), jnp.stack([other, mine]))
    across = swap_core(both)
    all_four = jnp.where(core == 0, jnp.stack([both, across], 1), jnp.stack([across, both], 1))
    return all_four.reshape(rows, columns)


def own_share(matrix, along):
    count = lax.axis_size("dp")
    width = matrix.shape[along] // count
    return lax.dynamic_slice_in_dim(matrix, lax.axis_index("dp") * width, width, along)


def factored(part, rows_old):
    square = part * part
    rows_new = decayed(rows_old, jnp.mean(square + EPS_STAT, axis=-1))
    return (
        rows_new,
        jnp.sum(square + EPS_STAT, axis=-2),
        jnp.sum(square / rows_new[..., None], axis=-2),
    )


def per_device(
    hidden_in,
    out_grad,
    segment_ids,
    parent_ids,
    positions,
    expert_ids,
    gate_weights,
    norm_gains,
    qkv_weight,
    out_weight,
    gate_up_weight,
    down_weight,
    gain_moment,
    qkv_rows,
    qkv_cols,
    out_rows,
    out_cols,
    gateup_rows,
    gateup_cols,
    down_rows,
    down_cols,
):
    rows_here = hidden_in.shape[0]
    dp_count = lax.axis_size("dp")
    groups = lax.axis_size("expert")
    experts_here = gate_up_weight.shape[0]
    total_experts = experts_here * groups
    capacity = 3 * rows_here * TOP // (2 * total_experts)
    half_experts = experts_here // 2
    dp_index = lax.axis_index("dp")
    pair_bit = lax.rem(dp_index // PAIR, 2)
    first_local = pair_bit * half_experts
    first_expert = lax.axis_index("expert") * experts_here + first_local

    weight_high = gate_weights.astype(jnp.bfloat16)
    weight_low = (gate_weights - weight_high.astype(jnp.float32)).astype(jnp.bfloat16)
    routing = jnp.concatenate([expert_ids.astype(jnp.bfloat16), weight_high, weight_low], axis=1).T
    routing = jnp.pad(routing, ((0, ROUTE_ROWS - routing.shape[0]), (0, D - rows_here)))
    grad_rows = jnp.concatenate([out_grad.astype(jnp.bfloat16), routing], axis=0)
    chip_grad_rows = swap_chip(grad_rows)
    pair_grad_rows = swap_pair(grad_rows)
    ids = jnp.stack([segment_ids, parent_ids, positions])
    normed, qkv, attended, lse, middle, normed_ffn = attend(
        hidden_in, ids, norm_gains, qkv_weight, out_weight
    )
    received, arrived, scale, code = gather_and_select(
        normed_ffn, grad_rows, chip_grad_rows, pair_grad_rows, capacity, experts_here, half_experts, TOP, 5
    )
    scalars = jnp.stack([first_local, lax.rem(dp_index, 2)])
    experts, chains = [], []

    def advance(j, after, come=None, passed=()):
        masks, stay, go = chains[j]
        come = swap(go, "dp", masks[0]) if come is None else come
        stay, go, *passed = settle(stay, come, masks[1], "%d_%d" % (j, masks[1]), after, passed)
        chains[j] = (masks[1:], stay, go)
        return (stay, *passed) if passed else stay

    masks = [1] + [1 << b for b in range(2, dp_count.bit_length() - 1)] + [PAIR]
    for j in range(half_experts):
        after = [experts[-1][2]] if experts else []
        if j == 3:
            after.append(advance(0, after))
        experts.append(
            run_expert(
                scalars, j, received, arrived, scale, gate_up_weight, down_weight, dp_count, after
            )
        )
        chains.append((masks, experts[j][0], experts[j][1]))
    mine, theirs = combine(code, [e[2] for e in experts], capacity, [])
    steps = [advance(1, [mine])]
    normed_f_grad, near_mix, far_mix, come = return_sums(
        code, mine, theirs, [e[3] for e in experts], capacity, chains[1][2], chains[1][0][0], 6, steps
    )
    steps = [normed_f_grad]
    steps.append(advance(0, steps))
    stay, far_mix = advance(2, steps[-1:], None, [far_mix])
    steps.append(stay)
    steps.append(advance(1, steps[-1:], come))
    input_grad, dense = attend_back(
        hidden_in, out_grad, middle, normed_f_grad, normed, qkv, attended, lse, ids, norm_gains, qkv_weight,
        out_weight, steps
    )
    got_mix = swap_chip(far_mix)
    qkv_columns = qkv_weight.shape[1]
    fast_tail = dp_count == experts_here and D // dp_count % 64 == 0
    if fast_tail:
        owns = [chains[j][1][0] for j in (0, 1)]
        gots = [swap_pair(chains[j][2][0]) for j in (0, 1)]
        settling = []
        for j in (2, 3):
            masks, stay, go = chains[j]
            settling += [stay, swap(go, "dp", masks[0])]
        settling[2:] = [x.reshape((2, 2) + x.shape[1:]) for x in settling[2:]]
        finished = finish(
            dense,
            owns,
            gots,
            settling,
            (near_mix, got_mix),
            (
                gateup_rows,
                down_rows,
                gateup_cols,
                down_cols,
                qkv_rows[None],
                out_rows[None],
                gain_moment,
                qkv_cols[None],
                out_cols[None],
            ),
            1,
        )
        (
            block_out,
            gate_up_new,
            down_new,
            gateup_rows_new,
            down_rows_new,
            gateup_cols_new,
            down_cols_new,
            qkv_new,
            out_new,
            qkv_cols_new,
            out_cols_new,
            qkv_rows_new,
            out_rows_new,
            gains_update,
            gain_moment_new,
            update_rms,
        ) = update(
            owns,
            gots,
            finished,
            (qkv_rows[None], out_rows[None]),
            middle,
            (near_mix, got_mix),
            gate_up_weight,
            down_weight,
            qkv_weight,
            out_weight,
        )
        qkv_cols_new, out_cols_new = qkv_cols_new[0], out_cols_new[0]
        qkv_rows_new, out_rows_new = qkv_rows_new[0], out_rows_new[0]
    else:
        for_pair = settle_mix(near_mix, got_mix, [input_grad])
        mix_parts = (near_mix[0], got_mix[0], swap_pair(for_pair))
        block_out = middle + sum(part.astype(jnp.float32) for part in mix_parts)
        dense_own = reduce_dense_far(dense)
        for j in range(half_experts):
            while len(chains[j][0]) > 1:
                advance(j, [dense_own])
        own_parts = [c[1][0] for c in chains]
        other_parts = [swap_pair(c[2][0]) for c in chains]
        own = jnp.stack(own_parts).astype(jnp.float32)
        other = jnp.stack(other_parts).astype(jnp.float32)
        parts = jnp.where(pair_bit == 0, jnp.concatenate([own, other]), jnp.concatenate([other, own]))
        gateup_part = parts[:, : D // dp_count]
        down_part = parts[:, D // dp_count :]
        gateup_rows_new, gateup_square, gateup_scaled = factored(gateup_part, own_share(gateup_rows, 1))
        down_rows_new, down_square, down_scaled = factored(down_part, own_share(down_rows, 1))
        sizes = [gateup_square.size, gateup_scaled.size, down_square.size, down_scaled.size]
        summed = total_over(
            jnp.concatenate(
                [
                    gateup_square.reshape(-1),
                    gateup_scaled.reshape(-1),
                    down_square.reshape(-1),
                    down_scaled.reshape(-1),
                    jnp.sum(gateup_rows_new, axis=1),
                    jnp.sum(down_rows_new, axis=1),
                ]
            ),
            "dp",
            1,
        )
        pieces = jnp.split(summed, [sum(sizes[: i + 1]) for i in range(4)])
        gateup_square, gateup_scaled, down_square, down_scaled = [
            p.reshape(experts_here, D) for p in pieces[:4]
        ]
        gateup_row_mean = pieces[4][:experts_here] / D
        down_row_mean = pieces[4][experts_here:] / FF
        gateup_cols_new = decayed(gateup_cols, gateup_square / D)
        down_cols_new = decayed(down_cols, down_square / FF)
        expert_squares = jnp.stack(
            [
                jnp.sum(gateup_row_mean * jnp.sum(gateup_scaled / gateup_cols_new, axis=1)),
                jnp.sum(down_row_mean * jnp.sum(down_scaled / down_cols_new, axis=1)),
            ]
        )
        spread_squares = collect(
            jnp.zeros((8, 128), jnp.float32).at[0, :2].set(expert_squares), "expert", 2
        )
        expert_squares = jnp.sum(spread_squares[:, 0, :2], axis=0)
        dense_own = dense_own.astype(jnp.float32)
        qkv_own = dense_own[:, :qkv_columns]
        out_own = dense_own[:, qkv_columns : qkv_columns + D]
        gains_own = dense_own[:, qkv_columns + D : qkv_columns + D + 2].T
        gain_moment_new = decayed(own_share(gain_moment, 1), gains_own * gains_own + EPS_STAT)
        gains_step = gains_own * lax.rsqrt(gain_moment_new)
        qkv_rows_new, qkv_square, qkv_scaled = factored(qkv_own, own_share(qkv_rows, 0))
        out_rows_new, out_square, out_scaled = factored(out_own, own_share(out_rows, 0))
        dense_sums = total_over(
            jnp.concatenate(
                [
                    qkv_square,
                    qkv_scaled,
                    out_square,
                    out_scaled,
                    jnp.stack(
                        [jnp.sum(qkv_rows_new), jnp.sum(out_rows_new), jnp.sum(gains_step * gains_step)]
                    ),
                ]
            ),
            "dp",
            4,
        )
        qkv_square, qkv_scaled, out_square, out_scaled, rest = jnp.split(
            dense_sums, [qkv_columns, 2 * qkv_columns, 2 * qkv_columns + D, 2 * qkv_columns + 2 * D]
        )
        qkv_row_mean = rest[0] / D
        out_row_mean = rest[1] / D
        qkv_cols_new = decayed(qkv_cols, qkv_square / D)
        out_cols_new = decayed(out_cols, out_square / D)
        squares = jnp.concatenate(
            [
                jnp.stack(
                    [
                        rest[2],
                        qkv_row_mean * jnp.sum(qkv_scaled / qkv_cols_new),
                        out_row_mean * jnp.sum(out_scaled / out_cols_new),
                    ]
                ),
                expert_squares,
            ]
        )
        element_counts = jnp.array(
            [2 * D, D * qkv_columns, D * D, total_experts * D * 2 * FF, total_experts * FF * D], jnp.float32
        )
        update_rms = jnp.sqrt(squares / element_counts)
        factors = LEARN_RATE / jnp.maximum(1.0, update_rms / CLIP_LEVEL)

        def stepped(weight, part, rows_new, row_mean, cols_new, factor):
            return weight.astype(jnp.float32) - part * (
                factor * lax.rsqrt(rows_new / row_mean[..., None])
            )[..., :, None] * lax.rsqrt(cols_new)[..., None, :]

        gains_update = -factors[0] * gains_step
        qkv_new = stepped(own_share(qkv_weight, 0), qkv_own, qkv_rows_new, qkv_row_mean, qkv_cols_new, factors[1])
        out_new = stepped(own_share(out_weight, 0), out_own, out_rows_new, out_row_mean, out_cols_new, factors[2])
        gate_up_new = stepped(
            own_share(gate_up_weight, 1), gateup_part, gateup_rows_new, gateup_row_mean, gateup_cols_new, factors[3]
        )
        down_new = stepped(
            own_share(down_weight, 1), down_part, down_rows_new, down_row_mean, down_cols_new, factors[4]
        )
    return (
        block_out,
        input_grad,
        update_rms,
        gains_update,
        gain_moment_new,
        qkv_new,
        qkv_rows_new,
        qkv_cols_new,
        out_new,
        out_rows_new,
        out_cols_new,
        gate_up_new,
        gateup_rows_new,
        gateup_cols_new,
        down_new,
        down_rows_new,
        down_cols_new,
    )


def solution(mesh):
    placed = (
        P(("dp", "expert"), None),
        P(("dp", "expert"), None),
        P(("dp", "expert")),
        P(("dp", "expert")),
        P(("dp", "expert")),
        P(("dp", "expert"), None),
        P(("dp", "expert"), None),
        P(),
        P(),
        P(),
        P("expert", None, None),
        P("expert", None, None),
        P(),
        P(),
        P(),
        P(),
        P(),
        P("expert", None),
        P("expert", None),
        P("expert", None),
        P("expert", None),
    )
    return jax.shard_map(
        per_device,
        mesh=mesh,
        in_specs=placed,
        out_specs=(
            P(("dp", "expert"), None),
            P(("dp", "expert"), None),
            P(),
            P(None, "dp"),
            P(None, "dp"),
            P("dp", None),
            P("dp"),
            P(),
            P("dp", None),
            P("dp"),
            P(),
            P("expert", "dp", None),
            P("expert", "dp"),
            P("expert", None),
            P("expert", "dp", None),
            P("expert", "dp"),
            P("expert", None),
        ),
        check_vma=False,
    )
```

```python
import functools
import math

import jax
import jax.numpy as jnp
from jax import lax
from jax.experimental import pallas as pl
from jax.experimental.pallas import tpu as pltpu
from jax.sharding import PartitionSpec as P

VM = 60 * 1024 * 1024
SCALE = 1e6


def lasts(microseconds):
    return pl.CostEstimate(
        flops=int(microseconds * SCALE), bytes_accessed=1024, transcendentals=0
    )


def dot(a, b, ca=1, cb=0):
    return lax.dot_general(a, b, (((ca,), (cb,)), ((), ())), preferred_element_type=jnp.float32)


def one_hot(code, capacity):
    count, rows = code.shape
    place = lax.broadcasted_iota(jnp.int32, (capacity, rows), 0).astype(jnp.float32)
    return [place == code[j : j + 1, :] for j in range(count)]


def expert_kernel(j, owners, tiles, waits, s_ref, rec_hbm, arr_hbm, scale_ref, up_hbm, down_hbm, *refs):
    (keep_hbm, give_hbm, back_hbm, mix_hbm,
     rec_s, arr_s, up_s, down_s, act_s, gug_s, wg_s, wd_s, parts_s, out_s, in_sem, out_sem) = refs[waits:]
    rows, ff = act_s.shape
    width = up_s.shape[0]
    sources, capacity = rec_s.shape[0], rec_s.shape[1]
    tile = rows // tiles
    per = sources // tiles

    def load(src, dst, at):
        copy = pltpu.make_async_copy(src, dst, in_sem.at[at])
        copy.start()
        return copy

    def load_rows(hbm, held, t, at):
        span = slice(t * per, (t + 1) * per)
        return load(hbm.at[j, span], held.at[span], at)

    expert = s_ref[0] + j
    rec_in = [load_rows(rec_hbm, rec_s, 0, 0)]
    up_in = load(up_hbm.at[expert], up_s, 2 * tiles)
    arr_in = [load_rows(arr_hbm, arr_s, 0, tiles)]
    down_in = load(down_hbm.at[expert], down_s, 2 * tiles + 1)
    for t in range(1, tiles):
        rec_in.append(load_rows(rec_hbm, rec_s, t, t))
        arr_in.append(load_rows(arr_hbm, arr_s, t, tiles + t))
    def products(t):
        span = slice(t * per, (t + 1) * per)
        return (
            dot(rec_s[span].reshape(tile, width), up_s[...]),
            dot(arr_s[span].reshape(tile, width), down_s[...], 1, 1),
        )

    for copy in (up_in, down_in, rec_in[0], arr_in[0]):
        copy.wait()
    following = products(0)
    for t in range(tiles):
        at = slice(t * tile, (t + 1) * tile)
        gate_up, act_grad = following
        if t + 1 < tiles:
            rec_in[t + 1].wait()
            arr_in[t + 1].wait()
            following = products(t + 1)
        gate = gate_up[:, :ff]
        up = gate_up[:, ff:]
        sig = 1.0 / (1.0 + jnp.exp(-gate))
        silu = gate * sig
        act_s[at, :] = (silu * up).astype(jnp.bfloat16)
        gug_s[at, :ff] = (act_grad * up * sig * (1.0 + gate * (1.0 - sig))).astype(jnp.bfloat16)
        gug_s[at, ff:] = (act_grad * silu).astype(jnp.bfloat16)
    wg_s[...] = dot(rec_s[...].reshape(rows, width), gug_s[...], 0, 0)
    wd_s[...] = dot(act_s[...], arr_s[...].reshape(rows, width), 0, 0)
    bit = s_ref[1]
    up_rows = width // owners
    down_rows = ff // owners
    leaving = []
    for k, (hbm, side) in enumerate(((give_hbm, 1 - bit), (keep_hbm, bit))):
        for slot in range(owners // 2):
            owner = 2 * slot + side
            parts_s[k, slot, :up_rows, :] = wg_s[
                pl.ds(pl.multiple_of(owner * up_rows, up_rows), up_rows), :
            ].astype(jnp.bfloat16)
            parts_s[k, slot, up_rows:, :] = wd_s[
                pl.ds(pl.multiple_of(owner * down_rows, down_rows), down_rows), :
            ].astype(jnp.bfloat16)
        copy = pltpu.make_async_copy(parts_s.at[k], hbm, out_sem.at[k])
        copy.start()
        leaving.append(copy)
    for t in range(tiles):
        at = slice(t * tile, (t + 1) * tile)
        out_s[0, at] = dot(gug_s[at, :], up_s[...], 1, 1).astype(jnp.bfloat16)
        scale = scale_ref[0, t * per : (t + 1) * per].reshape(tile, 1)
        out_s[1, at] = (dot(act_s[at, :], down_s[...]) * scale).astype(jnp.bfloat16)
        for k, hbm in enumerate((back_hbm, mix_hbm)):
            copy = pltpu.make_async_copy(out_s.at[k, at], hbm.at[at], out_sem.at[2 + 2 * t + k])
            copy.start()
            leaving.append(copy)
    for copy in leaving:
        copy.wait()


def run_expert(scalars, j, received, arrived, scale, up_w, down_w, owners, after=()):
    count, sources, capacity, width = received.shape
    ff = down_w.shape[1]
    rows = sources * capacity
    tiles = 2
    share = (owners // 2, (width + ff) // owners, width)
    slots = jax.ShapeDtypeStruct((rows, width), jnp.bfloat16)
    parts = jax.ShapeDtypeStruct(share, jnp.bfloat16)
    anywhere = pl.BlockSpec(memory_space=pl.ANY)
    return pl.pallas_call(
        functools.partial(expert_kernel, j, owners, tiles, len(after)),
        out_shape=(parts, parts, slots, slots),
        grid_spec=pltpu.PrefetchScalarGridSpec(
            num_scalar_prefetch=1,
            grid=(1,),
            in_specs=[
                anywhere,
                anywhere,
                pl.BlockSpec((1, sources, capacity, 1), lambda g, s: (j, 0, 0, 0)),
                anywhere,
                anywhere,
            ]
            + [anywhere] * len(after),
            out_specs=[anywhere] * 4,
            scratch_shapes=[
                pltpu.VMEM((sources, capacity, width), jnp.bfloat16),
                pltpu.VMEM((sources, capacity, width), jnp.bfloat16),
                pltpu.VMEM((width, 2 * ff), jnp.bfloat16),
                pltpu.VMEM((ff, width), jnp.bfloat16),
                pltpu.VMEM((rows, ff), jnp.bfloat16),
                pltpu.VMEM((rows, 2 * ff), jnp.bfloat16),
                pltpu.VMEM((width, 2 * ff), jnp.float32),
                pltpu.VMEM((ff, width), jnp.float32),
                pltpu.VMEM((2,) + share, jnp.bfloat16),
                pltpu.VMEM((2, rows, width), jnp.bfloat16),
                pltpu.SemaphoreType.DMA((2 * tiles + 2,)),
                pltpu.SemaphoreType.DMA((2 + 2 * tiles,)),
            ],
        ),
        compiler_params=pltpu.CompilerParams(vmem_limit_bytes=VM),
        cost_estimate=lasts(18),
        name="expert_%d" % j,
    )(scalars, received, arrived, scale, up_w, down_w, *after)


HEADS = 16
KV_HEADS = 8
HEAD_DIM = 64
EPS_NORM = 1e-06
ROPE_BASE = 10000.0
MASKED = -1e30
LANES = 128


def spread(row):
    rows = row.shape[1]
    by_column = jnp.broadcast_to(row.astype(jnp.float32), (rows, rows))
    return by_column, by_column.T


def mask_and_angles(ids_ref):
    seg_k, seg_q = spread(ids_ref[0:1, :])
    par_k, par_q = spread(ids_ref[1:2, :])
    pos_k, pos_q = spread(ids_ref[2:3, :])
    seen = ((seg_k == seg_q) | (seg_k == par_q) | (seg_k == par_k)) & (pos_k <= pos_q)
    bias = jnp.where(seen, 0.0, MASKED)
    lane = lax.broadcasted_iota(jnp.int32, (seg_k.shape[0], LANES), 1)
    half = HEAD_DIM // 2
    place = lax.rem(lane, half).astype(jnp.float32)
    frequency = jnp.exp(place * (-2.0 * math.log(ROPE_BASE) / HEAD_DIM))
    angles = pos_q[:, :LANES] * frequency
    front = lax.rem(lane, HEAD_DIM) < half
    sine = jnp.sin(angles)
    return bias, jnp.cos(angles), jnp.where(front, -sine, sine), front, lane


def turned(block, cosine, sine, front):
    other = jnp.where(
        front,
        pltpu.roll(block, LANES - HEAD_DIM // 2, 1),
        pltpu.roll(block, HEAD_DIM // 2, 1),
    )
    return block * cosine + other * sine


def two_diagonal(pair, which, lane):
    rolled = pltpu.roll(pair, HEAD_DIM, 1)
    first, last = (pair, rolled) if which == 0 else (rolled, pair)
    low = lane < HEAD_DIM
    return jnp.concatenate(
        [jnp.where(low, first, 0.0), jnp.where(low, 0.0, last)], axis=0
    ).astype(jnp.bfloat16)


def column_block(index):
    return pl.ds(pl.multiple_of(index * LANES, LANES), LANES)


def attend_kernel(hidden_ref, ids_ref, gains_ref, qkv_w_hbm, out_w_hbm,
                  normed_hbm, qkv_hbm, attended_hbm, lse_ref, middle_ref, normed_f_ref,
                  normed_ref, qkv_ref, attended_ref, qkv_w_ref, out_w_ref, proj_s, bias_s, sem):
    moving = [
        pltpu.make_async_copy(src, dst, sem.at[i])
        for i, (src, dst) in enumerate(
            (
                (qkv_w_hbm, qkv_w_ref),
                (out_w_hbm, out_w_ref),
                (normed_ref, normed_hbm),
                (qkv_ref, qkv_hbm),
                (attended_ref, attended_hbm),
            )
        )
    ]
    moving[0].start()
    moving[1].start()
    rows = hidden_ref.shape[0]
    att = HEADS * HEAD_DIM
    kv = KV_HEADS * HEAD_DIM
    hidden = hidden_ref[...]
    gains = gains_ref[...].astype(jnp.float32)
    inverse = lax.rsqrt(jnp.mean(hidden * hidden, axis=-1, keepdims=True) + EPS_NORM)
    normed_ref[...] = (hidden * inverse * gains[0:1, :]).astype(jnp.bfloat16)
    moving[2].start()
    bias, cosine, sine, front, lane = mask_and_angles(ids_ref)
    bias_s[...] = bias
    moving[0].wait()
    proj_s[...] = dot(normed_ref[...], qkv_w_ref[...])
    lse_ref[...] = jnp.zeros_like(lse_ref)

    def pair_step(p, carry):
        key_at = column_block(att // LANES + p)
        value_at = column_block((att + kv) // LANES + p)
        keys = turned(proj_s[:, key_at], cosine, sine, front).astype(jnp.bfloat16)
        values = proj_s[:, value_at].astype(jnp.bfloat16)
        qkv_ref[:, key_at] = keys
        qkv_ref[:, value_at] = values
        keys = keys.astype(jnp.float32)
        values = values.astype(jnp.float32)
        for which in range(2):
            query_at = column_block(2 * p + which)
            queries = turned(proj_s[:, query_at], cosine, sine, front).astype(jnp.bfloat16)
            queries = (queries.astype(jnp.float32) * HEAD_DIM**-0.5).astype(jnp.bfloat16)
            qkv_ref[:, query_at] = queries
            scores = dot(queries, two_diagonal(keys, which, lane), 1, 1)
            probs = []
            for head in range(2):
                part = scores[:, head * rows : (head + 1) * rows] + bias_s[...]
                top = jnp.max(part, axis=-1, keepdims=True)
                part = jnp.exp(part - top)
                total = jnp.sum(part, axis=-1, keepdims=True)
                probs.append((part * (1.0 / total)).astype(jnp.bfloat16))
                at = 4 * p + 2 * which + head
                lse_ref[...] = jnp.where(lane == at, top + jnp.log(total), lse_ref[...])
            attended_ref[:, query_at] = dot(
                jnp.concatenate(probs, axis=1), two_diagonal(values, which, lane)
            ).astype(jnp.bfloat16)
        return carry

    lax.fori_loop(0, KV_HEADS // 2, pair_step, 0, unroll=True)
    moving[3].start()
    moving[4].start()
    moving[1].wait()
    middle = hidden + dot(attended_ref[...], out_w_ref[...])
    middle_ref[...] = middle
    inverse_f = lax.rsqrt(jnp.mean(middle * middle, axis=-1, keepdims=True) + EPS_NORM)
    normed_f_ref[...] = (middle * inverse_f * gains[1:2, :]).astype(jnp.bfloat16)
    for copy in moving[2:]:
        copy.wait()


def attend(hidden, ids, gains, qkv_w, out_w):
    rows, width = hidden.shape
    shape = jax.ShapeDtypeStruct
    return pl.pallas_call(
        attend_kernel,
        out_shape=(
            shape((rows, width), jnp.bfloat16),
            shape((rows, qkv_w.shape[1]), jnp.bfloat16),
            shape((rows, out_w.shape[0]), jnp.bfloat16),
            shape((rows, LANES), jnp.float32),
            shape((rows, width), jnp.float32),
            shape((rows, width), jnp.bfloat16),
        ),
        in_specs=[pl.BlockSpec(memory_space=pltpu.VMEM)] * 3 + [pl.BlockSpec(memory_space=pl.ANY)] * 2,
        out_specs=[pl.BlockSpec(memory_space=pl.ANY)] * 3 + [pl.BlockSpec(memory_space=pltpu.VMEM)] * 3,
        scratch_shapes=[
            pltpu.VMEM((rows, width), jnp.bfloat16),
            pltpu.VMEM((rows, qkv_w.shape[1]), jnp.bfloat16),
            pltpu.VMEM((rows, out_w.shape[0]), jnp.bfloat16),
            pltpu.VMEM(qkv_w.shape, jnp.bfloat16),
            pltpu.VMEM(out_w.shape, jnp.bfloat16),
            pltpu.VMEM((rows, qkv_w.shape[1]), jnp.float32),
            pltpu.VMEM((rows, rows), jnp.float32),
            pltpu.SemaphoreType.DMA((5,)),
        ],
        compiler_params=pltpu.CompilerParams(vmem_limit_bytes=VM),
        cost_estimate=lasts(18),
        name="attend",
    )(hidden, ids, gains, qkv_w, out_w)


def attend_back_kernel(waits, grad_ref, middle_ref, normed_grad_ref, lse_ref, ids_ref, gains_ref,
                       hidden_hbm, normed_hbm, qkv_hbm, attended_hbm, qkv_w_hbm, out_w_hbm, *refs):
    (input_grad_ref, dense_hbm, dense_ref, hidden_ref, normed_ref, qkv_ref, attended_ref, qkv_w_ref, out_w_ref,
     proj_s, bias_s, back_s, sem) = refs[waits:]
    rows, width = hidden_ref.shape
    incoming = {
        name: pltpu.make_async_copy(src, dst, sem.at[i])
        for i, (name, src, dst) in enumerate(
            (
                ("attended", attended_hbm, attended_ref),
                ("out_w", out_w_hbm, out_w_ref),
                ("qkv", qkv_hbm, qkv_ref),
                ("normed", normed_hbm, normed_ref),
                ("qkv_w", qkv_w_hbm, qkv_w_ref),
                ("hidden", hidden_hbm, hidden_ref),
            )
        )
    }
    for copy in incoming.values():
        copy.start()
    leaving = []

    def leave(span):
        copy = pltpu.make_async_copy(dense_ref.at[:, span], dense_hbm.at[:, span], sem.at[6 + len(leaving)])
        copy.start()
        leaving.append(copy)

    att = HEADS * HEAD_DIM
    kv = KV_HEADS * HEAD_DIM
    gains = gains_ref[...].astype(jnp.float32)
    normed_grad = normed_grad_ref[...]
    middle = middle_ref[...]
    inverse_f = lax.rsqrt(jnp.mean(middle * middle, axis=-1, keepdims=True) + EPS_NORM)
    gain_f = jnp.sum(normed_grad * middle * inverse_f, axis=0, keepdims=True)
    weighted = normed_grad * gains[1:2, :]
    middle_grad = grad_ref[...] + (
        inverse_f * weighted
        - middle * (inverse_f * inverse_f * inverse_f)
        * jnp.mean(weighted * middle, axis=-1, keepdims=True)
    )
    input_grad_ref[...] = middle_grad
    branch = middle_grad.astype(jnp.bfloat16)
    columns = att + 2 * kv
    incoming["attended"].wait()
    dense_ref[:, columns : columns + width] = dot(attended_ref[...], branch, 0, 0).astype(jnp.bfloat16)
    leave(slice(columns, columns + width))
    incoming["out_w"].wait()
    back_s[...] = dot(branch, out_w_ref[...], 1, 1).astype(jnp.bfloat16)
    bias, cosine, sine, front, lane = mask_and_angles(ids_ref)
    bias_s[...] = bias
    low = lane < HEAD_DIM
    incoming["qkv"].wait()

    def pair_step(p, carry):
        key_at = column_block(att // LANES + p)
        value_at = column_block((att + kv) // LANES + p)
        keys = qkv_ref[:, key_at].astype(jnp.float32)
        values = qkv_ref[:, value_at].astype(jnp.float32)
        key_grads = []
        value_grads = []
        for which in range(2):
            query_at = column_block(2 * p + which)
            queries = qkv_ref[:, query_at]
            back = back_s[:, query_at]
            key_two = two_diagonal(keys, which, lane)
            scores = dot(queries, key_two, 1, 1)
            prob_grads = dot(back, two_diagonal(values, which, lane), 1, 1)
            probs = []
            score_grads = []
            for head in range(2):
                at = 4 * p + 2 * which + head
                level = jnp.sum(jnp.where(lane == at, lse_ref[...], 0.0), axis=-1, keepdims=True)
                span = slice(head * rows, (head + 1) * rows)
                prob = jnp.exp(scores[:, span] + bias_s[...] - level)
                prob_grad = prob_grads[:, span]
                row_dot = jnp.sum(prob * prob_grad, axis=-1, keepdims=True)
                probs.append(prob.astype(jnp.bfloat16))
                score_grads.append((prob * (prob_grad - row_dot)).astype(jnp.bfloat16))
            score_grads = jnp.concatenate(score_grads, axis=1)
            query_grad = dot(score_grads, key_two) * HEAD_DIM**-0.5
            proj_s[:, query_at] = turned(query_grad, cosine, -sine, front).astype(jnp.bfloat16)
            for grads, left, right in (
                (key_grads, score_grads, queries),
                (value_grads, jnp.concatenate(probs, axis=1), back),
            ):
                both = dot(left, right, 0, 0)
                first, last = both[:rows], both[rows:]
                if which == 0:
                    grads.append(first + pltpu.roll(last, HEAD_DIM, 1))
                else:
                    grads.append(pltpu.roll(first, HEAD_DIM, 1) + last)
        key_grad = jnp.where(low, key_grads[0], key_grads[1])
        proj_s[:, key_at] = turned(key_grad, cosine, -sine, front).astype(jnp.bfloat16)
        proj_s[:, value_at] = jnp.where(low, value_grads[0], value_grads[1]).astype(jnp.bfloat16)
        return carry

    lax.fori_loop(0, KV_HEADS // 2, pair_step, 0)
    for name in ("normed", "qkv_w", "hidden"):
        incoming[name].wait()
    for first in range(0, columns, columns // 2):
        span = slice(first, first + columns // 2)
        dense_ref[:, span] = dot(normed_ref[...], proj_s[:, span], 0, 0).astype(jnp.bfloat16)
        leave(span)
    normed_grad = dot(proj_s[...], qkv_w_ref[...], 1, 1)
    hidden = hidden_ref[...]
    inverse = lax.rsqrt(jnp.mean(hidden * hidden, axis=-1, keepdims=True) + EPS_NORM)
    gain_a = jnp.sum(normed_grad * hidden * inverse, axis=0, keepdims=True)
    weighted = normed_grad * gains[0:1, :]
    input_grad_ref[...] += inverse * weighted - hidden * (inverse * inverse * inverse) * jnp.mean(
        weighted * hidden, axis=-1, keepdims=True
    )
    both = jnp.concatenate([gain_a, gain_f, jnp.zeros((LANES - 2, width), jnp.float32)], axis=0)
    dense_ref[:, columns + width :] = both.T.astype(jnp.bfloat16)
    leave(slice(columns + width, columns + width + LANES))
    for copy in leaving:
        copy.wait()


def attend_back(hidden, out_grad, middle, normed_f_grad, normed, qkv, attended, lse, ids, gains, qkv_w, out_w, after=()):
    rows, width = hidden.shape
    columns = qkv_w.shape[1] + width + LANES
    return pl.pallas_call(
        functools.partial(attend_back_kernel, len(after)),
        out_shape=(
            jax.ShapeDtypeStruct((rows, width), jnp.float32),
            jax.ShapeDtypeStruct((width, columns), jnp.bfloat16),
        ),
        in_specs=[pl.BlockSpec(memory_space=pltpu.VMEM)] * 6
        + [pl.BlockSpec(memory_space=pl.ANY)] * (6 + len(after)),
        out_specs=[pl.BlockSpec(memory_space=pltpu.VMEM), pl.BlockSpec(memory_space=pl.ANY)],
        scratch_shapes=[
            pltpu.VMEM((width, columns), jnp.bfloat16),
            pltpu.VMEM((rows, width), jnp.float32),
            pltpu.VMEM((rows, width), jnp.bfloat16),
            pltpu.VMEM((rows, qkv_w.shape[1]), jnp.bfloat16),
            pltpu.VMEM((rows, out_w.shape[0]), jnp.bfloat16),
            pltpu.VMEM(qkv_w.shape, jnp.bfloat16),
            pltpu.VMEM(out_w.shape, jnp.bfloat16),
            pltpu.VMEM((rows, qkv_w.shape[1]), jnp.bfloat16),
            pltpu.VMEM((rows, rows), jnp.float32),
            pltpu.VMEM((rows, out_w.shape[0]), jnp.bfloat16),
            pltpu.SemaphoreType.DMA((10,)),
        ],
        compiler_params=pltpu.CompilerParams(vmem_limit_bytes=VM),
        cost_estimate=lasts(26),
        name="attend_back",
    )(out_grad, middle, normed_f_grad, lse, ids, gains, hidden, normed, qkv, attended, qkv_w, out_w, *after)


MESH = pl.DeviceIdType.MESH


def greet(peers):
    barrier = pltpu.get_barrier_semaphore()
    for peer in peers:
        pl.semaphore_signal(barrier, inc=1, device_id=peer, device_id_type=MESH)
    pl.semaphore_wait(barrier, len(peers))


def total_kernel(axis, count, mine_ref, *refs):
    out_ref, got_ref, send_sem, recv_sem = refs[-4:]
    me = lax.axis_index(axis)
    after = [lax.rem(me + k, count) for k in range(count)]
    greet([{axis: after[k]} for k in range(1, count)])
    scatter = [
        pltpu.make_async_remote_copy(
            src_ref=mine_ref.at[after[k]],
            dst_ref=got_ref.at[k],
            send_sem=send_sem.at[0, k],
            recv_sem=recv_sem.at[0, k],
            device_id={axis: after[k]},
            device_id_type=MESH,
        )
        for k in range(1, count)
    ]
    for copy in scatter:
        copy.start()
    total = mine_ref[me]
    for k in range(1, count):
        scatter[k - 1].wait_recv()
        total = total + got_ref[k]
    out_ref[me] = total
    share = [
        pltpu.make_async_remote_copy(
            src_ref=out_ref.at[me],
            dst_ref=out_ref.at[me],
            send_sem=send_sem.at[1, k],
            recv_sem=recv_sem.at[1, k],
            device_id={axis: after[k]},
            device_id_type=MESH,
        )
        for k in range(1, count)
    ]
    for copy in share:
        copy.start()
    for copy in share:
        copy.wait_recv()
    for copy in scatter + share:
        copy.wait_send()


def total_over(values, axis, label, after=()):
    count = lax.axis_size(axis)
    rows = -(-values.shape[0] // (8 * 128 * count)) * 8
    padded = jnp.pad(values, (0, count * rows * 128 - values.shape[0])).reshape(count, rows, 128)
    out = pl.pallas_call(
        functools.partial(total_kernel, axis, count),
        out_shape=jax.ShapeDtypeStruct(padded.shape, jnp.float32),
        in_specs=[pl.BlockSpec(memory_space=pltpu.VMEM)] + [pl.BlockSpec(memory_space=pl.ANY)] * len(after),
        out_specs=pl.BlockSpec(memory_space=pltpu.VMEM),
        scratch_shapes=[
            pltpu.VMEM(padded.shape, jnp.float32),
            pltpu.SemaphoreType.DMA((2, count)),
            pltpu.SemaphoreType.DMA((2, count)),
        ],
        compiler_params=pltpu.CompilerParams(
            collective_id=label, has_side_effects=True, vmem_limit_bytes=16 * 1024 * 1024
        ),
        cost_estimate=lasts(12),
        name="total_%d" % label,
    )(padded, *after)
    return out.reshape(-1)[: values.shape[0]]


def collect_kernel(axis, count, mine_ref, out_ref, send_sem, recv_sem, local_sem):
    me = lax.axis_index(axis)
    after = [lax.rem(me + k, count) for k in range(count)]
    greet([{axis: after[k]} for k in range(1, count)])
    copies = [
        pltpu.make_async_remote_copy(
            src_ref=mine_ref,
            dst_ref=out_ref.at[me],
            send_sem=send_sem.at[k],
            recv_sem=recv_sem.at[k],
            device_id={axis: after[k]},
            device_id_type=MESH,
        )
        for k in range(1, count)
    ]
    for copy in copies:
        copy.start()
    out_ref[me] = mine_ref[...]
    for copy in copies:
        copy.wait()


def collect(values, axis, label):
    count = lax.axis_size(axis)
    return pl.pallas_call(
        functools.partial(collect_kernel, axis, count),
        out_shape=jax.ShapeDtypeStruct((count,) + values.shape, jnp.float32),
        in_specs=[pl.BlockSpec(memory_space=pltpu.VMEM)],
        out_specs=pl.BlockSpec(memory_space=pltpu.VMEM),
        scratch_shapes=[
            pltpu.SemaphoreType.DMA((count,)),
            pltpu.SemaphoreType.DMA((count,)),
            pltpu.SemaphoreType.DMA,
        ],
        compiler_params=pltpu.CompilerParams(
            collective_id=label, has_side_effects=True, vmem_limit_bytes=16 * 1024 * 1024
        ),
        cost_estimate=lasts(4),
        name="collect_%d" % label,
    )(values)


def flipped(axis, mask):
    index = lax.axis_index(axis)
    bit = lax.rem(index // mask, 2)
    return bit, {axis: index + mask - 2 * mask * bit}


PAIR = 2
ROUTE_ROWS = 32


class Pusher:
    def __init__(self, send_sem, recv_sem):
        self.send_sem, self.recv_sem, self.copies = send_sem, recv_sem, []

    def __call__(self, src, dst, peer):
        at = len(self.copies)
        copy = pltpu.make_async_remote_copy(
            src_ref=src,
            dst_ref=dst,
            send_sem=self.send_sem.at[at],
            recv_sem=self.recv_sem.at[at],
            device_id=peer,
            device_id_type=MESH,
        )
        copy.start()
        self.copies.append(copy)
        return copy

    def finish(self):
        for copy in self.copies:
            copy.wait_send()


def picked(code, capacity):
    return jnp.concatenate(
        [c.astype(jnp.float32) for c in one_hot(code, capacity)], axis=0
    ).astype(jnp.bfloat16)


def gather_kernel(capacity, experts_here, half_experts, top, token_ref, grad_ref, chip_grad_ref, pair_grad_ref,
                  rec_ref, arr_ref, scale_ref, code_ref, tokens, grads, weight_s, stage, send_sem, recv_sem, local_sem):
    rows = token_ref.shape[0]
    half = rows // 2
    first = lax.axis_index("expert") * experts_here + lax.rem(lax.axis_index("dp") // PAIR, 2) * half_experts
    _, core = flipped("expert", 1)
    _, chip = flipped("expert", 2)
    _, pair = flipped("dp", PAIR)
    greet([core, chip, pair])
    push = Pusher(send_sem, recv_sem)
    everything, routing = slice(None), slice(rows, rows + ROUTE_ROWS)
    to_chip = push(token_ref, tokens.at[2], chip)
    to_pair = push(token_ref, tokens.at[4], pair)
    route_both = push(pair_grad_ref.at[routing], grads.at[6, routing], chip)
    to_core = push(token_ref, tokens.at[1], core)
    grad_core = push(grad_ref, grads.at[1], core)
    grad_chip_core = push(chip_grad_ref, grads.at[3], core)
    grad_pair_core = push(pair_grad_ref, grads.at[5], core)

    earlier = lax.broadcasted_iota(jnp.int32, (rows, rows), 0)
    later = lax.broadcasted_iota(jnp.int32, (rows, rows), 1)
    before = jnp.where(earlier < later, 1.0, 0.0).astype(jnp.bfloat16)

    def route(r, table):
        table = table.astype(jnp.float32)
        ids = table[:top]
        gates = table[top : 2 * top] + table[2 * top : 3 * top]
        hits = [ids == (first + j).astype(jnp.float32) for j in range(half_experts)]
        named = jnp.concatenate(
            [jnp.max(jnp.where(hit, 1.0, 0.0), axis=0, keepdims=True) for hit in hits], axis=0
        )
        weight_s[r] = jnp.concatenate(
            [jnp.sum(jnp.where(hit, gates, 0.0), axis=0, keepdims=True) for hit in hits], axis=0
        )
        code_ref[r] = jnp.where(named > 0.0, dot(named.astype(jnp.bfloat16), before), -1.0)

    leaving = []

    def select(r, source, out_ref, weighted):
        slot = len(leaving) % stage.shape[0]
        if len(leaving) >= stage.shape[0]:
            leaving[len(leaving) - stage.shape[0]].wait()
        chosen = one_hot(code_ref[r], capacity)
        pick = jnp.concatenate([c.astype(jnp.float32) for c in chosen], axis=0).astype(jnp.bfloat16)
        made = dot(pick, source)
        for j in range(half_experts):
            part = made[j * capacity : (j + 1) * capacity]
            if weighted:
                scale = jnp.sum(
                    jnp.where(chosen[j], weight_s[r, j : j + 1, :], 0.0), axis=1, keepdims=True
                )
                scale_ref[j, r] = scale
                part = part * scale
            stage[slot, j] = part.astype(jnp.bfloat16)
        copy = pltpu.make_async_copy(stage.at[slot], out_ref.at[:, r], local_sem.at[slot])
        copy.start()
        leaving.append(copy)

    def select_grad(r, ref):
        route(r, ref[rows:, :rows])
        select(r, ref[:rows, :], arr_ref, True)

    select_grad(0, grad_ref)
    select(0, token_ref[...], rec_ref, False)
    select_grad(2, chip_grad_ref)
    select_grad(4, pair_grad_ref)
    for r, copy in ((1, grad_core), (3, grad_chip_core), (5, grad_pair_core)):
        copy.wait_recv()
        select_grad(r, grads.at[r])
    to_core.wait_recv()
    select(1, tokens[1], rec_ref, False)
    route_both.wait_recv()
    route_core = push(grads.at[6, routing], grads.at[7, routing], core)
    to_chip.wait_recv()
    both_low = push(tokens.at[2, half:rows], tokens.at[6, half:rows], pair)
    chip_core = push(tokens.at[2], tokens.at[3], core)
    to_pair.wait_recv()
    both_high = push(tokens.at[4, 0:half], tokens.at[6, 0:half], chip)
    pair_core = push(tokens.at[4], tokens.at[5], core)
    grad_low = push(chip_grad_ref.at[half:rows], grads.at[6, half:rows], pair)
    grad_high = push(pair_grad_ref.at[0:half], grads.at[6, 0:half], chip)
    select(2, tokens[2], rec_ref, False)
    select(4, tokens[4], rec_ref, False)
    route(6, grads[6, rows:, :rows])
    route_core.wait_recv()
    route(7, grads[7, rows:, :rows])
    chip_core.wait_recv()
    select(3, tokens[3], rec_ref, False)
    pair_core.wait_recv()
    select(5, tokens[5], rec_ref, False)
    both_low.wait_recv()
    both_high.wait_recv()
    both_core = push(tokens.at[6], tokens.at[7], core)
    select(6, tokens[6], rec_ref, False)
    both_core.wait_recv()
    select(7, tokens[7], rec_ref, False)
    grad_low.wait_recv()
    grad_high.wait_recv()
    grad_both_core = push(grads.at[6, 0:rows], grads.at[7, 0:rows], core)
    select(6, grads[6, :rows], arr_ref, True)
    grad_both_core.wait_recv()
    select(7, grads[7, :rows], arr_ref, True)
    for copy in leaving[-stage.shape[0] :]:
        copy.wait()
    push.finish()


def gather_and_select(token, grad, chip_grad, pair_grad, capacity, experts_here, half_experts, top, label):
    rows, width = token.shape
    vmem = pl.BlockSpec(memory_space=pltpu.VMEM)
    anywhere = pl.BlockSpec(memory_space=pl.ANY)
    slots = jax.ShapeDtypeStruct((half_experts, 8, capacity, width), jnp.bfloat16)
    return pl.pallas_call(
        functools.partial(gather_kernel, capacity, experts_here, half_experts, top),
        out_shape=(
            slots,
            slots,
            jax.ShapeDtypeStruct((half_experts, 8, capacity, 1), jnp.float32),
            jax.ShapeDtypeStruct((8, half_experts, rows), jnp.float32),
        ),
        in_specs=[vmem] * 4,
        out_specs=[anywhere, anywhere, vmem, vmem],
        scratch_shapes=[
            pltpu.VMEM((8, rows, width), jnp.bfloat16),
            pltpu.VMEM((8, rows + ROUTE_ROWS, width), jnp.bfloat16),
            pltpu.VMEM((8, half_experts, rows), jnp.float32),
            pltpu.VMEM((4, half_experts, capacity, width), jnp.bfloat16),
            pltpu.SemaphoreType.DMA((18,)),
            pltpu.SemaphoreType.DMA((18,)),
            pltpu.SemaphoreType.DMA((4,)),
        ],
        compiler_params=pltpu.CompilerParams(
            collective_id=label, has_side_effects=True, vmem_limit_bytes=VM
        ),
        cost_estimate=lasts(44),
        name="gather_and_select",
    )(token, grad, chip_grad, pair_grad)


def fetcher(order, fetched, local_sem, capacity, code_ref):
    depth = fetched.shape[0]
    fetching = []
    done = []

    def fetch():
        n = len(fetching)
        if n < len(order):
            slots, r = order[n]
            fetching.append(
                [
                    pltpu.make_async_copy(
                        ref.at[r * capacity : (r + 1) * capacity],
                        fetched.at[n % depth, j * capacity : (j + 1) * capacity],
                        local_sem.at[n % depth, j],
                    )
                    for j, ref in enumerate(slots)
                ]
            )
            for copy in fetching[-1]:
                copy.start()

    for _ in range(depth - 1):
        fetch()

    def next_sum():
        fetch()
        n = len(done)
        for copy in fetching[n]:
            copy.wait()
        done.append(n)
        return dot(picked(code_ref[order[n][1]], capacity), fetched[n % depth], 0, 0)

    return next_sum


def combine_kernel(capacity, count, code_ref, *refs):
    slots = refs[:count]
    mine_ref, theirs_ref, fetched, local_sem = refs[-4:]
    order = [(slots, r) for r in (7, 6, 3, 2, 5, 4, 1, 0)]
    next_sum = fetcher(order, fetched, local_sem, capacity, code_ref)
    for _, r in order:
        (theirs_ref if r % 2 else mine_ref)[r // 2] = next_sum().astype(jnp.bfloat16)


def combine(code, slots, capacity, after):
    _, count, rows = code.shape
    width = slots[0].shape[1]
    vmem = pl.BlockSpec(memory_space=pltpu.VMEM)
    anywhere = pl.BlockSpec(memory_space=pl.ANY)
    four = jax.ShapeDtypeStruct((4, rows, width), jnp.bfloat16)
    return pl.pallas_call(
        functools.partial(combine_kernel, capacity, count),
        out_shape=(four, four),
        in_specs=[vmem] + [anywhere] * (count + len(after)),
        out_specs=[vmem, vmem],
        scratch_shapes=[
            pltpu.VMEM((4, count * capacity, width), jnp.bfloat16),
            pltpu.SemaphoreType.DMA((4, count)),
        ],
        compiler_params=pltpu.CompilerParams(vmem_limit_bytes=VM),
        cost_estimate=lasts(12),
        name="combine",
    )(code, *slots, *after)


def return_kernel(capacity, count, far_mask, code_ref, mine_ref, theirs_ref, go_ref, *refs):
    mixes = refs[:count]
    (out_ref, near_ref, far_ref, come_ref, fetched, core_got, own, theirs_mix, core_got_mix, half_pair, half_chip, from_chip,
     from_pair, send_sem, recv_sem, local_sem) = refs[-16:]
    rows = out_ref.shape[0]
    half = rows // 2
    _, core = flipped("expert", 1)
    _, chip = flipped("expert", 2)
    _, pair = flipped("dp", PAIR)
    _, far = flipped("dp", far_mask)
    greet([core, chip, pair, far])
    push = Pusher(send_sem, recv_sem)
    beside = push(go_ref, come_ref, far)
    crossing = {i: push(theirs_ref.at[i], core_got.at[i], core) for i in (3, 1, 2, 0)}
    order = [(mixes, r) for r in (7, 6, 3, 2, 5, 4, 1, 0)]
    next_sum = fetcher(order, fetched, local_sem, capacity, code_ref)

    def plus(a, b):
        return (a.astype(jnp.float32) + b.astype(jnp.float32)).astype(jnp.bfloat16)

    def mix(i, ref, at):
        theirs_mix[i] = next_sum().astype(jnp.bfloat16)
        copy = push(theirs_mix.at[i], core_got_mix.at[i], core)
        mine = next_sum()
        copy.wait_recv()
        ref[at] = plus(mine, core_got_mix[i])

    crossing[3].wait_recv()
    own[3] = plus(mine_ref[3], core_got[3])
    at_pair = push(own.at[3, 0:half], half_pair, pair)
    at_chip = push(own.at[3, half:rows], half_chip, chip)
    crossing[1].wait_recv()
    own[1] = plus(mine_ref[1], core_got[1])
    low_chip = push(own.at[1, half:rows], from_chip.at[half:rows], chip)
    crossing[2].wait_recv()
    own[2] = plus(mine_ref[2], core_got[2])
    high_pair = push(own.at[2, 0:half], from_pair.at[0:half], pair)
    crossing[0].wait_recv()
    out_ref[...] = mine_ref[0].astype(jnp.float32) + core_got[0].astype(jnp.float32)
    mix(3, far_ref, 1)
    mix(1, far_ref, 0)
    at_pair.wait_recv()
    own[1, :half] = plus(own[1, :half], half_pair[...])
    high_chip = push(own.at[1, 0:half], from_chip.at[0:half], chip)
    at_chip.wait_recv()
    own[2, half:] = plus(own[2, half:], half_chip[...])
    low_pair = push(own.at[2, half:rows], from_pair.at[half:rows], pair)
    mix(2, near_ref, 1)
    mix(0, near_ref, 0)
    low_chip.wait_recv()
    high_pair.wait_recv()
    high_chip.wait_recv()
    low_pair.wait_recv()
    out_ref[...] += from_chip[...].astype(jnp.float32) + from_pair[...].astype(jnp.float32)
    beside.wait_recv()
    push.finish()


def return_sums(code, mine, theirs, mixes, capacity, go, far_mask, label, after):
    _, count, rows = code.shape
    width = mine.shape[2]
    vmem = pl.BlockSpec(memory_space=pltpu.VMEM)
    anywhere = pl.BlockSpec(memory_space=pl.ANY)
    four = pltpu.VMEM((4, rows, width), jnp.bfloat16)
    two = jax.ShapeDtypeStruct((2, rows, width), jnp.bfloat16)
    return pl.pallas_call(
        functools.partial(return_kernel, capacity, count, far_mask),
        out_shape=(
            jax.ShapeDtypeStruct((rows, width), jnp.float32),
            two,
            two,
            jax.ShapeDtypeStruct(go.shape, jnp.bfloat16),
        ),
        in_specs=[vmem] * 3 + [anywhere] * (1 + count + len(after)),
        out_specs=[vmem] * 3 + [anywhere],
        scratch_shapes=[pltpu.VMEM((4, count * capacity, width), jnp.bfloat16), four, four, four, four]
        + [pltpu.VMEM((rows // 2, width), jnp.bfloat16)] * 2
        + [pltpu.VMEM((rows, width), jnp.bfloat16)] * 2
        + [
            pltpu.SemaphoreType.DMA((15,)),
            pltpu.SemaphoreType.DMA((15,)),
            pltpu.SemaphoreType.DMA((4, count)),
        ],
        compiler_params=pltpu.CompilerParams(
            collective_id=label, has_side_effects=True, vmem_limit_bytes=VM
        ),
        cost_estimate=lasts(37),
        name="return_sums",
    )(code, mine, theirs, go, *mixes, *after)


def settle_kernel(groups, waits, bits_ref, *refs):
    ins, outs = refs[: 2 * groups], refs[2 * groups + waits : 4 * groups + waits]
    held, sem = refs[-2 * groups - 1 : -1], refs[-1]
    arriving = [pltpu.make_async_copy(ins[i], held[i], sem.at[i]) for i in range(2 * groups)]
    for copy in arriving:
        copy.start()
    for g in range(groups):
        arriving[2 * g].wait()
        arriving[2 * g + 1].wait()
        keep_ref, got_ref, stay_ref, go_ref = held[2 * g], held[2 * g + 1], outs[2 * g], outs[2 * g + 1]
        bit = bits_ref[g]
        for high in range(keep_ref.shape[0]):
            for low in range(keep_ref.shape[2]):
                for ref, side in ((stay_ref, bit), (go_ref, 1 - bit)):
                    total = keep_ref[high, side, low].astype(jnp.float32) + got_ref[
                        high, side, low
                    ].astype(jnp.float32)
                    ref[high, low] = total.astype(jnp.bfloat16)


def settle(groups, label, after, passed=()):
    ins, shapes, outs, bits = [], [], [], []
    for keep, got, mask in groups:
        count, rows, columns = keep.shape
        low = 1 if mask == PAIR else 2
        shapes += [(count // 2 // low, 2, low, rows, columns)] * 2
        ins += [keep.reshape(shapes[-1]), got.reshape(shapes[-1])]
        outs += [jax.ShapeDtypeStruct((count // 2 // low, low, rows, columns), jnp.bfloat16)] * 2
        bits.append(lax.rem(lax.axis_index("dp") // mask, 2))
    waits = len(after) + len(passed)
    vmem = pl.BlockSpec(memory_space=pltpu.VMEM)
    anywhere = pl.BlockSpec(memory_space=pl.ANY)
    made = pl.pallas_call(
        functools.partial(settle_kernel, len(groups), waits),
        out_shape=outs + [jax.ShapeDtypeStruct(p.shape, p.dtype) for p in passed],
        in_specs=[pl.BlockSpec(memory_space=pltpu.SMEM)] + [anywhere] * (len(ins) + waits),
        scratch_shapes=[pltpu.VMEM(shape, jnp.bfloat16) for shape in shapes]
        + [pltpu.SemaphoreType.DMA((len(ins),))],
        out_specs=[vmem] * len(outs) + [anywhere] * len(passed),
        input_output_aliases={1 + len(ins) + len(after) + i: len(outs) + i for i in range(len(passed))},
        compiler_params=pltpu.CompilerParams(vmem_limit_bytes=VM),
        cost_estimate=lasts(3),
        name="settle_%s" % label,
    )(jnp.stack(bits), *ins, *after, *passed)
    sides = [x.reshape((-1,) + x.shape[2:]) for x in made[: len(outs)]]
    return list(zip(sides[::2], sides[1::2])), made[len(outs) :]


def settle_mix_kernel(near_ref, got_ref, *refs):
    refs[-1][...] = (near_ref[1].astype(jnp.float32) + got_ref[1].astype(jnp.float32)).astype(jnp.bfloat16)


def settle_mix(near, got, after):
    vmem = pl.BlockSpec(memory_space=pltpu.VMEM)
    return pl.pallas_call(
        settle_mix_kernel,
        out_shape=jax.ShapeDtypeStruct(near.shape[1:], jnp.bfloat16),
        in_specs=[vmem] * 2 + [pl.BlockSpec(memory_space=pl.ANY)] * len(after),
        out_specs=vmem,
        compiler_params=pltpu.CompilerParams(vmem_limit_bytes=VM),
        cost_estimate=lasts(3),
        name="settle_mix",
    )(near, got, *after)


EPS_STAT = 1e-30
STAT_DECAY = 0.5
LEARN_RATE = 0.5
CLIP_LEVEL = 0.05


def decayed(old, new):
    return STAT_DECAY * old + (1.0 - STAT_DECAY) * new


def finish_kernel(count, groups, half, orders, spans, *refs):
    bits = count.bit_length() - 1
    steps = len(orders[0])
    (mine_hbm, own_0, own_1, got_0, go_1, stay_2, come_2, keep_3, come_3, near_mix_ref, got_mix_ref,
     up_rows_ref, down_rows_ref, up_cols_ref, down_cols_ref, qkv_rows_ref, out_rows_ref, moments_ref, qkv_cols_ref,
     out_cols_ref) = refs[:20]
    (dense_ref, ends_ref, pair_mix_ref, out_ref, sums_ref, up_new_ref, down_new_ref, dense_out_ref,
     dense_new_ref) = refs[20:29]
    sum_ref, first_got, *got = refs[29 : 31 + steps]
    (mine_ref, load_sem, go_s, far_go_s, far_stay_s, far_got_s, mix_s, pay_s, got_s, dense_pay_s, dense_got_s, spread_s,
     up_old_ref, down_old_ref, dense_old_ref, dense_cols_ref, send_sem, recv_sem) = refs[31 + steps :]
    width = up_rows_ref.shape[1]
    ff = down_rows_ref.shape[1]
    wide = width // 2
    own_up = width // count
    own_down = ff // count
    me = lax.axis_index("dp")
    place = lax.axis_index("expert")
    after = [lax.rem(me + k, count) for k in range(count)]
    beside = [lax.rem(place + k, groups) for k in range(groups)]
    pair_bit, pair = flipped("dp", PAIR)
    far_bit, far = flipped("dp", FAR)
    core, core_peer = flipped("expert", 1)
    chip, chip_peer = flipped("expert", 2)
    links = [flipped("dp", 1 << b) for b in range(bits)] + [(chip, chip_peer)]
    whole = (slice(None),) * bits
    loading = pltpu.make_async_copy(mine_hbm.at[whole + (core,)], mine_ref, load_sem)
    loading.start()
    greet([{"dp": after[k]} for k in range(1, count)] + [{"expert": beside[k]} for k in range(1, groups)])
    push = Pusher(send_sem, recv_sem)

    def plus(a, b):
        return (a.astype(jnp.float32) + b.astype(jnp.float32)).astype(jnp.bfloat16)

    flying = [
        push(mine_hbm.at[whole + (1 - core, slice(None), slice(None), span)], first_got.at[..., span], core_peer)
        for span in spans
    ]
    for low in range(2):
        far_go_s[low] = plus(keep_3[1 - far_bit, low], come_3[1 - far_bit, low])
    far_exchange = push(far_go_s, far_got_s, far)
    go_s[0] = plus(stay_2[1 - pair_bit], come_2[1 - pair_bit])
    cross_1 = push(go_1, ends_ref.at[4], pair)
    cross_2 = push(go_s.at[0], ends_ref.at[2], pair)
    mix_s[...] = plus(near_mix_ref[1], got_mix_ref[1])
    cross_mix = push(mix_s, pair_mix_ref, pair)
    ends_ref[0] = plus(stay_2[pair_bit], come_2[pair_bit])
    for low in range(2):
        far_stay_s[low] = plus(keep_3[far_bit, low], come_3[far_bit, low])

    def own_columns(*tables):
        here = pl.ds(pl.multiple_of(me * LANES, LANES), LANES)
        rows = [table[:, here] for table in tables]
        return padded(jnp.concatenate(rows, axis=0)).T

    def padded(rows):
        return jnp.concatenate([rows, jnp.zeros((LANES - rows.shape[0], LANES), jnp.float32)], axis=0)

    up_old_ref[...] = own_columns(up_rows_ref)
    dense_old_ref[...] = own_columns(qkv_rows_ref, out_rows_ref, moments_ref)
    around = down_rows_ref[:, pl.ds(pl.multiple_of(me // 2 * LANES, LANES), LANES)]
    both_halves = padded(around).T
    down_old_ref[...] = jnp.where(lax.rem(me, 2) == 0, both_halves[:own_down], both_halves[own_down:])
    dense_cols_ref[:, : qkv_cols_ref.shape[1]] = qkv_cols_ref[...]
    dense_cols_ref[:, qkv_cols_ref.shape[1] :] = out_cols_ref[...]

    def column_of(table_ref, lane, at):
        return jnp.sum(jnp.where(lane == at, table_ref[...], 0.0), axis=1, keepdims=True)

    up_lane = lax.broadcasted_iota(jnp.int32, (own_up, LANES), 1)
    down_lane = lax.broadcasted_iota(jnp.int32, (own_down, LANES), 1)
    up_new_ref[...] = jnp.zeros_like(up_new_ref)
    down_new_ref[...] = jnp.zeros_like(down_new_ref)

    def factored(grad, old):
        square = grad * grad
        new = decayed(old, jnp.mean(square + EPS_STAT, axis=1, keepdims=True))
        return (
            new,
            jnp.sum(square + EPS_STAT, axis=0, keepdims=True),
            jnp.sum(square * (1.0 / new), axis=0, keepdims=True),
        )

    def expert(values, at):
        for kind, (part, old_ref, new_ref, lane, rows) in enumerate(
            (
                (values[:own_up, :], up_old_ref, up_new_ref, up_lane, own_up),
                (values[own_up:, :], down_old_ref, down_new_ref, down_lane, own_down),
            )
        ):
            new, total, scaled = factored(part.astype(jnp.float32), column_of(old_ref, lane, at))
            new_ref[:rows, :] = jnp.where(lane == at, new, new_ref[:rows, :])
            for h in range(2):
                span = slice(h * wide, (h + 1) * wide)
                pay_s[at, 4 * kind + h : 4 * kind + h + 1, :] = total[:, span]
                pay_s[at, 4 * kind + 2 + h : 4 * kind + 3 + h, :] = scaled[:, span]

    own_at, got_at = pair_bit * half, (1 - pair_bit) * half

    def at_place(chosen, span):
        return tuple(chosen.get(bits - 1 - i, slice(None)) for i in range(bits)) + (
            chosen.get(bits, slice(None)),
            slice(None),
            span,
        )

    def got_place(step, span):
        return (slice(None),) * (steps - 1 - step) + (slice(None), span)

    loading.wait()
    chosen = [{} for _ in spans]
    for step in range(steps + 1):
        for part, span in enumerate(spans):
            flying[part].wait_recv()
            if step == 0:
                sum_ref[..., span] = plus(mine_ref[..., span], first_got[..., span])
            else:
                here = at_place(chosen[part], span)
                sum_ref[here] = plus(sum_ref[here], got[step - 1][got_place(step - 1, span)])
            if step < steps:
                link = orders[part][step]
                bit, peer = links[link]
                away = at_place({**chosen[part], link: 1 - bit}, span)
                flying[part] = push(sum_ref.at[away], got[step].at[got_place(step, span)], peer)
                chosen[part] = {**chosen[part], link: bit}
            else:
                dense_ref[core, chip, :, span] = sum_ref[at_place(chosen[part], span)]
                block = dense_ref.at[core, chip, :, span]
                flying[part] = push(block, block, chip_peer)
        if step == 0:
            expert(own_0, own_at)
            expert(got_0, got_at)
            expert(own_1, own_at + 1)
        elif step == 1:
            expert(ends_ref[0], own_at + 2)
        elif step == steps - 1:
            cross_1.wait_recv()
            expert(ends_ref[4], got_at + 1)
            cross_2.wait_recv()
            expert(ends_ref[2], got_at + 2)
            far_exchange.wait_recv()
            go_s[1] = plus(far_stay_s[1 - pair_bit], far_got_s[1 - pair_bit])
            cross_3 = push(go_s.at[1], ends_ref.at[3], pair)
            ends_ref[1] = plus(far_stay_s[pair_bit], far_got_s[pair_bit])
            expert(ends_ref[1], own_at + 3)
    for part, span in enumerate(spans):
        flying[part].wait_recv()
        block = dense_ref.at[core, :, :, span]
        flying[part] = push(block, block, core_peer)
    cross_3.wait_recv()
    expert(ends_ref[3], got_at + 3)
    arriving = [push(pay_s.at[after[k]], got_s.at[k], {"dp": after[k]}) for k in range(1, count)]
    for copy in flying:
        copy.wait_recv()

    columns = dense_cols_ref.shape[1]
    piece = columns // count
    dense = dense_ref[...].reshape(own_up, dense_ref.shape[3])
    dense_lane = lax.broadcasted_iota(jnp.int32, dense_new_ref.shape, 1)
    old = dense_old_ref[...]
    qkv_columns = columns - width
    totals, scaleds, rows_new = [], [], []
    for at, span in enumerate((slice(0, qkv_columns), slice(qkv_columns, columns))):
        new, total, scaled = factored(
            dense[:, span].astype(jnp.float32), column_of(dense_old_ref, dense_lane, at)
        )
        rows_new.append(new)
        totals.append(total)
        scaleds.append(scaled)
    gain_lanes = (dense_lane == 2) | (dense_lane == 3)
    gains = pltpu.roll(dense[:, columns:].astype(jnp.float32), 2, 1)
    moments = jnp.where(gain_lanes, decayed(old, gains * gains + EPS_STAT), 1.0)
    gain_steps = jnp.where(gain_lanes, gains * lax.rsqrt(moments), 0.0)
    dense_new_ref[...] = jnp.where(
        dense_lane == 0,
        rows_new[0],
        jnp.where(dense_lane == 1, rows_new[1], jnp.where(gain_lanes, gain_steps, pltpu.roll(moments, 2, 1))),
    )
    gain_squares = jnp.sum(jnp.sum(gain_steps * gain_steps, axis=1, keepdims=True), axis=0, keepdims=True)
    total = jnp.concatenate(totals, axis=1)
    scaled = jnp.concatenate(scaleds, axis=1)
    for d in range(count):
        span = slice(d * piece, (d + 1) * piece)
        dense_pay_s[d] = jnp.concatenate(
            [total[:, span], scaled[:, span], jnp.broadcast_to(gain_squares, (1, piece)), jnp.zeros((5, piece), jnp.float32)],
            axis=0,
        )
    dense_arriving = [push(dense_pay_s.at[after[k]], dense_got_s.at[k], {"dp": after[k]}) for k in range(1, count)]

    tile = pay_s[me]
    for k in range(1, count):
        arriving[k - 1].wait_recv()
        tile = tile + got_s[k]
    made = []
    tops = []
    for kind, (rows_ref, cols_ref, rows) in enumerate(
        ((up_rows_ref, up_cols_ref, width), (down_rows_ref, down_cols_ref, ff))
    ):
        here = pl.ds(me, 1)
        square = jnp.concatenate([tile[4 * kind + h : 4 * kind + h + 1] for h in range(2)], axis=1)
        scaled = jnp.concatenate([tile[4 * kind + 2 + h : 4 * kind + 3 + h] for h in range(2)], axis=1)
        new_columns = decayed(cols_ref[here, :], square / rows)
        row_mean = decayed(
            jnp.mean(rows_ref[here, :], axis=1, keepdims=True),
            jnp.sum(square, axis=1, keepdims=True) / (rows * width),
        )
        squares = row_mean * jnp.sum(scaled / new_columns, axis=1, keepdims=True)
        made += [new_columns[:, :wide], new_columns[:, wide:]]
        tops += [jnp.broadcast_to(v, (1, wide)) for v in (row_mean, squares)]
    out_ref[me] = jnp.concatenate(made + tops, axis=0)
    arriving = [push(out_ref.at[me], out_ref.at[me], {"dp": after[k]}) for k in range(1, count)]

    tile = dense_pay_s[me]
    for k in range(1, count):
        dense_arriving[k - 1].wait_recv()
        tile = tile + dense_got_s[k]
    own_piece = pl.ds(pl.multiple_of(me * piece, LANES), piece)
    new_columns = decayed(dense_cols_ref[:, own_piece], tile[0:1] / width)
    is_qkv = lax.broadcasted_iota(jnp.int32, (1, piece), 1) + me * piece < qkv_columns
    ratio = tile[1:2] / new_columns
    sums = [
        jnp.sum(jnp.where(chosen_columns, row, 0.0), axis=1, keepdims=True)
        for row in (ratio, tile[0:1])
        for chosen_columns in (is_qkv, ~is_qkv)
    ]
    dense_out_ref[me] = jnp.concatenate(
        [new_columns]
        + [jnp.broadcast_to(v, (1, piece)) for v in sums]
        + [tile[2:3], jnp.zeros((2, piece), jnp.float32)],
        axis=0,
    )
    dense_arriving = [push(dense_out_ref.at[me], dense_out_ref.at[me], {"dp": after[k]}) for k in range(1, count)]

    for copy in arriving:
        copy.wait_recv()
    total = out_ref[0, :, :LANES]
    for a in range(1, count):
        total = total + out_ref[a, :, :LANES]
    spread_s[place] = total
    arriving = [push(spread_s.at[place], spread_s.at[place], {"expert": beside[k]}) for k in range(1, groups)]
    for copy in arriving + dense_arriving + [cross_mix]:
        copy.wait_recv()
    total = spread_s[0]
    for e in range(1, groups):
        total = total + spread_s[e]
    sums_ref[...] = total
    push.finish()


FAR = 4


def finish(dense, owns, gots, settling, mixes, statistics, label):
    count = lax.axis_size("dp")
    groups = lax.axis_size("expert")
    width, dense_width = dense.shape
    bits = count.bit_length() - 1
    quarter = width // count // 4
    parts = 6
    tiles = dense_width // LANES
    bounds = [LANES * (tiles * i // parts) for i in range(parts + 1)]
    spans = [slice(a, b) for a, b in zip(bounds[:-1], bounds[1:])]
    last = tuple(range(1, bits))
    orders = [((bits, 0) if part % 2 == 0 else (0, bits)) + last for part in range(parts)]
    half = (2,) * bits + (2, quarter, dense_width)
    rows = owns[0].shape[0]
    own_up, own_down = width // count, rows - width // count
    dense_columns = dense_width - LANES
    piece = dense_columns // count
    vmem = pl.BlockSpec(memory_space=pltpu.VMEM)
    stat_tiles = (count, 8, width // 2)
    dense_tiles = (count, 8, piece)
    copies = parts * (bits + 4) + 4 * (count - 1) + groups - 1 + 5
    shape = lambda *s: jax.ShapeDtypeStruct(s, jnp.float32)
    low = lambda *s: jax.ShapeDtypeStruct(s, jnp.bfloat16)
    held = lambda *s: pltpu.VMEM(s, jnp.bfloat16)
    outs = (
        low(2, 2, quarter, dense_width),
        low(5, rows, width),
        low(*mixes[0].shape[1:]),
        shape(*stat_tiles),
        shape(8, LANES),
        shape(LANES, LANES),
        shape(LANES, LANES),
        shape(*dense_tiles),
        shape(width // count, LANES),
    )
    args = (
        dense.reshape((2,) * bits + (2, 2, quarter, dense_width)),
        *owns, *gots, *settling, *mixes, *statistics,
    )
    own, *rest = pl.pallas_call(
        functools.partial(finish_kernel, count, groups, 4, orders, spans),
        out_shape=outs,
        in_specs=[pl.BlockSpec(memory_space=pl.ANY)] + [vmem] * (len(args) - 1),
        out_specs=[vmem] * len(outs),
        scratch_shapes=[held(*half), held(*half)]
        + [held(*((2,) * (bits - step)), quarter, dense_width) for step in range(bits + 1)]
        + [
            held(*half),
            pltpu.SemaphoreType.DMA,
            held(2, rows, width),
            held(2, rows, width),
            held(2, rows, width),
            held(2, rows, width),
            held(*mixes[0].shape[1:]),
            pltpu.VMEM(stat_tiles, jnp.float32),
            pltpu.VMEM(stat_tiles, jnp.float32),
            pltpu.VMEM(dense_tiles, jnp.float32),
            pltpu.VMEM(dense_tiles, jnp.float32),
            pltpu.VMEM((groups, 8, LANES), jnp.float32),
            pltpu.VMEM((own_up, LANES), jnp.float32),
            pltpu.VMEM((own_down, LANES), jnp.float32),
            pltpu.VMEM((own_up, LANES), jnp.float32),
            pltpu.VMEM((1, dense_columns), jnp.float32),
            pltpu.SemaphoreType.DMA((copies,)),
            pltpu.SemaphoreType.DMA((copies,)),
        ],
        compiler_params=pltpu.CompilerParams(
            collective_id=label, has_side_effects=True, vmem_limit_bytes=VM
        ),
        cost_estimate=lasts(75),
        name="finish",
    )(*args)
    return own.reshape(width // count, dense_width), *rest


def update_kernel(counts, half, early, s_ref, *refs):
    owns, gots = refs[:early], refs[early : 2 * early - 1]
    (dense_ref, ends_ref, pair_mix_ref, tiles_ref, sums_ref, up_new_ref, down_new_ref, dense_tiles_ref, dense_new_ref,
     qkv_old_ref, out_old_ref, middle_hbm, near_mix_hbm, got_mix_hbm, up_w_hbm, down_w_hbm, qkv_w_hbm, out_w_hbm,
     block_hbm, up_out_hbm, down_out_hbm, up_rows_ref, down_rows_ref, up_cols_ref, down_cols_ref,
     qkv_out_ref, out_out_ref, qkv_cols_ref, out_cols_ref, qkv_rows_ref, out_rows_ref, gains_ref, moments_ref,
     rms_ref, middle_ref, near_mix_ref, got_mix_ref, up_w_ref, down_w_ref, qkv_w_ref, out_w_ref,
     block_ref, up_out_ref, down_out_ref, in_sem, out_sem) = refs[2 * early - 1 :]
    me = s_ref[1]

    def rows_of(hbm, count, along=0):
        rows = pl.ds(pl.multiple_of(me * count, count), count)
        return hbm.at[:, rows] if along else hbm.at[rows]

    incoming = [
        pltpu.make_async_copy(src, dst, in_sem.at[i])
        for i, (src, dst) in enumerate(
            (
                (rows_of(up_w_hbm, up_w_ref.shape[1], 1), up_w_ref),
                (rows_of(down_w_hbm, down_w_ref.shape[1], 1), down_w_ref),
                (rows_of(qkv_w_hbm, qkv_w_ref.shape[0]), qkv_w_ref),
                (rows_of(out_w_hbm, out_w_ref.shape[0]), out_w_ref),
                (middle_hbm, middle_ref),
                (near_mix_hbm.at[0], near_mix_ref),
                (got_mix_hbm.at[0], got_mix_ref),
            )
        )
    ]
    for copy in incoming:
        copy.start()
    leaving = []

    def leave(src, dst):
        copy = pltpu.make_async_copy(src, dst, out_sem.at[len(leaving)])
        copy.start()
        leaving.append(copy)

    late = half - early
    own_up = up_out_ref.shape[1]
    own_down = down_out_ref.shape[1]
    wide = tiles_ref.shape[2]
    pair_bit = s_ref[0]
    count = dense_tiles_ref.shape[0]
    dense_sums = dense_tiles_ref[0, :, 0:1]
    for a in range(1, count):
        dense_sums = dense_sums + dense_tiles_ref[a, :, 0:1]
    width = qkv_old_ref.shape[1]
    qkv_columns = qkv_out_ref.shape[1]
    row_means = []
    squares = [dense_tiles_ref[0, 5:6, 0:1]]
    for at, (old_ref, columns) in enumerate(((qkv_old_ref, qkv_columns), (out_old_ref, width))):
        row_means.append(
            decayed(
                jnp.mean(old_ref[...], axis=1, keepdims=True),
                dense_sums[3 + at : 4 + at] / (width * columns),
            )
        )
        squares.append(row_means[-1] * dense_sums[1 + at : 2 + at])
    squares += [sums_ref[5:6, 0:1], sums_ref[7:8, 0:1]]
    roots = [jnp.sqrt(square / number) for square, number in zip(squares, counts)]
    factors = [LEARN_RATE / jnp.maximum(1.0, root / CLIP_LEVEL) for root in roots]
    rms_ref[...] = jnp.concatenate(
        [jnp.broadcast_to(root, (1, LANES)) for root in roots] + [jnp.zeros((3, LANES), jnp.float32)], axis=0
    )

    up_table = up_new_ref[...]
    down_table = down_new_ref[...]
    lane = lax.broadcasted_iota(jnp.int32, up_table.shape, 1)

    def expert(ref, at):
        tile = tiles_ref[at]
        for kind, (table, weight_ref, out_ref, first, rows) in enumerate(
            (
                (up_table, up_w_ref, up_out_ref, 0, own_up),
                (down_table, down_w_ref, down_out_ref, own_up, own_down),
            )
        ):
            row_mean = tile[4 + 2 * kind : 5 + 2 * kind, 0:1]
            column = jnp.sum(jnp.where(lane == at, table, 0.0), axis=1, keepdims=True)[:rows]
            scale = factors[3 + kind] * lax.rsqrt(column / row_mean)
            for h in range(2):
                span = slice(h * wide, (h + 1) * wide)
                columns = lax.rsqrt(tile[2 * kind + h : 2 * kind + h + 1, :])
                out_ref[at, :, span] = (
                    weight_ref[at, :, span].astype(jnp.float32)
                    - ref[first : first + rows, span].astype(jnp.float32) * scale * columns
                )
        leave(up_out_ref.at[at], up_out_hbm.at[at])
        leave(down_out_ref.at[at], down_out_hbm.at[at])

    own_at, got_at = pair_bit * half, (1 - pair_bit) * half
    gots = (*gots, ends_ref.at[4])
    incoming[0].wait()
    incoming[1].wait()
    for j in range(early):
        expert(owns[j], own_at + j)
        expert(gots[j], got_at + j)
    for j in range(late):
        expert(ends_ref.at[j], own_at + early + j)
        expert(ends_ref.at[late + j], got_at + early + j)
    for copy in incoming[2:]:
        copy.wait()
    block_ref[...] = middle_ref[...] + (
        near_mix_ref[...].astype(jnp.float32)
        + got_mix_ref[...].astype(jnp.float32)
        + pair_mix_ref[...].astype(jnp.float32)
    )
    leave(block_ref, block_hbm)
    up_rows_ref[...] = up_table.T[: up_rows_ref.shape[0], :own_up]
    down_rows_ref[...] = down_table.T[: down_rows_ref.shape[0], :own_down]
    for a in range(up_cols_ref.shape[0]):
        for h in range(2):
            span = slice(h * wide, (h + 1) * wide)
            up_cols_ref[a : a + 1, span] = tiles_ref[a, h : h + 1, :]
            down_cols_ref[a : a + 1, span] = tiles_ref[a, 2 + h : 3 + h, :]

    table = dense_new_ref[...]
    scales = [
        factors[1 + at] * lax.rsqrt(table[:, at : at + 1] / row_means[at]) for at in range(2)
    ]
    piece = dense_tiles_ref.shape[2]
    for first in range(0, qkv_columns + width, LANES):
        at = 0 if first < qkv_columns else 1
        weight_ref, out_ref, cols_ref = (
            (qkv_w_ref, qkv_out_ref, qkv_cols_ref) if at == 0 else (out_w_ref, out_out_ref, out_cols_ref)
        )
        here = slice(first - at * qkv_columns, first - at * qkv_columns + LANES)
        within = first % piece
        columns = dense_tiles_ref[first // piece, 0:1, within : within + LANES]
        cols_ref[:, here] = columns
        out_ref[:, here] = weight_ref[:, here].astype(jnp.float32) - dense_ref[
            :, first : first + LANES
        ].astype(jnp.float32) * scales[at] * lax.rsqrt(columns)
    turned = table.T
    qkv_rows_ref[...] = turned[0:1]
    out_rows_ref[...] = turned[1:2]
    gains_ref[...] = -factors[0] * turned[2:4]
    moments_ref[...] = turned[4:6]
    for copy in leaving:
        copy.wait()


def update(owns, gots, finished, row_statistics, middle, mixes, up_w, down_w, qkv_w, out_w):
    count = lax.axis_size("dp")
    groups = lax.axis_size("expert")
    me = lax.axis_index("dp")
    experts, width, up_columns = up_w.shape
    ff = down_w.shape[1]
    qkv_columns = qkv_w.shape[1]
    own_up, own_down = width // count, ff // count
    counts = (
        float(2 * width),
        float(width * qkv_columns),
        float(width * width),
        float(groups * experts * width * up_columns),
        float(groups * experts * ff * width),
    )
    ends = finished[1]
    early = len(owns)
    whole = lambda *shape: pl.BlockSpec(shape, lambda g, s: (0,) * len(shape))
    shape = lambda *s: jax.ShapeDtypeStruct(s, jnp.float32)
    rows = own_up + own_down
    outs = [
        shape(*middle.shape),
        shape(experts, own_up, up_columns),
        shape(experts, own_down, width),
        shape(experts, own_up),
        shape(experts, own_down),
        shape(experts, up_columns),
        shape(experts, width),
        shape(own_up, qkv_columns),
        shape(own_up, width),
        shape(1, qkv_columns),
        shape(1, width),
        shape(1, own_up),
        shape(1, own_up),
        shape(2, own_up),
        shape(2, own_up),
        shape(8, LANES),
    ]
    return pl.pallas_call(
        functools.partial(update_kernel, counts, 2 * early, early),
        out_shape=outs,
        grid_spec=pltpu.PrefetchScalarGridSpec(
            num_scalar_prefetch=1,
            grid=(1,),
            in_specs=[whole(rows, width)] * (2 * early - 1)
            + [whole(*a.shape) for a in (*finished, *row_statistics)]
            + [pl.BlockSpec(memory_space=pl.ANY)] * 7,
            out_specs=[pl.BlockSpec(memory_space=pl.ANY)] * 3
            + [whole(*o.shape) for o in outs[3:]],
            scratch_shapes=[
                pltpu.VMEM(middle.shape, jnp.float32),
                pltpu.VMEM(middle.shape, jnp.bfloat16),
                pltpu.VMEM(middle.shape, jnp.bfloat16),
                pltpu.VMEM((experts, own_up, up_columns), jnp.bfloat16),
                pltpu.VMEM((experts, own_down, width), jnp.bfloat16),
                pltpu.VMEM((own_up, qkv_columns), jnp.bfloat16),
                pltpu.VMEM((own_up, width), jnp.bfloat16),
                pltpu.VMEM(middle.shape, jnp.float32),
                pltpu.VMEM((experts, own_up, up_columns), jnp.float32),
                pltpu.VMEM((experts, own_down, width), jnp.float32),
                pltpu.SemaphoreType.DMA((7,)),
                pltpu.SemaphoreType.DMA((2 * experts + 1,)),
            ],
        ),
        compiler_params=pltpu.CompilerParams(vmem_limit_bytes=VM),
        cost_estimate=lasts(6),
        name="update",
    )(
        jnp.stack([lax.rem(me // PAIR, 2), me]),
        *owns, *gots, *finished, *row_statistics, middle, *mixes, up_w, down_w, qkv_w, out_w,
    )


D = 1024
FF = 512
TOP = 8


def swap(values, axis, mask):
    count = lax.axis_size(axis)
    return lax.ppermute(values, axis, [(i, i ^ mask) for i in range(count)])


def swap_pair(values):
    return swap(values, "dp", PAIR)


def swap_chip(values):
    return swap(values, "expert", 2)


def swap_core(values):
    return swap(values, "expert", 1)


def plus(a, b):
    return (a.astype(jnp.float32) + b.astype(jnp.float32)).astype(jnp.bfloat16)


def halve(blocks, axis, mask):
    bit = lax.rem(lax.axis_index(axis) // mask, 2)
    keep = lax.dynamic_index_in_dim(blocks, bit, 1, keepdims=False)
    give = lax.dynamic_index_in_dim(blocks, 1 - bit, 1, keepdims=False)
    return keep, swap(give, axis, mask)


def reduce_dense_far(blocks):
    count = lax.axis_size("dp")
    width, columns = blocks.shape
    rows = width // count
    blocks = blocks.reshape(count, 2, 2, rows // 4, columns)
    keep, got = halve(jnp.moveaxis(blocks, 2, 1), "expert", 1)
    keep, got = halve(plus(keep, got), "expert", 2)
    blocks = plus(keep, got)
    low = 1
    while low < count:
        keep, got = halve(blocks.reshape((-1, 2, 1) + blocks.shape[1:]), "dp", low)
        blocks = plus(keep, got).reshape((-1,) + blocks.shape[1:])
        low *= 2
    mine = blocks[0]
    chip = lax.axis_index("expert") // 2
    core = lax.rem(lax.axis_index("expert"), 2)
    other = swap_chip(mine)
    both = jnp.where(chip == 0, jnp.stack([mine, other]), jnp.stack([other, mine]))
    across = swap_core(both)
    all_four = jnp.where(core == 0, jnp.stack([both, across], 1), jnp.stack([across, both], 1))
    return all_four.reshape(rows, columns)


def own_share(matrix, along):
    count = lax.axis_size("dp")
    width = matrix.shape[along] // count
    return lax.dynamic_slice_in_dim(matrix, lax.axis_index("dp") * width, width, along)


def factored(part, rows_old):
    square = part * part
    rows_new = decayed(rows_old, jnp.mean(square + EPS_STAT, axis=-1))
    return (
        rows_new,
        jnp.sum(square + EPS_STAT, axis=-2),
        jnp.sum(square / rows_new[..., None], axis=-2),
    )


def per_device(
    hidden_in,
    out_grad,
    segment_ids,
    parent_ids,
    positions,
    expert_ids,
    gate_weights,
    norm_gains,
    qkv_weight,
    out_weight,
    gate_up_weight,
    down_weight,
    gain_moment,
    qkv_rows,
    qkv_cols,
    out_rows,
    out_cols,
    gateup_rows,
    gateup_cols,
    down_rows,
    down_cols,
):
    rows_here = hidden_in.shape[0]
    dp_count = lax.axis_size("dp")
    groups = lax.axis_size("expert")
    experts_here = gate_up_weight.shape[0]
    total_experts = experts_here * groups
    capacity = 3 * rows_here * TOP // (2 * total_experts)
    half_experts = experts_here // 2
    dp_index = lax.axis_index("dp")
    pair_bit = lax.rem(dp_index // PAIR, 2)
    first_local = pair_bit * half_experts
    first_expert = lax.axis_index("expert") * experts_here + first_local

    weight_high = gate_weights.astype(jnp.bfloat16)
    weight_low = (gate_weights - weight_high.astype(jnp.float32)).astype(jnp.bfloat16)
    routing = jnp.concatenate([expert_ids.astype(jnp.bfloat16), weight_high, weight_low], axis=1).T
    routing = jnp.pad(routing, ((0, ROUTE_ROWS - routing.shape[0]), (0, D - rows_here)))
    grad_rows = jnp.concatenate([out_grad.astype(jnp.bfloat16), routing], axis=0)
    chip_grad_rows = swap_chip(grad_rows)
    pair_grad_rows = swap_pair(grad_rows)
    ids = jnp.stack([segment_ids, parent_ids, positions])
    normed, qkv, attended, lse, middle, normed_ffn = attend(
        hidden_in, ids, norm_gains, qkv_weight, out_weight
    )
    received, arrived, scale, code = gather_and_select(
        normed_ffn, grad_rows, chip_grad_rows, pair_grad_rows, capacity, experts_here, half_experts, TOP, 5
    )
    scalars = jnp.stack([first_local, lax.rem(dp_index, 2)])
    experts, chains = [], []

    def advance(which, after, comes=(), passed=()):
        comes = dict(comes)
        groups = []
        for j in which:
            masks, stay, go = chains[j]
            groups.append((stay, comes[j] if j in comes else swap(go, "dp", masks[0]), masks[1]))
        label = "_".join("%d_%d" % (j, chains[j][0][1]) for j in which)
        sides, passed = settle(groups, label, after, passed)
        for j, (stay, go) in zip(which, sides):
            chains[j] = (chains[j][0][1:], stay, go)
        return [chains[j][1] for j in which], passed

    masks = [1] + [1 << b for b in range(2, dp_count.bit_length() - 1)] + [PAIR]
    for j in range(half_experts):
        after = [experts[-1][2]] if experts else []
        if j == 3:
            after += advance([0], after)[0]
        experts.append(
            run_expert(
                scalars, j, received, arrived, scale, gate_up_weight, down_weight, dp_count, after
            )
        )
        chains.append((masks, experts[j][0], experts[j][1]))
    mine, theirs = combine(code, [e[2] for e in experts], capacity, [])
    steps, _ = advance([1], [mine])
    normed_f_grad, near_mix, far_mix, come = return_sums(
        code, mine, theirs, [e[3] for e in experts], capacity, chains[1][2], chains[1][0][0], 6, steps
    )
    steps, (far_mix,) = advance([2, 0, 1], [normed_f_grad], [(1, come)], [far_mix])
    input_grad, dense = attend_back(
        hidden_in, out_grad, middle, normed_f_grad, normed, qkv, attended, lse, ids, norm_gains, qkv_weight,
        out_weight, steps
    )
    got_mix = swap_chip(far_mix)
    qkv_columns = qkv_weight.shape[1]
    fast_tail = dp_count == experts_here and D // dp_count % 64 == 0
    if fast_tail:
        owns = [chains[j][1][0] for j in (0, 1)]
        gots = [swap_pair(chains[0][2][0]), chains[1][2][0]]
        settling = []
        for j in (2, 3):
            masks, stay, go = chains[j]
            settling += [stay, swap(go, "dp", masks[0])]
        settling[2:] = [x.reshape((2, 2) + x.shape[1:]) for x in settling[2:]]
        finished = finish(
            dense,
            owns,
            gots,
            settling,
            (near_mix, got_mix),
            (
                gateup_rows,
                down_rows,
                gateup_cols,
                down_cols,
                qkv_rows[None],
                out_rows[None],
                gain_moment,
                qkv_cols[None],
                out_cols[None],
            ),
            1,
        )
        (
            block_out,
            gate_up_new,
            down_new,
            gateup_rows_new,
            down_rows_new,
            gateup_cols_new,
            down_cols_new,
            qkv_new,
            out_new,
            qkv_cols_new,
            out_cols_new,
            qkv_rows_new,
            out_rows_new,
            gains_update,
            gain_moment_new,
            roots,
        ) = update(
            owns,
            gots[:1],
            finished,
            (qkv_rows[None], out_rows[None]),
            middle,
            (near_mix, got_mix),
            gate_up_weight,
            down_weight,
            qkv_weight,
            out_weight,
        )
        qkv_cols_new, out_cols_new = qkv_cols_new[0], out_cols_new[0]
        update_rms = roots[:5, 0]
        qkv_rows_new, out_rows_new = qkv_rows_new[0], out_rows_new[0]
    else:
        for_pair = settle_mix(near_mix, got_mix, [input_grad])
        mix_parts = (near_mix[0], got_mix[0], swap_pair(for_pair))
        block_out = middle + sum(part.astype(jnp.float32) for part in mix_parts)
        dense_own = reduce_dense_far(dense)
        for j in range(half_experts):
            while len(chains[j][0]) > 1:
                advance([j], [dense_own])
        own_parts = [c[1][0] for c in chains]
        other_parts = [swap_pair(c[2][0]) for c in chains]
        own = jnp.stack(own_parts).astype(jnp.float32)
        other = jnp.stack(other_parts).astype(jnp.float32)
        parts = jnp.where(pair_bit == 0, jnp.concatenate([own, other]), jnp.concatenate([other, own]))
        gateup_part = parts[:, : D // dp_count]
        down_part = parts[:, D // dp_count :]
        gateup_rows_new, gateup_square, gateup_scaled = factored(gateup_part, own_share(gateup_rows, 1))
        down_rows_new, down_square, down_scaled = factored(down_part, own_share(down_rows, 1))
        sizes = [gateup_square.size, gateup_scaled.size, down_square.size, down_scaled.size]
        summed = total_over(
            jnp.concatenate(
                [
                    gateup_square.reshape(-1),
                    gateup_scaled.reshape(-1),
                    down_square.reshape(-1),
                    down_scaled.reshape(-1),
                    jnp.sum(gateup_rows_new, axis=1),
                    jnp.sum(down_rows_new, axis=1),
                ]
            ),
            "dp",
            1,
        )
        pieces = jnp.split(summed, [sum(sizes[: i + 1]) for i in range(4)])
        gateup_square, gateup_scaled, down_square, down_scaled = [
            p.reshape(experts_here, D) for p in pieces[:4]
        ]
        gateup_row_mean = pieces[4][:experts_here] / D
        down_row_mean = pieces[4][experts_here:] / FF
        gateup_cols_new = decayed(gateup_cols, gateup_square / D)
        down_cols_new = decayed(down_cols, down_square / FF)
        expert_squares = jnp.stack(
            [
                jnp.sum(gateup_row_mean * jnp.sum(gateup_scaled / gateup_cols_new, axis=1)),
                jnp.sum(down_row_mean * jnp.sum(down_scaled / down_cols_new, axis=1)),
            ]
        )
        spread_squares = collect(
            jnp.zeros((8, 128), jnp.float32).at[0, :2].set(expert_squares), "expert", 2
        )
        expert_squares = jnp.sum(spread_squares[:, 0, :2], axis=0)
        dense_own = dense_own.astype(jnp.float32)
        qkv_own = dense_own[:, :qkv_columns]
        out_own = dense_own[:, qkv_columns : qkv_columns + D]
        gains_own = dense_own[:, qkv_columns + D : qkv_columns + D + 2].T
        gain_moment_new = decayed(own_share(gain_moment, 1), gains_own * gains_own + EPS_STAT)
        gains_step = gains_own * lax.rsqrt(gain_moment_new)
        qkv_rows_new, qkv_square, qkv_scaled = factored(qkv_own, own_share(qkv_rows, 0))
        out_rows_new, out_square, out_scaled = factored(out_own, own_share(out_rows, 0))
        dense_sums = total_over(
            jnp.concatenate(
                [
                    qkv_square,
                    qkv_scaled,
                    out_square,
                    out_scaled,
                    jnp.stack(
                        [jnp.sum(qkv_rows_new), jnp.sum(out_rows_new), jnp.sum(gains_step * gains_step)]
                    ),
                ]
            ),
            "dp",
            4,
        )
        qkv_square, qkv_scaled, out_square, out_scaled, rest = jnp.split(
            dense_sums, [qkv_columns, 2 * qkv_columns, 2 * qkv_columns + D, 2 * qkv_columns + 2 * D]
        )
        qkv_row_mean = rest[0] / D
        out_row_mean = rest[1] / D
        qkv_cols_new = decayed(qkv_cols, qkv_square / D)
        out_cols_new = decayed(out_cols, out_square / D)
        squares = jnp.concatenate(
            [
                jnp.stack(
                    [
                        rest[2],
                        qkv_row_mean * jnp.sum(qkv_scaled / qkv_cols_new),
                        out_row_mean * jnp.sum(out_scaled / out_cols_new),
                    ]
                ),
                expert_squares,
            ]
        )
        element_counts = jnp.array(
            [2 * D, D * qkv_columns, D * D, total_experts * D * 2 * FF, total_experts * FF * D], jnp.float32
        )
        update_rms = jnp.sqrt(squares / element_counts)
        factors = LEARN_RATE / jnp.maximum(1.0, update_rms / CLIP_LEVEL)

        def stepped(weight, part, rows_new, row_mean, cols_new, factor):
            return weight.astype(jnp.float32) - part * (
                factor * lax.rsqrt(rows_new / row_mean[..., None])
            )[..., :, None] * lax.rsqrt(cols_new)[..., None, :]

        gains_update = -factors[0] * gains_step
        qkv_new = stepped(own_share(qkv_weight, 0), qkv_own, qkv_rows_new, qkv_row_mean, qkv_cols_new, factors[1])
        out_new = stepped(own_share(out_weight, 0), out_own, out_rows_new, out_row_mean, out_cols_new, factors[2])
        gate_up_new = stepped(
            own_share(gate_up_weight, 1), gateup_part, gateup_rows_new, gateup_row_mean, gateup_cols_new, factors[3]
        )
        down_new = stepped(
            own_share(down_weight, 1), down_part, down_rows_new, down_row_mean, down_cols_new, factors[4]
        )
    return (
        block_out,
        input_grad,
        update_rms,
        gains_update,
        gain_moment_new,
        qkv_new,
        qkv_rows_new,
        qkv_cols_new,
        out_new,
        out_rows_new,
        out_cols_new,
        gate_up_new,
        gateup_rows_new,
        gateup_cols_new,
        down_new,
        down_rows_new,
        down_cols_new,
    )


def solution(mesh):
    placed = (
        P(("dp", "expert"), None),
        P(("dp", "expert"), None),
        P(("dp", "expert")),
        P(("dp", "expert")),
        P(("dp", "expert")),
        P(("dp", "expert"), None),
        P(("dp", "expert"), None),
        P(),
        P(),
        P(),
        P("expert", None, None),
        P("expert", None, None),
        P(),
        P(),
        P(),
        P(),
        P(),
        P("expert", None),
        P("expert", None),
        P("expert", None),
        P("expert", None),
    )
    return jax.shard_map(
        per_device,
        mesh=mesh,
        in_specs=placed,
        out_specs=(
            P(("dp", "expert"), None),
            P(("dp", "expert"), None),
            P(),
            P(None, "dp"),
            P(None, "dp"),
            P("dp", None),
            P("dp"),
            P(),
            P("dp", None),
            P("dp"),
            P(),
            P("expert", "dp", None),
            P("expert", "dp"),
            P("expert", None),
            P("expert", "dp", None),
            P("expert", "dp"),
            P("expert", None),
        ),
        check_vma=False,
    )
```

```python
import functools
import math

import jax
import jax.numpy as jnp
from jax import lax
from jax.experimental import pallas as pl
from jax.experimental.pallas import tpu as pltpu
from jax.sharding import PartitionSpec as P

VM = 60 * 1024 * 1024
SCALE = 1e6


def lasts(microseconds):
    return pl.CostEstimate(
        flops=int(microseconds * SCALE), bytes_accessed=1024, transcendentals=0
    )


def dot(a, b, ca=1, cb=0):
    return lax.dot_general(a, b, (((ca,), (cb,)), ((), ())), preferred_element_type=jnp.float32)


def one_hot(code, capacity):
    count, rows = code.shape
    place = lax.broadcasted_iota(jnp.int32, (capacity, rows), 0).astype(jnp.float32)
    return [place == code[j : j + 1, :] for j in range(count)]


def expert_kernel(j, owners, tiles, waits, s_ref, rec_hbm, arr_hbm, scale_ref, up_hbm, down_hbm, *refs):
    (keep_hbm, give_hbm, back_hbm, mix_hbm,
     rec_s, arr_s, up_s, down_s, act_s, gug_s, wg_s, wd_s, parts_s, out_s, in_sem, out_sem) = refs[waits:]
    rows, ff = act_s.shape
    width = up_s.shape[0]
    sources, capacity = rec_s.shape[0], rec_s.shape[1]
    tile = rows // tiles
    per = sources // tiles

    def load(src, dst, at):
        copy = pltpu.make_async_copy(src, dst, in_sem.at[at])
        copy.start()
        return copy

    def load_rows(hbm, held, t, at):
        span = slice(t * per, (t + 1) * per)
        return load(hbm.at[j, span], held.at[span], at)

    expert = s_ref[0] + j
    rec_in = [load_rows(rec_hbm, rec_s, 0, 0)]
    up_in = load(up_hbm.at[expert], up_s, 2 * tiles)
    arr_in = [load_rows(arr_hbm, arr_s, 0, tiles)]
    down_in = load(down_hbm.at[expert], down_s, 2 * tiles + 1)
    for t in range(1, tiles):
        rec_in.append(load_rows(rec_hbm, rec_s, t, t))
        arr_in.append(load_rows(arr_hbm, arr_s, t, tiles + t))
    def products(t):
        span = slice(t * per, (t + 1) * per)
        return (
            dot(rec_s[span].reshape(tile, width), up_s[...]),
            dot(arr_s[span].reshape(tile, width), down_s[...], 1, 1),
        )

    for copy in (up_in, down_in, rec_in[0], arr_in[0]):
        copy.wait()
    following = products(0)
    for t in range(tiles):
        at = slice(t * tile, (t + 1) * tile)
        gate_up, act_grad = following
        if t + 1 < tiles:
            rec_in[t + 1].wait()
            arr_in[t + 1].wait()
            following = products(t + 1)
        gate = gate_up[:, :ff]
        up = gate_up[:, ff:]
        sig = 1.0 / (1.0 + jnp.exp(-gate))
        silu = gate * sig
        act_s[at, :] = (silu * up).astype(jnp.bfloat16)
        gug_s[at, :ff] = (act_grad * up * sig * (1.0 + gate * (1.0 - sig))).astype(jnp.bfloat16)
        gug_s[at, ff:] = (act_grad * silu).astype(jnp.bfloat16)
    wg_s[...] = dot(rec_s[...].reshape(rows, width), gug_s[...], 0, 0)
    wd_s[...] = dot(act_s[...], arr_s[...].reshape(rows, width), 0, 0)
    bit = s_ref[1]
    up_rows = width // owners
    down_rows = ff // owners
    leaving = []
    for k, (hbm, side) in enumerate(((give_hbm, 1 - bit), (keep_hbm, bit))):
        for slot in range(owners // 2):
            owner = 2 * slot + side
            parts_s[k, slot, :up_rows, :] = wg_s[
                pl.ds(pl.multiple_of(owner * up_rows, up_rows), up_rows), :
            ].astype(jnp.bfloat16)
            parts_s[k, slot, up_rows:, :] = wd_s[
                pl.ds(pl.multiple_of(owner * down_rows, down_rows), down_rows), :
            ].astype(jnp.bfloat16)
        copy = pltpu.make_async_copy(parts_s.at[k], hbm, out_sem.at[k])
        copy.start()
        leaving.append(copy)
    for t in range(tiles):
        at = slice(t * tile, (t + 1) * tile)
        out_s[0, at] = dot(gug_s[at, :], up_s[...], 1, 1).astype(jnp.bfloat16)
        scale = scale_ref[0, t * per : (t + 1) * per].reshape(tile, 1)
        out_s[1, at] = (dot(act_s[at, :], down_s[...]) * scale).astype(jnp.bfloat16)
        for k, hbm in enumerate((back_hbm, mix_hbm)):
            copy = pltpu.make_async_copy(out_s.at[k, at], hbm.at[at], out_sem.at[2 + 2 * t + k])
            copy.start()
            leaving.append(copy)
    for copy in leaving:
        copy.wait()


def run_expert(scalars, j, received, arrived, scale, up_w, down_w, owners, after=()):
    count, sources, capacity, width = received.shape
    ff = down_w.shape[1]
    rows = sources * capacity
    tiles = 2
    share = (owners // 2, (width + ff) // owners, width)
    slots = jax.ShapeDtypeStruct((rows, width), jnp.bfloat16)
    parts = jax.ShapeDtypeStruct(share, jnp.bfloat16)
    anywhere = pl.BlockSpec(memory_space=pl.ANY)
    return pl.pallas_call(
        functools.partial(expert_kernel, j, owners, tiles, len(after)),
        out_shape=(parts, parts, slots, slots),
        grid_spec=pltpu.PrefetchScalarGridSpec(
            num_scalar_prefetch=1,
            grid=(1,),
            in_specs=[
                anywhere,
                anywhere,
                pl.BlockSpec((1, sources, capacity, 1), lambda g, s: (j, 0, 0, 0)),
                anywhere,
                anywhere,
            ]
            + [anywhere] * len(after),
            out_specs=[anywhere] * 4,
            scratch_shapes=[
                pltpu.VMEM((sources, capacity, width), jnp.bfloat16),
                pltpu.VMEM((sources, capacity, width), jnp.bfloat16),
                pltpu.VMEM((width, 2 * ff), jnp.bfloat16),
                pltpu.VMEM((ff, width), jnp.bfloat16),
                pltpu.VMEM((rows, ff), jnp.bfloat16),
                pltpu.VMEM((rows, 2 * ff), jnp.bfloat16),
                pltpu.VMEM((width, 2 * ff), jnp.float32),
                pltpu.VMEM((ff, width), jnp.float32),
                pltpu.VMEM((2,) + share, jnp.bfloat16),
                pltpu.VMEM((2, rows, width), jnp.bfloat16),
                pltpu.SemaphoreType.DMA((2 * tiles + 2,)),
                pltpu.SemaphoreType.DMA((2 + 2 * tiles,)),
            ],
        ),
        compiler_params=pltpu.CompilerParams(vmem_limit_bytes=VM),
        cost_estimate=lasts(18),
        name="expert_%d" % j,
    )(scalars, received, arrived, scale, up_w, down_w, *after)


HEADS = 16
KV_HEADS = 8
HEAD_DIM = 64
EPS_NORM = 1e-06
ROPE_BASE = 10000.0
MASKED = -1e30
LANES = 128


def spread(row):
    rows = row.shape[1]
    by_column = jnp.broadcast_to(row.astype(jnp.float32), (rows, rows))
    return by_column, by_column.T


def mask_and_angles(ids_ref):
    seg_k, seg_q = spread(ids_ref[0:1, :])
    par_k, par_q = spread(ids_ref[1:2, :])
    pos_k, pos_q = spread(ids_ref[2:3, :])
    seen = ((seg_k == seg_q) | (seg_k == par_q) | (seg_k == par_k)) & (pos_k <= pos_q)
    bias = jnp.where(seen, 0.0, MASKED)
    lane = lax.broadcasted_iota(jnp.int32, (seg_k.shape[0], LANES), 1)
    half = HEAD_DIM // 2
    place = lax.rem(lane, half).astype(jnp.float32)
    frequency = jnp.exp(place * (-2.0 * math.log(ROPE_BASE) / HEAD_DIM))
    angles = pos_q[:, :LANES] * frequency
    front = lax.rem(lane, HEAD_DIM) < half
    sine = jnp.sin(angles)
    return bias, jnp.cos(angles), jnp.where(front, -sine, sine), front, lane


def turned(block, cosine, sine, front):
    other = jnp.where(
        front,
        pltpu.roll(block, LANES - HEAD_DIM // 2, 1),
        pltpu.roll(block, HEAD_DIM // 2, 1),
    )
    return block * cosine + other * sine


def two_diagonal(pair, which, lane):
    rolled = pltpu.roll(pair, HEAD_DIM, 1)
    first, last = (pair, rolled) if which == 0 else (rolled, pair)
    low = lane < HEAD_DIM
    return jnp.concatenate(
        [jnp.where(low, first, 0.0), jnp.where(low, 0.0, last)], axis=0
    ).astype(jnp.bfloat16)


def column_block(index):
    return pl.ds(pl.multiple_of(index * LANES, LANES), LANES)


def attend_kernel(hidden_ref, ids_ref, gains_ref, qkv_w_hbm, out_w_hbm,
                  normed_hbm, qkv_hbm, attended_hbm, lse_ref, middle_ref, normed_f_ref,
                  normed_ref, qkv_ref, attended_ref, qkv_w_ref, out_w_ref, proj_s, bias_s, sem):
    moving = [
        pltpu.make_async_copy(src, dst, sem.at[i])
        for i, (src, dst) in enumerate(
            (
                (qkv_w_hbm, qkv_w_ref),
                (out_w_hbm, out_w_ref),
                (normed_ref, normed_hbm),
                (qkv_ref, qkv_hbm),
                (attended_ref, attended_hbm),
            )
        )
    ]
    moving[0].start()
    moving[1].start()
    rows = hidden_ref.shape[0]
    att = HEADS * HEAD_DIM
    kv = KV_HEADS * HEAD_DIM
    hidden = hidden_ref[...]
    gains = gains_ref[...].astype(jnp.float32)
    inverse = lax.rsqrt(jnp.mean(hidden * hidden, axis=-1, keepdims=True) + EPS_NORM)
    normed_ref[...] = (hidden * inverse * gains[0:1, :]).astype(jnp.bfloat16)
    moving[2].start()
    bias, cosine, sine, front, lane = mask_and_angles(ids_ref)
    bias_s[...] = bias
    moving[0].wait()
    proj_s[...] = dot(normed_ref[...], qkv_w_ref[...])
    lse_ref[...] = jnp.zeros_like(lse_ref)

    def pair_step(p, carry):
        key_at = column_block(att // LANES + p)
        value_at = column_block((att + kv) // LANES + p)
        keys = turned(proj_s[:, key_at], cosine, sine, front).astype(jnp.bfloat16)
        values = proj_s[:, value_at].astype(jnp.bfloat16)
        qkv_ref[:, key_at] = keys
        qkv_ref[:, value_at] = values
        keys = keys.astype(jnp.float32)
        values = values.astype(jnp.float32)
        for which in range(2):
            query_at = column_block(2 * p + which)
            queries = turned(proj_s[:, query_at], cosine, sine, front).astype(jnp.bfloat16)
            queries = (queries.astype(jnp.float32) * HEAD_DIM**-0.5).astype(jnp.bfloat16)
            qkv_ref[:, query_at] = queries
            scores = dot(queries, two_diagonal(keys, which, lane), 1, 1)
            probs = []
            for head in range(2):
                part = scores[:, head * rows : (head + 1) * rows] + bias_s[...]
                top = jnp.max(part, axis=-1, keepdims=True)
                part = jnp.exp(part - top)
                total = jnp.sum(part, axis=-1, keepdims=True)
                probs.append((part * (1.0 / total)).astype(jnp.bfloat16))
                at = 4 * p + 2 * which + head
                lse_ref[...] = jnp.where(lane == at, top + jnp.log(total), lse_ref[...])
            attended_ref[:, query_at] = dot(
                jnp.concatenate(probs, axis=1), two_diagonal(values, which, lane)
            ).astype(jnp.bfloat16)
        return carry

    lax.fori_loop(0, KV_HEADS // 2, pair_step, 0)
    moving[3].start()
    moving[4].start()
    moving[1].wait()
    middle = hidden + dot(attended_ref[...], out_w_ref[...])
    middle_ref[...] = middle
    inverse_f = lax.rsqrt(jnp.mean(middle * middle, axis=-1, keepdims=True) + EPS_NORM)
    normed_f_ref[...] = (middle * inverse_f * gains[1:2, :]).astype(jnp.bfloat16)
    for copy in moving[2:]:
        copy.wait()


def attend(hidden, ids, gains, qkv_w, out_w):
    rows, width = hidden.shape
    shape = jax.ShapeDtypeStruct
    return pl.pallas_call(
        attend_kernel,
        out_shape=(
            shape((rows, width), jnp.bfloat16),
            shape((rows, qkv_w.shape[1]), jnp.bfloat16),
            shape((rows, out_w.shape[0]), jnp.bfloat16),
            shape((rows, LANES), jnp.float32),
            shape((rows, width), jnp.float32),
            shape((rows, width), jnp.bfloat16),
        ),
        in_specs=[pl.BlockSpec(memory_space=pltpu.VMEM)] * 3 + [pl.BlockSpec(memory_space=pl.ANY)] * 2,
        out_specs=[pl.BlockSpec(memory_space=pl.ANY)] * 3 + [pl.BlockSpec(memory_space=pltpu.VMEM)] * 3,
        scratch_shapes=[
            pltpu.VMEM((rows, width), jnp.bfloat16),
            pltpu.VMEM((rows, qkv_w.shape[1]), jnp.bfloat16),
            pltpu.VMEM((rows, out_w.shape[0]), jnp.bfloat16),
            pltpu.VMEM(qkv_w.shape, jnp.bfloat16),
            pltpu.VMEM(out_w.shape, jnp.bfloat16),
            pltpu.VMEM((rows, qkv_w.shape[1]), jnp.float32),
            pltpu.VMEM((rows, rows), jnp.float32),
            pltpu.SemaphoreType.DMA((5,)),
        ],
        compiler_params=pltpu.CompilerParams(vmem_limit_bytes=VM),
        cost_estimate=lasts(18),
        name="attend",
    )(hidden, ids, gains, qkv_w, out_w)


def attend_back_kernel(waits, grad_ref, middle_ref, normed_grad_ref, lse_ref, ids_ref, gains_ref,
                       hidden_hbm, normed_hbm, qkv_hbm, attended_hbm, qkv_w_hbm, out_w_hbm, *refs):
    (input_grad_ref, dense_hbm, dense_ref, hidden_ref, normed_ref, qkv_ref, attended_ref, qkv_w_ref, out_w_ref,
     proj_s, bias_s, back_s, sem) = refs[waits:]
    rows, width = hidden_ref.shape
    incoming = {
        name: pltpu.make_async_copy(src, dst, sem.at[i])
        for i, (name, src, dst) in enumerate(
            (
                ("attended", attended_hbm, attended_ref),
                ("out_w", out_w_hbm, out_w_ref),
                ("qkv", qkv_hbm, qkv_ref),
                ("normed", normed_hbm, normed_ref),
                ("qkv_w", qkv_w_hbm, qkv_w_ref),
                ("hidden", hidden_hbm, hidden_ref),
            )
        )
    }
    for copy in incoming.values():
        copy.start()
    leaving = []

    def leave(span):
        copy = pltpu.make_async_copy(dense_ref.at[:, span], dense_hbm.at[:, span], sem.at[6 + len(leaving)])
        copy.start()
        leaving.append(copy)

    att = HEADS * HEAD_DIM
    kv = KV_HEADS * HEAD_DIM
    gains = gains_ref[...].astype(jnp.float32)
    normed_grad = normed_grad_ref[...]
    middle = middle_ref[...]
    inverse_f = lax.rsqrt(jnp.mean(middle * middle, axis=-1, keepdims=True) + EPS_NORM)
    gain_f = jnp.sum(normed_grad * middle * inverse_f, axis=0, keepdims=True)
    weighted = normed_grad * gains[1:2, :]
    middle_grad = grad_ref[...] + (
        inverse_f * weighted
        - middle * (inverse_f * inverse_f * inverse_f)
        * jnp.mean(weighted * middle, axis=-1, keepdims=True)
    )
    input_grad_ref[...] = middle_grad
    branch = middle_grad.astype(jnp.bfloat16)
    columns = att + 2 * kv
    incoming["attended"].wait()
    dense_ref[:, columns : columns + width] = dot(attended_ref[...], branch, 0, 0).astype(jnp.bfloat16)
    leave(slice(columns, columns + width))
    incoming["out_w"].wait()
    back_s[...] = dot(branch, out_w_ref[...], 1, 1).astype(jnp.bfloat16)
    bias, cosine, sine, front, lane = mask_and_angles(ids_ref)
    bias_s[...] = bias
    low = lane < HEAD_DIM
    incoming["qkv"].wait()

    def pair_step(p, carry):
        key_at = column_block(att // LANES + p)
        value_at = column_block((att + kv) // LANES + p)
        keys = qkv_ref[:, key_at].astype(jnp.float32)
        values = qkv_ref[:, value_at].astype(jnp.float32)
        key_grads = []
        value_grads = []
        for which in range(2):
            query_at = column_block(2 * p + which)
            queries = qkv_ref[:, query_at]
            back = back_s[:, query_at]
            key_two = two_diagonal(keys, which, lane)
            scores = dot(queries, key_two, 1, 1)
            prob_grads = dot(back, two_diagonal(values, which, lane), 1, 1)
            probs = []
            score_grads = []
            for head in range(2):
                at = 4 * p + 2 * which + head
                level = jnp.sum(jnp.where(lane == at, lse_ref[...], 0.0), axis=-1, keepdims=True)
                span = slice(head * rows, (head + 1) * rows)
                prob = jnp.exp(scores[:, span] + bias_s[...] - level)
                prob_grad = prob_grads[:, span]
                row_dot = jnp.sum(prob * prob_grad, axis=-1, keepdims=True)
                probs.append(prob.astype(jnp.bfloat16))
                score_grads.append((prob * (prob_grad - row_dot)).astype(jnp.bfloat16))
            score_grads = jnp.concatenate(score_grads, axis=1)
            query_grad = dot(score_grads, key_two) * HEAD_DIM**-0.5
            proj_s[:, query_at] = turned(query_grad, cosine, -sine, front).astype(jnp.bfloat16)
            for grads, left, right in (
                (key_grads, score_grads, queries),
                (value_grads, jnp.concatenate(probs, axis=1), back),
            ):
                both = dot(left, right, 0, 0)
                first, last = both[:rows], both[rows:]
                if which == 0:
                    grads.append(first + pltpu.roll(last, HEAD_DIM, 1))
                else:
                    grads.append(pltpu.roll(first, HEAD_DIM, 1) + last)
        key_grad = jnp.where(low, key_grads[0], key_grads[1])
        proj_s[:, key_at] = turned(key_grad, cosine, -sine, front).astype(jnp.bfloat16)
        proj_s[:, value_at] = jnp.where(low, value_grads[0], value_grads[1]).astype(jnp.bfloat16)
        return carry

    lax.fori_loop(0, KV_HEADS // 2, pair_step, 0)
    for name in ("normed", "qkv_w", "hidden"):
        incoming[name].wait()
    for first in range(0, columns, columns // 2):
        span = slice(first, first + columns // 2)
        dense_ref[:, span] = dot(normed_ref[...], proj_s[:, span], 0, 0).astype(jnp.bfloat16)
        leave(span)
    normed_grad = dot(proj_s[...], qkv_w_ref[...], 1, 1)
    hidden = hidden_ref[...]
    inverse = lax.rsqrt(jnp.mean(hidden * hidden, axis=-1, keepdims=True) + EPS_NORM)
    gain_a = jnp.sum(normed_grad * hidden * inverse, axis=0, keepdims=True)
    weighted = normed_grad * gains[0:1, :]
    input_grad_ref[...] += inverse * weighted - hidden * (inverse * inverse * inverse) * jnp.mean(
        weighted * hidden, axis=-1, keepdims=True
    )
    both = jnp.concatenate([gain_a, gain_f, jnp.zeros((LANES - 2, width), jnp.float32)], axis=0)
    dense_ref[:, columns + width :] = both.T.astype(jnp.bfloat16)
    leave(slice(columns + width, columns + width + LANES))
    for copy in leaving:
        copy.wait()


def attend_back(hidden, out_grad, middle, normed_f_grad, normed, qkv, attended, lse, ids, gains, qkv_w, out_w, after=()):
    rows, width = hidden.shape
    columns = qkv_w.shape[1] + width + LANES
    return pl.pallas_call(
        functools.partial(attend_back_kernel, len(after)),
        out_shape=(
            jax.ShapeDtypeStruct((rows, width), jnp.float32),
            jax.ShapeDtypeStruct((width, columns), jnp.bfloat16),
        ),
        in_specs=[pl.BlockSpec(memory_space=pltpu.VMEM)] * 6
        + [pl.BlockSpec(memory_space=pl.ANY)] * (6 + len(after)),
        out_specs=[pl.BlockSpec(memory_space=pltpu.VMEM), pl.BlockSpec(memory_space=pl.ANY)],
        scratch_shapes=[
            pltpu.VMEM((width, columns), jnp.bfloat16),
            pltpu.VMEM((rows, width), jnp.float32),
            pltpu.VMEM((rows, width), jnp.bfloat16),
            pltpu.VMEM((rows, qkv_w.shape[1]), jnp.bfloat16),
            pltpu.VMEM((rows, out_w.shape[0]), jnp.bfloat16),
            pltpu.VMEM(qkv_w.shape, jnp.bfloat16),
            pltpu.VMEM(out_w.shape, jnp.bfloat16),
            pltpu.VMEM((rows, qkv_w.shape[1]), jnp.bfloat16),
            pltpu.VMEM((rows, rows), jnp.float32),
            pltpu.VMEM((rows, out_w.shape[0]), jnp.bfloat16),
            pltpu.SemaphoreType.DMA((10,)),
        ],
        compiler_params=pltpu.CompilerParams(vmem_limit_bytes=VM),
        cost_estimate=lasts(26),
        name="attend_back",
    )(out_grad, middle, normed_f_grad, lse, ids, gains, hidden, normed, qkv, attended, qkv_w, out_w, *after)


MESH = pl.DeviceIdType.MESH


def greet(peers):
    barrier = pltpu.get_barrier_semaphore()
    for peer in peers:
        pl.semaphore_signal(barrier, inc=1, device_id=peer, device_id_type=MESH)
    pl.semaphore_wait(barrier, len(peers))


def total_kernel(axis, count, mine_ref, *refs):
    out_ref, got_ref, send_sem, recv_sem = refs[-4:]
    me = lax.axis_index(axis)
    after = [lax.rem(me + k, count) for k in range(count)]
    greet([{axis: after[k]} for k in range(1, count)])
    scatter = [
        pltpu.make_async_remote_copy(
            src_ref=mine_ref.at[after[k]],
            dst_ref=got_ref.at[k],
            send_sem=send_sem.at[0, k],
            recv_sem=recv_sem.at[0, k],
            device_id={axis: after[k]},
            device_id_type=MESH,
        )
        for k in range(1, count)
    ]
    for copy in scatter:
        copy.start()
    total = mine_ref[me]
    for k in range(1, count):
        scatter[k - 1].wait_recv()
        total = total + got_ref[k]
    out_ref[me] = total
    share = [
        pltpu.make_async_remote_copy(
            src_ref=out_ref.at[me],
            dst_ref=out_ref.at[me],
            send_sem=send_sem.at[1, k],
            recv_sem=recv_sem.at[1, k],
            device_id={axis: after[k]},
            device_id_type=MESH,
        )
        for k in range(1, count)
    ]
    for copy in share:
        copy.start()
    for copy in share:
        copy.wait_recv()
    for copy in scatter + share:
        copy.wait_send()


def total_over(values, axis, label, after=()):
    count = lax.axis_size(axis)
    rows = -(-values.shape[0] // (8 * 128 * count)) * 8
    padded = jnp.pad(values, (0, count * rows * 128 - values.shape[0])).reshape(count, rows, 128)
    out = pl.pallas_call(
        functools.partial(total_kernel, axis, count),
        out_shape=jax.ShapeDtypeStruct(padded.shape, jnp.float32),
        in_specs=[pl.BlockSpec(memory_space=pltpu.VMEM)] + [pl.BlockSpec(memory_space=pl.ANY)] * len(after),
        out_specs=pl.BlockSpec(memory_space=pltpu.VMEM),
        scratch_shapes=[
            pltpu.VMEM(padded.shape, jnp.float32),
            pltpu.SemaphoreType.DMA((2, count)),
            pltpu.SemaphoreType.DMA((2, count)),
        ],
        compiler_params=pltpu.CompilerParams(
            collective_id=label, has_side_effects=True, vmem_limit_bytes=16 * 1024 * 1024
        ),
        cost_estimate=lasts(12),
        name="total_%d" % label,
    )(padded, *after)
    return out.reshape(-1)[: values.shape[0]]


def collect_kernel(axis, count, mine_ref, out_ref, send_sem, recv_sem, local_sem):
    me = lax.axis_index(axis)
    after = [lax.rem(me + k, count) for k in range(count)]
    greet([{axis: after[k]} for k in range(1, count)])
    copies = [
        pltpu.make_async_remote_copy(
            src_ref=mine_ref,
            dst_ref=out_ref.at[me],
            send_sem=send_sem.at[k],
            recv_sem=recv_sem.at[k],
            device_id={axis: after[k]},
            device_id_type=MESH,
        )
        for k in range(1, count)
    ]
    for copy in copies:
        copy.start()
    out_ref[me] = mine_ref[...]
    for copy in copies:
        copy.wait()


def collect(values, axis, label):
    count = lax.axis_size(axis)
    return pl.pallas_call(
        functools.partial(collect_kernel, axis, count),
        out_shape=jax.ShapeDtypeStruct((count,) + values.shape, jnp.float32),
        in_specs=[pl.BlockSpec(memory_space=pltpu.VMEM)],
        out_specs=pl.BlockSpec(memory_space=pltpu.VMEM),
        scratch_shapes=[
            pltpu.SemaphoreType.DMA((count,)),
            pltpu.SemaphoreType.DMA((count,)),
            pltpu.SemaphoreType.DMA,
        ],
        compiler_params=pltpu.CompilerParams(
            collective_id=label, has_side_effects=True, vmem_limit_bytes=16 * 1024 * 1024
        ),
        cost_estimate=lasts(4),
        name="collect_%d" % label,
    )(values)


def flipped(axis, mask):
    index = lax.axis_index(axis)
    bit = lax.rem(index // mask, 2)
    return bit, {axis: index + mask - 2 * mask * bit}


PAIR = 2
ROUTE_ROWS = 32


class Pusher:
    def __init__(self, send_sem, recv_sem):
        self.send_sem, self.recv_sem, self.copies = send_sem, recv_sem, []

    def __call__(self, src, dst, peer):
        at = len(self.copies)
        copy = pltpu.make_async_remote_copy(
            src_ref=src,
            dst_ref=dst,
            send_sem=self.send_sem.at[at],
            recv_sem=self.recv_sem.at[at],
            device_id=peer,
            device_id_type=MESH,
        )
        copy.start()
        self.copies.append(copy)
        return copy

    def finish(self):
        for copy in self.copies:
            copy.wait_send()


def picked(code, capacity):
    return jnp.concatenate(
        [c.astype(jnp.float32) for c in one_hot(code, capacity)], axis=0
    ).astype(jnp.bfloat16)


def gather_kernel(capacity, experts_here, half_experts, top, token_ref, grad_ref, chip_grad_ref, pair_grad_ref,
                  rec_ref, arr_ref, scale_ref, code_ref, tokens, grads, weight_s, stage, send_sem, recv_sem, local_sem):
    rows = token_ref.shape[0]
    half = rows // 2
    first = lax.axis_index("expert") * experts_here + lax.rem(lax.axis_index("dp") // PAIR, 2) * half_experts
    _, core = flipped("expert", 1)
    _, chip = flipped("expert", 2)
    _, pair = flipped("dp", PAIR)
    greet([core, chip, pair])
    push = Pusher(send_sem, recv_sem)
    everything, routing = slice(None), slice(rows, rows + ROUTE_ROWS)
    to_chip = push(token_ref, tokens.at[2], chip)
    to_pair = push(token_ref, tokens.at[4], pair)
    route_both = push(pair_grad_ref.at[routing], grads.at[6, routing], chip)
    to_core = push(token_ref, tokens.at[1], core)
    grad_core = push(grad_ref, grads.at[1], core)
    grad_chip_core = push(chip_grad_ref, grads.at[3], core)
    grad_pair_core = push(pair_grad_ref, grads.at[5], core)

    earlier = lax.broadcasted_iota(jnp.int32, (rows, rows), 0)
    later = lax.broadcasted_iota(jnp.int32, (rows, rows), 1)
    before = jnp.where(earlier < later, 1.0, 0.0).astype(jnp.bfloat16)

    def route(r, table):
        table = table.astype(jnp.float32)
        ids = table[:top]
        gates = table[top : 2 * top] + table[2 * top : 3 * top]
        hits = [ids == (first + j).astype(jnp.float32) for j in range(half_experts)]
        named = jnp.concatenate(
            [jnp.max(jnp.where(hit, 1.0, 0.0), axis=0, keepdims=True) for hit in hits], axis=0
        )
        weight_s[r] = jnp.concatenate(
            [jnp.sum(jnp.where(hit, gates, 0.0), axis=0, keepdims=True) for hit in hits], axis=0
        )
        code_ref[r] = jnp.where(named > 0.0, dot(named.astype(jnp.bfloat16), before), -1.0)

    leaving = []

    def select(r, source, out_ref, weighted):
        slot = len(leaving) % stage.shape[0]
        if len(leaving) >= stage.shape[0]:
            leaving[len(leaving) - stage.shape[0]].wait()
        chosen = one_hot(code_ref[r], capacity)
        pick = jnp.concatenate([c.astype(jnp.float32) for c in chosen], axis=0).astype(jnp.bfloat16)
        made = dot(pick, source)
        for j in range(half_experts):
            part = made[j * capacity : (j + 1) * capacity]
            if weighted:
                scale = jnp.sum(
                    jnp.where(chosen[j], weight_s[r, j : j + 1, :], 0.0), axis=1, keepdims=True
                )
                scale_ref[j, r] = scale
                part = part * scale
            stage[slot, j] = part.astype(jnp.bfloat16)
        copy = pltpu.make_async_copy(stage.at[slot], out_ref.at[:, r], local_sem.at[slot])
        copy.start()
        leaving.append(copy)

    def select_grad(r, ref):
        route(r, ref[rows:, :rows])
        select(r, ref[:rows, :], arr_ref, True)

    select_grad(0, grad_ref)
    select(0, token_ref[...], rec_ref, False)
    select_grad(2, chip_grad_ref)
    select_grad(4, pair_grad_ref)
    for r, copy in ((1, grad_core), (3, grad_chip_core), (5, grad_pair_core)):
        copy.wait_recv()
        select_grad(r, grads.at[r])
    to_core.wait_recv()
    select(1, tokens[1], rec_ref, False)
    route_both.wait_recv()
    route_core = push(grads.at[6, routing], grads.at[7, routing], core)
    to_chip.wait_recv()
    both_low = push(tokens.at[2, half:rows], tokens.at[6, half:rows], pair)
    chip_core = push(tokens.at[2], tokens.at[3], core)
    to_pair.wait_recv()
    both_high = push(tokens.at[4, 0:half], tokens.at[6, 0:half], chip)
    pair_core = push(tokens.at[4], tokens.at[5], core)
    grad_low = push(chip_grad_ref.at[half:rows], grads.at[6, half:rows], pair)
    grad_high = push(pair_grad_ref.at[0:half], grads.at[6, 0:half], chip)
    select(2, tokens[2], rec_ref, False)
    select(4, tokens[4], rec_ref, False)
    route(6, grads[6, rows:, :rows])
    route_core.wait_recv()
    route(7, grads[7, rows:, :rows])
    chip_core.wait_recv()
    select(3, tokens[3], rec_ref, False)
    pair_core.wait_recv()
    select(5, tokens[5], rec_ref, False)
    both_low.wait_recv()
    both_high.wait_recv()
    both_core = push(tokens.at[6], tokens.at[7], core)
    select(6, tokens[6], rec_ref, False)
    both_core.wait_recv()
    select(7, tokens[7], rec_ref, False)
    grad_low.wait_recv()
    grad_high.wait_recv()
    grad_both_core = push(grads.at[6, 0:rows], grads.at[7, 0:rows], core)
    select(6, grads[6, :rows], arr_ref, True)
    grad_both_core.wait_recv()
    select(7, grads[7, :rows], arr_ref, True)
    for copy in leaving[-stage.shape[0] :]:
        copy.wait()
    push.finish()


def gather_and_select(token, grad, chip_grad, pair_grad, capacity, experts_here, half_experts, top, label):
    rows, width = token.shape
    vmem = pl.BlockSpec(memory_space=pltpu.VMEM)
    anywhere = pl.BlockSpec(memory_space=pl.ANY)
    slots = jax.ShapeDtypeStruct((half_experts, 8, capacity, width), jnp.bfloat16)
    return pl.pallas_call(
        functools.partial(gather_kernel, capacity, experts_here, half_experts, top),
        out_shape=(
            slots,
            slots,
            jax.ShapeDtypeStruct((half_experts, 8, capacity, 1), jnp.float32),
            jax.ShapeDtypeStruct((8, half_experts, rows), jnp.float32),
        ),
        in_specs=[vmem] * 4,
        out_specs=[anywhere, anywhere, vmem, vmem],
        scratch_shapes=[
            pltpu.VMEM((8, rows, width), jnp.bfloat16),
            pltpu.VMEM((8, rows + ROUTE_ROWS, width), jnp.bfloat16),
            pltpu.VMEM((8, half_experts, rows), jnp.float32),
            pltpu.VMEM((4, half_experts, capacity, width), jnp.bfloat16),
            pltpu.SemaphoreType.DMA((18,)),
            pltpu.SemaphoreType.DMA((18,)),
            pltpu.SemaphoreType.DMA((4,)),
        ],
        compiler_params=pltpu.CompilerParams(
            collective_id=label, has_side_effects=True, vmem_limit_bytes=VM
        ),
        cost_estimate=lasts(44),
        name="gather_and_select",
    )(token, grad, chip_grad, pair_grad)


def fetcher(order, fetched, local_sem, capacity, code_ref):
    depth = fetched.shape[0]
    fetching = []
    done = []

    def fetch():
        n = len(fetching)
        if n < len(order):
            slots, r = order[n]
            fetching.append(
                [
                    pltpu.make_async_copy(
                        ref.at[r * capacity : (r + 1) * capacity],
                        fetched.at[n % depth, j * capacity : (j + 1) * capacity],
                        local_sem.at[n % depth, j],
                    )
                    for j, ref in enumerate(slots)
                ]
            )
            for copy in fetching[-1]:
                copy.start()

    for _ in range(depth - 1):
        fetch()

    def next_sum():
        fetch()
        n = len(done)
        for copy in fetching[n]:
            copy.wait()
        done.append(n)
        return dot(picked(code_ref[order[n][1]], capacity), fetched[n % depth], 0, 0)

    return next_sum


def combine_kernel(capacity, count, code_ref, *refs):
    slots = refs[:count]
    mine_ref, theirs_ref, fetched, local_sem = refs[-4:]
    order = [(slots, r) for r in (7, 6, 3, 2, 5, 4, 1, 0)]
    next_sum = fetcher(order, fetched, local_sem, capacity, code_ref)
    for _, r in order:
        (theirs_ref if r % 2 else mine_ref)[r // 2] = next_sum().astype(jnp.bfloat16)


def combine(code, slots, capacity, after):
    _, count, rows = code.shape
    width = slots[0].shape[1]
    vmem = pl.BlockSpec(memory_space=pltpu.VMEM)
    anywhere = pl.BlockSpec(memory_space=pl.ANY)
    four = jax.ShapeDtypeStruct((4, rows, width), jnp.bfloat16)
    return pl.pallas_call(
        functools.partial(combine_kernel, capacity, count),
        out_shape=(four, four),
        in_specs=[vmem] + [anywhere] * (count + len(after)),
        out_specs=[vmem, vmem],
        scratch_shapes=[
            pltpu.VMEM((4, count * capacity, width), jnp.bfloat16),
            pltpu.SemaphoreType.DMA((4, count)),
        ],
        compiler_params=pltpu.CompilerParams(vmem_limit_bytes=VM),
        cost_estimate=lasts(12),
        name="combine",
    )(code, *slots, *after)


def return_kernel(capacity, count, far_mask, code_ref, mine_ref, theirs_ref, go_ref, *refs):
    mixes = refs[:count]
    (out_ref, near_ref, far_ref, come_ref, fetched, core_got, own, theirs_mix, core_got_mix, half_pair, half_chip, from_chip,
     from_pair, send_sem, recv_sem, local_sem) = refs[-16:]
    rows = out_ref.shape[0]
    half = rows // 2
    _, core = flipped("expert", 1)
    _, chip = flipped("expert", 2)
    _, pair = flipped("dp", PAIR)
    _, far = flipped("dp", far_mask)
    greet([core, chip, pair, far])
    push = Pusher(send_sem, recv_sem)
    beside = push(go_ref, come_ref, far)
    crossing = {i: push(theirs_ref.at[i], core_got.at[i], core) for i in (3, 1, 2, 0)}
    order = [(mixes, r) for r in (7, 6, 3, 2, 5, 4, 1, 0)]
    next_sum = fetcher(order, fetched, local_sem, capacity, code_ref)

    def plus(a, b):
        return (a.astype(jnp.float32) + b.astype(jnp.float32)).astype(jnp.bfloat16)

    def mix(i, ref, at):
        theirs_mix[i] = next_sum().astype(jnp.bfloat16)
        copy = push(theirs_mix.at[i], core_got_mix.at[i], core)
        mine = next_sum()
        copy.wait_recv()
        ref[at] = plus(mine, core_got_mix[i])

    crossing[3].wait_recv()
    own[3] = plus(mine_ref[3], core_got[3])
    at_pair = push(own.at[3, 0:half], half_pair, pair)
    at_chip = push(own.at[3, half:rows], half_chip, chip)
    crossing[1].wait_recv()
    own[1] = plus(mine_ref[1], core_got[1])
    low_chip = push(own.at[1, half:rows], from_chip.at[half:rows], chip)
    crossing[2].wait_recv()
    own[2] = plus(mine_ref[2], core_got[2])
    high_pair = push(own.at[2, 0:half], from_pair.at[0:half], pair)
    crossing[0].wait_recv()
    out_ref[...] = mine_ref[0].astype(jnp.float32) + core_got[0].astype(jnp.float32)
    mix(3, far_ref, 1)
    mix(1, far_ref, 0)
    at_pair.wait_recv()
    own[1, :half] = plus(own[1, :half], half_pair[...])
    high_chip = push(own.at[1, 0:half], from_chip.at[0:half], chip)
    at_chip.wait_recv()
    own[2, half:] = plus(own[2, half:], half_chip[...])
    low_pair = push(own.at[2, half:rows], from_pair.at[half:rows], pair)
    mix(2, near_ref, 1)
    mix(0, near_ref, 0)
    low_chip.wait_recv()
    high_pair.wait_recv()
    high_chip.wait_recv()
    low_pair.wait_recv()
    out_ref[...] += from_chip[...].astype(jnp.float32) + from_pair[...].astype(jnp.float32)
    beside.wait_recv()
    push.finish()


def return_sums(code, mine, theirs, mixes, capacity, go, far_mask, label, after):
    _, count, rows = code.shape
    width = mine.shape[2]
    vmem = pl.BlockSpec(memory_space=pltpu.VMEM)
    anywhere = pl.BlockSpec(memory_space=pl.ANY)
    four = pltpu.VMEM((4, rows, width), jnp.bfloat16)
    two = jax.ShapeDtypeStruct((2, rows, width), jnp.bfloat16)
    return pl.pallas_call(
        functools.partial(return_kernel, capacity, count, far_mask),
        out_shape=(
            jax.ShapeDtypeStruct((rows, width), jnp.float32),
            two,
            two,
            jax.ShapeDtypeStruct(go.shape, jnp.bfloat16),
        ),
        in_specs=[vmem] * 3 + [anywhere] * (1 + count + len(after)),
        out_specs=[vmem] * 3 + [anywhere],
        scratch_shapes=[pltpu.VMEM((4, count * capacity, width), jnp.bfloat16), four, four, four, four]
        + [pltpu.VMEM((rows // 2, width), jnp.bfloat16)] * 2
        + [pltpu.VMEM((rows, width), jnp.bfloat16)] * 2
        + [
            pltpu.SemaphoreType.DMA((15,)),
            pltpu.SemaphoreType.DMA((15,)),
            pltpu.SemaphoreType.DMA((4, count)),
        ],
        compiler_params=pltpu.CompilerParams(
            collective_id=label, has_side_effects=True, vmem_limit_bytes=VM
        ),
        cost_estimate=lasts(37),
        name="return_sums",
    )(code, mine, theirs, go, *mixes, *after)


def settle_kernel(waits, bit_ref, keep_hbm, got_hbm, *refs):
    stay_ref, go_ref = refs[waits : waits + 2]
    keep_ref, got_ref, sem = refs[-3:]
    arriving = [
        pltpu.make_async_copy(src, dst, sem.at[i])
        for i, (src, dst) in enumerate(((keep_hbm, keep_ref), (got_hbm, got_ref)))
    ]
    for copy in arriving:
        copy.start()
    for copy in arriving:
        copy.wait()
    bit = bit_ref[0]
    for high in range(keep_ref.shape[0]):
        for low in range(keep_ref.shape[2]):
            for ref, side in ((stay_ref, bit), (go_ref, 1 - bit)):
                total = keep_ref[high, side, low].astype(jnp.float32) + got_ref[
                    high, side, low
                ].astype(jnp.float32)
                ref[high, low] = total.astype(jnp.bfloat16)


def settle(keep, got, mask, label, after, passed=()):
    count, rows, columns = keep.shape
    low = 1 if mask == PAIR else 2
    shape = (count // 2 // low, 2, low, rows, columns)
    half = jax.ShapeDtypeStruct((count // 2 // low, low, rows, columns), jnp.bfloat16)
    bit = lax.rem(lax.axis_index("dp") // mask, 2)
    vmem = pl.BlockSpec(memory_space=pltpu.VMEM)
    anywhere = pl.BlockSpec(memory_space=pl.ANY)
    stay, go, *passed = pl.pallas_call(
        functools.partial(settle_kernel, len(after) + len(passed)),
        out_shape=[half, half] + [jax.ShapeDtypeStruct(p.shape, p.dtype) for p in passed],
        in_specs=[pl.BlockSpec(memory_space=pltpu.SMEM)] + [anywhere] * (2 + len(after) + len(passed)),
        scratch_shapes=[
            pltpu.VMEM(shape, jnp.bfloat16),
            pltpu.VMEM(shape, jnp.bfloat16),
            pltpu.SemaphoreType.DMA((2,)),
        ],
        out_specs=[vmem, vmem] + [anywhere] * len(passed),
        input_output_aliases={3 + len(after) + i: 2 + i for i in range(len(passed))},
        compiler_params=pltpu.CompilerParams(vmem_limit_bytes=VM),
        cost_estimate=lasts(3),
        name="settle_%s" % label,
    )(bit.reshape(1), keep.reshape(shape), got.reshape(shape), *after, *passed)
    return stay.reshape(-1, rows, columns), go.reshape(-1, rows, columns), *passed


def settle_mix_kernel(near_ref, got_ref, *refs):
    refs[-1][...] = (near_ref[1].astype(jnp.float32) + got_ref[1].astype(jnp.float32)).astype(jnp.bfloat16)


def settle_mix(near, got, after):
    vmem = pl.BlockSpec(memory_space=pltpu.VMEM)
    return pl.pallas_call(
        settle_mix_kernel,
        out_shape=jax.ShapeDtypeStruct(near.shape[1:], jnp.bfloat16),
        in_specs=[vmem] * 2 + [pl.BlockSpec(memory_space=pl.ANY)] * len(after),
        out_specs=vmem,
        compiler_params=pltpu.CompilerParams(vmem_limit_bytes=VM),
        cost_estimate=lasts(3),
        name="settle_mix",
    )(near, got, *after)


EPS_STAT = 1e-30
STAT_DECAY = 0.5
LEARN_RATE = 0.5
CLIP_LEVEL = 0.05


def decayed(old, new):
    return STAT_DECAY * old + (1.0 - STAT_DECAY) * new


def finish_kernel(count, groups, half, orders, spans, *refs):
    bits = count.bit_length() - 1
    steps = len(orders[0])
    (mine_hbm, own_0, own_1, got_0, got_1, stay_2, come_2, keep_3, come_3, near_mix_ref, got_mix_ref,
     up_rows_ref, down_rows_ref, up_cols_ref, down_cols_ref, qkv_rows_ref, out_rows_ref, moments_ref, qkv_cols_ref,
     out_cols_ref) = refs[:20]
    (dense_ref, ends_ref, pair_mix_ref, out_ref, sums_ref, up_new_ref, down_new_ref, dense_out_ref,
     dense_new_ref) = refs[20:29]
    sum_ref, first_got, *got = refs[29 : 31 + steps]
    (mine_ref, load_sem, go_s, far_go_s, far_stay_s, far_got_s, mix_s, pay_s, got_s, dense_pay_s, dense_got_s, spread_s,
     up_old_ref, down_old_ref, dense_old_ref, dense_cols_ref, send_sem, recv_sem) = refs[31 + steps :]
    width = up_rows_ref.shape[1]
    ff = down_rows_ref.shape[1]
    wide = width // 2
    own_up = width // count
    own_down = ff // count
    me = lax.axis_index("dp")
    place = lax.axis_index("expert")
    after = [lax.rem(me + k, count) for k in range(count)]
    beside = [lax.rem(place + k, groups) for k in range(groups)]
    pair_bit, pair = flipped("dp", PAIR)
    far_bit, far = flipped("dp", FAR)
    core, core_peer = flipped("expert", 1)
    chip, chip_peer = flipped("expert", 2)
    links = [flipped("dp", 1 << b) for b in range(bits)] + [(chip, chip_peer)]
    whole = (slice(None),) * bits
    loading = pltpu.make_async_copy(mine_hbm.at[whole + (core,)], mine_ref, load_sem)
    loading.start()
    greet([{"dp": after[k]} for k in range(1, count)] + [{"expert": beside[k]} for k in range(1, groups)])
    push = Pusher(send_sem, recv_sem)

    def plus(a, b):
        return (a.astype(jnp.float32) + b.astype(jnp.float32)).astype(jnp.bfloat16)

    flying = [
        push(mine_hbm.at[whole + (1 - core, slice(None), slice(None), span)], first_got.at[..., span], core_peer)
        for span in spans
    ]
    for low in range(2):
        far_go_s[low] = plus(keep_3[1 - far_bit, low], come_3[1 - far_bit, low])
    far_exchange = push(far_go_s, far_got_s, far)
    go_s[0] = plus(stay_2[1 - pair_bit], come_2[1 - pair_bit])
    cross_2 = push(go_s.at[0], ends_ref.at[2], pair)
    mix_s[...] = plus(near_mix_ref[1], got_mix_ref[1])
    cross_mix = push(mix_s, pair_mix_ref, pair)
    ends_ref[0] = plus(stay_2[pair_bit], come_2[pair_bit])
    for low in range(2):
        far_stay_s[low] = plus(keep_3[far_bit, low], come_3[far_bit, low])

    def own_columns(*tables):
        here = pl.ds(pl.multiple_of(me * LANES, LANES), LANES)
        rows = [table[:, here] for table in tables]
        return padded(jnp.concatenate(rows, axis=0)).T

    def padded(rows):
        return jnp.concatenate([rows, jnp.zeros((LANES - rows.shape[0], LANES), jnp.float32)], axis=0)

    up_old_ref[...] = own_columns(up_rows_ref)
    dense_old_ref[...] = own_columns(qkv_rows_ref, out_rows_ref, moments_ref)
    around = down_rows_ref[:, pl.ds(pl.multiple_of(me // 2 * LANES, LANES), LANES)]
    both_halves = padded(around).T
    down_old_ref[...] = jnp.where(lax.rem(me, 2) == 0, both_halves[:own_down], both_halves[own_down:])
    dense_cols_ref[:, : qkv_cols_ref.shape[1]] = qkv_cols_ref[...]
    dense_cols_ref[:, qkv_cols_ref.shape[1] :] = out_cols_ref[...]

    def column_of(table_ref, lane, at):
        return jnp.sum(jnp.where(lane == at, table_ref[...], 0.0), axis=1, keepdims=True)

    up_lane = lax.broadcasted_iota(jnp.int32, (own_up, LANES), 1)
    down_lane = lax.broadcasted_iota(jnp.int32, (own_down, LANES), 1)
    up_new_ref[...] = jnp.zeros_like(up_new_ref)
    down_new_ref[...] = jnp.zeros_like(down_new_ref)

    def factored(grad, old):
        square = grad * grad
        new = decayed(old, jnp.mean(square + EPS_STAT, axis=1, keepdims=True))
        return (
            new,
            jnp.sum(square + EPS_STAT, axis=0, keepdims=True),
            jnp.sum(square * (1.0 / new), axis=0, keepdims=True),
        )

    def expert(values, at):
        for kind, (part, old_ref, new_ref, lane, rows) in enumerate(
            (
                (values[:own_up, :], up_old_ref, up_new_ref, up_lane, own_up),
                (values[own_up:, :], down_old_ref, down_new_ref, down_lane, own_down),
            )
        ):
            new, total, scaled = factored(part.astype(jnp.float32), column_of(old_ref, lane, at))
            new_ref[:rows, :] = jnp.where(lane == at, new, new_ref[:rows, :])
            for h in range(2):
                span = slice(h * wide, (h + 1) * wide)
                pay_s[at, 4 * kind + h : 4 * kind + h + 1, :] = total[:, span]
                pay_s[at, 4 * kind + 2 + h : 4 * kind + 3 + h, :] = scaled[:, span]

    own_at, got_at = pair_bit * half, (1 - pair_bit) * half

    def at_place(chosen, span):
        return tuple(chosen.get(bits - 1 - i, slice(None)) for i in range(bits)) + (
            chosen.get(bits, slice(None)),
            slice(None),
            span,
        )

    def got_place(step, span):
        return (slice(None),) * (steps - 1 - step) + (slice(None), span)

    loading.wait()
    chosen = [{} for _ in spans]
    for step in range(steps + 1):
        for part, span in enumerate(spans):
            flying[part].wait_recv()
            if step == 0:
                sum_ref[..., span] = plus(mine_ref[..., span], first_got[..., span])
            else:
                here = at_place(chosen[part], span)
                sum_ref[here] = plus(sum_ref[here], got[step - 1][got_place(step - 1, span)])
            if step < steps:
                link = orders[part][step]
                bit, peer = links[link]
                away = at_place({**chosen[part], link: 1 - bit}, span)
                flying[part] = push(sum_ref.at[away], got[step].at[got_place(step, span)], peer)
                chosen[part] = {**chosen[part], link: bit}
            else:
                dense_ref[core, chip, :, span] = sum_ref[at_place(chosen[part], span)]
                block = dense_ref.at[core, chip, :, span]
                flying[part] = push(block, block, chip_peer)
        if step == 0:
            expert(own_0, own_at)
            expert(got_0, got_at)
            expert(own_1, own_at + 1)
            expert(got_1, got_at + 1)
        elif step == 1:
            expert(ends_ref[0], own_at + 2)
        elif step == steps - 1:
            cross_2.wait_recv()
            expert(ends_ref[2], got_at + 2)
            far_exchange.wait_recv()
            go_s[1] = plus(far_stay_s[1 - pair_bit], far_got_s[1 - pair_bit])
            cross_3 = push(go_s.at[1], ends_ref.at[3], pair)
            ends_ref[1] = plus(far_stay_s[pair_bit], far_got_s[pair_bit])
            expert(ends_ref[1], own_at + 3)
    for part, span in enumerate(spans):
        flying[part].wait_recv()
        block = dense_ref.at[core, :, :, span]
        flying[part] = push(block, block, core_peer)
    cross_3.wait_recv()
    expert(ends_ref[3], got_at + 3)
    arriving = [push(pay_s.at[after[k]], got_s.at[k], {"dp": after[k]}) for k in range(1, count)]
    for copy in flying:
        copy.wait_recv()

    columns = dense_cols_ref.shape[1]
    piece = columns // count
    dense = dense_ref[...].reshape(own_up, dense_ref.shape[3])
    dense_lane = lax.broadcasted_iota(jnp.int32, dense_new_ref.shape, 1)
    old = dense_old_ref[...]
    qkv_columns = columns - width
    totals, scaleds, rows_new = [], [], []
    for at, span in enumerate((slice(0, qkv_columns), slice(qkv_columns, columns))):
        new, total, scaled = factored(
            dense[:, span].astype(jnp.float32), column_of(dense_old_ref, dense_lane, at)
        )
        rows_new.append(new)
        totals.append(total)
        scaleds.append(scaled)
    gain_lanes = (dense_lane == 2) | (dense_lane == 3)
    gains = pltpu.roll(dense[:, columns:].astype(jnp.float32), 2, 1)
    moments = jnp.where(gain_lanes, decayed(old, gains * gains + EPS_STAT), 1.0)
    gain_steps = jnp.where(gain_lanes, gains * lax.rsqrt(moments), 0.0)
    dense_new_ref[...] = jnp.where(
        dense_lane == 0,
        rows_new[0],
        jnp.where(dense_lane == 1, rows_new[1], jnp.where(gain_lanes, gain_steps, pltpu.roll(moments, 2, 1))),
    )
    gain_squares = jnp.sum(jnp.sum(gain_steps * gain_steps, axis=1, keepdims=True), axis=0, keepdims=True)
    total = jnp.concatenate(totals, axis=1)
    scaled = jnp.concatenate(scaleds, axis=1)
    for d in range(count):
        span = slice(d * piece, (d + 1) * piece)
        dense_pay_s[d] = jnp.concatenate(
            [total[:, span], scaled[:, span], jnp.broadcast_to(gain_squares, (1, piece)), jnp.zeros((5, piece), jnp.float32)],
            axis=0,
        )
    dense_arriving = [push(dense_pay_s.at[after[k]], dense_got_s.at[k], {"dp": after[k]}) for k in range(1, count)]

    tile = pay_s[me]
    for k in range(1, count):
        arriving[k - 1].wait_recv()
        tile = tile + got_s[k]
    made = []
    tops = []
    for kind, (rows_ref, cols_ref, rows) in enumerate(
        ((up_rows_ref, up_cols_ref, width), (down_rows_ref, down_cols_ref, ff))
    ):
        here = pl.ds(me, 1)
        square = jnp.concatenate([tile[4 * kind + h : 4 * kind + h + 1] for h in range(2)], axis=1)
        scaled = jnp.concatenate([tile[4 * kind + 2 + h : 4 * kind + 3 + h] for h in range(2)], axis=1)
        new_columns = decayed(cols_ref[here, :], square / rows)
        row_mean = decayed(
            jnp.mean(rows_ref[here, :], axis=1, keepdims=True),
            jnp.sum(square, axis=1, keepdims=True) / (rows * width),
        )
        squares = row_mean * jnp.sum(scaled / new_columns, axis=1, keepdims=True)
        made += [new_columns[:, :wide], new_columns[:, wide:]]
        tops += [jnp.broadcast_to(v, (1, wide)) for v in (row_mean, squares)]
    out_ref[me] = jnp.concatenate(made + tops, axis=0)
    arriving = [push(out_ref.at[me], out_ref.at[me], {"dp": after[k]}) for k in range(1, count)]

    tile = dense_pay_s[me]
    for k in range(1, count):
        dense_arriving[k - 1].wait_recv()
        tile = tile + dense_got_s[k]
    own_piece = pl.ds(pl.multiple_of(me * piece, LANES), piece)
    new_columns = decayed(dense_cols_ref[:, own_piece], tile[0:1] / width)
    is_qkv = lax.broadcasted_iota(jnp.int32, (1, piece), 1) + me * piece < qkv_columns
    ratio = tile[1:2] / new_columns
    sums = [
        jnp.sum(jnp.where(chosen_columns, row, 0.0), axis=1, keepdims=True)
        for row in (ratio, tile[0:1])
        for chosen_columns in (is_qkv, ~is_qkv)
    ]
    dense_out_ref[me] = jnp.concatenate(
        [new_columns]
        + [jnp.broadcast_to(v, (1, piece)) for v in sums]
        + [tile[2:3], jnp.zeros((2, piece), jnp.float32)],
        axis=0,
    )
    dense_arriving = [push(dense_out_ref.at[me], dense_out_ref.at[me], {"dp": after[k]}) for k in range(1, count)]

    for copy in arriving:
        copy.wait_recv()
    total = out_ref[0, :, :LANES]
    for a in range(1, count):
        total = total + out_ref[a, :, :LANES]
    spread_s[place] = total
    arriving = [push(spread_s.at[place], spread_s.at[place], {"expert": beside[k]}) for k in range(1, groups)]
    for copy in arriving + dense_arriving + [cross_mix]:
        copy.wait_recv()
    total = spread_s[0]
    for e in range(1, groups):
        total = total + spread_s[e]
    sums_ref[...] = total
    push.finish()


FAR = 4


def finish(dense, owns, gots, settling, mixes, statistics, label):
    count = lax.axis_size("dp")
    groups = lax.axis_size("expert")
    width, dense_width = dense.shape
    bits = count.bit_length() - 1
    quarter = width // count // 4
    parts = 6
    tiles = dense_width // LANES
    bounds = [LANES * (tiles * i // parts) for i in range(parts + 1)]
    spans = [slice(a, b) for a, b in zip(bounds[:-1], bounds[1:])]
    last = tuple(range(1, bits))
    orders = [((bits, 0) if part % 2 == 0 else (0, bits)) + last for part in range(parts)]
    half = (2,) * bits + (2, quarter, dense_width)
    rows = owns[0].shape[0]
    own_up, own_down = width // count, rows - width // count
    dense_columns = dense_width - LANES
    piece = dense_columns // count
    vmem = pl.BlockSpec(memory_space=pltpu.VMEM)
    stat_tiles = (count, 8, width // 2)
    dense_tiles = (count, 8, piece)
    copies = parts * (bits + 4) + 4 * (count - 1) + groups - 1 + 4
    shape = lambda *s: jax.ShapeDtypeStruct(s, jnp.float32)
    low = lambda *s: jax.ShapeDtypeStruct(s, jnp.bfloat16)
    held = lambda *s: pltpu.VMEM(s, jnp.bfloat16)
    outs = (
        low(2, 2, quarter, dense_width),
        low(4, rows, width),
        low(*mixes[0].shape[1:]),
        shape(*stat_tiles),
        shape(8, LANES),
        shape(LANES, LANES),
        shape(LANES, LANES),
        shape(*dense_tiles),
        shape(width // count, LANES),
    )
    args = (
        dense.reshape((2,) * bits + (2, 2, quarter, dense_width)),
        *owns, *gots, *settling, *mixes, *statistics,
    )
    own, *rest = pl.pallas_call(
        functools.partial(finish_kernel, count, groups, 4, orders, spans),
        out_shape=outs,
        in_specs=[pl.BlockSpec(memory_space=pl.ANY)] + [vmem] * (len(args) - 1),
        out_specs=[vmem] * len(outs),
        scratch_shapes=[held(*half), held(*half)]
        + [held(*((2,) * (bits - step)), quarter, dense_width) for step in range(bits + 1)]
        + [
            held(*half),
            pltpu.SemaphoreType.DMA,
            held(2, rows, width),
            held(2, rows, width),
            held(2, rows, width),
            held(2, rows, width),
            held(*mixes[0].shape[1:]),
            pltpu.VMEM(stat_tiles, jnp.float32),
            pltpu.VMEM(stat_tiles, jnp.float32),
            pltpu.VMEM(dense_tiles, jnp.float32),
            pltpu.VMEM(dense_tiles, jnp.float32),
            pltpu.VMEM((groups, 8, LANES), jnp.float32),
            pltpu.VMEM((own_up, LANES), jnp.float32),
            pltpu.VMEM((own_down, LANES), jnp.float32),
            pltpu.VMEM((own_up, LANES), jnp.float32),
            pltpu.VMEM((1, dense_columns), jnp.float32),
            pltpu.SemaphoreType.DMA((copies,)),
            pltpu.SemaphoreType.DMA((copies,)),
        ],
        compiler_params=pltpu.CompilerParams(
            collective_id=label, has_side_effects=True, vmem_limit_bytes=VM
        ),
        cost_estimate=lasts(75),
        name="finish",
    )(*args)
    return own.reshape(width // count, dense_width), *rest


def update_kernel(counts, half, early, s_ref, *refs):
    owns, gots = refs[:early], refs[early : 2 * early]
    (dense_ref, ends_ref, pair_mix_ref, tiles_ref, sums_ref, up_new_ref, down_new_ref, dense_tiles_ref, dense_new_ref,
     qkv_old_ref, out_old_ref, middle_ref, near_mix_ref, got_mix_ref, up_w_ref, down_w_ref, qkv_w_ref, out_w_ref,
     block_ref, up_out_ref, down_out_ref, up_rows_ref, down_rows_ref, up_cols_ref, down_cols_ref,
     qkv_out_ref, out_out_ref, qkv_cols_ref, out_cols_ref, qkv_rows_ref, out_rows_ref, gains_ref, moments_ref,
     rms_ref) = refs[2 * early :]
    block_ref[...] = middle_ref[...] + (
        near_mix_ref[0].astype(jnp.float32)
        + got_mix_ref[0].astype(jnp.float32)
        + pair_mix_ref[...].astype(jnp.float32)
    )
    late = half - early
    own_up = up_out_ref.shape[1]
    own_down = down_out_ref.shape[1]
    wide = tiles_ref.shape[2]
    pair_bit = s_ref[0]
    count = dense_tiles_ref.shape[0]
    dense_sums = dense_tiles_ref[0, :, 0:1]
    for a in range(1, count):
        dense_sums = dense_sums + dense_tiles_ref[a, :, 0:1]
    width = qkv_old_ref.shape[1]
    qkv_columns = qkv_out_ref.shape[1]
    row_means = []
    squares = [dense_tiles_ref[0, 5:6, 0:1]]
    for at, (old_ref, columns) in enumerate(((qkv_old_ref, qkv_columns), (out_old_ref, width))):
        row_means.append(
            decayed(
                jnp.mean(old_ref[...], axis=1, keepdims=True),
                dense_sums[3 + at : 4 + at] / (width * columns),
            )
        )
        squares.append(row_means[-1] * dense_sums[1 + at : 2 + at])
    squares += [sums_ref[5:6, 0:1], sums_ref[7:8, 0:1]]
    roots = [jnp.sqrt(square / number) for square, number in zip(squares, counts)]
    factors = [LEARN_RATE / jnp.maximum(1.0, root / CLIP_LEVEL) for root in roots]
    for i, root in enumerate(roots):
        rms_ref[i] = root[0, 0]

    up_table = up_new_ref[...]
    down_table = down_new_ref[...]
    lane = lax.broadcasted_iota(jnp.int32, up_table.shape, 1)

    def expert(ref, at):
        tile = tiles_ref[at]
        for kind, (table, weight_ref, out_ref, first, rows) in enumerate(
            (
                (up_table, up_w_ref, up_out_ref, 0, own_up),
                (down_table, down_w_ref, down_out_ref, own_up, own_down),
            )
        ):
            row_mean = tile[4 + 2 * kind : 5 + 2 * kind, 0:1]
            column = jnp.sum(jnp.where(lane == at, table, 0.0), axis=1, keepdims=True)[:rows]
            scale = factors[3 + kind] * lax.rsqrt(column / row_mean)
            for h in range(2):
                span = slice(h * wide, (h + 1) * wide)
                columns = lax.rsqrt(tile[2 * kind + h : 2 * kind + h + 1, :])
                out_ref[at, :, span] = (
                    weight_ref[at, :, span].astype(jnp.float32)
                    - ref[first : first + rows, span].astype(jnp.float32) * scale * columns
                )

    own_at, got_at = pair_bit * half, (1 - pair_bit) * half
    for j in range(early):
        expert(owns[j], own_at + j)
        expert(gots[j], got_at + j)
    for j in range(late):
        expert(ends_ref.at[j], own_at + early + j)
        expert(ends_ref.at[late + j], got_at + early + j)
    up_rows_ref[...] = up_table.T[: up_rows_ref.shape[0], :own_up]
    down_rows_ref[...] = down_table.T[: down_rows_ref.shape[0], :own_down]
    for a in range(up_cols_ref.shape[0]):
        for h in range(2):
            span = slice(h * wide, (h + 1) * wide)
            up_cols_ref[a : a + 1, span] = tiles_ref[a, h : h + 1, :]
            down_cols_ref[a : a + 1, span] = tiles_ref[a, 2 + h : 3 + h, :]

    table = dense_new_ref[...]
    scales = [
        factors[1 + at] * lax.rsqrt(table[:, at : at + 1] / row_means[at]) for at in range(2)
    ]
    piece = dense_tiles_ref.shape[2]
    for first in range(0, qkv_columns + width, LANES):
        at = 0 if first < qkv_columns else 1
        weight_ref, out_ref, cols_ref = (
            (qkv_w_ref, qkv_out_ref, qkv_cols_ref) if at == 0 else (out_w_ref, out_out_ref, out_cols_ref)
        )
        here = slice(first - at * qkv_columns, first - at * qkv_columns + LANES)
        within = first % piece
        columns = dense_tiles_ref[first // piece, 0:1, within : within + LANES]
        cols_ref[:, here] = columns
        out_ref[:, here] = weight_ref[:, here].astype(jnp.float32) - dense_ref[
            :, first : first + LANES
        ].astype(jnp.float32) * scales[at] * lax.rsqrt(columns)
    turned = table.T
    qkv_rows_ref[...] = turned[0:1]
    out_rows_ref[...] = turned[1:2]
    gains_ref[...] = -factors[0] * turned[2:4]
    moments_ref[...] = turned[4:6]


def update(owns, gots, finished, row_statistics, middle, mixes, up_w, down_w, qkv_w, out_w):
    count = lax.axis_size("dp")
    groups = lax.axis_size("expert")
    me = lax.axis_index("dp")
    experts, width, up_columns = up_w.shape
    ff = down_w.shape[1]
    qkv_columns = qkv_w.shape[1]
    own_up, own_down = width // count, ff // count
    counts = (
        float(2 * width),
        float(width * qkv_columns),
        float(width * width),
        float(groups * experts * width * up_columns),
        float(groups * experts * ff * width),
    )
    ends = finished[1]
    early = len(owns)
    whole = lambda *shape: pl.BlockSpec(shape, lambda g, s: (0,) * len(shape))
    shape = lambda *s: jax.ShapeDtypeStruct(s, jnp.float32)
    rows = own_up + own_down
    outs = [
        shape(*middle.shape),
        shape(experts, own_up, up_columns),
        shape(experts, own_down, width),
        shape(experts, own_up),
        shape(experts, own_down),
        shape(experts, up_columns),
        shape(experts, width),
        shape(own_up, qkv_columns),
        shape(own_up, width),
        shape(1, qkv_columns),
        shape(1, width),
        shape(1, own_up),
        shape(1, own_up),
        shape(2, own_up),
        shape(2, own_up),
        shape(len(counts)),
    ]
    return pl.pallas_call(
        functools.partial(update_kernel, counts, early + ends.shape[0] // 2, early),
        out_shape=outs,
        grid_spec=pltpu.PrefetchScalarGridSpec(
            num_scalar_prefetch=1,
            grid=(1,),
            in_specs=[whole(rows, width)] * (2 * early)
            + [whole(*a.shape) for a in (*finished, *row_statistics, middle, *mixes)]
            + [
                pl.BlockSpec((experts, own_up, up_columns), lambda g, s: (0, s[1], 0)),
                pl.BlockSpec((experts, own_down, width), lambda g, s: (0, s[1], 0)),
                pl.BlockSpec((own_up, qkv_columns), lambda g, s: (s[1], 0)),
                pl.BlockSpec((own_up, width), lambda g, s: (s[1], 0)),
            ],
            out_specs=[whole(*o.shape) for o in outs[:-1]] + [pl.BlockSpec(memory_space=pltpu.SMEM)],
        ),
        compiler_params=pltpu.CompilerParams(vmem_limit_bytes=VM),
        cost_estimate=lasts(6),
        name="update",
    )(
        jnp.stack([lax.rem(me // PAIR, 2), me]),
        *owns, *gots, *finished, *row_statistics, middle, *mixes, up_w, down_w, qkv_w, out_w,
    )


D = 1024
FF = 512
TOP = 8


def swap(values, axis, mask):
    count = lax.axis_size(axis)
    return lax.ppermute(values, axis, [(i, i ^ mask) for i in range(count)])


def swap_pair(values):
    return swap(values, "dp", PAIR)


def swap_chip(values):
    return swap(values, "expert", 2)


def swap_core(values):
    return swap(values, "expert", 1)


def plus(a, b):
    return (a.astype(jnp.float32) + b.astype(jnp.float32)).astype(jnp.bfloat16)


def halve(blocks, axis, mask):
    bit = lax.rem(lax.axis_index(axis) // mask, 2)
    keep = lax.dynamic_index_in_dim(blocks, bit, 1, keepdims=False)
    give = lax.dynamic_index_in_dim(blocks, 1 - bit, 1, keepdims=False)
    return keep, swap(give, axis, mask)


def reduce_dense_far(blocks):
    count = lax.axis_size("dp")
    width, columns = blocks.shape
    rows = width // count
    blocks = blocks.reshape(count, 2, 2, rows // 4, columns)
    keep, got = halve(jnp.moveaxis(blocks, 2, 1), "expert", 1)
    keep, got = halve(plus(keep, got), "expert", 2)
    blocks = plus(keep, got)
    low = 1
    while low < count:
        keep, got = halve(blocks.reshape((-1, 2, 1) + blocks.shape[1:]), "dp", low)
        blocks = plus(keep, got).reshape((-1,) + blocks.shape[1:])
        low *= 2
    mine = blocks[0]
    chip = lax.axis_index("expert") // 2
    core = lax.rem(lax.axis_index("expert"), 2)
    other = swap_chip(mine)
    both = jnp.where(chip == 0, jnp.stack([mine, other]), jnp.stack([other, mine]))
    across = swap_core(both)
    all_four = jnp.where(core == 0, jnp.stack([both, across], 1), jnp.stack([across, both], 1))
    return all_four.reshape(rows, columns)


def own_share(matrix, along):
    count = lax.axis_size("dp")
    width = matrix.shape[along] // count
    return lax.dynamic_slice_in_dim(matrix, lax.axis_index("dp") * width, width, along)


def factored(part, rows_old):
    square = part * part
    rows_new = decayed(rows_old, jnp.mean(square + EPS_STAT, axis=-1))
    return (
        rows_new,
        jnp.sum(square + EPS_STAT, axis=-2),
        jnp.sum(square / rows_new[..., None], axis=-2),
    )


def per_device(
    hidden_in,
    out_grad,
    segment_ids,
    parent_ids,
    positions,
    expert_ids,
    gate_weights,
    norm_gains,
    qkv_weight,
    out_weight,
    gate_up_weight,
    down_weight,
    gain_moment,
    qkv_rows,
    qkv_cols,
    out_rows,
    out_cols,
    gateup_rows,
    gateup_cols,
    down_rows,
    down_cols,
):
    rows_here = hidden_in.shape[0]
    dp_count = lax.axis_size("dp")
    groups = lax.axis_size("expert")
    experts_here = gate_up_weight.shape[0]
    total_experts = experts_here * groups
    capacity = 3 * rows_here * TOP // (2 * total_experts)
    half_experts = experts_here // 2
    dp_index = lax.axis_index("dp")
    pair_bit = lax.rem(dp_index // PAIR, 2)
    first_local = pair_bit * half_experts
    first_expert = lax.axis_index("expert") * experts_here + first_local

    weight_high = gate_weights.astype(jnp.bfloat16)
    weight_low = (gate_weights - weight_high.astype(jnp.float32)).astype(jnp.bfloat16)
    routing = jnp.concatenate([expert_ids.astype(jnp.bfloat16), weight_high, weight_low], axis=1).T
    routing = jnp.pad(routing, ((0, ROUTE_ROWS - routing.shape[0]), (0, D - rows_here)))
    grad_rows = jnp.concatenate([out_grad.astype(jnp.bfloat16), routing], axis=0)
    chip_grad_rows = swap_chip(grad_rows)
    pair_grad_rows = swap_pair(grad_rows)
    ids = jnp.stack([segment_ids, parent_ids, positions])
    normed, qkv, attended, lse, middle, normed_ffn = attend(
        hidden_in, ids, norm_gains, qkv_weight, out_weight
    )
    received, arrived, scale, code = gather_and_select(
        normed_ffn, grad_rows, chip_grad_rows, pair_grad_rows, capacity, experts_here, half_experts, TOP, 5
    )
    scalars = jnp.stack([first_local, lax.rem(dp_index, 2)])
    experts, chains = [], []

    def advance(j, after, come=None, passed=()):
        masks, stay, go = chains[j]
        come = swap(go, "dp", masks[0]) if come is None else come
        stay, go, *passed = settle(stay, come, masks[1], "%d_%d" % (j, masks[1]), after, passed)
        chains[j] = (masks[1:], stay, go)
        return (stay, *passed) if passed else stay

    masks = [1] + [1 << b for b in range(2, dp_count.bit_length() - 1)] + [PAIR]
    for j in range(half_experts):
        after = [experts[-1][2]] if experts else []
        if j == 3:
            after.append(advance(0, after))
        experts.append(
            run_expert(
                scalars, j, received, arrived, scale, gate_up_weight, down_weight, dp_count, after
            )
        )
        chains.append((masks, experts[j][0], experts[j][1]))
    mine, theirs = combine(code, [e[2] for e in experts], capacity, [])
    steps = [advance(1, [mine])]
    normed_f_grad, near_mix, far_mix, come = return_sums(
        code, mine, theirs, [e[3] for e in experts], capacity, chains[1][2], chains[1][0][0], 6, steps
    )
    steps = [normed_f_grad]
    steps.append(advance(0, steps))
    stay, far_mix = advance(2, steps[-1:], None, [far_mix])
    steps.append(stay)
    steps.append(advance(1, steps[-1:], come))
    input_grad, dense = attend_back(
        hidden_in, out_grad, middle, normed_f_grad, normed, qkv, attended, lse, ids, norm_gains, qkv_weight,
        out_weight, steps
    )
    got_mix = swap_chip(far_mix)
    qkv_columns = qkv_weight.shape[1]
    fast_tail = dp_count == experts_here and D // dp_count % 64 == 0
    if fast_tail:
        owns = [chains[j][1][0] for j in (0, 1)]
        gots = [swap_pair(chains[j][2][0]) for j in (0, 1)]
        settling = []
        for j in (2, 3):
            masks, stay, go = chains[j]
            settling += [stay, swap(go, "dp", masks[0])]
        settling[2:] = [x.reshape((2, 2) + x.shape[1:]) for x in settling[2:]]
        finished = finish(
            dense,
            owns,
            gots,
            settling,
            (near_mix, got_mix),
            (
                gateup_rows,
                down_rows,
                gateup_cols,
                down_cols,
                qkv_rows[None],
                out_rows[None],
                gain_moment,
                qkv_cols[None],
                out_cols[None],
            ),
            1,
        )
        (
            block_out,
            gate_up_new,
            down_new,
            gateup_rows_new,
            down_rows_new,
            gateup_cols_new,
            down_cols_new,
            qkv_new,
            out_new,
            qkv_cols_new,
            out_cols_new,
            qkv_rows_new,
            out_rows_new,
            gains_update,
            gain_moment_new,
            update_rms,
        ) = update(
            owns,
            gots,
            finished,
            (qkv_rows[None], out_rows[None]),
            middle,
            (near_mix, got_mix),
            gate_up_weight,
            down_weight,
            qkv_weight,
            out_weight,
        )
        qkv_cols_new, out_cols_new = qkv_cols_new[0], out_cols_new[0]
        qkv_rows_new, out_rows_new = qkv_rows_new[0], out_rows_new[0]
    else:
        for_pair = settle_mix(near_mix, got_mix, [input_grad])
        mix_parts = (near_mix[0], got_mix[0], swap_pair(for_pair))
        block_out = middle + sum(part.astype(jnp.float32) for part in mix_parts)
        dense_own = reduce_dense_far(dense)
        for j in range(half_experts):
            while len(chains[j][0]) > 1:
                advance(j, [dense_own])
        own_parts = [c[1][0] for c in chains]
        other_parts = [swap_pair(c[2][0]) for c in chains]
        own = jnp.stack(own_parts).astype(jnp.float32)
        other = jnp.stack(other_parts).astype(jnp.float32)
        parts = jnp.where(pair_bit == 0, jnp.concatenate([own, other]), jnp.concatenate([other, own]))
        gateup_part = parts[:, : D // dp_count]
        down_part = parts[:, D // dp_count :]
        gateup_rows_new, gateup_square, gateup_scaled = factored(gateup_part, own_share(gateup_rows, 1))
        down_rows_new, down_square, down_scaled = factored(down_part, own_share(down_rows, 1))
        sizes = [gateup_square.size, gateup_scaled.size, down_square.size, down_scaled.size]
        summed = total_over(
            jnp.concatenate(
                [
                    gateup_square.reshape(-1),
                    gateup_scaled.reshape(-1),
                    down_square.reshape(-1),
                    down_scaled.reshape(-1),
                    jnp.sum(gateup_rows_new, axis=1),
                    jnp.sum(down_rows_new, axis=1),
                ]
            ),
            "dp",
            1,
        )
        pieces = jnp.split(summed, [sum(sizes[: i + 1]) for i in range(4)])
        gateup_square, gateup_scaled, down_square, down_scaled = [
            p.reshape(experts_here, D) for p in pieces[:4]
        ]
        gateup_row_mean = pieces[4][:experts_here] / D
        down_row_mean = pieces[4][experts_here:] / FF
        gateup_cols_new = decayed(gateup_cols, gateup_square / D)
        down_cols_new = decayed(down_cols, down_square / FF)
        expert_squares = jnp.stack(
            [
                jnp.sum(gateup_row_mean * jnp.sum(gateup_scaled / gateup_cols_new, axis=1)),
                jnp.sum(down_row_mean * jnp.sum(down_scaled / down_cols_new, axis=1)),
            ]
        )
        spread_squares = collect(
            jnp.zeros((8, 128), jnp.float32).at[0, :2].set(expert_squares), "expert", 2
        )
        expert_squares = jnp.sum(spread_squares[:, 0, :2], axis=0)
        dense_own = dense_own.astype(jnp.float32)
        qkv_own = dense_own[:, :qkv_columns]
        out_own = dense_own[:, qkv_columns : qkv_columns + D]
        gains_own = dense_own[:, qkv_columns + D : qkv_columns + D + 2].T
        gain_moment_new = decayed(own_share(gain_moment, 1), gains_own * gains_own + EPS_STAT)
        gains_step = gains_own * lax.rsqrt(gain_moment_new)
        qkv_rows_new, qkv_square, qkv_scaled = factored(qkv_own, own_share(qkv_rows, 0))
        out_rows_new, out_square, out_scaled = factored(out_own, own_share(out_rows, 0))
        dense_sums = total_over(
            jnp.concatenate(
                [
                    qkv_square,
                    qkv_scaled,
                    out_square,
                    out_scaled,
                    jnp.stack(
                        [jnp.sum(qkv_rows_new), jnp.sum(out_rows_new), jnp.sum(gains_step * gains_step)]
                    ),
                ]
            ),
            "dp",
            4,
        )
        qkv_square, qkv_scaled, out_square, out_scaled, rest = jnp.split(
            dense_sums, [qkv_columns, 2 * qkv_columns, 2 * qkv_columns + D, 2 * qkv_columns + 2 * D]
        )
        qkv_row_mean = rest[0] / D
        out_row_mean = rest[1] / D
        qkv_cols_new = decayed(qkv_cols, qkv_square / D)
        out_cols_new = decayed(out_cols, out_square / D)
        squares = jnp.concatenate(
            [
                jnp.stack(
                    [
                        rest[2],
                        qkv_row_mean * jnp.sum(qkv_scaled / qkv_cols_new),
                        out_row_mean * jnp.sum(out_scaled / out_cols_new),
                    ]
                ),
                expert_squares,
            ]
        )
        element_counts = jnp.array(
            [2 * D, D * qkv_columns, D * D, total_experts * D * 2 * FF, total_experts * FF * D], jnp.float32
        )
        update_rms = jnp.sqrt(squares / element_counts)
        factors = LEARN_RATE / jnp.maximum(1.0, update_rms / CLIP_LEVEL)

        def stepped(weight, part, rows_new, row_mean, cols_new, factor):
            return weight.astype(jnp.float32) - part * (
                factor * lax.rsqrt(rows_new / row_mean[..., None])
            )[..., :, None] * lax.rsqrt(cols_new)[..., None, :]

        gains_update = -factors[0] * gains_step
        qkv_new = stepped(own_share(qkv_weight, 0), qkv_own, qkv_rows_new, qkv_row_mean, qkv_cols_new, factors[1])
        out_new = stepped(own_share(out_weight, 0), out_own, out_rows_new, out_row_mean, out_cols_new, factors[2])
        gate_up_new = stepped(
            own_share(gate_up_weight, 1), gateup_part, gateup_rows_new, gateup_row_mean, gateup_cols_new, factors[3]
        )
        down_new = stepped(
            own_share(down_weight, 1), down_part, down_rows_new, down_row_mean, down_cols_new, factors[4]
        )
    return (
        block_out,
        input_grad,
        update_rms,
        gains_update,
        gain_moment_new,
        qkv_new,
        qkv_rows_new,
        qkv_cols_new,
        out_new,
        out_rows_new,
        out_cols_new,
        gate_up_new,
        gateup_rows_new,
        gateup_cols_new,
        down_new,
        down_rows_new,
        down_cols_new,
    )


def solution(mesh):
    placed = (
        P(("dp", "expert"), None),
        P(("dp", "expert"), None),
        P(("dp", "expert")),
        P(("dp", "expert")),
        P(("dp", "expert")),
        P(("dp", "expert"), None),
        P(("dp", "expert"), None),
        P(),
        P(),
        P(),
        P("expert", None, None),
        P("expert", None, None),
        P(),
        P(),
        P(),
        P(),
        P(),
        P("expert", None),
        P("expert", None),
        P("expert", None),
        P("expert", None),
    )
    return jax.shard_map(
        per_device,
        mesh=mesh,
        in_specs=placed,
        out_specs=(
            P(("dp", "expert"), None),
            P(("dp", "expert"), None),
            P(),
            P(None, "dp"),
            P(None, "dp"),
            P("dp", None),
            P("dp"),
            P(),
            P("dp", None),
            P("dp"),
            P(),
            P("expert", "dp", None),
            P("expert", "dp"),
            P("expert", None),
            P("expert", "dp", None),
            P("expert", "dp"),
            P("expert", None),
        ),
        check_vma=False,
    )
```

```python
import functools
import math

import jax
import jax.numpy as jnp
from jax import lax
from jax.experimental import pallas as pl
from jax.experimental.pallas import tpu as pltpu
from jax.sharding import PartitionSpec as P

VM = 60 * 1024 * 1024
SCALE = 1e6


def lasts(microseconds):
    return pl.CostEstimate(
        flops=int(microseconds * SCALE), bytes_accessed=1024, transcendentals=0
    )


def dot(a, b, ca=1, cb=0):
    return lax.dot_general(a, b, (((ca,), (cb,)), ((), ())), preferred_element_type=jnp.float32)


def one_hot(code, capacity):
    count, rows = code.shape
    place = lax.broadcasted_iota(jnp.int32, (capacity, rows), 0).astype(jnp.float32)
    return [place == code[j : j + 1, :] for j in range(count)]


def expert_kernel(j, owners, tiles, waits, s_ref, rec_hbm, arr_hbm, scale_ref, up_hbm, down_hbm, *refs):
    (keep_hbm, give_hbm, back_hbm, mix_hbm,
     rec_s, arr_s, up_s, down_s, act_s, gug_s, wg_s, wd_s, parts_s, out_s, in_sem, out_sem) = refs[waits:]
    rows, ff = act_s.shape
    width = up_s.shape[0]
    sources, capacity = rec_s.shape[0], rec_s.shape[1]
    tile = rows // tiles
    per = sources // tiles

    def load(src, dst, at):
        copy = pltpu.make_async_copy(src, dst, in_sem.at[at])
        copy.start()
        return copy

    def load_rows(hbm, held, t, at):
        span = slice(t * per, (t + 1) * per)
        return load(hbm.at[j, span], held.at[span], at)

    expert = s_ref[0] + j
    rec_in = [load_rows(rec_hbm, rec_s, 0, 0)]
    up_in = load(up_hbm.at[expert], up_s, 2 * tiles)
    arr_in = [load_rows(arr_hbm, arr_s, 0, tiles)]
    down_in = load(down_hbm.at[expert], down_s, 2 * tiles + 1)
    for t in range(1, tiles):
        rec_in.append(load_rows(rec_hbm, rec_s, t, t))
        arr_in.append(load_rows(arr_hbm, arr_s, t, tiles + t))
    def products(t):
        span = slice(t * per, (t + 1) * per)
        return (
            dot(rec_s[span].reshape(tile, width), up_s[...]),
            dot(arr_s[span].reshape(tile, width), down_s[...], 1, 1),
        )

    for copy in (up_in, down_in, rec_in[0], arr_in[0]):
        copy.wait()
    following = products(0)
    for t in range(tiles):
        at = slice(t * tile, (t + 1) * tile)
        gate_up, act_grad = following
        if t + 1 < tiles:
            rec_in[t + 1].wait()
            arr_in[t + 1].wait()
            following = products(t + 1)
        gate = gate_up[:, :ff]
        up = gate_up[:, ff:]
        sig = 1.0 / (1.0 + jnp.exp(-gate))
        silu = gate * sig
        act_s[at, :] = (silu * up).astype(jnp.bfloat16)
        gug_s[at, :ff] = (act_grad * up * sig * (1.0 + gate * (1.0 - sig))).astype(jnp.bfloat16)
        gug_s[at, ff:] = (act_grad * silu).astype(jnp.bfloat16)
    wg_s[...] = dot(rec_s[...].reshape(rows, width), gug_s[...], 0, 0)
    wd_s[...] = dot(act_s[...], arr_s[...].reshape(rows, width), 0, 0)
    bit = s_ref[1]
    up_rows = width // owners
    down_rows = ff // owners
    leaving = []
    for k, (hbm, side) in enumerate(((give_hbm, 1 - bit), (keep_hbm, bit))):
        for slot in range(owners // 2):
            owner = 2 * slot + side
            parts_s[k, slot, :up_rows, :] = wg_s[
                pl.ds(pl.multiple_of(owner * up_rows, up_rows), up_rows), :
            ].astype(jnp.bfloat16)
            parts_s[k, slot, up_rows:, :] = wd_s[
                pl.ds(pl.multiple_of(owner * down_rows, down_rows), down_rows), :
            ].astype(jnp.bfloat16)
        copy = pltpu.make_async_copy(parts_s.at[k], hbm, out_sem.at[k])
        copy.start()
        leaving.append(copy)
    for t in range(tiles):
        at = slice(t * tile, (t + 1) * tile)
        out_s[0, at] = dot(gug_s[at, :], up_s[...], 1, 1).astype(jnp.bfloat16)
        scale = scale_ref[0, t * per : (t + 1) * per].reshape(tile, 1)
        out_s[1, at] = (dot(act_s[at, :], down_s[...]) * scale).astype(jnp.bfloat16)
        for k, hbm in enumerate((back_hbm, mix_hbm)):
            copy = pltpu.make_async_copy(out_s.at[k, at], hbm.at[at], out_sem.at[2 + 2 * t + k])
            copy.start()
            leaving.append(copy)
    for copy in leaving:
        copy.wait()


def run_expert(scalars, j, received, arrived, scale, up_w, down_w, owners, after=()):
    count, sources, capacity, width = received.shape
    ff = down_w.shape[1]
    rows = sources * capacity
    tiles = 2
    share = (owners // 2, (width + ff) // owners, width)
    slots = jax.ShapeDtypeStruct((rows, width), jnp.bfloat16)
    parts = jax.ShapeDtypeStruct(share, jnp.bfloat16)
    anywhere = pl.BlockSpec(memory_space=pl.ANY)
    return pl.pallas_call(
        functools.partial(expert_kernel, j, owners, tiles, len(after)),
        out_shape=(parts, parts, slots, slots),
        grid_spec=pltpu.PrefetchScalarGridSpec(
            num_scalar_prefetch=1,
            grid=(1,),
            in_specs=[
                anywhere,
                anywhere,
                pl.BlockSpec((1, sources, capacity, 1), lambda g, s: (j, 0, 0, 0)),
                anywhere,
                anywhere,
            ]
            + [anywhere] * len(after),
            out_specs=[anywhere] * 4,
            scratch_shapes=[
                pltpu.VMEM((sources, capacity, width), jnp.bfloat16),
                pltpu.VMEM((sources, capacity, width), jnp.bfloat16),
                pltpu.VMEM((width, 2 * ff), jnp.bfloat16),
                pltpu.VMEM((ff, width), jnp.bfloat16),
                pltpu.VMEM((rows, ff), jnp.bfloat16),
                pltpu.VMEM((rows, 2 * ff), jnp.bfloat16),
                pltpu.VMEM((width, 2 * ff), jnp.float32),
                pltpu.VMEM((ff, width), jnp.float32),
                pltpu.VMEM((2,) + share, jnp.bfloat16),
                pltpu.VMEM((2, rows, width), jnp.bfloat16),
                pltpu.SemaphoreType.DMA((2 * tiles + 2,)),
                pltpu.SemaphoreType.DMA((2 + 2 * tiles,)),
            ],
        ),
        compiler_params=pltpu.CompilerParams(vmem_limit_bytes=VM),
        cost_estimate=lasts(18),
        name="expert_%d" % j,
    )(scalars, received, arrived, scale, up_w, down_w, *after)


HEADS = 16
KV_HEADS = 8
HEAD_DIM = 64
EPS_NORM = 1e-06
ROPE_BASE = 10000.0
MASKED = -1e30
LANES = 128


def spread(row):
    rows = row.shape[1]
    by_column = jnp.broadcast_to(row.astype(jnp.float32), (rows, rows))
    return by_column, by_column.T


def mask_and_angles(ids_ref):
    seg_k, seg_q = spread(ids_ref[0:1, :])
    par_k, par_q = spread(ids_ref[1:2, :])
    pos_k, pos_q = spread(ids_ref[2:3, :])
    seen = ((seg_k == seg_q) | (seg_k == par_q) | (seg_k == par_k)) & (pos_k <= pos_q)
    bias = jnp.where(seen, 0.0, MASKED)
    lane = lax.broadcasted_iota(jnp.int32, (seg_k.shape[0], LANES), 1)
    half = HEAD_DIM // 2
    place = lax.rem(lane, half).astype(jnp.float32)
    frequency = jnp.exp(place * (-2.0 * math.log(ROPE_BASE) / HEAD_DIM))
    angles = pos_q[:, :LANES] * frequency
    front = lax.rem(lane, HEAD_DIM) < half
    sine = jnp.sin(angles)
    return bias, jnp.cos(angles), jnp.where(front, -sine, sine), front, lane


def turned(block, cosine, sine, front):
    other = jnp.where(
        front,
        pltpu.roll(block, LANES - HEAD_DIM // 2, 1),
        pltpu.roll(block, HEAD_DIM // 2, 1),
    )
    return block * cosine + other * sine


def two_diagonal(pair, which, lane):
    rolled = pltpu.roll(pair, HEAD_DIM, 1)
    first, last = (pair, rolled) if which == 0 else (rolled, pair)
    low = lane < HEAD_DIM
    return jnp.concatenate(
        [jnp.where(low, first, 0.0), jnp.where(low, 0.0, last)], axis=0
    ).astype(jnp.bfloat16)


def column_block(index):
    return pl.ds(pl.multiple_of(index * LANES, LANES), LANES)


def attend_kernel(hidden_ref, ids_ref, gains_ref, qkv_w_hbm, out_w_hbm,
                  normed_hbm, qkv_hbm, attended_hbm, lse_ref, middle_ref, normed_f_ref,
                  normed_ref, qkv_ref, attended_ref, qkv_w_ref, out_w_ref, proj_s, bias_s, sem):
    moving = [
        pltpu.make_async_copy(src, dst, sem.at[i])
        for i, (src, dst) in enumerate(
            (
                (qkv_w_hbm, qkv_w_ref),
                (out_w_hbm, out_w_ref),
                (normed_ref, normed_hbm),
                (qkv_ref, qkv_hbm),
                (attended_ref, attended_hbm),
            )
        )
    ]
    moving[0].start()
    moving[1].start()
    rows = hidden_ref.shape[0]
    att = HEADS * HEAD_DIM
    kv = KV_HEADS * HEAD_DIM
    hidden = hidden_ref[...]
    gains = gains_ref[...].astype(jnp.float32)
    inverse = lax.rsqrt(jnp.mean(hidden * hidden, axis=-1, keepdims=True) + EPS_NORM)
    normed_ref[...] = (hidden * inverse * gains[0:1, :]).astype(jnp.bfloat16)
    moving[2].start()
    bias, cosine, sine, front, lane = mask_and_angles(ids_ref)
    bias_s[...] = bias
    moving[0].wait()
    proj_s[...] = dot(normed_ref[...], qkv_w_ref[...])
    lse_ref[...] = jnp.zeros_like(lse_ref)

    def pair_step(p, carry):
        key_at = column_block(att // LANES + p)
        value_at = column_block((att + kv) // LANES + p)
        keys = turned(proj_s[:, key_at], cosine, sine, front).astype(jnp.bfloat16)
        values = proj_s[:, value_at].astype(jnp.bfloat16)
        qkv_ref[:, key_at] = keys
        qkv_ref[:, value_at] = values
        keys = keys.astype(jnp.float32)
        values = values.astype(jnp.float32)
        for which in range(2):
            query_at = column_block(2 * p + which)
            queries = turned(proj_s[:, query_at], cosine, sine, front).astype(jnp.bfloat16)
            queries = (queries.astype(jnp.float32) * HEAD_DIM**-0.5).astype(jnp.bfloat16)
            qkv_ref[:, query_at] = queries
            scores = dot(queries, two_diagonal(keys, which, lane), 1, 1)
            probs = []
            for head in range(2):
                part = scores[:, head * rows : (head + 1) * rows] + bias_s[...]
                top = jnp.max(part, axis=-1, keepdims=True)
                part = jnp.exp(part - top)
                total = jnp.sum(part, axis=-1, keepdims=True)
                probs.append((part * (1.0 / total)).astype(jnp.bfloat16))
                at = 4 * p + 2 * which + head
                lse_ref[...] = jnp.where(lane == at, top + jnp.log(total), lse_ref[...])
            attended_ref[:, query_at] = dot(
                jnp.concatenate(probs, axis=1), two_diagonal(values, which, lane)
            ).astype(jnp.bfloat16)
        return carry

    lax.fori_loop(0, KV_HEADS // 2, pair_step, 0)
    moving[3].start()
    moving[4].start()
    moving[1].wait()
    middle = hidden + dot(attended_ref[...], out_w_ref[...])
    middle_ref[...] = middle
    inverse_f = lax.rsqrt(jnp.mean(middle * middle, axis=-1, keepdims=True) + EPS_NORM)
    normed_f_ref[...] = (middle * inverse_f * gains[1:2, :]).astype(jnp.bfloat16)
    for copy in moving[2:]:
        copy.wait()


def attend(hidden, ids, gains, qkv_w, out_w):
    rows, width = hidden.shape
    shape = jax.ShapeDtypeStruct
    return pl.pallas_call(
        attend_kernel,
        out_shape=(
            shape((rows, width), jnp.bfloat16),
            shape((rows, qkv_w.shape[1]), jnp.bfloat16),
            shape((rows, out_w.shape[0]), jnp.bfloat16),
            shape((rows, LANES), jnp.float32),
            shape((rows, width), jnp.float32),
            shape((rows, width), jnp.bfloat16),
        ),
        in_specs=[pl.BlockSpec(memory_space=pltpu.VMEM)] * 3 + [pl.BlockSpec(memory_space=pl.ANY)] * 2,
        out_specs=[pl.BlockSpec(memory_space=pl.ANY)] * 3 + [pl.BlockSpec(memory_space=pltpu.VMEM)] * 3,
        scratch_shapes=[
            pltpu.VMEM((rows, width), jnp.bfloat16),
            pltpu.VMEM((rows, qkv_w.shape[1]), jnp.bfloat16),
            pltpu.VMEM((rows, out_w.shape[0]), jnp.bfloat16),
            pltpu.VMEM(qkv_w.shape, jnp.bfloat16),
            pltpu.VMEM(out_w.shape, jnp.bfloat16),
            pltpu.VMEM((rows, qkv_w.shape[1]), jnp.float32),
            pltpu.VMEM((rows, rows), jnp.float32),
            pltpu.SemaphoreType.DMA((5,)),
        ],
        compiler_params=pltpu.CompilerParams(vmem_limit_bytes=VM),
        cost_estimate=lasts(18),
        name="attend",
    )(hidden, ids, gains, qkv_w, out_w)


def attend_back_kernel(waits, grad_ref, middle_ref, normed_grad_ref, lse_ref, ids_ref, gains_ref,
                       hidden_hbm, normed_hbm, qkv_hbm, attended_hbm, qkv_w_hbm, out_w_hbm, *refs):
    (input_grad_ref, dense_hbm, dense_ref, hidden_ref, normed_ref, qkv_ref, attended_ref, qkv_w_ref, out_w_ref,
     proj_s, bias_s, back_s, sem) = refs[waits:]
    rows, width = hidden_ref.shape
    incoming = {
        name: pltpu.make_async_copy(src, dst, sem.at[i])
        for i, (name, src, dst) in enumerate(
            (
                ("attended", attended_hbm, attended_ref),
                ("out_w", out_w_hbm, out_w_ref),
                ("qkv", qkv_hbm, qkv_ref),
                ("normed", normed_hbm, normed_ref),
                ("qkv_w", qkv_w_hbm, qkv_w_ref),
                ("hidden", hidden_hbm, hidden_ref),
            )
        )
    }
    for copy in incoming.values():
        copy.start()
    leaving = []

    def leave(span):
        copy = pltpu.make_async_copy(dense_ref.at[:, span], dense_hbm.at[:, span], sem.at[6 + len(leaving)])
        copy.start()
        leaving.append(copy)

    att = HEADS * HEAD_DIM
    kv = KV_HEADS * HEAD_DIM
    gains = gains_ref[...].astype(jnp.float32)
    normed_grad = normed_grad_ref[...]
    middle = middle_ref[...]
    inverse_f = lax.rsqrt(jnp.mean(middle * middle, axis=-1, keepdims=True) + EPS_NORM)
    gain_f = jnp.sum(normed_grad * middle * inverse_f, axis=0, keepdims=True)
    weighted = normed_grad * gains[1:2, :]
    middle_grad = grad_ref[...] + (
        inverse_f * weighted
        - middle * (inverse_f * inverse_f * inverse_f)
        * jnp.mean(weighted * middle, axis=-1, keepdims=True)
    )
    input_grad_ref[...] = middle_grad
    branch = middle_grad.astype(jnp.bfloat16)
    columns = att + 2 * kv
    incoming["attended"].wait()
    dense_ref[:, columns : columns + width] = dot(attended_ref[...], branch, 0, 0).astype(jnp.bfloat16)
    leave(slice(columns, columns + width))
    incoming["out_w"].wait()
    back_s[...] = dot(branch, out_w_ref[...], 1, 1).astype(jnp.bfloat16)
    bias, cosine, sine, front, lane = mask_and_angles(ids_ref)
    bias_s[...] = bias
    low = lane < HEAD_DIM
    incoming["qkv"].wait()

    def pair_step(p, carry):
        key_at = column_block(att // LANES + p)
        value_at = column_block((att + kv) // LANES + p)
        keys = qkv_ref[:, key_at].astype(jnp.float32)
        values = qkv_ref[:, value_at].astype(jnp.float32)
        key_grads = []
        value_grads = []
        for which in range(2):
            query_at = column_block(2 * p + which)
            queries = qkv_ref[:, query_at]
            back = back_s[:, query_at]
            key_two = two_diagonal(keys, which, lane)
            scores = dot(queries, key_two, 1, 1)
            prob_grads = dot(back, two_diagonal(values, which, lane), 1, 1)
            probs = []
            score_grads = []
            for head in range(2):
                at = 4 * p + 2 * which + head
                level = jnp.sum(jnp.where(lane == at, lse_ref[...], 0.0), axis=-1, keepdims=True)
                span = slice(head * rows, (head + 1) * rows)
                prob = jnp.exp(scores[:, span] + bias_s[...] - level)
                prob_grad = prob_grads[:, span]
                row_dot = jnp.sum(prob * prob_grad, axis=-1, keepdims=True)
                probs.append(prob.astype(jnp.bfloat16))
                score_grads.append((prob * (prob_grad - row_dot)).astype(jnp.bfloat16))
            score_grads = jnp.concatenate(score_grads, axis=1)
            query_grad = dot(score_grads, key_two) * HEAD_DIM**-0.5
            proj_s[:, query_at] = turned(query_grad, cosine, -sine, front).astype(jnp.bfloat16)
            for grads, left, right in (
                (key_grads, score_grads, queries),
                (value_grads, jnp.concatenate(probs, axis=1), back),
            ):
                both = dot(left, right, 0, 0)
                first, last = both[:rows], both[rows:]
                if which == 0:
                    grads.append(first + pltpu.roll(last, HEAD_DIM, 1))
                else:
                    grads.append(pltpu.roll(first, HEAD_DIM, 1) + last)
        key_grad = jnp.where(low, key_grads[0], key_grads[1])
        proj_s[:, key_at] = turned(key_grad, cosine, -sine, front).astype(jnp.bfloat16)
        proj_s[:, value_at] = jnp.where(low, value_grads[0], value_grads[1]).astype(jnp.bfloat16)
        return carry

    lax.fori_loop(0, KV_HEADS // 2, pair_step, 0)
    for name in ("normed", "qkv_w", "hidden"):
        incoming[name].wait()
    for first in range(0, columns, columns // 2):
        span = slice(first, first + columns // 2)
        dense_ref[:, span] = dot(normed_ref[...], proj_s[:, span], 0, 0).astype(jnp.bfloat16)
        leave(span)
    normed_grad = dot(proj_s[...], qkv_w_ref[...], 1, 1)
    hidden = hidden_ref[...]
    inverse = lax.rsqrt(jnp.mean(hidden * hidden, axis=-1, keepdims=True) + EPS_NORM)
    gain_a = jnp.sum(normed_grad * hidden * inverse, axis=0, keepdims=True)
    weighted = normed_grad * gains[0:1, :]
    input_grad_ref[...] += inverse * weighted - hidden * (inverse * inverse * inverse) * jnp.mean(
        weighted * hidden, axis=-1, keepdims=True
    )
    both = jnp.concatenate([gain_a, gain_f, jnp.zeros((LANES - 2, width), jnp.float32)], axis=0)
    dense_ref[:, columns + width :] = both.T.astype(jnp.bfloat16)
    leave(slice(columns + width, columns + width + LANES))
    for copy in leaving:
        copy.wait()


def attend_back(hidden, out_grad, middle, normed_f_grad, normed, qkv, attended, lse, ids, gains, qkv_w, out_w, after=()):
    rows, width = hidden.shape
    columns = qkv_w.shape[1] + width + LANES
    return pl.pallas_call(
        functools.partial(attend_back_kernel, len(after)),
        out_shape=(
            jax.ShapeDtypeStruct((rows, width), jnp.float32),
            jax.ShapeDtypeStruct((width, columns), jnp.bfloat16),
        ),
        in_specs=[pl.BlockSpec(memory_space=pltpu.VMEM)] * 6
        + [pl.BlockSpec(memory_space=pl.ANY)] * (6 + len(after)),
        out_specs=[pl.BlockSpec(memory_space=pltpu.VMEM), pl.BlockSpec(memory_space=pl.ANY)],
        scratch_shapes=[
            pltpu.VMEM((width, columns), jnp.bfloat16),
            pltpu.VMEM((rows, width), jnp.float32),
            pltpu.VMEM((rows, width), jnp.bfloat16),
            pltpu.VMEM((rows, qkv_w.shape[1]), jnp.bfloat16),
            pltpu.VMEM((rows, out_w.shape[0]), jnp.bfloat16),
            pltpu.VMEM(qkv_w.shape, jnp.bfloat16),
            pltpu.VMEM(out_w.shape, jnp.bfloat16),
            pltpu.VMEM((rows, qkv_w.shape[1]), jnp.bfloat16),
            pltpu.VMEM((rows, rows), jnp.float32),
            pltpu.VMEM((rows, out_w.shape[0]), jnp.bfloat16),
            pltpu.SemaphoreType.DMA((10,)),
        ],
        compiler_params=pltpu.CompilerParams(vmem_limit_bytes=VM),
        cost_estimate=lasts(26),
        name="attend_back",
    )(out_grad, middle, normed_f_grad, lse, ids, gains, hidden, normed, qkv, attended, qkv_w, out_w, *after)


MESH = pl.DeviceIdType.MESH


def greet(peers):
    barrier = pltpu.get_barrier_semaphore()
    for peer in peers:
        pl.semaphore_signal(barrier, inc=1, device_id=peer, device_id_type=MESH)
    pl.semaphore_wait(barrier, len(peers))


def total_kernel(axis, count, mine_ref, *refs):
    out_ref, got_ref, send_sem, recv_sem = refs[-4:]
    me = lax.axis_index(axis)
    after = [lax.rem(me + k, count) for k in range(count)]
    greet([{axis: after[k]} for k in range(1, count)])
    scatter = [
        pltpu.make_async_remote_copy(
            src_ref=mine_ref.at[after[k]],
            dst_ref=got_ref.at[k],
            send_sem=send_sem.at[0, k],
            recv_sem=recv_sem.at[0, k],
            device_id={axis: after[k]},
            device_id_type=MESH,
        )
        for k in range(1, count)
    ]
    for copy in scatter:
        copy.start()
    total = mine_ref[me]
    for k in range(1, count):
        scatter[k - 1].wait_recv()
        total = total + got_ref[k]
    out_ref[me] = total
    share = [
        pltpu.make_async_remote_copy(
            src_ref=out_ref.at[me],
            dst_ref=out_ref.at[me],
            send_sem=send_sem.at[1, k],
            recv_sem=recv_sem.at[1, k],
            device_id={axis: after[k]},
            device_id_type=MESH,
        )
        for k in range(1, count)
    ]
    for copy in share:
        copy.start()
    for copy in share:
        copy.wait_recv()
    for copy in scatter + share:
        copy.wait_send()


def total_over(values, axis, label, after=()):
    count = lax.axis_size(axis)
    rows = -(-values.shape[0] // (8 * 128 * count)) * 8
    padded = jnp.pad(values, (0, count * rows * 128 - values.shape[0])).reshape(count, rows, 128)
    out = pl.pallas_call(
        functools.partial(total_kernel, axis, count),
        out_shape=jax.ShapeDtypeStruct(padded.shape, jnp.float32),
        in_specs=[pl.BlockSpec(memory_space=pltpu.VMEM)] + [pl.BlockSpec(memory_space=pl.ANY)] * len(after),
        out_specs=pl.BlockSpec(memory_space=pltpu.VMEM),
        scratch_shapes=[
            pltpu.VMEM(padded.shape, jnp.float32),
            pltpu.SemaphoreType.DMA((2, count)),
            pltpu.SemaphoreType.DMA((2, count)),
        ],
        compiler_params=pltpu.CompilerParams(
            collective_id=label, has_side_effects=True, vmem_limit_bytes=16 * 1024 * 1024
        ),
        cost_estimate=lasts(12),
        name="total_%d" % label,
    )(padded, *after)
    return out.reshape(-1)[: values.shape[0]]


def collect_kernel(axis, count, mine_ref, out_ref, send_sem, recv_sem, local_sem):
    me = lax.axis_index(axis)
    after = [lax.rem(me + k, count) for k in range(count)]
    greet([{axis: after[k]} for k in range(1, count)])
    copies = [
        pltpu.make_async_remote_copy(
            src_ref=mine_ref,
            dst_ref=out_ref.at[me],
            send_sem=send_sem.at[k],
            recv_sem=recv_sem.at[k],
            device_id={axis: after[k]},
            device_id_type=MESH,
        )
        for k in range(1, count)
    ]
    for copy in copies:
        copy.start()
    out_ref[me] = mine_ref[...]
    for copy in copies:
        copy.wait()


def collect(values, axis, label):
    count = lax.axis_size(axis)
    return pl.pallas_call(
        functools.partial(collect_kernel, axis, count),
        out_shape=jax.ShapeDtypeStruct((count,) + values.shape, jnp.float32),
        in_specs=[pl.BlockSpec(memory_space=pltpu.VMEM)],
        out_specs=pl.BlockSpec(memory_space=pltpu.VMEM),
        scratch_shapes=[
            pltpu.SemaphoreType.DMA((count,)),
            pltpu.SemaphoreType.DMA((count,)),
            pltpu.SemaphoreType.DMA,
        ],
        compiler_params=pltpu.CompilerParams(
            collective_id=label, has_side_effects=True, vmem_limit_bytes=16 * 1024 * 1024
        ),
        cost_estimate=lasts(4),
        name="collect_%d" % label,
    )(values)


def flipped(axis, mask):
    index = lax.axis_index(axis)
    bit = lax.rem(index // mask, 2)
    return bit, {axis: index + mask - 2 * mask * bit}


PAIR = 2
ROUTE_ROWS = 32


class Pusher:
    def __init__(self, send_sem, recv_sem):
        self.send_sem, self.recv_sem, self.copies = send_sem, recv_sem, []

    def __call__(self, src, dst, peer):
        at = len(self.copies)
        copy = pltpu.make_async_remote_copy(
            src_ref=src,
            dst_ref=dst,
            send_sem=self.send_sem.at[at],
            recv_sem=self.recv_sem.at[at],
            device_id=peer,
            device_id_type=MESH,
        )
        copy.start()
        self.copies.append(copy)
        return copy

    def finish(self):
        for copy in self.copies:
            copy.wait_send()


def picked(code, capacity):
    return jnp.concatenate(
        [c.astype(jnp.float32) for c in one_hot(code, capacity)], axis=0
    ).astype(jnp.bfloat16)


def gather_kernel(capacity, experts_here, half_experts, top, token_ref, grad_ref, chip_grad_ref, pair_grad_ref,
                  rec_ref, arr_ref, scale_ref, code_ref, tokens, grads, weight_s, stage, send_sem, recv_sem, local_sem):
    rows = token_ref.shape[0]
    half = rows // 2
    first = lax.axis_index("expert") * experts_here + lax.rem(lax.axis_index("dp") // PAIR, 2) * half_experts
    _, core = flipped("expert", 1)
    _, chip = flipped("expert", 2)
    _, pair = flipped("dp", PAIR)
    greet([core, chip, pair])
    push = Pusher(send_sem, recv_sem)
    everything, routing = slice(None), slice(rows, rows + ROUTE_ROWS)
    to_chip = push(token_ref, tokens.at[2], chip)
    to_pair = push(token_ref, tokens.at[4], pair)
    route_both = push(pair_grad_ref.at[routing], grads.at[6, routing], chip)
    to_core = push(token_ref, tokens.at[1], core)
    grad_core = push(grad_ref, grads.at[1], core)
    grad_chip_core = push(chip_grad_ref, grads.at[3], core)
    grad_pair_core = push(pair_grad_ref, grads.at[5], core)

    earlier = lax.broadcasted_iota(jnp.int32, (rows, rows), 0)
    later = lax.broadcasted_iota(jnp.int32, (rows, rows), 1)
    before = jnp.where(earlier < later, 1.0, 0.0).astype(jnp.bfloat16)

    def route(r, table):
        table = table.astype(jnp.float32)
        ids = table[:top]
        gates = table[top : 2 * top] + table[2 * top : 3 * top]
        hits = [ids == (first + j).astype(jnp.float32) for j in range(half_experts)]
        named = jnp.concatenate(
            [jnp.max(jnp.where(hit, 1.0, 0.0), axis=0, keepdims=True) for hit in hits], axis=0
        )
        weight_s[r] = jnp.concatenate(
            [jnp.sum(jnp.where(hit, gates, 0.0), axis=0, keepdims=True) for hit in hits], axis=0
        )
        code_ref[r] = jnp.where(named > 0.0, dot(named.astype(jnp.bfloat16), before), -1.0)

    leaving = []

    def select(r, source, out_ref, weighted):
        slot = len(leaving) % stage.shape[0]
        if len(leaving) >= stage.shape[0]:
            leaving[len(leaving) - stage.shape[0]].wait()
        chosen = one_hot(code_ref[r], capacity)
        pick = jnp.concatenate([c.astype(jnp.float32) for c in chosen], axis=0).astype(jnp.bfloat16)
        made = dot(pick, source)
        for j in range(half_experts):
            part = made[j * capacity : (j + 1) * capacity]
            if weighted:
                scale = jnp.sum(
                    jnp.where(chosen[j], weight_s[r, j : j + 1, :], 0.0), axis=1, keepdims=True
                )
                scale_ref[j, r] = scale
                part = part * scale
            stage[slot, j] = part.astype(jnp.bfloat16)
        copy = pltpu.make_async_copy(stage.at[slot], out_ref.at[:, r], local_sem.at[slot])
        copy.start()
        leaving.append(copy)

    def select_grad(r, ref):
        route(r, ref[rows:, :rows])
        select(r, ref[:rows, :], arr_ref, True)

    select_grad(0, grad_ref)
    select(0, token_ref[...], rec_ref, False)
    select_grad(2, chip_grad_ref)
    select_grad(4, pair_grad_ref)
    for r, copy in ((1, grad_core), (3, grad_chip_core), (5, grad_pair_core)):
        copy.wait_recv()
        select_grad(r, grads.at[r])
    to_core.wait_recv()
    select(1, tokens[1], rec_ref, False)
    route_both.wait_recv()
    route_core = push(grads.at[6, routing], grads.at[7, routing], core)
    to_chip.wait_recv()
    both_low = push(tokens.at[2, half:rows], tokens.at[6, half:rows], pair)
    chip_core = push(tokens.at[2], tokens.at[3], core)
    to_pair.wait_recv()
    both_high = push(tokens.at[4, 0:half], tokens.at[6, 0:half], chip)
    pair_core = push(tokens.at[4], tokens.at[5], core)
    grad_low = push(chip_grad_ref.at[half:rows], grads.at[6, half:rows], pair)
    grad_high = push(pair_grad_ref.at[0:half], grads.at[6, 0:half], chip)
    select(2, tokens[2], rec_ref, False)
    select(4, tokens[4], rec_ref, False)
    route(6, grads[6, rows:, :rows])
    route_core.wait_recv()
    route(7, grads[7, rows:, :rows])
    chip_core.wait_recv()
    select(3, tokens[3], rec_ref, False)
    pair_core.wait_recv()
    select(5, tokens[5], rec_ref, False)
    both_low.wait_recv()
    both_high.wait_recv()
    both_core = push(tokens.at[6], tokens.at[7], core)
    select(6, tokens[6], rec_ref, False)
    both_core.wait_recv()
    select(7, tokens[7], rec_ref, False)
    grad_low.wait_recv()
    grad_high.wait_recv()
    grad_both_core = push(grads.at[6, 0:rows], grads.at[7, 0:rows], core)
    select(6, grads[6, :rows], arr_ref, True)
    grad_both_core.wait_recv()
    select(7, grads[7, :rows], arr_ref, True)
    for copy in leaving[-stage.shape[0] :]:
        copy.wait()
    push.finish()


def gather_and_select(token, grad, chip_grad, pair_grad, capacity, experts_here, half_experts, top, label):
    rows, width = token.shape
    vmem = pl.BlockSpec(memory_space=pltpu.VMEM)
    anywhere = pl.BlockSpec(memory_space=pl.ANY)
    slots = jax.ShapeDtypeStruct((half_experts, 8, capacity, width), jnp.bfloat16)
    return pl.pallas_call(
        functools.partial(gather_kernel, capacity, experts_here, half_experts, top),
        out_shape=(
            slots,
            slots,
            jax.ShapeDtypeStruct((half_experts, 8, capacity, 1), jnp.float32),
            jax.ShapeDtypeStruct((8, half_experts, rows), jnp.float32),
        ),
        in_specs=[vmem] * 4,
        out_specs=[anywhere, anywhere, vmem, vmem],
        scratch_shapes=[
            pltpu.VMEM((8, rows, width), jnp.bfloat16),
            pltpu.VMEM((8, rows + ROUTE_ROWS, width), jnp.bfloat16),
            pltpu.VMEM((8, half_experts, rows), jnp.float32),
            pltpu.VMEM((4, half_experts, capacity, width), jnp.bfloat16),
            pltpu.SemaphoreType.DMA((18,)),
            pltpu.SemaphoreType.DMA((18,)),
            pltpu.SemaphoreType.DMA((4,)),
        ],
        compiler_params=pltpu.CompilerParams(
            collective_id=label, has_side_effects=True, vmem_limit_bytes=VM
        ),
        cost_estimate=lasts(44),
        name="gather_and_select",
    )(token, grad, chip_grad, pair_grad)


def fetcher(order, fetched, local_sem, capacity, code_ref):
    depth = fetched.shape[0]
    fetching = []
    done = []

    def fetch():
        n = len(fetching)
        if n < len(order):
            slots, r = order[n]
            fetching.append(
                [
                    pltpu.make_async_copy(
                        ref.at[r * capacity : (r + 1) * capacity],
                        fetched.at[n % depth, j * capacity : (j + 1) * capacity],
                        local_sem.at[n % depth, j],
                    )
                    for j, ref in enumerate(slots)
                ]
            )
            for copy in fetching[-1]:
                copy.start()

    for _ in range(depth - 1):
        fetch()

    def next_sum():
        fetch()
        n = len(done)
        for copy in fetching[n]:
            copy.wait()
        done.append(n)
        return dot(picked(code_ref[order[n][1]], capacity), fetched[n % depth], 0, 0)

    return next_sum


def combine_kernel(capacity, count, code_ref, *refs):
    slots = refs[:count]
    mine_ref, theirs_ref, fetched, local_sem = refs[-4:]
    order = [(slots, r) for r in (7, 6, 3, 2, 5, 4, 1, 0)]
    next_sum = fetcher(order, fetched, local_sem, capacity, code_ref)
    for _, r in order:
        (theirs_ref if r % 2 else mine_ref)[r // 2] = next_sum().astype(jnp.bfloat16)


def combine(code, slots, capacity, after):
    _, count, rows = code.shape
    width = slots[0].shape[1]
    vmem = pl.BlockSpec(memory_space=pltpu.VMEM)
    anywhere = pl.BlockSpec(memory_space=pl.ANY)
    four = jax.ShapeDtypeStruct((4, rows, width), jnp.bfloat16)
    return pl.pallas_call(
        functools.partial(combine_kernel, capacity, count),
        out_shape=(four, four),
        in_specs=[vmem] + [anywhere] * (count + len(after)),
        out_specs=[vmem, vmem],
        scratch_shapes=[
            pltpu.VMEM((4, count * capacity, width), jnp.bfloat16),
            pltpu.SemaphoreType.DMA((4, count)),
        ],
        compiler_params=pltpu.CompilerParams(vmem_limit_bytes=VM),
        cost_estimate=lasts(12),
        name="combine",
    )(code, *slots, *after)


def return_kernel(capacity, count, far_mask, code_ref, mine_ref, theirs_ref, go_ref, *refs):
    mixes = refs[:count]
    (out_ref, near_ref, far_ref, come_ref, fetched, core_got, own, theirs_mix, core_got_mix, half_pair, half_chip, from_chip,
     from_pair, send_sem, recv_sem, local_sem) = refs[-16:]
    rows = out_ref.shape[0]
    half = rows // 2
    _, core = flipped("expert", 1)
    _, chip = flipped("expert", 2)
    _, pair = flipped("dp", PAIR)
    _, far = flipped("dp", far_mask)
    greet([core, chip, pair, far])
    push = Pusher(send_sem, recv_sem)
    beside = push(go_ref, come_ref, far)
    crossing = {i: push(theirs_ref.at[i], core_got.at[i], core) for i in (3, 1, 2, 0)}
    order = [(mixes, r) for r in (7, 6, 3, 2, 5, 4, 1, 0)]
    next_sum = fetcher(order, fetched, local_sem, capacity, code_ref)

    def plus(a, b):
        return (a.astype(jnp.float32) + b.astype(jnp.float32)).astype(jnp.bfloat16)

    def mix(i, ref, at):
        theirs_mix[i] = next_sum().astype(jnp.bfloat16)
        copy = push(theirs_mix.at[i], core_got_mix.at[i], core)
        mine = next_sum()
        copy.wait_recv()
        ref[at] = plus(mine, core_got_mix[i])

    crossing[3].wait_recv()
    own[3] = plus(mine_ref[3], core_got[3])
    at_pair = push(own.at[3, 0:half], half_pair, pair)
    at_chip = push(own.at[3, half:rows], half_chip, chip)
    crossing[1].wait_recv()
    own[1] = plus(mine_ref[1], core_got[1])
    low_chip = push(own.at[1, half:rows], from_chip.at[half:rows], chip)
    crossing[2].wait_recv()
    own[2] = plus(mine_ref[2], core_got[2])
    high_pair = push(own.at[2, 0:half], from_pair.at[0:half], pair)
    crossing[0].wait_recv()
    out_ref[...] = mine_ref[0].astype(jnp.float32) + core_got[0].astype(jnp.float32)
    mix(3, far_ref, 1)
    mix(1, far_ref, 0)
    at_pair.wait_recv()
    own[1, :half] = plus(own[1, :half], half_pair[...])
    high_chip = push(own.at[1, 0:half], from_chip.at[0:half], chip)
    at_chip.wait_recv()
    own[2, half:] = plus(own[2, half:], half_chip[...])
    low_pair = push(own.at[2, half:rows], from_pair.at[half:rows], pair)
    mix(2, near_ref, 1)
    mix(0, near_ref, 0)
    low_chip.wait_recv()
    high_pair.wait_recv()
    high_chip.wait_recv()
    low_pair.wait_recv()
    out_ref[...] += from_chip[...].astype(jnp.float32) + from_pair[...].astype(jnp.float32)
    beside.wait_recv()
    push.finish()


def return_sums(code, mine, theirs, mixes, capacity, go, far_mask, label, after):
    _, count, rows = code.shape
    width = mine.shape[2]
    vmem = pl.BlockSpec(memory_space=pltpu.VMEM)
    anywhere = pl.BlockSpec(memory_space=pl.ANY)
    four = pltpu.VMEM((4, rows, width), jnp.bfloat16)
    two = jax.ShapeDtypeStruct((2, rows, width), jnp.bfloat16)
    return pl.pallas_call(
        functools.partial(return_kernel, capacity, count, far_mask),
        out_shape=(
            jax.ShapeDtypeStruct((rows, width), jnp.float32),
            two,
            two,
            jax.ShapeDtypeStruct(go.shape, jnp.bfloat16),
        ),
        in_specs=[vmem] * 3 + [anywhere] * (1 + count + len(after)),
        out_specs=[vmem] * 3 + [anywhere],
        scratch_shapes=[pltpu.VMEM((4, count * capacity, width), jnp.bfloat16), four, four, four, four]
        + [pltpu.VMEM((rows // 2, width), jnp.bfloat16)] * 2
        + [pltpu.VMEM((rows, width), jnp.bfloat16)] * 2
        + [
            pltpu.SemaphoreType.DMA((15,)),
            pltpu.SemaphoreType.DMA((15,)),
            pltpu.SemaphoreType.DMA((4, count)),
        ],
        compiler_params=pltpu.CompilerParams(
            collective_id=label, has_side_effects=True, vmem_limit_bytes=VM
        ),
        cost_estimate=lasts(37),
        name="return_sums",
    )(code, mine, theirs, go, *mixes, *after)


def settle_kernel(groups, waits, bits_ref, *refs):
    ins, outs = refs[: 2 * groups], refs[2 * groups + waits : 4 * groups + waits]
    held, sem = refs[-2 * groups - 1 : -1], refs[-1]
    arriving = [pltpu.make_async_copy(ins[i], held[i], sem.at[i]) for i in range(2 * groups)]
    for copy in arriving:
        copy.start()
    for g in range(groups):
        arriving[2 * g].wait()
        arriving[2 * g + 1].wait()
        keep_ref, got_ref, stay_ref, go_ref = held[2 * g], held[2 * g + 1], outs[2 * g], outs[2 * g + 1]
        bit = bits_ref[g]
        for high in range(keep_ref.shape[0]):
            for low in range(keep_ref.shape[2]):
                for ref, side in ((stay_ref, bit), (go_ref, 1 - bit)):
                    total = keep_ref[high, side, low].astype(jnp.float32) + got_ref[
                        high, side, low
                    ].astype(jnp.float32)
                    ref[high, low] = total.astype(jnp.bfloat16)


def settle(groups, label, after, passed=()):
    ins, shapes, outs, bits = [], [], [], []
    for keep, got, mask in groups:
        count, rows, columns = keep.shape
        low = 1 if mask == PAIR else 2
        shapes += [(count // 2 // low, 2, low, rows, columns)] * 2
        ins += [keep.reshape(shapes[-1]), got.reshape(shapes[-1])]
        outs += [jax.ShapeDtypeStruct((count // 2 // low, low, rows, columns), jnp.bfloat16)] * 2
        bits.append(lax.rem(lax.axis_index("dp") // mask, 2))
    waits = len(after) + len(passed)
    vmem = pl.BlockSpec(memory_space=pltpu.VMEM)
    anywhere = pl.BlockSpec(memory_space=pl.ANY)
    made = pl.pallas_call(
        functools.partial(settle_kernel, len(groups), waits),
        out_shape=outs + [jax.ShapeDtypeStruct(p.shape, p.dtype) for p in passed],
        in_specs=[pl.BlockSpec(memory_space=pltpu.SMEM)] + [anywhere] * (len(ins) + waits),
        scratch_shapes=[pltpu.VMEM(shape, jnp.bfloat16) for shape in shapes]
        + [pltpu.SemaphoreType.DMA((len(ins),))],
        out_specs=[vmem] * len(outs) + [anywhere] * len(passed),
        input_output_aliases={1 + len(ins) + len(after) + i: len(outs) + i for i in range(len(passed))},
        compiler_params=pltpu.CompilerParams(vmem_limit_bytes=VM),
        cost_estimate=lasts(3),
        name="settle_%s" % label,
    )(jnp.stack(bits), *ins, *after, *passed)
    sides = [x.reshape((-1,) + x.shape[2:]) for x in made[: len(outs)]]
    return list(zip(sides[::2], sides[1::2])), made[len(outs) :]


def settle_mix_kernel(near_ref, got_ref, *refs):
    refs[-1][...] = (near_ref[1].astype(jnp.float32) + got_ref[1].astype(jnp.float32)).astype(jnp.bfloat16)


def settle_mix(near, got, after):
    vmem = pl.BlockSpec(memory_space=pltpu.VMEM)
    return pl.pallas_call(
        settle_mix_kernel,
        out_shape=jax.ShapeDtypeStruct(near.shape[1:], jnp.bfloat16),
        in_specs=[vmem] * 2 + [pl.BlockSpec(memory_space=pl.ANY)] * len(after),
        out_specs=vmem,
        compiler_params=pltpu.CompilerParams(vmem_limit_bytes=VM),
        cost_estimate=lasts(3),
        name="settle_mix",
    )(near, got, *after)


EPS_STAT = 1e-30
STAT_DECAY = 0.5
LEARN_RATE = 0.5
CLIP_LEVEL = 0.05


def decayed(old, new):
    return STAT_DECAY * old + (1.0 - STAT_DECAY) * new


def finish_kernel(count, groups, half, orders, spans, *refs):
    bits = count.bit_length() - 1
    steps = len(orders[0])
    (mine_hbm, own_0, own_1, got_0, got_1, stay_2, come_2, keep_3, come_3, near_mix_ref, got_mix_ref,
     up_rows_ref, down_rows_ref, up_cols_ref, down_cols_ref, qkv_rows_ref, out_rows_ref, moments_ref, qkv_cols_ref,
     out_cols_ref) = refs[:20]
    (dense_ref, ends_ref, pair_mix_ref, out_ref, sums_ref, up_new_ref, down_new_ref, dense_out_ref,
     dense_new_ref) = refs[20:29]
    sum_ref, first_got, *got = refs[29 : 31 + steps]
    (mine_ref, load_sem, go_s, far_go_s, far_stay_s, far_got_s, mix_s, pay_s, got_s, dense_pay_s, dense_got_s, spread_s,
     up_old_ref, down_old_ref, dense_old_ref, dense_cols_ref, send_sem, recv_sem) = refs[31 + steps :]
    width = up_rows_ref.shape[1]
    ff = down_rows_ref.shape[1]
    wide = width // 2
    own_up = width // count
    own_down = ff // count
    me = lax.axis_index("dp")
    place = lax.axis_index("expert")
    after = [lax.rem(me + k, count) for k in range(count)]
    beside = [lax.rem(place + k, groups) for k in range(groups)]
    pair_bit, pair = flipped("dp", PAIR)
    far_bit, far = flipped("dp", FAR)
    core, core_peer = flipped("expert", 1)
    chip, chip_peer = flipped("expert", 2)
    links = [flipped("dp", 1 << b) for b in range(bits)] + [(chip, chip_peer)]
    whole = (slice(None),) * bits
    loading = pltpu.make_async_copy(mine_hbm.at[whole + (core,)], mine_ref, load_sem)
    loading.start()
    greet([{"dp": after[k]} for k in range(1, count)] + [{"expert": beside[k]} for k in range(1, groups)])
    push = Pusher(send_sem, recv_sem)

    def plus(a, b):
        return (a.astype(jnp.float32) + b.astype(jnp.float32)).astype(jnp.bfloat16)

    flying = [
        push(mine_hbm.at[whole + (1 - core, slice(None), slice(None), span)], first_got.at[..., span], core_peer)
        for span in spans
    ]
    for low in range(2):
        far_go_s[low] = plus(keep_3[1 - far_bit, low], come_3[1 - far_bit, low])
    far_exchange = push(far_go_s, far_got_s, far)
    go_s[0] = plus(stay_2[1 - pair_bit], come_2[1 - pair_bit])
    cross_2 = push(go_s.at[0], ends_ref.at[2], pair)
    mix_s[...] = plus(near_mix_ref[1], got_mix_ref[1])
    cross_mix = push(mix_s, pair_mix_ref, pair)
    ends_ref[0] = plus(stay_2[pair_bit], come_2[pair_bit])
    for low in range(2):
        far_stay_s[low] = plus(keep_3[far_bit, low], come_3[far_bit, low])

    def own_columns(*tables):
        here = pl.ds(pl.multiple_of(me * LANES, LANES), LANES)
        rows = [table[:, here] for table in tables]
        return padded(jnp.concatenate(rows, axis=0)).T

    def padded(rows):
        return jnp.concatenate([rows, jnp.zeros((LANES - rows.shape[0], LANES), jnp.float32)], axis=0)

    up_old_ref[...] = own_columns(up_rows_ref)
    dense_old_ref[...] = own_columns(qkv_rows_ref, out_rows_ref, moments_ref)
    around = down_rows_ref[:, pl.ds(pl.multiple_of(me // 2 * LANES, LANES), LANES)]
    both_halves = padded(around).T
    down_old_ref[...] = jnp.where(lax.rem(me, 2) == 0, both_halves[:own_down], both_halves[own_down:])
    dense_cols_ref[:, : qkv_cols_ref.shape[1]] = qkv_cols_ref[...]
    dense_cols_ref[:, qkv_cols_ref.shape[1] :] = out_cols_ref[...]

    def column_of(table_ref, lane, at):
        return jnp.sum(jnp.where(lane == at, table_ref[...], 0.0), axis=1, keepdims=True)

    up_lane = lax.broadcasted_iota(jnp.int32, (own_up, LANES), 1)
    down_lane = lax.broadcasted_iota(jnp.int32, (own_down, LANES), 1)
    up_new_ref[...] = jnp.zeros_like(up_new_ref)
    down_new_ref[...] = jnp.zeros_like(down_new_ref)

    def factored(grad, old):
        square = grad * grad
        new = decayed(old, jnp.mean(square + EPS_STAT, axis=1, keepdims=True))
        return (
            new,
            jnp.sum(square + EPS_STAT, axis=0, keepdims=True),
            jnp.sum(square * (1.0 / new), axis=0, keepdims=True),
        )

    def expert(values, at):
        for kind, (part, old_ref, new_ref, lane, rows) in enumerate(
            (
                (values[:own_up, :], up_old_ref, up_new_ref, up_lane, own_up),
                (values[own_up:, :], down_old_ref, down_new_ref, down_lane, own_down),
            )
        ):
            new, total, scaled = factored(part.astype(jnp.float32), column_of(old_ref, lane, at))
            new_ref[:rows, :] = jnp.where(lane == at, new, new_ref[:rows, :])
            for h in range(2):
                span = slice(h * wide, (h + 1) * wide)
                pay_s[at, 4 * kind + h : 4 * kind + h + 1, :] = total[:, span]
                pay_s[at, 4 * kind + 2 + h : 4 * kind + 3 + h, :] = scaled[:, span]

    own_at, got_at = pair_bit * half, (1 - pair_bit) * half

    def at_place(chosen, span):
        return tuple(chosen.get(bits - 1 - i, slice(None)) for i in range(bits)) + (
            chosen.get(bits, slice(None)),
            slice(None),
            span,
        )

    def got_place(step, span):
        return (slice(None),) * (steps - 1 - step) + (slice(None), span)

    loading.wait()
    chosen = [{} for _ in spans]
    for step in range(steps + 1):
        for part, span in enumerate(spans):
            flying[part].wait_recv()
            if step == 0:
                sum_ref[..., span] = plus(mine_ref[..., span], first_got[..., span])
            else:
                here = at_place(chosen[part], span)
                sum_ref[here] = plus(sum_ref[here], got[step - 1][got_place(step - 1, span)])
            if step < steps:
                link = orders[part][step]
                bit, peer = links[link]
                away = at_place({**chosen[part], link: 1 - bit}, span)
                flying[part] = push(sum_ref.at[away], got[step].at[got_place(step, span)], peer)
                chosen[part] = {**chosen[part], link: bit}
            else:
                dense_ref[core, chip, :, span] = sum_ref[at_place(chosen[part], span)]
                block = dense_ref.at[core, chip, :, span]
                flying[part] = push(block, block, chip_peer)
        if step == 0:
            expert(own_0, own_at)
            expert(got_0, got_at)
            expert(own_1, own_at + 1)
            expert(got_1, got_at + 1)
        elif step == 1:
            expert(ends_ref[0], own_at + 2)
        elif step == steps - 1:
            cross_2.wait_recv()
            expert(ends_ref[2], got_at + 2)
            far_exchange.wait_recv()
            go_s[1] = plus(far_stay_s[1 - pair_bit], far_got_s[1 - pair_bit])
            cross_3 = push(go_s.at[1], ends_ref.at[3], pair)
            ends_ref[1] = plus(far_stay_s[pair_bit], far_got_s[pair_bit])
            expert(ends_ref[1], own_at + 3)
    for part, span in enumerate(spans):
        flying[part].wait_recv()
        block = dense_ref.at[core, :, :, span]
        flying[part] = push(block, block, core_peer)
    cross_3.wait_recv()
    expert(ends_ref[3], got_at + 3)
    arriving = [push(pay_s.at[after[k]], got_s.at[k], {"dp": after[k]}) for k in range(1, count)]
    for copy in flying:
        copy.wait_recv()

    columns = dense_cols_ref.shape[1]
    piece = columns // count
    dense = dense_ref[...].reshape(own_up, dense_ref.shape[3])
    dense_lane = lax.broadcasted_iota(jnp.int32, dense_new_ref.shape, 1)
    old = dense_old_ref[...]
    qkv_columns = columns - width
    totals, scaleds, rows_new = [], [], []
    for at, span in enumerate((slice(0, qkv_columns), slice(qkv_columns, columns))):
        new, total, scaled = factored(
            dense[:, span].astype(jnp.float32), column_of(dense_old_ref, dense_lane, at)
        )
        rows_new.append(new)
        totals.append(total)
        scaleds.append(scaled)
    gain_lanes = (dense_lane == 2) | (dense_lane == 3)
    gains = pltpu.roll(dense[:, columns:].astype(jnp.float32), 2, 1)
    moments = jnp.where(gain_lanes, decayed(old, gains * gains + EPS_STAT), 1.0)
    gain_steps = jnp.where(gain_lanes, gains * lax.rsqrt(moments), 0.0)
    dense_new_ref[...] = jnp.where(
        dense_lane == 0,
        rows_new[0],
        jnp.where(dense_lane == 1, rows_new[1], jnp.where(gain_lanes, gain_steps, pltpu.roll(moments, 2, 1))),
    )
    gain_squares = jnp.sum(jnp.sum(gain_steps * gain_steps, axis=1, keepdims=True), axis=0, keepdims=True)
    total = jnp.concatenate(totals, axis=1)
    scaled = jnp.concatenate(scaleds, axis=1)
    for d in range(count):
        span = slice(d * piece, (d + 1) * piece)
        dense_pay_s[d] = jnp.concatenate(
            [total[:, span], scaled[:, span], jnp.broadcast_to(gain_squares, (1, piece)), jnp.zeros((5, piece), jnp.float32)],
            axis=0,
        )
    dense_arriving = [push(dense_pay_s.at[after[k]], dense_got_s.at[k], {"dp": after[k]}) for k in range(1, count)]

    tile = pay_s[me]
    for k in range(1, count):
        arriving[k - 1].wait_recv()
        tile = tile + got_s[k]
    made = []
    tops = []
    for kind, (rows_ref, cols_ref, rows) in enumerate(
        ((up_rows_ref, up_cols_ref, width), (down_rows_ref, down_cols_ref, ff))
    ):
        here = pl.ds(me, 1)
        square = jnp.concatenate([tile[4 * kind + h : 4 * kind + h + 1] for h in range(2)], axis=1)
        scaled = jnp.concatenate([tile[4 * kind + 2 + h : 4 * kind + 3 + h] for h in range(2)], axis=1)
        new_columns = decayed(cols_ref[here, :], square / rows)
        row_mean = decayed(
            jnp.mean(rows_ref[here, :], axis=1, keepdims=True),
            jnp.sum(square, axis=1, keepdims=True) / (rows * width),
        )
        squares = row_mean * jnp.sum(scaled / new_columns, axis=1, keepdims=True)
        made += [new_columns[:, :wide], new_columns[:, wide:]]
        tops += [jnp.broadcast_to(v, (1, wide)) for v in (row_mean, squares)]
    out_ref[me] = jnp.concatenate(made + tops, axis=0)
    arriving = [push(out_ref.at[me], out_ref.at[me], {"dp": after[k]}) for k in range(1, count)]

    tile = dense_pay_s[me]
    for k in range(1, count):
        dense_arriving[k - 1].wait_recv()
        tile = tile + dense_got_s[k]
    own_piece = pl.ds(pl.multiple_of(me * piece, LANES), piece)
    new_columns = decayed(dense_cols_ref[:, own_piece], tile[0:1] / width)
    is_qkv = lax.broadcasted_iota(jnp.int32, (1, piece), 1) + me * piece < qkv_columns
    ratio = tile[1:2] / new_columns
    sums = [
        jnp.sum(jnp.where(chosen_columns, row, 0.0), axis=1, keepdims=True)
        for row in (ratio, tile[0:1])
        for chosen_columns in (is_qkv, ~is_qkv)
    ]
    dense_out_ref[me] = jnp.concatenate(
        [new_columns]
        + [jnp.broadcast_to(v, (1, piece)) for v in sums]
        + [tile[2:3], jnp.zeros((2, piece), jnp.float32)],
        axis=0,
    )
    dense_arriving = [push(dense_out_ref.at[me], dense_out_ref.at[me], {"dp": after[k]}) for k in range(1, count)]

    for copy in arriving:
        copy.wait_recv()
    total = out_ref[0, :, :LANES]
    for a in range(1, count):
        total = total + out_ref[a, :, :LANES]
    spread_s[place] = total
    arriving = [push(spread_s.at[place], spread_s.at[place], {"expert": beside[k]}) for k in range(1, groups)]
    for copy in arriving + dense_arriving + [cross_mix]:
        copy.wait_recv()
    total = spread_s[0]
    for e in range(1, groups):
        total = total + spread_s[e]
    sums_ref[...] = total
    push.finish()


FAR = 4


def finish(dense, owns, gots, settling, mixes, statistics, label):
    count = lax.axis_size("dp")
    groups = lax.axis_size("expert")
    width, dense_width = dense.shape
    bits = count.bit_length() - 1
    quarter = width // count // 4
    parts = 6
    tiles = dense_width // LANES
    bounds = [LANES * (tiles * i // parts) for i in range(parts + 1)]
    spans = [slice(a, b) for a, b in zip(bounds[:-1], bounds[1:])]
    last = tuple(range(1, bits))
    orders = [((bits, 0) if part % 2 == 0 else (0, bits)) + last for part in range(parts)]
    half = (2,) * bits + (2, quarter, dense_width)
    rows = owns[0].shape[0]
    own_up, own_down = width // count, rows - width // count
    dense_columns = dense_width - LANES
    piece = dense_columns // count
    vmem = pl.BlockSpec(memory_space=pltpu.VMEM)
    stat_tiles = (count, 8, width // 2)
    dense_tiles = (count, 8, piece)
    copies = parts * (bits + 4) + 4 * (count - 1) + groups - 1 + 4
    shape = lambda *s: jax.ShapeDtypeStruct(s, jnp.float32)
    low = lambda *s: jax.ShapeDtypeStruct(s, jnp.bfloat16)
    held = lambda *s: pltpu.VMEM(s, jnp.bfloat16)
    outs = (
        low(2, 2, quarter, dense_width),
        low(4, rows, width),
        low(*mixes[0].shape[1:]),
        shape(*stat_tiles),
        shape(8, LANES),
        shape(LANES, LANES),
        shape(LANES, LANES),
        shape(*dense_tiles),
        shape(width // count, LANES),
    )
    args = (
        dense.reshape((2,) * bits + (2, 2, quarter, dense_width)),
        *owns, *gots, *settling, *mixes, *statistics,
    )
    own, *rest = pl.pallas_call(
        functools.partial(finish_kernel, count, groups, 4, orders, spans),
        out_shape=outs,
        in_specs=[pl.BlockSpec(memory_space=pl.ANY)] + [vmem] * (len(args) - 1),
        out_specs=[vmem] * len(outs),
        scratch_shapes=[held(*half), held(*half)]
        + [held(*((2,) * (bits - step)), quarter, dense_width) for step in range(bits + 1)]
        + [
            held(*half),
            pltpu.SemaphoreType.DMA,
            held(2, rows, width),
            held(2, rows, width),
            held(2, rows, width),
            held(2, rows, width),
            held(*mixes[0].shape[1:]),
            pltpu.VMEM(stat_tiles, jnp.float32),
            pltpu.VMEM(stat_tiles, jnp.float32),
            pltpu.VMEM(dense_tiles, jnp.float32),
            pltpu.VMEM(dense_tiles, jnp.float32),
            pltpu.VMEM((groups, 8, LANES), jnp.float32),
            pltpu.VMEM((own_up, LANES), jnp.float32),
            pltpu.VMEM((own_down, LANES), jnp.float32),
            pltpu.VMEM((own_up, LANES), jnp.float32),
            pltpu.VMEM((1, dense_columns), jnp.float32),
            pltpu.SemaphoreType.DMA((copies,)),
            pltpu.SemaphoreType.DMA((copies,)),
        ],
        compiler_params=pltpu.CompilerParams(
            collective_id=label, has_side_effects=True, vmem_limit_bytes=VM
        ),
        cost_estimate=lasts(75),
        name="finish",
    )(*args)
    return own.reshape(width // count, dense_width), *rest


def update_kernel(counts, half, early, s_ref, *refs):
    owns, gots = refs[:early], refs[early : 2 * early]
    (dense_ref, ends_ref, pair_mix_ref, tiles_ref, sums_ref, up_new_ref, down_new_ref, dense_tiles_ref, dense_new_ref,
     qkv_old_ref, out_old_ref, middle_ref, near_mix_ref, got_mix_ref, up_w_ref, down_w_ref, qkv_w_ref, out_w_ref,
     block_ref, up_out_ref, down_out_ref, up_rows_ref, down_rows_ref, up_cols_ref, down_cols_ref,
     qkv_out_ref, out_out_ref, qkv_cols_ref, out_cols_ref, qkv_rows_ref, out_rows_ref, gains_ref, moments_ref,
     rms_ref) = refs[2 * early :]
    block_ref[...] = middle_ref[...] + (
        near_mix_ref[0].astype(jnp.float32)
        + got_mix_ref[0].astype(jnp.float32)
        + pair_mix_ref[...].astype(jnp.float32)
    )
    late = half - early
    own_up = up_out_ref.shape[1]
    own_down = down_out_ref.shape[1]
    wide = tiles_ref.shape[2]
    pair_bit = s_ref[0]
    count = dense_tiles_ref.shape[0]
    dense_sums = dense_tiles_ref[0, :, 0:1]
    for a in range(1, count):
        dense_sums = dense_sums + dense_tiles_ref[a, :, 0:1]
    width = qkv_old_ref.shape[1]
    qkv_columns = qkv_out_ref.shape[1]
    row_means = []
    squares = [dense_tiles_ref[0, 5:6, 0:1]]
    for at, (old_ref, columns) in enumerate(((qkv_old_ref, qkv_columns), (out_old_ref, width))):
        row_means.append(
            decayed(
                jnp.mean(old_ref[...], axis=1, keepdims=True),
                dense_sums[3 + at : 4 + at] / (width * columns),
            )
        )
        squares.append(row_means[-1] * dense_sums[1 + at : 2 + at])
    squares += [sums_ref[5:6, 0:1], sums_ref[7:8, 0:1]]
    roots = [jnp.sqrt(square / number) for square, number in zip(squares, counts)]
    factors = [LEARN_RATE / jnp.maximum(1.0, root / CLIP_LEVEL) for root in roots]
    for i, root in enumerate(roots):
        rms_ref[i] = root[0, 0]

    up_table = up_new_ref[...]
    down_table = down_new_ref[...]
    lane = lax.broadcasted_iota(jnp.int32, up_table.shape, 1)

    def expert(ref, at):
        tile = tiles_ref[at]
        for kind, (table, weight_ref, out_ref, first, rows) in enumerate(
            (
                (up_table, up_w_ref, up_out_ref, 0, own_up),
                (down_table, down_w_ref, down_out_ref, own_up, own_down),
            )
        ):
            row_mean = tile[4 + 2 * kind : 5 + 2 * kind, 0:1]
            column = jnp.sum(jnp.where(lane == at, table, 0.0), axis=1, keepdims=True)[:rows]
            scale = factors[3 + kind] * lax.rsqrt(column / row_mean)
            for h in range(2):
                span = slice(h * wide, (h + 1) * wide)
                columns = lax.rsqrt(tile[2 * kind + h : 2 * kind + h + 1, :])
                out_ref[at, :, span] = (
                    weight_ref[at, :, span].astype(jnp.float32)
                    - ref[first : first + rows, span].astype(jnp.float32) * scale * columns
                )

    own_at, got_at = pair_bit * half, (1 - pair_bit) * half
    for j in range(early):
        expert(owns[j], own_at + j)
        expert(gots[j], got_at + j)
    for j in range(late):
        expert(ends_ref.at[j], own_at + early + j)
        expert(ends_ref.at[late + j], got_at + early + j)
    up_rows_ref[...] = up_table.T[: up_rows_ref.shape[0], :own_up]
    down_rows_ref[...] = down_table.T[: down_rows_ref.shape[0], :own_down]
    for a in range(up_cols_ref.shape[0]):
        for h in range(2):
            span = slice(h * wide, (h + 1) * wide)
            up_cols_ref[a : a + 1, span] = tiles_ref[a, h : h + 1, :]
            down_cols_ref[a : a + 1, span] = tiles_ref[a, 2 + h : 3 + h, :]

    table = dense_new_ref[...]
    scales = [
        factors[1 + at] * lax.rsqrt(table[:, at : at + 1] / row_means[at]) for at in range(2)
    ]
    piece = dense_tiles_ref.shape[2]
    for first in range(0, qkv_columns + width, LANES):
        at = 0 if first < qkv_columns else 1
        weight_ref, out_ref, cols_ref = (
            (qkv_w_ref, qkv_out_ref, qkv_cols_ref) if at == 0 else (out_w_ref, out_out_ref, out_cols_ref)
        )
        here = slice(first - at * qkv_columns, first - at * qkv_columns + LANES)
        within = first % piece
        columns = dense_tiles_ref[first // piece, 0:1, within : within + LANES]
        cols_ref[:, here] = columns
        out_ref[:, here] = weight_ref[:, here].astype(jnp.float32) - dense_ref[
            :, first : first + LANES
        ].astype(jnp.float32) * scales[at] * lax.rsqrt(columns)
    turned = table.T
    qkv_rows_ref[...] = turned[0:1]
    out_rows_ref[...] = turned[1:2]
    gains_ref[...] = -factors[0] * turned[2:4]
    moments_ref[...] = turned[4:6]


def update(owns, gots, finished, row_statistics, middle, mixes, up_w, down_w, qkv_w, out_w):
    count = lax.axis_size("dp")
    groups = lax.axis_size("expert")
    me = lax.axis_index("dp")
    experts, width, up_columns = up_w.shape
    ff = down_w.shape[1]
    qkv_columns = qkv_w.shape[1]
    own_up, own_down = width // count, ff // count
    counts = (
        float(2 * width),
        float(width * qkv_columns),
        float(width * width),
        float(groups * experts * width * up_columns),
        float(groups * experts * ff * width),
    )
    ends = finished[1]
    early = len(owns)
    whole = lambda *shape: pl.BlockSpec(shape, lambda g, s: (0,) * len(shape))
    shape = lambda *s: jax.ShapeDtypeStruct(s, jnp.float32)
    rows = own_up + own_down
    outs = [
        shape(*middle.shape),
        shape(experts, own_up, up_columns),
        shape(experts, own_down, width),
        shape(experts, own_up),
        shape(experts, own_down),
        shape(experts, up_columns),
        shape(experts, width),
        shape(own_up, qkv_columns),
        shape(own_up, width),
        shape(1, qkv_columns),
        shape(1, width),
        shape(1, own_up),
        shape(1, own_up),
        shape(2, own_up),
        shape(2, own_up),
        shape(len(counts)),
    ]
    return pl.pallas_call(
        functools.partial(update_kernel, counts, early + ends.shape[0] // 2, early),
        out_shape=outs,
        grid_spec=pltpu.PrefetchScalarGridSpec(
            num_scalar_prefetch=1,
            grid=(1,),
            in_specs=[whole(rows, width)] * (2 * early)
            + [whole(*a.shape) for a in (*finished, *row_statistics, middle, *mixes)]
            + [
                pl.BlockSpec((experts, own_up, up_columns), lambda g, s: (0, s[1], 0)),
                pl.BlockSpec((experts, own_down, width), lambda g, s: (0, s[1], 0)),
                pl.BlockSpec((own_up, qkv_columns), lambda g, s: (s[1], 0)),
                pl.BlockSpec((own_up, width), lambda g, s: (s[1], 0)),
            ],
            out_specs=[whole(*o.shape) for o in outs[:-1]] + [pl.BlockSpec(memory_space=pltpu.SMEM)],
        ),
        compiler_params=pltpu.CompilerParams(vmem_limit_bytes=VM),
        cost_estimate=lasts(6),
        name="update",
    )(
        jnp.stack([lax.rem(me // PAIR, 2), me]),
        *owns, *gots, *finished, *row_statistics, middle, *mixes, up_w, down_w, qkv_w, out_w,
    )


D = 1024
FF = 512
TOP = 8


def swap(values, axis, mask):
    count = lax.axis_size(axis)
    return lax.ppermute(values, axis, [(i, i ^ mask) for i in range(count)])


def swap_pair(values):
    return swap(values, "dp", PAIR)


def swap_chip(values):
    return swap(values, "expert", 2)


def swap_core(values):
    return swap(values, "expert", 1)


def plus(a, b):
    return (a.astype(jnp.float32) + b.astype(jnp.float32)).astype(jnp.bfloat16)


def halve(blocks, axis, mask):
    bit = lax.rem(lax.axis_index(axis) // mask, 2)
    keep = lax.dynamic_index_in_dim(blocks, bit, 1, keepdims=False)
    give = lax.dynamic_index_in_dim(blocks, 1 - bit, 1, keepdims=False)
    return keep, swap(give, axis, mask)


def reduce_dense_far(blocks):
    count = lax.axis_size("dp")
    width, columns = blocks.shape
    rows = width // count
    blocks = blocks.reshape(count, 2, 2, rows // 4, columns)
    keep, got = halve(jnp.moveaxis(blocks, 2, 1), "expert", 1)
    keep, got = halve(plus(keep, got), "expert", 2)
    blocks = plus(keep, got)
    low = 1
    while low < count:
        keep, got = halve(blocks.reshape((-1, 2, 1) + blocks.shape[1:]), "dp", low)
        blocks = plus(keep, got).reshape((-1,) + blocks.shape[1:])
        low *= 2
    mine = blocks[0]
    chip = lax.axis_index("expert") // 2
    core = lax.rem(lax.axis_index("expert"), 2)
    other = swap_chip(mine)
    both = jnp.where(chip == 0, jnp.stack([mine, other]), jnp.stack([other, mine]))
    across = swap_core(both)
    all_four = jnp.where(core == 0, jnp.stack([both, across], 1), jnp.stack([across, both], 1))
    return all_four.reshape(rows, columns)


def own_share(matrix, along):
    count = lax.axis_size("dp")
    width = matrix.shape[along] // count
    return lax.dynamic_slice_in_dim(matrix, lax.axis_index("dp") * width, width, along)


def factored(part, rows_old):
    square = part * part
    rows_new = decayed(rows_old, jnp.mean(square + EPS_STAT, axis=-1))
    return (
        rows_new,
        jnp.sum(square + EPS_STAT, axis=-2),
        jnp.sum(square / rows_new[..., None], axis=-2),
    )


def per_device(
    hidden_in,
    out_grad,
    segment_ids,
    parent_ids,
    positions,
    expert_ids,
    gate_weights,
    norm_gains,
    qkv_weight,
    out_weight,
    gate_up_weight,
    down_weight,
    gain_moment,
    qkv_rows,
    qkv_cols,
    out_rows,
    out_cols,
    gateup_rows,
    gateup_cols,
    down_rows,
    down_cols,
):
    rows_here = hidden_in.shape[0]
    dp_count = lax.axis_size("dp")
    groups = lax.axis_size("expert")
    experts_here = gate_up_weight.shape[0]
    total_experts = experts_here * groups
    capacity = 3 * rows_here * TOP // (2 * total_experts)
    half_experts = experts_here // 2
    dp_index = lax.axis_index("dp")
    pair_bit = lax.rem(dp_index // PAIR, 2)
    first_local = pair_bit * half_experts
    first_expert = lax.axis_index("expert") * experts_here + first_local

    weight_high = gate_weights.astype(jnp.bfloat16)
    weight_low = (gate_weights - weight_high.astype(jnp.float32)).astype(jnp.bfloat16)
    routing = jnp.concatenate([expert_ids.astype(jnp.bfloat16), weight_high, weight_low], axis=1).T
    routing = jnp.pad(routing, ((0, ROUTE_ROWS - routing.shape[0]), (0, D - rows_here)))
    grad_rows = jnp.concatenate([out_grad.astype(jnp.bfloat16), routing], axis=0)
    chip_grad_rows = swap_chip(grad_rows)
    pair_grad_rows = swap_pair(grad_rows)
    ids = jnp.stack([segment_ids, parent_ids, positions])
    normed, qkv, attended, lse, middle, normed_ffn = attend(
        hidden_in, ids, norm_gains, qkv_weight, out_weight
    )
    received, arrived, scale, code = gather_and_select(
        normed_ffn, grad_rows, chip_grad_rows, pair_grad_rows, capacity, experts_here, half_experts, TOP, 5
    )
    scalars = jnp.stack([first_local, lax.rem(dp_index, 2)])
    experts, chains = [], []

    def advance(which, after, comes=(), passed=()):
        comes = dict(comes)
        groups = []
        for j in which:
            masks, stay, go = chains[j]
            groups.append((stay, comes[j] if j in comes else swap(go, "dp", masks[0]), masks[1]))
        label = "_".join("%d_%d" % (j, chains[j][0][1]) for j in which)
        sides, passed = settle(groups, label, after, passed)
        for j, (stay, go) in zip(which, sides):
            chains[j] = (chains[j][0][1:], stay, go)
        return [chains[j][1] for j in which], passed

    masks = [1] + [1 << b for b in range(2, dp_count.bit_length() - 1)] + [PAIR]
    for j in range(half_experts):
        after = [experts[-1][2]] if experts else []
        if j == 3:
            after += advance([0], after)[0]
        experts.append(
            run_expert(
                scalars, j, received, arrived, scale, gate_up_weight, down_weight, dp_count, after
            )
        )
        chains.append((masks, experts[j][0], experts[j][1]))
    mine, theirs = combine(code, [e[2] for e in experts], capacity, [])
    steps, _ = advance([1], [mine])
    normed_f_grad, near_mix, far_mix, come = return_sums(
        code, mine, theirs, [e[3] for e in experts], capacity, chains[1][2], chains[1][0][0], 6, steps
    )
    steps, (far_mix,) = advance([2, 0, 1], [normed_f_grad], [(1, come)], [far_mix])
    input_grad, dense = attend_back(
        hidden_in, out_grad, middle, normed_f_grad, normed, qkv, attended, lse, ids, norm_gains, qkv_weight,
        out_weight, steps
    )
    got_mix = swap_chip(far_mix)
    qkv_columns = qkv_weight.shape[1]
    fast_tail = dp_count == experts_here and D // dp_count % 64 == 0
    if fast_tail:
        owns = [chains[j][1][0] for j in (0, 1)]
        gots = [swap_pair(chains[j][2][0]) for j in (0, 1)]
        settling = []
        for j in (2, 3):
            masks, stay, go = chains[j]
            settling += [stay, swap(go, "dp", masks[0])]
        settling[2:] = [x.reshape((2, 2) + x.shape[1:]) for x in settling[2:]]
        finished = finish(
            dense,
            owns,
            gots,
            settling,
            (near_mix, got_mix),
            (
                gateup_rows,
                down_rows,
                gateup_cols,
                down_cols,
                qkv_rows[None],
                out_rows[None],
                gain_moment,
                qkv_cols[None],
                out_cols[None],
            ),
            1,
        )
        (
            block_out,
            gate_up_new,
            down_new,
            gateup_rows_new,
            down_rows_new,
            gateup_cols_new,
            down_cols_new,
            qkv_new,
            out_new,
            qkv_cols_new,
            out_cols_new,
            qkv_rows_new,
            out_rows_new,
            gains_update,
            gain_moment_new,
            update_rms,
        ) = update(
            owns,
            gots,
            finished,
            (qkv_rows[None], out_rows[None]),
            middle,
            (near_mix, got_mix),
            gate_up_weight,
            down_weight,
            qkv_weight,
            out_weight,
        )
        qkv_cols_new, out_cols_new = qkv_cols_new[0], out_cols_new[0]
        qkv_rows_new, out_rows_new = qkv_rows_new[0], out_rows_new[0]
    else:
        for_pair = settle_mix(near_mix, got_mix, [input_grad])
        mix_parts = (near_mix[0], got_mix[0], swap_pair(for_pair))
        block_out = middle + sum(part.astype(jnp.float32) for part in mix_parts)
        dense_own = reduce_dense_far(dense)
        for j in range(half_experts):
            while len(chains[j][0]) > 1:
                advance([j], [dense_own])
        own_parts = [c[1][0] for c in chains]
        other_parts = [swap_pair(c[2][0]) for c in chains]
        own = jnp.stack(own_parts).astype(jnp.float32)
        other = jnp.stack(other_parts).astype(jnp.float32)
        parts = jnp.where(pair_bit == 0, jnp.concatenate([own, other]), jnp.concatenate([other, own]))
        gateup_part = parts[:, : D // dp_count]
        down_part = parts[:, D // dp_count :]
        gateup_rows_new, gateup_square, gateup_scaled = factored(gateup_part, own_share(gateup_rows, 1))
        down_rows_new, down_square, down_scaled = factored(down_part, own_share(down_rows, 1))
        sizes = [gateup_square.size, gateup_scaled.size, down_square.size, down_scaled.size]
        summed = total_over(
            jnp.concatenate(
                [
                    gateup_square.reshape(-1),
                    gateup_scaled.reshape(-1),
                    down_square.reshape(-1),
                    down_scaled.reshape(-1),
                    jnp.sum(gateup_rows_new, axis=1),
                    jnp.sum(down_rows_new, axis=1),
                ]
            ),
            "dp",
            1,
        )
        pieces = jnp.split(summed, [sum(sizes[: i + 1]) for i in range(4)])
        gateup_square, gateup_scaled, down_square, down_scaled = [
            p.reshape(experts_here, D) for p in pieces[:4]
        ]
        gateup_row_mean = pieces[4][:experts_here] / D
        down_row_mean = pieces[4][experts_here:] / FF
        gateup_cols_new = decayed(gateup_cols, gateup_square / D)
        down_cols_new = decayed(down_cols, down_square / FF)
        expert_squares = jnp.stack(
            [
                jnp.sum(gateup_row_mean * jnp.sum(gateup_scaled / gateup_cols_new, axis=1)),
                jnp.sum(down_row_mean * jnp.sum(down_scaled / down_cols_new, axis=1)),
            ]
        )
        spread_squares = collect(
            jnp.zeros((8, 128), jnp.float32).at[0, :2].set(expert_squares), "expert", 2
        )
        expert_squares = jnp.sum(spread_squares[:, 0, :2], axis=0)
        dense_own = dense_own.astype(jnp.float32)
        qkv_own = dense_own[:, :qkv_columns]
        out_own = dense_own[:, qkv_columns : qkv_columns + D]
        gains_own = dense_own[:, qkv_columns + D : qkv_columns + D + 2].T
        gain_moment_new = decayed(own_share(gain_moment, 1), gains_own * gains_own + EPS_STAT)
        gains_step = gains_own * lax.rsqrt(gain_moment_new)
        qkv_rows_new, qkv_square, qkv_scaled = factored(qkv_own, own_share(qkv_rows, 0))
        out_rows_new, out_square, out_scaled = factored(out_own, own_share(out_rows, 0))
        dense_sums = total_over(
            jnp.concatenate(
                [
                    qkv_square,
                    qkv_scaled,
                    out_square,
                    out_scaled,
                    jnp.stack(
                        [jnp.sum(qkv_rows_new), jnp.sum(out_rows_new), jnp.sum(gains_step * gains_step)]
                    ),
                ]
            ),
            "dp",
            4,
        )
        qkv_square, qkv_scaled, out_square, out_scaled, rest = jnp.split(
            dense_sums, [qkv_columns, 2 * qkv_columns, 2 * qkv_columns + D, 2 * qkv_columns + 2 * D]
        )
        qkv_row_mean = rest[0] / D
        out_row_mean = rest[1] / D
        qkv_cols_new = decayed(qkv_cols, qkv_square / D)
        out_cols_new = decayed(out_cols, out_square / D)
        squares = jnp.concatenate(
            [
                jnp.stack(
                    [
                        rest[2],
                        qkv_row_mean * jnp.sum(qkv_scaled / qkv_cols_new),
                        out_row_mean * jnp.sum(out_scaled / out_cols_new),
                    ]
                ),
                expert_squares,
            ]
        )
        element_counts = jnp.array(
            [2 * D, D * qkv_columns, D * D, total_experts * D * 2 * FF, total_experts * FF * D], jnp.float32
        )
        update_rms = jnp.sqrt(squares / element_counts)
        factors = LEARN_RATE / jnp.maximum(1.0, update_rms / CLIP_LEVEL)

        def stepped(weight, part, rows_new, row_mean, cols_new, factor):
            return weight.astype(jnp.float32) - part * (
                factor * lax.rsqrt(rows_new / row_mean[..., None])
            )[..., :, None] * lax.rsqrt(cols_new)[..., None, :]

        gains_update = -factors[0] * gains_step
        qkv_new = stepped(own_share(qkv_weight, 0), qkv_own, qkv_rows_new, qkv_row_mean, qkv_cols_new, factors[1])
        out_new = stepped(own_share(out_weight, 0), out_own, out_rows_new, out_row_mean, out_cols_new, factors[2])
        gate_up_new = stepped(
            own_share(gate_up_weight, 1), gateup_part, gateup_rows_new, gateup_row_mean, gateup_cols_new, factors[3]
        )
        down_new = stepped(
            own_share(down_weight, 1), down_part, down_rows_new, down_row_mean, down_cols_new, factors[4]
        )
    return (
        block_out,
        input_grad,
        update_rms,
        gains_update,
        gain_moment_new,
        qkv_new,
        qkv_rows_new,
        qkv_cols_new,
        out_new,
        out_rows_new,
        out_cols_new,
        gate_up_new,
        gateup_rows_new,
        gateup_cols_new,
        down_new,
        down_rows_new,
        down_cols_new,
    )


def solution(mesh):
    placed = (
        P(("dp", "expert"), None),
        P(("dp", "expert"), None),
        P(("dp", "expert")),
        P(("dp", "expert")),
        P(("dp", "expert")),
        P(("dp", "expert"), None),
        P(("dp", "expert"), None),
        P(),
        P(),
        P(),
        P("expert", None, None),
        P("expert", None, None),
        P(),
        P(),
        P(),
        P(),
        P(),
        P("expert", None),
        P("expert", None),
        P("expert", None),
        P("expert", None),
    )
    return jax.shard_map(
        per_device,
        mesh=mesh,
        in_specs=placed,
        out_specs=(
            P(("dp", "expert"), None),
            P(("dp", "expert"), None),
            P(),
            P(None, "dp"),
            P(None, "dp"),
            P("dp", None),
            P("dp"),
            P(),
            P("dp", None),
            P("dp"),
            P(),
            P("expert", "dp", None),
            P("expert", "dp"),
            P("expert", None),
            P("expert", "dp", None),
            P("expert", "dp"),
            P("expert", None),
        ),
        check_vma=False,
    )
```
